32 devices in a mesh: grp: 4 (over z), sub: 8 (over y, x, core).
Axes of the slice: x: 2, y: 2, z: 4, core: 2. Of those that a mesh axis runs over, the one named last changes fastest.
Arguments:
- right_side: float32 [512, 512], P(('grp', 'sub')), may hold values from -8 to 8
- metric: float32 [512, 1536], P(('grp', 'sub')), may hold values from 0.3 to 3
- helmholtz: float32 [512, 512], P(('grp', 'sub')), may hold values from 0.5 to 2
- jacobi: float32 [512, 512], P(('grp', 'sub')), may hold values from 0.05 to 0.5
- pair_list: int32 [2, 32768], P(None, ('grp', 'sub')), may hold values from 0 to 8191
- shared_slots: int32 [32, 8, 128], P(('grp', 'sub')), may hold values from 0 to 8192, as said below
- face_points: int32 [2, 16384], P(None, ('grp', 'sub')), may hold values from 0 to 8191
- coarse_map: int32 [8, 512], P(None, ('grp', 'sub')), may hold values from 0 to 63
- coarse_inverse: float32 [4, 64, 64], P('grp'), as said below
Outputs:
- solution: float32 [512, 512], P(('grp', 'sub'))
- residual: float32 [512, 512], P(('grp', 'sub'))
The draws below stay inside these ranges and needn't reach their ends.
Inputs may be any that keep to these rules, and one draw needn't show every extreme that they name: `shared_slots`: entries equal to 8192 mark empty slots; the slot of device a for peer b in one group is filled exactly when the slot of b for a at the same position is; a device's slots for itself are empty; filled slots come first in each row. `coarse_inverse`: each group's matrix is symmetric and positive definite.
All inputs are finite; a program needn't handle non-finite values.
Results may differ from the reference program's by a relative error of at most 0.0003.
Values sent between devices are 32-bit elements; how exact they have to be, the bound alone decides.
No kernel may reach another device: no remote copies, remote signals or barrier semaphores. Data moves between devices by JAX's collectives and lax.ppermute only.
A program may use at most 64 MiB of HBM per device.

```python
import math
import jax
import jax.numpy as jnp
import numpy as np
from jax import lax

POINTS = 512
E_DEV = 16
CAP = 128
ITERS = 2
LP = 1024
FC = 512
NC = 64
ELEMENTS = 512
N_GRP = 4
N_SUB = 8
DEVICES = 32


def draw_shared_slots(key, part):
    key_near, key_count, key_index = jax.random.split(key, 3)
    first_peer = jnp.arange(N_SUB, dtype=jnp.int32)[None, :, None]
    second_peer = jnp.arange(N_SUB, dtype=jnp.int32)[None, None, :]
    upper = first_peer < second_peer
    near = (jax.random.randint(key_near, (N_GRP, N_SUB, N_SUB), 0, 10) < 7).astype(jnp.int32)
    counts = jax.random.randint(key_count, (N_GRP, N_SUB, N_SUB), 3 * CAP // 8, CAP + 1)
    near = jnp.where(upper, near, jnp.swapaxes(near, 1, 2))
    counts = jnp.where(upper, counts, jnp.swapaxes(counts, 1, 2))
    pinned = (first_peer == 0) & (second_peer == 1) | (first_peer == 1) & (second_peer == 0)
    counts = jnp.where(pinned, CAP, jnp.where(near == 1, counts, 0))
    counts = jnp.where(first_peer == second_peer, 0, counts)
    indices = jax.random.randint(key_index, (N_GRP, N_SUB, N_SUB, CAP), 0, E_DEV * 512)
    position = jnp.arange(CAP, dtype=jnp.int32)[None, None, None, :]
    filled = position < counts[:, :, :, None]
    slots = jnp.where(filled, indices, E_DEV * 512)
    return slots.reshape(N_GRP * N_SUB, N_SUB, CAP).astype(jnp.int32)


def draw_coarse_inverse(key, part):
    key_off, key_diag = jax.random.split(key, 2)
    mixed = jax.random.uniform(key_off, (N_GRP, NC, NC), jnp.float32, -1.0, 1.0)
    symmetric = 0.5 * (mixed + jnp.swapaxes(mixed, 1, 2))
    diagonal = jax.random.uniform(key_diag, (N_GRP, NC), jnp.float32, 0.002, 0.004)
    row_index = jnp.arange(NC)[:, None]
    column_index = jnp.arange(NC)[None, :]
    result = jnp.where((row_index == column_index)[None, :, :], diagonal[:, :, None], 0.002 * symmetric / NC)
    return result.astype(jnp.float32)


def with_ends(array, key, low, largest):
    shape = array.shape
    index_at = [jax.random.randint(jax.random.fold_in(key, axis), (), 0, shape[axis]) for axis in range(len(shape))]
    array = array.at[tuple(index_at)].set(low)
    longest = shape.index(max(shape))
    index_at[longest] = (index_at[longest] + 1) % shape[longest]
    return array.at[tuple(index_at)].set(largest)


def shard_levels(own_key, shape, shards, smallest, high):
    def one(dim, parts):
        heights = jax.random.uniform(jax.random.fold_in(jax.random.fold_in(own_key, 6), dim), (parts,), jnp.float32, smallest / len(shards), high / len(shards))
        return jnp.repeat(jnp.exp(heights), shape[dim] // parts).reshape((-1,) + (1,) * (len(shape) - dim - 1))

    level = one(*shards[0])
    for cut in shards[1:]:
        level = level * one(*cut)
    return level


def gaussian(stream_key, dims, scale, reach, shards=(), kind=jnp.bfloat16):
    gain = shard_levels(stream_key, dims, shards, -0.22, 0.18) if shards else 1.0
    array = jax.random.normal(stream_key, dims, jnp.float32) * scale * gain
    return jnp.minimum(jnp.maximum(array, -reach), reach).astype(kind)


def setup_inputs(seed: int = 0) -> dict:
    seeds = jax.random.split(jax.random.key(seed), 10)
    return {
        "right_side": gaussian(seeds[0], (ELEMENTS, POINTS), 1.0, 8.0, ((0, 32),), jnp.float32),
        "metric": jnp.clip(jnp.exp(math.log(3.0) - 2.3025851 * jax.random.uniform(seeds[1], (ELEMENTS, 3 * POINTS), jnp.float32) ** shard_levels(seeds[1], (ELEMENTS, 3 * POINTS), ((0, 32),), -0.2, 0.2)), 0.3, 3.0),
        "helmholtz": jnp.clip(jnp.exp(math.log(2.0) - 1.3862944 * jax.random.uniform(seeds[2], (ELEMENTS, POINTS), jnp.float32) ** shard_levels(seeds[2], (ELEMENTS, POINTS), ((0, 32),), -0.2, 0.2)), 0.5, 2.0),
        "jacobi": jnp.clip(jnp.exp(math.log(0.5) - 2.3025851 * jax.random.uniform(seeds[3], (ELEMENTS, POINTS), jnp.float32) ** shard_levels(seeds[3], (ELEMENTS, POINTS), ((0, 32),), -0.2, 0.2)), 0.05, 0.5),
        "pair_list": with_ends(jax.random.randint(seeds[4], (2, LP * DEVICES), 0, E_DEV * 512), jax.random.fold_in(seeds[4], 1), 0, (E_DEV * 512) - 1).astype(jnp.int32),
        "shared_slots": draw_shared_slots(jax.random.fold_in(seeds[9], 71), 0),
        "face_points": with_ends(jax.random.randint(seeds[6], (2, FC * DEVICES), 0, E_DEV * 512), jax.random.fold_in(seeds[6], 1), 0, (E_DEV * 512) - 1).astype(jnp.int32),
        "coarse_map": with_ends(jax.random.randint(seeds[7], (8, ELEMENTS), 0, NC), jax.random.fold_in(seeds[7], 1), 0, NC - 1).astype(jnp.int32),
        "coarse_inverse": draw_coarse_inverse(jax.random.fold_in(seeds[9], 71), 0),
    }


def tables():
    order_index = np.arange(8)
    colloc = np.cos(np.pi * order_index / 7.0)
    end_weights = np.where((order_index == 0) | (order_index == 7), 2.0, 1.0) * (-1.0) ** order_index
    spacing = colloc[:, None] - colloc[None, :] + np.eye(8)
    raw_matrix = np.outer(end_weights, 1.0 / end_weights) / spacing
    off_part = raw_matrix * (1.0 - np.eye(8))
    derivative = 0.25 * (off_part - np.eye(8) * off_part.sum(axis=1)[:, None])
    point_index = np.arange(512)
    corner_index = np.arange(8)
    sign_first = 1.0 - 2.0 * ((corner_index >> 2) & 1)
    sign_second = 1.0 - 2.0 * ((corner_index >> 1) & 1)
    sign_third = 1.0 - 2.0 * (corner_index & 1)
    node_first = colloc[point_index // 64][:, None]
    node_second = colloc[(point_index // 8) % 8][:, None]
    node_third = colloc[point_index % 8][:, None]
    corner = (0.5 * (1.0 + sign_first[None, :] * node_first)) * (0.5 * (1.0 + sign_second[None, :] * node_second)) * (0.5 * (1.0 + sign_third[None, :] * node_third))
    return jnp.asarray(derivative, jnp.float32), jnp.asarray(corner, jnp.float32)


def reference(right_side, metric, helmholtz, jacobi, pair_list, shared_slots, face_points, coarse_map, coarse_inverse):
    derivative, corner = tables()
    highest = lax.Precision.HIGHEST
    points = E_DEV * 512
    devices_all = N_GRP * N_SUB

    def assemble(field):
        flat = field.reshape(-1)
        owner = jnp.arange(devices_all * LP, dtype=jnp.int32) // LP
        first = owner * points + pair_list[0]
        second = owner * points + pair_list[1]
        total = flat.at[first].add(flat[second]).at[second].add(flat[first])
        by_device = field.reshape(devices_all, points)
        padded = jnp.concatenate([by_device, jnp.zeros((devices_all, 1), jnp.float32)], axis=1)
        slots = shared_slots.reshape(devices_all, N_SUB * CAP)
        sent = jnp.take_along_axis(padded, slots, axis=1).reshape(N_GRP, N_SUB, N_SUB, CAP)
        received = jnp.swapaxes(sent, 1, 2).reshape(devices_all, N_SUB * CAP)
        row_base = (jnp.arange(devices_all, dtype=jnp.int32) * (points + 1))[:, None]
        spread = jnp.zeros((devices_all * (points + 1),), jnp.float32)
        spread = spread.at[(row_base + slots).reshape(-1)].add(received.reshape(-1))
        total = total + spread.reshape(devices_all, points + 1)[:, :points].reshape(-1)
        faces = face_points.reshape(2, devices_all, FC)
        values_down = jnp.take_along_axis(by_device, faces[0], axis=1).reshape(N_GRP, N_SUB, FC)
        values_up = jnp.take_along_axis(by_device, faces[1], axis=1).reshape(N_GRP, N_SUB, FC)
        zero_row = jnp.zeros((1, N_SUB, FC), jnp.float32)
        into_down = jnp.concatenate([zero_row, values_up[:-1]], axis=0).reshape(-1)
        into_up = jnp.concatenate([values_down[1:], zero_row], axis=0).reshape(-1)
        base = (jnp.arange(devices_all, dtype=jnp.int32) * points)[:, None]
        total = total.at[(base + faces[0]).reshape(-1)].add(into_down)
        total = total.at[(base + faces[1]).reshape(-1)].add(into_up)
        return total.reshape(field.shape)

    def stiffness(field):
        cube = field.reshape(-1, 8, 8, 8)
        grad_first = jnp.einsum('ai,eijk->eajk', derivative, cube, precision=highest)
        grad_second = jnp.einsum('bj,eijk->eibk', derivative, cube, precision=highest)
        grad_third = jnp.einsum('ck,eijk->eijc', derivative, cube, precision=highest)
        flux_first = metric[:, :512].reshape(-1, 8, 8, 8) * grad_first
        flux_second = metric[:, 512:1024].reshape(-1, 8, 8, 8) * grad_second
        flux_third = metric[:, 1024:].reshape(-1, 8, 8, 8) * grad_third
        back = jnp.einsum('ai,eajk->eijk', derivative, flux_first, precision=highest)
        back = back + jnp.einsum('bj,eibk->eijk', derivative, flux_second, precision=highest)
        back = back + jnp.einsum('ck,eijc->eijk', derivative, flux_third, precision=highest)
        return back.reshape(-1, 512)

    def operate(field):
        return assemble(stiffness(assemble(field))) + helmholtz * field

    group_of = jnp.arange(ELEMENTS, dtype=jnp.int32) // (E_DEV * N_SUB)
    vertex_ids = group_of[:, None] * NC + coarse_map.T

    def precondition(resid):
        vertex = jnp.dot(resid, corner, precision=highest)
        coarse = jax.ops.segment_sum(vertex.reshape(-1), vertex_ids.reshape(-1), num_segments=N_GRP * NC).reshape(N_GRP, NC)
        solved = jnp.einsum('gij,gj->gi', coarse_inverse, coarse, precision=highest)
        at_vertex = solved.reshape(-1)[vertex_ids]
        return jacobi * resid + jnp.dot(at_vertex, corner.T, precision=highest)

    solution = jnp.zeros_like(right_side)
    residual = right_side
    smoothed = precondition(residual)
    direction = smoothed
    rz_now = jnp.sum(residual * smoothed)
    for iteration in range(ITERS):
        image = operate(direction)
        alpha = rz_now / jnp.sum(direction * image)
        solution = solution + alpha * direction
        residual = residual - alpha * image
        if iteration + 1 < ITERS:
            smoothed = precondition(residual)
            rz_new = jnp.sum(residual * smoothed)
            direction = smoothed + (rz_new / rz_now) * direction
            rz_now = rz_new
    return solution, residual
```

```python
import jax
import jax.numpy as jnp
import ml_dtypes
import numpy as np
from jax import lax
from jax.experimental import pallas as pl
from jax.experimental.pallas import tpu as pltpu
from jax.sharding import PartitionSpec as P

NC = 64
POINTS = 512
LANES = 128
STEP = 256
F32 = jnp.float32
BF16 = jnp.bfloat16
NT = (((1,), (1,)), ((), ()))


def split_constant(array):
    high = array.astype(ml_dtypes.bfloat16)
    low = (array - high.astype(np.float64)).astype(ml_dtypes.bfloat16)
    return high, low


def tables(elements):
    order_index = np.arange(8)
    colloc = np.cos(np.pi * order_index / 7.0)
    end_weights = (
        np.where((order_index == 0) | (order_index == 7), 2.0, 1.0) * (-1.0) ** order_index
    )
    spacing = colloc[:, None] - colloc[None, :] + np.eye(8)
    raw_matrix = np.outer(end_weights, 1.0 / end_weights) / spacing
    off_part = raw_matrix * (1.0 - np.eye(8))
    derivative = 0.25 * (off_part - np.eye(8) * off_part.sum(axis=1)[:, None])
    along_inner = np.concatenate(
        [np.kron(np.eye(2), np.kron(derivative, np.eye(8))).T, np.kron(np.eye(16), derivative).T],
        axis=1,
    )
    high, low = split_constant(along_inner)
    inner = np.concatenate([high, high, low], axis=0)
    inner_back = np.concatenate([high.T, high.T, low.T], axis=0)

    half = np.arange(LANES) // 64

    def first_rows(matrix):
        rows = []
        for to in range(4):
            for at in range(4):
                rows.append(matrix[2 * to + half, 2 * at + half])
                rows.append(matrix[2 * to + half, 2 * at + 1 - half])
        return np.stack(rows).astype(np.float32)

    point_index = np.arange(POINTS)
    corner_index = np.arange(8)
    sign_first = 1.0 - 2.0 * (corner_index >> 2 & 1)
    sign_second = 1.0 - 2.0 * (corner_index >> 1 & 1)
    sign_third = 1.0 - 2.0 * (corner_index & 1)
    node_first = colloc[point_index // 64][:, None]
    node_second = colloc[point_index // 8 % 8][:, None]
    node_third = colloc[point_index % 8][:, None]
    corner = (
        0.5
        * (1.0 + sign_first[None, :] * node_first)
        * (0.5 * (1.0 + sign_second[None, :] * node_second))
        * (0.5 * (1.0 + sign_third[None, :] * node_third))
    )
    corner_high, corner_low = split_constant(np.repeat(corner.T, elements, axis=0))
    spread = np.tile(np.eye(elements), (1, 8)).astype(np.float32)
    return {
        "inner": inner,
        "inner_back": inner_back,
        "first": first_rows(derivative),
        "first_back": first_rows(derivative.T),
        "corner_high": corner_high,
        "corner_low": corner_low,
        "spread": spread,
    }


def split(value):
    high = value.astype(BF16)
    return high, (value - high.astype(F32)).astype(BF16)


def rows_of(wide):
    return jnp.concatenate([wide[:, LANES * c : LANES * (c + 1)] for c in range(4)], axis=0)


def wide_of(rows):
    elements = rows.shape[0] // 4
    return jnp.concatenate([rows[c * elements : (c + 1) * elements] for c in range(4)], axis=1)


def locate(points, elements):
    element = points >> 9
    chunk = (points >> 7) & 3
    row = jnp.where(points < elements * POINTS, chunk * elements + element, 4 * elements)
    return row, points & (LANES - 1)


def one_hot(index, count):
    steps = lax.broadcasted_iota(jnp.int32, (count, index.shape[1]), 0)
    return steps == index


def gather(field, chunks):
    high, low = split(field)
    both = jnp.concatenate([high, low], axis=1)
    out = []
    for row, lane in chunks:
        lanes = one_hot(lane, LANES).astype(F32).astype(BF16)
        picked = jnp.dot(
            both, jnp.concatenate([lanes, lanes], axis=0), preferred_element_type=F32
        )
        out.append(
            jnp.sum(
                jnp.where(one_hot(row, field.shape[0]), picked, 0.0), axis=0, keepdims=True
            )
        )
    return out


def scatter(rows, chunks, values):
    total = jnp.zeros((2 * rows, LANES), F32)
    for (row, lane), value in zip(chunks, values):
        lanes = one_hot(lane, LANES).astype(F32).astype(BF16)
        high, low = split(jnp.where(one_hot(row, rows), value, 0.0))
        total = total + lax.dot_general(
            jnp.concatenate([high, low], axis=0), lanes, NT, preferred_element_type=F32
        )
    return total[:rows] + total[rows:]


def chunked(row, lane):
    return [
        (row[:, at : at + STEP], lane[:, at : at + STEP]) for at in range(0, row.shape[1], STEP)
    ]


def cut(row):
    return [row[:, at : at + STEP] for at in range(0, row.shape[1], STEP)]


def index_chunks(pair_ref, slot_ref, face_ref, elements):
    pair_row, pair_lane = locate(pair_ref[...], elements)
    slot_row, slot_lane = locate(slot_ref[0], elements)
    face_row, face_lane = locate(face_ref[...], elements)
    pairs = chunked(pair_row[0:1], pair_lane[0:1]) + chunked(pair_row[1:2], pair_lane[1:2])
    slots = []
    for at in range(0, slot_row.shape[0], 2):
        slots.append(
            tuple(
                jnp.concatenate([part[at : at + 1], part[at + 1 : at + 2]], axis=1)
                for part in (slot_row, slot_lane)
            )
        )
    faces = chunked(face_row[0:1], face_lane[0:1]) + chunked(face_row[1:2], face_lane[1:2])
    return pairs, slots, faces


def gather_all(field, refs, outs):
    pair_ref, slot_ref, face_ref = refs
    local_ref, sent_ref, down_ref, up_ref = outs
    pairs, slots, faces = index_chunks(pair_ref, slot_ref, face_ref, field.shape[0] // 4)
    values = gather(field, pairs + slots + faces)
    count = pair_ref.shape[1] // STEP
    for k in range(count):
        local_ref[0:1, k * STEP : (k + 1) * STEP] = values[k]
        local_ref[1:2, k * STEP : (k + 1) * STEP] = values[count + k]
    values = values[2 * count :]
    for k in range(len(slots)):
        sent_ref[2 * k : 2 * k + 1, 0:LANES] = values[k][:, :LANES]
        sent_ref[2 * k + 1 : 2 * k + 2, 0:LANES] = values[k][:, LANES:]
    values = values[len(slots) :]
    count = face_ref.shape[1] // STEP
    for k in range(count):
        down_ref[0:1, k * STEP : (k + 1) * STEP] = values[k]
        up_ref[0:1, k * STEP : (k + 1) * STEP] = values[count + k]


def assembled(field, refs, local, received, below, above):
    pair_ref, slot_ref, face_ref = refs
    pairs, slots, faces = index_chunks(pair_ref, slot_ref, face_ref, field.shape[0] // 4)
    values = cut(local[1:2]) + cut(local[0:1])
    for at in range(0, received.shape[0], 2):
        values.append(jnp.concatenate([received[at : at + 1], received[at + 1 : at + 2]], axis=1))
    values = values + cut(below) + cut(above)
    return field + scatter(field.shape[0], pairs + slots + faces, values)


def along_first(field, table_ref):
    elements = field.shape[0] // 4
    turned = pltpu.roll(field, 64, axis=1)
    out = []
    for to in range(4):
        total = None
        for at in range(4):
            place = 2 * (4 * to + at)
            rows = slice(at * elements, (at + 1) * elements)
            term = (
                table_ref[place : place + 1, :] * field[rows]
                + table_ref[place + 1 : place + 2, :] * turned[rows]
            )
            total = term if total is None else total + term
        out.append(total)
    return jnp.concatenate(out, axis=0)


def stiffness(field, metric_ref, first_ref, first_back_ref, inner_ref, inner_back_ref):
    metric = [rows_of(metric_ref[:, POINTS * d : POINTS * (d + 1)]) for d in range(3)]
    grad_first = along_first(field, first_ref)
    high, low = split(field)
    inner = jnp.dot(
        jnp.concatenate([high, low, high], axis=1), inner_ref[...], preferred_element_type=F32
    )
    flux_first = metric[0] * grad_first
    flux = jnp.concatenate([metric[1], metric[2]], axis=1) * inner
    high, low = split(flux)
    back = along_first(flux_first, first_back_ref) + jnp.dot(
        jnp.concatenate([high, low, high], axis=1), inner_back_ref[...], preferred_element_type=F32
    )
    energy = flux * inner
    return back, flux_first * grad_first + energy[:, :LANES] + energy[:, LANES:]


def vertex_map(map_ref, spread_ref):
    wide = jnp.dot(
        map_ref[...].astype(F32),
        spread_ref[...],
        precision=lax.Precision.HIGHEST,
        preferred_element_type=F32,
    )
    corners, width = wide.shape
    own = lax.broadcasted_iota(jnp.int32, wide.shape, 0) == (
        lax.broadcasted_iota(jnp.int32, wide.shape, 1) // (width // corners)
    )
    flat = jnp.sum(jnp.where(own, wide, 0.0), axis=0, keepdims=True)
    flat = (flat + 0.5).astype(jnp.int32)
    return jnp.where(one_hot(flat, NC), 1.0, 0.0)


def own_element(elements, width):
    shape = (elements, width)
    return lax.broadcasted_iota(jnp.int32, shape, 0) == (
        lax.broadcasted_iota(jnp.int32, shape, 1) % elements
    )


def coarse_part(wide, vertices, corner_high_ref, corner_low_ref):
    elements = wide.shape[0]
    high, low = split(wide)
    both = lax.dot_general(
        jnp.concatenate([high, low], axis=0), corner_high_ref[...], NT, preferred_element_type=F32
    )
    inner = (
        both[:elements]
        + both[elements:]
        + lax.dot_general(high, corner_low_ref[...], NT, preferred_element_type=F32)
    )
    inner = jnp.where(own_element(elements, inner.shape[1]), inner, 0.0)
    flat = jnp.sum(inner, axis=0, keepdims=True)
    return lax.dot_general(
        jnp.broadcast_to(flat, (8, flat.shape[1])),
        vertices,
        NT,
        precision=lax.Precision.HIGHEST,
        preferred_element_type=F32,
    )[0:1]


def prolonged(coarse, inverse_ref, vertices, elements, corner_high_ref, corner_low_ref):
    solved = jnp.sum(inverse_ref[0] * coarse, axis=1, keepdims=True)
    flat = jnp.sum(vertices * solved, axis=0, keepdims=True)
    spread = jnp.where(own_element(elements, flat.shape[1]), flat, 0.0)
    high, low = split(spread)
    both = jnp.dot(
        jnp.concatenate([high, low], axis=0), corner_high_ref[...], preferred_element_type=F32
    )
    return (
        both[:elements]
        + both[elements:]
        + jnp.dot(high, corner_low_ref[...], preferred_element_type=F32)
    )


def total_of(array):
    return jnp.sum(jnp.sum(array, axis=0, keepdims=True), axis=1, keepdims=True)


def packed(values):
    lane = lax.broadcasted_iota(jnp.int32, (1, LANES), 1)
    out = jnp.zeros((1, LANES), F32)
    for k, value in enumerate(values):
        out = jnp.where(lane == k, value, out)
    return out


def unpacked(row, count):
    lane = lax.broadcasted_iota(jnp.int32, row.shape, 1)
    return [
        jnp.sum(jnp.where(lane == k, row, 0.0), axis=1, keepdims=True) for k in range(count)
    ]


def first_kernel(right_ref, map_ref, spread_ref, high_ref, low_ref, sent_ref):
    vertices = vertex_map(map_ref, spread_ref)
    part = coarse_part(right_ref[...], vertices, high_ref, low_ref)
    sent_ref[...] = jnp.broadcast_to(part, sent_ref.shape)


def smooth_kernel(
    right_ref, jacobi_ref, coarse_ref, inverse_ref, map_ref, spread_ref, high_ref, low_ref,
    pair_ref, slot_ref, face_ref,
    smoothed_ref, total_ref, dots_ref, local_ref, sent_ref, down_ref, up_ref,
):
    vertices = vertex_map(map_ref, spread_ref)
    coarse = jnp.sum(coarse_ref[...], axis=0, keepdims=True)
    total_ref[...] = coarse
    resid = right_ref[...]
    smoothed = jacobi_ref[...] * resid + prolonged(
        coarse, inverse_ref, vertices, resid.shape[0], high_ref, low_ref
    )
    dots_ref[...] = packed([total_of(resid * smoothed)])
    field = rows_of(smoothed)
    smoothed_ref[...] = field
    gather_all(field, (pair_ref, slot_ref, face_ref), (local_ref, sent_ref, down_ref, up_ref))


def apply_kernel(
    field_ref, dots_in_ref, local_in_ref, received_ref, below_ref, above_ref,
    metric_ref, helmholtz_ref, first_ref, first_back_ref, inner_ref, inner_back_ref,
    pair_ref, slot_ref, face_ref,
    back_ref, local_ref, sent_ref, down_ref, up_ref,
):
    refs = (pair_ref, slot_ref, face_ref)
    field = field_ref[...]
    summed = assembled(
        field, refs, local_in_ref[...], received_ref[...], below_ref[...], above_ref[...]
    )
    back, energy = stiffness(
        summed, metric_ref, first_ref, first_back_ref, inner_ref, inner_back_ref
    )
    energy = energy + rows_of(helmholtz_ref[...]) * field * field
    dots = dots_in_ref[...]
    lane = lax.broadcasted_iota(jnp.int32, dots.shape, 1)
    dots = jnp.where(lane == 7, total_of(energy), dots)
    back_ref[...] = back
    gather_all(back, refs, (local_ref, sent_ref, down_ref, up_ref))
    sent_ref[:, LANES:] = jnp.broadcast_to(dots, (sent_ref.shape[0], LANES))


def image_of(field_ref, back_ref, local_in_ref, received_ref, below_ref, above_ref, helmholtz_ref, refs):
    summed = assembled(
        back_ref[...],
        refs,
        local_in_ref[...],
        received_ref[:, :LANES],
        below_ref[...],
        above_ref[...],
    )
    return summed + rows_of(helmholtz_ref[...]) * field_ref[...]


def image_kernel(
    field_ref, back_ref, local_in_ref, received_ref, below_ref, above_ref,
    helmholtz_ref, map_ref, spread_ref, high_ref, low_ref,
    pair_ref, slot_ref, face_ref,
    image_ref, sent_ref, dots_ref,
):
    image = image_of(
        field_ref, back_ref, local_in_ref, received_ref, below_ref, above_ref, helmholtz_ref,
        (pair_ref, slot_ref, face_ref),
    )
    image_ref[...] = image
    vertices = vertex_map(map_ref, spread_ref)
    part = coarse_part(wide_of(image), vertices, high_ref, low_ref)
    sent_ref[...] = jnp.broadcast_to(part, sent_ref.shape)
    dots = jnp.sum(received_ref[:, LANES:], axis=0, keepdims=True)
    dots_ref[...] = jnp.broadcast_to(dots, dots_ref.shape)


def second_kernel(
    right_ref, image_ref, jacobi_ref, dots_in_ref, total_ref, coarse_ref, inverse_ref,
    map_ref, spread_ref, high_ref, low_ref,
    pair_ref, slot_ref, face_ref,
    smoothed_ref, resid_ref, scalars_ref, dots_ref, local_ref, sent_ref, down_ref, up_ref,
):
    dots = jnp.sum(dots_in_ref[...], axis=0, keepdims=True)
    scalars_ref[...] = dots
    values = unpacked(dots, 8)
    alpha = values[0] / values[7]
    vertices = vertex_map(map_ref, spread_ref)
    coarse = total_ref[...] - alpha * jnp.sum(coarse_ref[...], axis=0, keepdims=True)
    image = image_ref[...]
    resid = rows_of(right_ref[...]) - alpha * image
    resid_ref[...] = resid
    elements = right_ref.shape[0]
    field = rows_of(jacobi_ref[...]) * resid + rows_of(
        prolonged(coarse, inverse_ref, vertices, elements, high_ref, low_ref)
    )
    smoothed_ref[...] = field
    dots_ref[...] = packed([total_of(resid * field), total_of(image * field)])
    gather_all(field, (pair_ref, slot_ref, face_ref), (local_ref, sent_ref, down_ref, up_ref))


def last_image_kernel(
    field_ref, back_ref, local_in_ref, received_ref, below_ref, above_ref,
    helmholtz_ref, pair_ref, slot_ref, face_ref,
    image_ref, dots_ref,
):
    image_ref[...] = image_of(
        field_ref, back_ref, local_in_ref, received_ref, below_ref, above_ref, helmholtz_ref,
        (pair_ref, slot_ref, face_ref),
    )
    dots = jnp.sum(received_ref[:, LANES:], axis=0, keepdims=True)
    dots_ref[...] = jnp.broadcast_to(dots, dots_ref.shape)


def final_kernel(
    old_ref, field_ref, resid_ref, old_image_ref, image_ref, scalars_ref, dots_ref,
    solution_ref, residual_ref,
):
    before = unpacked(scalars_ref[...], 8)
    now = unpacked(jnp.sum(dots_ref[...], axis=0, keepdims=True), 8)
    alpha = before[0] / before[7]
    beta = now[0] / before[0]
    curved = now[7] + beta * (2.0 * now[1] + beta * before[7])
    step = now[0] / curved
    old = old_ref[...]
    direction = field_ref[...] + beta * old
    solution_ref[...] = wide_of(alpha * old + step * direction)
    image = image_ref[...] + beta * old_image_ref[...]
    residual_ref[...] = wide_of(resid_ref[...] - step * image)


def call(kernel, outs, *args):
    return pl.pallas_call(
        kernel,
        out_shape=[jax.ShapeDtypeStruct(shape, F32) for shape in outs],
        in_specs=[pl.BlockSpec(memory_space=pltpu.VMEM)] * len(args),
        out_specs=[pl.BlockSpec(memory_space=pltpu.VMEM)] * len(outs),
        compiler_params=pltpu.CompilerParams(vmem_limit_bytes=24 * 1024 * 1024),
    )(*args)


def swap(array, axis):
    return lax.all_to_all(array, axis, split_axis=0, concat_axis=0, tiled=True)


def body(
    right_side,
    metric,
    helmholtz,
    jacobi,
    pair_list,
    shared_slots,
    face_points,
    coarse_map,
    coarse_inverse,
):
    elements = right_side.shape[0]
    peers = lax.axis_size("sub")
    groups = lax.axis_size("grp")
    t = {name: jnp.asarray(value) for name, value in tables(elements).items()}
    field = (4 * elements, LANES)
    local = pair_list.shape
    face = (1, face_points.shape[1])
    points = (pair_list, shared_slots, face_points)
    corners = (coarse_map, t["spread"], t["corner_high"], t["corner_low"])
    derivatives = (t["first"], t["first_back"], t["inner"], t["inner_back"])
    ups = [(g, g + 1) for g in range(groups - 1)]
    downs = [(g + 1, g) for g in range(groups - 1)]

    def exchange(sent, down, up):
        below = lax.ppermute(up, "grp", ups)
        above = lax.ppermute(down, "grp", downs)
        return swap(sent, "sub"), below, above

    (sent,) = call(first_kernel, [(peers, NC)], right_side, *corners)
    coarse = swap(sent, "sub")
    smoothed, total, dots, near, sent, down, up = call(
        smooth_kernel,
        [field, (1, NC), (1, LANES), local, (peers, LANES), face, face],
        right_side, jacobi, coarse, coarse_inverse, *corners, *points,
    )
    received, below, above = exchange(sent, down, up)
    apply_outs = [field, local, (peers, 2 * LANES), face, face]
    back, near, sent, down, up = call(
        apply_kernel, apply_outs,
        smoothed, dots, near, received, below, above, metric, helmholtz, *derivatives, *points,
    )
    received, below, above = exchange(sent, down, up)
    image, sent, dots = call(
        image_kernel,
        [field, (peers, NC), (groups, LANES)],
        smoothed, back, near, received, below, above, helmholtz, *corners, *points,
    )
    coarse = swap(sent, "sub")
    dots = swap(dots, "grp")
    second, resid, scalars, dots, near, sent, down, up = call(
        second_kernel,
        [field, field, (1, LANES), (1, LANES), local, (peers, LANES), face, face],
        right_side, image, jacobi, dots, total, coarse, coarse_inverse, *corners, *points,
    )
    received, below, above = exchange(sent, down, up)
    back, near, sent, down, up = call(
        apply_kernel, apply_outs,
        second, dots, near, received, below, above, metric, helmholtz, *derivatives, *points,
    )
    received, below, above = exchange(sent, down, up)
    second_image, dots = call(
        last_image_kernel,
        [field, (groups, LANES)],
        second, back, near, received, below, above, helmholtz, *points,
    )
    dots = swap(dots, "grp")
    return tuple(
        call(
            final_kernel,
            [right_side.shape, right_side.shape],
            smoothed, second, resid, image, second_image, scalars, dots,
        )
    )


def solution(mesh):
    in_specs = (
        P(("grp", "sub"), None),
        P(("grp", "sub"), None),
        P(("grp", "sub"), None),
        P(("grp", "sub"), None),
        P(None, ("grp", "sub")),
        P(("grp", "sub"), None, None),
        P(None, ("grp", "sub")),
        P(None, ("grp", "sub")),
        P("grp", None, None),
    )
    out_specs = (P(("grp", "sub"), None), P(("grp", "sub"), None))
    return jax.shard_map(body, mesh=mesh, in_specs=in_specs, out_specs=out_specs, check_vma=False)
```

```python
import jax
import jax.numpy as jnp
import ml_dtypes
import numpy as np
from jax import lax
from jax.experimental import pallas as pl
from jax.experimental.pallas import tpu as pltpu
from jax.sharding import PartitionSpec as P

NC = 64
POINTS = 512
LANES = 128
STEP = 256
FACE_ROWS = 4
ROWS = FACE_ROWS + 1
F32 = jnp.float32
BF16 = jnp.bfloat16
NT = (((1,), (1,)), ((), ()))


def split_constant(array):
    high = array.astype(ml_dtypes.bfloat16)
    low = (array - high.astype(np.float64)).astype(ml_dtypes.bfloat16)
    return high, low


def tables(elements):
    order_index = np.arange(8)
    colloc = np.cos(np.pi * order_index / 7.0)
    end_weights = (
        np.where((order_index == 0) | (order_index == 7), 2.0, 1.0) * (-1.0) ** order_index
    )
    spacing = colloc[:, None] - colloc[None, :] + np.eye(8)
    raw_matrix = np.outer(end_weights, 1.0 / end_weights) / spacing
    off_part = raw_matrix * (1.0 - np.eye(8))
    derivative = 0.25 * (off_part - np.eye(8) * off_part.sum(axis=1)[:, None])
    along_inner = np.concatenate(
        [np.kron(np.eye(2), np.kron(derivative, np.eye(8))).T, np.kron(np.eye(16), derivative).T],
        axis=1,
    )
    high, low = split_constant(along_inner)
    inner = np.concatenate([high, high, low], axis=0)
    inner_back = np.concatenate([high.T, high.T, low.T], axis=0)

    half = np.arange(LANES) // 64

    def first_rows(matrix):
        rows = []
        for to in range(4):
            for at in range(4):
                rows.append(matrix[2 * to + half, 2 * at + half])
                rows.append(matrix[2 * to + half, 2 * at + 1 - half])
        return np.stack(rows).astype(np.float32)

    point_index = np.arange(POINTS)
    corner_index = np.arange(8)
    sign_first = 1.0 - 2.0 * (corner_index >> 2 & 1)
    sign_second = 1.0 - 2.0 * (corner_index >> 1 & 1)
    sign_third = 1.0 - 2.0 * (corner_index & 1)
    node_first = colloc[point_index // 64][:, None]
    node_second = colloc[point_index // 8 % 8][:, None]
    node_third = colloc[point_index % 8][:, None]
    corner = (
        0.5
        * (1.0 + sign_first[None, :] * node_first)
        * (0.5 * (1.0 + sign_second[None, :] * node_second))
        * (0.5 * (1.0 + sign_third[None, :] * node_third))
    )
    corner_high, corner_low = split_constant(np.repeat(corner.T, elements, axis=0))
    spread = np.tile(np.eye(elements), (1, 8)).astype(np.float32)
    return {
        "inner": inner,
        "inner_back": inner_back,
        "first": first_rows(derivative),
        "first_back": first_rows(derivative.T),
        "corner_high": corner_high,
        "corner_low": corner_low,
        "spread": spread,
    }


def split(value):
    high = value.astype(BF16)
    return high, (value - high.astype(F32)).astype(BF16)


def rows_of(wide):
    return jnp.concatenate([wide[:, LANES * c : LANES * (c + 1)] for c in range(4)], axis=0)


def wide_of(rows):
    elements = rows.shape[0] // 4
    return jnp.concatenate([rows[c * elements : (c + 1) * elements] for c in range(4)], axis=1)


def locate(points, elements):
    element = points >> 9
    chunk = (points >> 7) & 3
    row = jnp.where(points < elements * POINTS, chunk * elements + element, 4 * elements)
    return row, points & (LANES - 1)


def one_hot(index, count):
    steps = lax.broadcasted_iota(jnp.int32, (count, index.shape[1]), 0)
    return steps == index


def gather(field, chunks):
    high, low = split(field)
    both = jnp.concatenate([high, low], axis=1)
    out = []
    for row, lane in chunks:
        lanes = one_hot(lane, LANES).astype(F32).astype(BF16)
        picked = jnp.dot(
            both, jnp.concatenate([lanes, lanes], axis=0), preferred_element_type=F32
        )
        out.append(
            jnp.sum(
                jnp.where(one_hot(row, field.shape[0]), picked, 0.0), axis=0, keepdims=True
            )
        )
    return out


def scatter(rows, chunks, values):
    total = jnp.zeros((2 * rows, LANES), F32)
    for (row, lane), value in zip(chunks, values):
        lanes = one_hot(lane, LANES).astype(F32).astype(BF16)
        high, low = split(jnp.where(one_hot(row, rows), value, 0.0))
        total = total + lax.dot_general(
            jnp.concatenate([high, low], axis=0), lanes, NT, preferred_element_type=F32
        )
    return total[:rows] + total[rows:]


def chunked(row, lane):
    return [
        (row[:, at : at + STEP], lane[:, at : at + STEP]) for at in range(0, row.shape[1], STEP)
    ]


def cut(row):
    return [row[:, at : at + STEP] for at in range(0, row.shape[1], STEP)]


def index_chunks(pair_ref, slot_ref, face_ref, elements):
    pair_row, pair_lane = locate(pair_ref[...], elements)
    slot_row, slot_lane = locate(slot_ref[0], elements)
    face_row, face_lane = locate(face_ref[...], elements)
    pairs = chunked(pair_row[0:1], pair_lane[0:1]) + chunked(pair_row[1:2], pair_lane[1:2])
    slots = []
    for at in range(0, slot_row.shape[0], 2):
        slots.append(
            tuple(
                jnp.concatenate([part[at : at + 1], part[at + 1 : at + 2]], axis=1)
                for part in (slot_row, slot_lane)
            )
        )
    faces = chunked(face_row[0:1], face_lane[0:1]) + chunked(face_row[1:2], face_lane[1:2])
    return pairs, slots, faces


def halves(wide):
    return [wide[:, at : at + LANES] for at in range(0, wide.shape[1], LANES)]


def own_group(devices, peers, away=0):
    shape = (devices, LANES)
    return lax.broadcasted_iota(jnp.int32, shape, 0) // peers - lax.axis_index("grp") == away


def gather_all(field, refs, outs, extra):
    pair_ref, slot_ref, face_ref = refs
    local_ref, sent_ref = outs
    pairs, slots, faces = index_chunks(pair_ref, slot_ref, face_ref, field.shape[0] // 4)
    values = gather(field, pairs + slots + faces)
    count = pair_ref.shape[1] // STEP
    for k in range(count):
        local_ref[0:1, k * STEP : (k + 1) * STEP] = values[k]
        local_ref[1:2, k * STEP : (k + 1) * STEP] = values[count + k]
    values = values[2 * count :]
    peers = slot_ref.shape[1]
    devices = sent_ref.shape[0] // ROWS
    shared = jnp.concatenate([row for pair in values[: len(slots)] for row in halves(pair)], axis=0)
    shared = jnp.concatenate([shared] * (devices // peers), axis=0)
    values = values[len(slots) :]
    count = face_ref.shape[1] // STEP
    down = [row for pair in values[:count] for row in halves(pair)]
    up = [row for pair in values[count:] for row in halves(pair)]
    above = own_group(devices, peers, 1)
    for r in range(FACE_ROWS):
        rows = jnp.where(above, up[r], down[r])
        if r == 0:
            rows = jnp.where(own_group(devices, peers), shared, rows)
        sent_ref[pl.ds(r, devices, ROWS), :] = rows
    sent_ref[pl.ds(FACE_ROWS, devices, ROWS), :] = jnp.broadcast_to(extra, (devices, LANES))


def terms(received_ref):
    devices = received_ref.shape[0] // ROWS
    return jnp.sum(received_ref[pl.ds(FACE_ROWS, devices, ROWS), :], axis=0, keepdims=True)


def assembled(field, refs, local, received_ref):
    pair_ref, slot_ref, face_ref = refs
    pairs, slots, faces = index_chunks(pair_ref, slot_ref, face_ref, field.shape[0] // 4)
    values = cut(local[1:2]) + cut(local[0:1])
    peers = slot_ref.shape[1]
    devices = received_ref.shape[0] // ROWS
    rows = [received_ref[pl.ds(r, devices, ROWS), :] for r in range(FACE_ROWS)]
    mine = jnp.where(own_group(devices, peers), rows[0], 0.0)
    shared = mine[:peers]
    for g in range(1, devices // peers):
        shared = shared + mine[g * peers : (g + 1) * peers]
    for at in range(0, peers, 2):
        values.append(jnp.concatenate([shared[at : at + 1], shared[at + 1 : at + 2]], axis=1))
    place = lax.broadcasted_iota(jnp.int32, (devices, LANES), 0)
    here = lax.axis_index("grp") * peers + lax.axis_index("sub")
    for away in (-peers, peers):
        side = [
            jnp.sum(jnp.where(place - here == away, part, 0.0), axis=0, keepdims=True)
            for part in rows
        ]
        values = values + cut(jnp.concatenate(side, axis=1))
    return field + scatter(field.shape[0], pairs + slots + faces, values)


def along_first(field, table_ref):
    elements = field.shape[0] // 4
    turned = pltpu.roll(field, 64, axis=1)
    out = []
    for to in range(4):
        total = None
        for at in range(4):
            place = 2 * (4 * to + at)
            rows = slice(at * elements, (at + 1) * elements)
            term = (
                table_ref[place : place + 1, :] * field[rows]
                + table_ref[place + 1 : place + 2, :] * turned[rows]
            )
            total = term if total is None else total + term
        out.append(total)
    return jnp.concatenate(out, axis=0)


def stiffness(field, metric_ref, first_ref, first_back_ref, inner_ref, inner_back_ref):
    metric = [rows_of(metric_ref[:, POINTS * d : POINTS * (d + 1)]) for d in range(3)]
    grad_first = along_first(field, first_ref)
    high, low = split(field)
    inner = jnp.dot(
        jnp.concatenate([high, low, high], axis=1), inner_ref[...], preferred_element_type=F32
    )
    flux_first = metric[0] * grad_first
    flux = jnp.concatenate([metric[1], metric[2]], axis=1) * inner
    high, low = split(flux)
    back = along_first(flux_first, first_back_ref) + jnp.dot(
        jnp.concatenate([high, low, high], axis=1), inner_back_ref[...], preferred_element_type=F32
    )
    energy = flux * inner
    return back, flux_first * grad_first + energy[:, :LANES] + energy[:, LANES:]


def vertex_map(map_ref, spread_ref):
    wide = jnp.dot(
        map_ref[...].astype(F32),
        spread_ref[...],
        precision=lax.Precision.HIGHEST,
        preferred_element_type=F32,
    )
    corners, width = wide.shape
    own = lax.broadcasted_iota(jnp.int32, wide.shape, 0) == (
        lax.broadcasted_iota(jnp.int32, wide.shape, 1) // (width // corners)
    )
    flat = jnp.sum(jnp.where(own, wide, 0.0), axis=0, keepdims=True)
    flat = (flat + 0.5).astype(jnp.int32)
    return jnp.where(one_hot(flat, NC), 1.0, 0.0)


def own_element(elements, width):
    shape = (elements, width)
    return lax.broadcasted_iota(jnp.int32, shape, 0) == (
        lax.broadcasted_iota(jnp.int32, shape, 1) % elements
    )


def coarse_part(wide, vertices, corner_high_ref, corner_low_ref):
    elements = wide.shape[0]
    high, low = split(wide)
    both = lax.dot_general(
        jnp.concatenate([high, low], axis=0), corner_high_ref[...], NT, preferred_element_type=F32
    )
    inner = (
        both[:elements]
        + both[elements:]
        + lax.dot_general(high, corner_low_ref[...], NT, preferred_element_type=F32)
    )
    inner = jnp.where(own_element(elements, inner.shape[1]), inner, 0.0)
    flat = jnp.sum(inner, axis=0, keepdims=True)
    return lax.dot_general(
        jnp.broadcast_to(flat, (8, flat.shape[1])),
        vertices,
        NT,
        precision=lax.Precision.HIGHEST,
        preferred_element_type=F32,
    )[0:1]


def prolonged(coarse, inverse_ref, vertices, elements, corner_high_ref, corner_low_ref):
    solved = jnp.sum(inverse_ref[0] * coarse, axis=1, keepdims=True)
    flat = jnp.sum(vertices * solved, axis=0, keepdims=True)
    spread = jnp.where(own_element(elements, flat.shape[1]), flat, 0.0)
    high, low = split(spread)
    both = jnp.dot(
        jnp.concatenate([high, low], axis=0), corner_high_ref[...], preferred_element_type=F32
    )
    return (
        both[:elements]
        + both[elements:]
        + jnp.dot(high, corner_low_ref[...], preferred_element_type=F32)
    )


def total_of(array):
    return jnp.sum(jnp.sum(array, axis=0, keepdims=True), axis=1, keepdims=True)


def packed(values):
    lane = lax.broadcasted_iota(jnp.int32, (1, LANES), 1)
    out = jnp.zeros((1, LANES), F32)
    for k, value in enumerate(values):
        out = jnp.where(lane == k, value, out)
    return out


def unpacked(row, count):
    lane = lax.broadcasted_iota(jnp.int32, row.shape, 1)
    return [
        jnp.sum(jnp.where(lane == k, row, 0.0), axis=1, keepdims=True) for k in range(count)
    ]


def first_kernel(right_ref, map_ref, spread_ref, high_ref, low_ref, sent_ref):
    vertices = vertex_map(map_ref, spread_ref)
    part = coarse_part(right_ref[...], vertices, high_ref, low_ref)
    sent_ref[...] = jnp.broadcast_to(part, sent_ref.shape)


def smooth_kernel(
    right_ref, jacobi_ref, coarse_ref, inverse_ref, map_ref, spread_ref, high_ref, low_ref,
    pair_ref, slot_ref, face_ref,
    smoothed_ref, dots_ref, local_ref, sent_ref,
):
    vertices = vertex_map(map_ref, spread_ref)
    coarse = jnp.sum(coarse_ref[...], axis=0, keepdims=True)
    resid = right_ref[...]
    smoothed = jacobi_ref[...] * resid + prolonged(
        coarse, inverse_ref, vertices, resid.shape[0], high_ref, low_ref
    )
    dots = packed([total_of(resid * smoothed)])
    dots_ref[...] = dots
    field = rows_of(smoothed)
    smoothed_ref[...] = field
    gather_all(field, (pair_ref, slot_ref, face_ref), (local_ref, sent_ref), dots)


def apply_kernel(
    field_ref, dots_in_ref, local_in_ref, received_ref, metric_ref, helmholtz_ref, first_ref, first_back_ref, inner_ref, inner_back_ref,
    pair_ref, slot_ref, face_ref,
    back_ref, local_ref, sent_ref,
):
    refs = (pair_ref, slot_ref, face_ref)
    field = field_ref[...]
    summed = assembled(field, refs, local_in_ref[...], received_ref)
    back, energy = stiffness(
        summed, metric_ref, first_ref, first_back_ref, inner_ref, inner_back_ref
    )
    energy = energy + rows_of(helmholtz_ref[...]) * field * field
    dots = dots_in_ref[...]
    lane = lax.broadcasted_iota(jnp.int32, dots.shape, 1)
    dots = jnp.where(lane == 7, total_of(energy), dots)
    back_ref[...] = back
    gather_all(back, refs, (local_ref, sent_ref), dots)


def image_of(field_ref, back_ref, local_in_ref, received_ref, helmholtz_ref, refs):
    summed = assembled(back_ref[...], refs, local_in_ref[...], received_ref)
    return summed + rows_of(helmholtz_ref[...]) * field_ref[...]


def image_kernel(
    right_ref, field_ref, back_ref, local_in_ref, received_ref, helmholtz_ref,
    map_ref, spread_ref, high_ref, low_ref,
    pair_ref, slot_ref, face_ref,
    image_ref, resid_ref, scalars_ref, sent_ref,
):
    dots = terms(received_ref)
    scalars_ref[...] = dots
    values = unpacked(dots, 8)
    alpha = values[0] / values[7]
    image = image_of(
        field_ref, back_ref, local_in_ref, received_ref, helmholtz_ref,
        (pair_ref, slot_ref, face_ref),
    )
    image_ref[...] = image
    resid = rows_of(right_ref[...]) - alpha * image
    resid_ref[...] = resid
    vertices = vertex_map(map_ref, spread_ref)
    part = coarse_part(wide_of(resid), vertices, high_ref, low_ref)
    sent_ref[...] = jnp.broadcast_to(part, sent_ref.shape)


def second_kernel(
    resid_ref, image_ref, jacobi_ref, coarse_ref, inverse_ref,
    map_ref, spread_ref, high_ref, low_ref,
    pair_ref, slot_ref, face_ref,
    smoothed_ref, dots_ref, local_ref, sent_ref,
):
    vertices = vertex_map(map_ref, spread_ref)
    coarse = jnp.sum(coarse_ref[...], axis=0, keepdims=True)
    resid = resid_ref[...]
    elements = jacobi_ref.shape[0]
    field = rows_of(jacobi_ref[...]) * resid + rows_of(
        prolonged(coarse, inverse_ref, vertices, elements, high_ref, low_ref)
    )
    smoothed_ref[...] = field
    dots = packed([total_of(resid * field), total_of(image_ref[...] * field)])
    dots_ref[...] = dots
    gather_all(field, (pair_ref, slot_ref, face_ref), (local_ref, sent_ref), dots)


def final_kernel(
    old_ref, field_ref, resid_ref, old_image_ref, scalars_ref,
    back_ref, local_in_ref, received_ref, helmholtz_ref, pair_ref, slot_ref, face_ref,
    solution_ref, residual_ref,
):
    before = unpacked(scalars_ref[...], 8)
    now = unpacked(terms(received_ref), 8)
    alpha = before[0] / before[7]
    beta = now[0] / before[0]
    curved = now[7] + beta * (2.0 * now[1] + beta * before[7])
    step = now[0] / curved
    old = old_ref[...]
    direction = field_ref[...] + beta * old
    solution_ref[...] = wide_of(alpha * old + step * direction)
    image = image_of(
        field_ref, back_ref, local_in_ref, received_ref, helmholtz_ref,
        (pair_ref, slot_ref, face_ref),
    )
    image = image + beta * old_image_ref[...]
    residual_ref[...] = wide_of(resid_ref[...] - step * image)


def call(kernel, outs, *args):
    return pl.pallas_call(
        kernel,
        out_shape=[jax.ShapeDtypeStruct(shape, F32) for shape in outs],
        in_specs=[pl.BlockSpec(memory_space=pltpu.VMEM)] * len(args),
        out_specs=[pl.BlockSpec(memory_space=pltpu.VMEM)] * len(outs),
        compiler_params=pltpu.CompilerParams(vmem_limit_bytes=24 * 1024 * 1024),
    )(*args)


def swap(array, axis):
    return lax.all_to_all(array, axis, split_axis=0, concat_axis=0, tiled=True)


def body(
    right_side,
    metric,
    helmholtz,
    jacobi,
    pair_list,
    shared_slots,
    face_points,
    coarse_map,
    coarse_inverse,
):
    elements = right_side.shape[0]
    peers = lax.axis_size("sub")
    groups = lax.axis_size("grp")
    t = {name: jnp.asarray(value) for name, value in tables(elements).items()}
    field = (4 * elements, LANES)
    local = pair_list.shape
    sent_rows = (groups * peers * ROWS, LANES)
    points = (pair_list, shared_slots, face_points)
    corners = (coarse_map, t["spread"], t["corner_high"], t["corner_low"])
    derivatives = (t["first"], t["first_back"], t["inner"], t["inner_back"])

    def exchange(sent):
        rows = sent.reshape(groups * peers, 1, ROWS * LANES)
        return swap(rows, ("grp", "sub")).reshape(sent_rows)

    (sent,) = call(first_kernel, [(peers, NC)], right_side, *corners)
    coarse = swap(sent, "sub")
    smoothed, dots, near, sent = call(
        smooth_kernel,
        [field, (1, LANES), local, sent_rows],
        right_side, jacobi, coarse, coarse_inverse, *corners, *points,
    )
    received = exchange(sent)
    apply_outs = [field, local, sent_rows]
    back, near, sent = call(
        apply_kernel, apply_outs,
        smoothed, dots, near, received, metric, helmholtz, *derivatives, *points,
    )
    received = exchange(sent)
    image, resid, scalars, sent = call(
        image_kernel,
        [field, field, (1, LANES), (peers, NC)],
        right_side, smoothed, back, near, received, helmholtz, *corners, *points,
    )
    coarse = swap(sent, "sub")
    second, dots, near, sent = call(
        second_kernel,
        [field, (1, LANES), local, sent_rows],
        resid, image, jacobi, coarse, coarse_inverse, *corners, *points,
    )
    received = exchange(sent)
    back, near, sent = call(
        apply_kernel, apply_outs,
        second, dots, near, received, metric, helmholtz, *derivatives, *points,
    )
    received = exchange(sent)
    return tuple(
        call(
            final_kernel,
            [right_side.shape, right_side.shape],
            smoothed, second, resid, image, scalars, back, near, received, helmholtz, *points,
        )
    )


def solution(mesh):
    in_specs = (
        P(("grp", "sub"), None),
        P(("grp", "sub"), None),
        P(("grp", "sub"), None),
        P(("grp", "sub"), None),
        P(None, ("grp", "sub")),
        P(("grp", "sub"), None, None),
        P(None, ("grp", "sub")),
        P(None, ("grp", "sub")),
        P("grp", None, None),
    )
    out_specs = (P(("grp", "sub"), None), P(("grp", "sub"), None))
    return jax.shard_map(body, mesh=mesh, in_specs=in_specs, out_specs=out_specs, check_vma=False)
```

```python
import jax
import jax.numpy as jnp
import ml_dtypes
import numpy as np
from jax import lax
from jax.experimental import pallas as pl
from jax.experimental.pallas import tpu as pltpu
from jax.sharding import PartitionSpec as P

NC = 64
POINTS = 512
LANES = 128
STEP = 256
FACE_ROWS = 4
ROWS = FACE_ROWS + 1
FIRST_ROWS = ROWS + 1 + FACE_ROWS
F32 = jnp.float32
BF16 = jnp.bfloat16
NT = (((1,), (1,)), ((), ()))


def split_constant(array):
    high = array.astype(ml_dtypes.bfloat16)
    low = (array - high.astype(np.float64)).astype(ml_dtypes.bfloat16)
    return high, low


def tables():
    order_index = np.arange(8)
    colloc = np.cos(np.pi * order_index / 7.0)
    end_weights = (
        np.where((order_index == 0) | (order_index == 7), 2.0, 1.0) * (-1.0) ** order_index
    )
    spacing = colloc[:, None] - colloc[None, :] + np.eye(8)
    raw_matrix = np.outer(end_weights, 1.0 / end_weights) / spacing
    off_part = raw_matrix * (1.0 - np.eye(8))
    derivative = 0.25 * (off_part - np.eye(8) * off_part.sum(axis=1)[:, None])
    along_inner = np.concatenate(
        [np.kron(np.eye(2), np.kron(derivative, np.eye(8))).T, np.kron(np.eye(16), derivative).T],
        axis=1,
    )
    high, low = split_constant(along_inner)
    inner = np.concatenate([high, high, low], axis=0)
    inner_back = np.concatenate([high.T, high.T, low.T], axis=0)

    half = np.arange(LANES) // 64

    def first_rows(matrix):
        rows = []
        for to in range(4):
            for at in range(4):
                rows.append(matrix[2 * to + half, 2 * at + half])
                rows.append(matrix[2 * to + half, 2 * at + 1 - half])
        return np.stack(rows).astype(np.float32)

    return {
        "inner": inner,
        "inner_back": inner_back,
        "first": first_rows(derivative),
        "first_back": first_rows(derivative.T),
    }


def split(value):
    high = value.astype(BF16)
    return high, (value - high.astype(F32)).astype(BF16)


def rows_of(wide):
    return jnp.concatenate([wide[:, LANES * c : LANES * (c + 1)] for c in range(4)], axis=0)


def wide_of(rows):
    elements = rows.shape[0] // 4
    return jnp.concatenate([rows[c * elements : (c + 1) * elements] for c in range(4)], axis=1)


def locate(points, elements):
    element = points >> 9
    chunk = (points >> 7) & 3
    row = jnp.where(points < elements * POINTS, chunk * elements + element, 4 * elements)
    return row, points & (LANES - 1)


def one_hot(index, count):
    steps = lax.broadcasted_iota(jnp.int32, (count, index.shape[1]), 0)
    return steps == index


def gather(field, chunks):
    high, low = split(field)
    both = jnp.concatenate([high, low], axis=1)
    out = []
    for row, lane in chunks:
        lanes = one_hot(lane, LANES).astype(F32).astype(BF16)
        picked = jnp.dot(
            both, jnp.concatenate([lanes, lanes], axis=0), preferred_element_type=F32
        )
        out.append(
            jnp.sum(
                jnp.where(one_hot(row, field.shape[0]), picked, 0.0), axis=0, keepdims=True
            )
        )
    return out


def scatter(rows, chunks, values):
    total = jnp.zeros((2 * rows, LANES), F32)
    for (row, lane), value in zip(chunks, values):
        lanes = one_hot(lane, LANES).astype(F32).astype(BF16)
        high, low = split(jnp.where(one_hot(row, rows), value, 0.0))
        total = total + lax.dot_general(
            jnp.concatenate([high, low], axis=0), lanes, NT, preferred_element_type=F32
        )
    return total[:rows] + total[rows:]


def chunked(row, lane):
    return [
        (row[:, at : at + STEP], lane[:, at : at + STEP]) for at in range(0, row.shape[1], STEP)
    ]


def cut(row):
    return [row[:, at : at + STEP] for at in range(0, row.shape[1], STEP)]


def pair_chunks(pair_ref, elements):
    row, lane = locate(pair_ref[...], elements)
    return chunked(row[0:1], lane[0:1]) + chunked(row[1:2], lane[1:2])


def far_chunks(slots, faces, elements):
    row, lane = locate(slots, elements)
    chunks = []
    for at in range(0, row.shape[0], 2):
        chunks.append(
            tuple(
                jnp.concatenate([part[at : at + 1], part[at + 1 : at + 2]], axis=1)
                for part in (row, lane)
            )
        )
    row, lane = locate(faces, elements)
    return chunks + chunked(row[0:1], lane[0:1]) + chunked(row[1:2], lane[1:2])


def halves(wide):
    return [wide[:, at : at + LANES] for at in range(0, wide.shape[1], LANES)]


def own_group(devices, peers, away=0):
    shape = (devices, LANES)
    return lax.broadcasted_iota(jnp.int32, shape, 0) // peers - lax.axis_index("grp") == away


def send(sent_ref, count, first, shared, down, up):
    devices = sent_ref.shape[0] // count
    peers = shared.shape[0]
    above = own_group(devices, peers, 1)
    shared = jnp.concatenate([shared] * (devices // peers), axis=0)
    for r in range(FACE_ROWS):
        rows = jnp.where(above, up[r], down[r])
        if r == 0:
            rows = jnp.where(own_group(devices, peers), shared, rows)
        sent_ref[pl.ds(first + r, devices, count), :] = rows


def send_same(sent_ref, count, at, row):
    devices = sent_ref.shape[0] // count
    sent_ref[pl.ds(at, devices, count), :] = jnp.broadcast_to(row, (devices, LANES))


def send_values(sent_ref, count, values, peers):
    shared = jnp.concatenate([row for pair in values[: peers // 2] for row in halves(pair)], axis=0)
    faces = [row for pair in values[peers // 2 :] for row in halves(pair)]
    send(sent_ref, count, 0, shared, faces[:FACE_ROWS], faces[FACE_ROWS:])


def get(received_ref, count, first, peers):
    devices = received_ref.shape[0] // count
    rows = [received_ref[pl.ds(first + r, devices, count), :] for r in range(FACE_ROWS)]
    mine = jnp.where(own_group(devices, peers), rows[0], 0.0)
    shared = mine[:peers]
    for g in range(1, devices // peers):
        shared = shared + mine[g * peers : (g + 1) * peers]
    return (shared, *[get_sides(rows, peers, away) for away in (-1, 1)])


def get_sides(rows, peers, away):
    here = lax.axis_index("grp") * peers + lax.axis_index("sub")
    source = lax.broadcasted_iota(jnp.int32, rows[0].shape, 0) - here == away * peers
    return jnp.concatenate(
        [jnp.sum(jnp.where(source, part, 0.0), axis=0, keepdims=True) for part in rows], axis=1
    )


def get_terms(received_ref, count):
    devices = received_ref.shape[0] // count
    return received_ref[pl.ds(FACE_ROWS, devices, count), :]


def far_values(shared, below, above):
    values = []
    for at in range(0, shared.shape[0], 2):
        values.append(jnp.concatenate([shared[at : at + 1], shared[at + 1 : at + 2]], axis=1))
    return values + cut(below) + cut(above)


def swapped(values):
    count = len(values) // 2
    return values[count:] + values[:count]


def along_first(field, table_ref):
    elements = field.shape[0] // 4
    turned = pltpu.roll(field, 64, axis=1)
    out = []
    for to in range(4):
        total = None
        for at in range(4):
            place = 2 * (4 * to + at)
            rows = slice(at * elements, (at + 1) * elements)
            term = (
                table_ref[place : place + 1, :] * field[rows]
                + table_ref[place + 1 : place + 2, :] * turned[rows]
            )
            total = term if total is None else total + term
        out.append(total)
    return jnp.concatenate(out, axis=0)


def stiffness(field, metric_ref, first_ref, first_back_ref, inner_ref, inner_back_ref):
    metric = [rows_of(metric_ref[:, POINTS * d : POINTS * (d + 1)]) for d in range(3)]
    grad_first = along_first(field, first_ref)
    high, low = split(field)
    inner = jnp.dot(
        jnp.concatenate([high, low, high], axis=1), inner_ref[...], preferred_element_type=F32
    )
    flux_first = metric[0] * grad_first
    flux = jnp.concatenate([metric[1], metric[2]], axis=1) * inner
    high, low = split(flux)
    back = along_first(flux_first, first_back_ref) + jnp.dot(
        jnp.concatenate([high, low, high], axis=1), inner_back_ref[...], preferred_element_type=F32
    )
    energy = flux * inner
    return back, flux_first * grad_first + energy[:, :LANES] + energy[:, LANES:]


def factors(points):
    nodes = 0.5 * (1.0 + np.cos(np.pi * np.arange(8) / 7.0))
    out = []
    for shift in (6, 3, 0):
        index = (points >> shift) & 7
        near = jnp.full(points.shape, nodes[7], F32)
        far = jnp.full(points.shape, nodes[0], F32)
        for m in range(7):
            near = jnp.where(index == m, float(nodes[m]), near)
            far = jnp.where(index == m, float(nodes[7 - m]), far)
        out.append((near, far))
    return out


def corners(points):
    first, second, third = factors(points)
    return [
        first[q >> 2 & 1] * (second[q >> 1 & 1] * third[q & 1]) for q in range(8)
    ]


def own_corners():
    return corners(lax.broadcasted_iota(jnp.int32, (1, POINTS), 1))


def flat_map(mapped):
    elements = mapped.shape[1]
    width = 8 * elements
    own = own_element(elements, width)
    place = lax.broadcasted_iota(jnp.int32, (8, width), 1) // elements
    spread = jnp.where(own, 1.0, 0.0).astype(BF16)
    wide = jnp.dot(mapped.astype(F32).astype(BF16), spread, preferred_element_type=F32)
    keep = lax.broadcasted_iota(jnp.int32, (8, width), 0) == place
    return jnp.sum(jnp.where(keep, wide, 0.0), axis=0, keepdims=True)


def one_vertex(flat):
    return jnp.where(one_hot(whole(flat), NC), 1.0, 0.0)


def whole(values):
    return (values + 0.5).astype(jnp.int32)


def own_element(elements, width):
    shape = (elements, width)
    return lax.broadcasted_iota(jnp.int32, shape, 0) == (
        lax.broadcasted_iota(jnp.int32, shape, 1) % elements
    )


def own_place(elements, q):
    shape = (elements, 8 * elements)
    lane = lax.broadcasted_iota(jnp.int32, shape, 1)
    return lane == lax.broadcasted_iota(jnp.int32, shape, 0) + q * elements


def coarse_part(field, vertices, inverse):
    elements = field.shape[0] // 4
    flat = jnp.zeros((elements, 8 * elements), F32)
    for q, corner in enumerate(own_corners()):
        inner = None
        for c in range(4):
            term = field[c * elements : (c + 1) * elements] * corner[:, c * LANES : (c + 1) * LANES]
            inner = term if inner is None else inner + term
        flat = jnp.where(own_place(elements, q), jnp.sum(inner, axis=1, keepdims=True), flat)
    flat = jnp.sum(flat, axis=0, keepdims=True)
    part = jnp.sum(vertices * flat, axis=1, keepdims=True)
    part = jnp.sum(inverse * part, axis=0, keepdims=True)
    return jnp.concatenate([part, jnp.zeros((1, LANES - NC), F32)], axis=1)


def column(row):
    shape = (NC, LANES)
    keep = lax.broadcasted_iota(jnp.int32, shape, 0) == lax.broadcasted_iota(jnp.int32, shape, 1)
    return jnp.sum(jnp.where(keep, row, 0.0), axis=1, keepdims=True)


def get_solved(received_ref, count, peers):
    rows = get_terms(received_ref, count)
    return [
        column(
            jnp.sum(
                jnp.where(own_group(rows.shape[0], peers, away), rows, 0.0), axis=0, keepdims=True
            )
        )
        for away in (0, -1, 1)
    ]


def prolonged(solved, vertices, elements):
    flat = jnp.sum(vertices * solved, axis=0, keepdims=True)
    out = [None] * 4
    for q, corner in enumerate(own_corners()):
        value = jnp.sum(jnp.where(own_place(elements, q), flat, 0.0), axis=1, keepdims=True)
        for c in range(4):
            term = value * corner[:, c * LANES : (c + 1) * LANES]
            out[c] = term if out[c] is None else out[c] + term
    return jnp.concatenate(out, axis=0)


def prolong_at(points, vertices, elements):
    mine = lax.broadcasted_iota(jnp.int32, (elements, points.shape[1]), 0) == points >> 9
    weights = jnp.concatenate([jnp.where(mine, corner, 0.0) for corner in corners(points)], axis=0)
    high, low = split(weights)
    both = jnp.dot(
        vertices.astype(BF16),
        jnp.concatenate([high, low], axis=1),
        preferred_element_type=F32,
    )
    return both[:, : points.shape[1]] + both[:, points.shape[1] :]


def total_of(array):
    return jnp.sum(jnp.sum(array, axis=0, keepdims=True), axis=1, keepdims=True)


def packed(values):
    lane = lax.broadcasted_iota(jnp.int32, (1, LANES), 1)
    out = jnp.zeros((1, LANES), F32)
    for k, value in enumerate(values):
        out = jnp.where(lane == k, value, out)
    return out


def unpacked(row, count):
    lane = lax.broadcasted_iota(jnp.int32, row.shape, 1)
    return [
        jnp.sum(jnp.where(lane == k, row, 0.0), axis=1, keepdims=True) for k in range(count)
    ]


def first_kernel(
    right_hbm, jacobi_hbm, inverse_hbm, map_hbm, slot_hbm, face_hbm,
    sent_ref,
    right_ref, jacobi_ref, inverse_ref, map_ref, slot_ref, face_ref, sems,
):
    copies = []
    for k, (source, target) in enumerate(
        (
            (face_hbm, face_ref),
            (slot_hbm, slot_ref),
            (right_hbm, right_ref),
            (jacobi_hbm, jacobi_ref),
            (map_hbm, map_ref),
            (inverse_hbm, inverse_ref),
        )
    ):
        copy = pltpu.make_async_copy(source, target, sems.at[k])
        copy.start()
        copies.append(copy)
    for copy in copies:
        copy.wait()
    elements = right_ref.shape[0]
    peers = slot_ref.shape[1]
    resid = rows_of(right_ref[...])
    flat = flat_map(map_ref[...])
    part = coarse_part(resid, one_vertex(flat), inverse_ref[0])
    smoothed = rows_of(jacobi_ref[...]) * resid
    values = gather(smoothed, far_chunks(slot_ref[0], face_ref[...], elements))
    send_values(sent_ref, FIRST_ROWS, values, peers)
    send_same(sent_ref, FIRST_ROWS, FACE_ROWS, part)
    send_same(sent_ref, FIRST_ROWS, ROWS, flat)
    faces = face_ref[...].astype(F32)
    send(
        sent_ref, FIRST_ROWS, ROWS + 1, slot_ref[0].astype(F32),
        halves(faces[0:1]), halves(faces[1:2]),
    )


def static_of(received_ref, peers, elements):
    shared, below, above = get(received_ref, FIRST_ROWS, ROWS + 1, peers)
    devices = received_ref.shape[0] // FIRST_ROWS
    maps = received_ref[pl.ds(ROWS, devices, FIRST_ROWS), :]
    mine = jnp.where(own_group(devices, peers), maps, 0.0)
    own = mine[:peers]
    for g in range(1, devices // peers):
        own = own + mine[g * peers : (g + 1) * peers]
    out = []
    for b in range(peers):
        out.append(
            prolong_at(whole(shared[b : b + 1]), one_vertex(own[b : b + 1]), elements)
        )
    for points, away in ((below, -1), (above, 1)):
        flat = get_sides([maps], peers, away)
        out.append(prolong_at(whole(points), one_vertex(flat), elements))
    return jnp.concatenate(out, axis=1)


def apply(
    smoothed, count, received_ref, weights, solved, metric_ref, helmholtz_ref, derivatives, points,
    dots, back_ref, local_ref, sent_ref,
):
    pair_ref, slot_ref, face_ref = points
    elements = smoothed.shape[0] // 4
    peers = slot_ref.shape[1]
    pairs = pair_chunks(pair_ref, elements)
    far = far_chunks(slot_ref[0], face_ref[...], elements)
    shared, below, above = get(received_ref, count, 0, peers)
    ends = (0, peers * LANES, peers * LANES + below.shape[1], weights.shape[1])
    coarse = [
        jnp.sum(weights[:, ends[k] : ends[k + 1]] * solved[k], axis=0, keepdims=True)
        for k in range(3)
    ]
    shared = shared + jnp.concatenate(halves(coarse[0]), axis=0)
    values = swapped(gather(smoothed, pairs))
    values = values + far_values(shared, below + coarse[1], above + coarse[2])
    summed = smoothed + scatter(smoothed.shape[0], pairs + far, values)
    back, energy = stiffness(summed, metric_ref, *derivatives)
    energy = energy + rows_of(helmholtz_ref[...]) * smoothed * smoothed
    back_ref[...] = back
    values = gather(back, pairs + far)
    near = swapped(values[: len(pairs)])
    for k, value in enumerate(near):
        local_ref[0:1, k * STEP : (k + 1) * STEP] = value
    send_values(sent_ref, ROWS, values[len(pairs) :], peers)
    send_same(sent_ref, ROWS, FACE_ROWS, packed(dots + [total_of(energy)]))


def image_of(field_ref, back_ref, local_ref, received_ref, helmholtz_ref, points):
    pair_ref, slot_ref, face_ref = points
    elements = field_ref.shape[0] // 4
    chunks = pair_chunks(pair_ref, elements) + far_chunks(slot_ref[0], face_ref[...], elements)
    values = cut(local_ref[...]) + far_values(*get(received_ref, ROWS, 0, slot_ref.shape[1]))
    summed = back_ref[...] + scatter(field_ref.shape[0], chunks, values)
    return summed + rows_of(helmholtz_ref[...]) * field_ref[...]


def start_kernel(
    received_ref, right_ref, jacobi_ref, metric_ref, helmholtz_ref, map_ref,
    pair_ref, slot_ref, face_ref, first_ref, first_back_ref, inner_ref, inner_back_ref,
    smoothed_ref, weights_ref, back_ref, local_ref, sent_ref,
):
    elements = right_ref.shape[0]
    peers = slot_ref.shape[1]
    solved = get_solved(received_ref, FIRST_ROWS, peers)
    resid = rows_of(right_ref[...])
    vertices = one_vertex(flat_map(map_ref[...]))
    smoothed = rows_of(jacobi_ref[...]) * resid + prolonged(solved[0], vertices, elements)
    smoothed_ref[...] = smoothed
    weights = static_of(received_ref, peers, elements)
    weights_ref[...] = weights
    apply(
        smoothed, FIRST_ROWS, received_ref, weights, solved, metric_ref, helmholtz_ref,
        (first_ref, first_back_ref, inner_ref, inner_back_ref), (pair_ref, slot_ref, face_ref),
        [total_of(resid * smoothed)], back_ref, local_ref, sent_ref,
    )


def middle_kernel(
    received_ref, right_ref, jacobi_ref, helmholtz_ref, map_ref, inverse_ref,
    smoothed_ref, back_ref, local_ref, pair_ref, slot_ref, face_ref,
    image_ref, resid_ref, scalars_ref, sent_ref,
):
    elements = right_ref.shape[0]
    points = (pair_ref, slot_ref, face_ref)
    dots = jnp.sum(get_terms(received_ref, ROWS), axis=0, keepdims=True)
    scalars_ref[...] = dots
    values = unpacked(dots, 2)
    alpha = values[0] / values[1]
    image = image_of(smoothed_ref, back_ref, local_ref, received_ref, helmholtz_ref, points)
    image_ref[...] = image
    resid = rows_of(right_ref[...]) - alpha * image
    resid_ref[...] = resid
    part = coarse_part(resid, one_vertex(flat_map(map_ref[...])), inverse_ref[0])
    values = gather(
        rows_of(jacobi_ref[...]) * resid, far_chunks(slot_ref[0], face_ref[...], elements)
    )
    send_values(sent_ref, ROWS, values, slot_ref.shape[1])
    send_same(sent_ref, ROWS, FACE_ROWS, part)


def second_kernel(
    received_ref, resid_ref, image_ref, weights_ref, jacobi_ref, metric_ref, helmholtz_ref, map_ref,
    pair_ref, slot_ref, face_ref, first_ref, first_back_ref, inner_ref, inner_back_ref,
    smoothed_ref, back_ref, local_ref, sent_ref,
):
    elements = jacobi_ref.shape[0]
    solved = get_solved(received_ref, ROWS, slot_ref.shape[1])
    resid = resid_ref[...]
    vertices = one_vertex(flat_map(map_ref[...]))
    smoothed = rows_of(jacobi_ref[...]) * resid + prolonged(solved[0], vertices, elements)
    smoothed_ref[...] = smoothed
    apply(
        smoothed, ROWS, received_ref, weights_ref[...], solved, metric_ref, helmholtz_ref,
        (first_ref, first_back_ref, inner_ref, inner_back_ref), (pair_ref, slot_ref, face_ref),
        [total_of(resid * smoothed), total_of(image_ref[...] * smoothed)],
        back_ref, local_ref, sent_ref,
    )


def final_kernel(
    received_ref, old_ref, field_ref, resid_ref, old_image_ref, scalars_ref,
    back_ref, local_ref, helmholtz_ref, pair_ref, slot_ref, face_ref,
    solution_ref, residual_ref,
):
    before = unpacked(scalars_ref[...], 2)
    now = unpacked(jnp.sum(get_terms(received_ref, ROWS), axis=0, keepdims=True), 3)
    alpha = before[0] / before[1]
    beta = now[0] / before[0]
    curved = now[2] + beta * (2.0 * now[1] + beta * before[1])
    step = now[0] / curved
    old = old_ref[...]
    direction = field_ref[...] + beta * old
    solution_ref[...] = wide_of(alpha * old + step * direction)
    image = image_of(
        field_ref, back_ref, local_ref, received_ref, helmholtz_ref, (pair_ref, slot_ref, face_ref)
    )
    image = image + beta * old_image_ref[...]
    residual_ref[...] = wide_of(resid_ref[...] - step * image)


def call(kernel, outs, *args, copied=False):
    space = pl.ANY if copied else pltpu.VMEM
    scratch = [pltpu.VMEM(arg.shape, arg.dtype) for arg in args] if copied else []
    return pl.pallas_call(
        kernel,
        out_shape=[jax.ShapeDtypeStruct(shape, F32) for shape in outs],
        in_specs=[pl.BlockSpec(memory_space=space)] * len(args),
        out_specs=[pl.BlockSpec(memory_space=pltpu.VMEM)] * len(outs),
        scratch_shapes=scratch + ([pltpu.SemaphoreType.DMA((len(args),))] if copied else []),
        compiler_params=pltpu.CompilerParams(vmem_limit_bytes=(60 if copied else 24) * 1024 * 1024),
    )(*args)


def body(
    right_side,
    metric,
    helmholtz,
    jacobi,
    pair_list,
    shared_slots,
    face_points,
    coarse_map,
    coarse_inverse,
):
    peers = lax.axis_size("sub")
    groups = lax.axis_size("grp")
    t = {name: jnp.asarray(value) for name, value in tables().items()}
    field = (4 * right_side.shape[0], LANES)
    local = (1, pair_list.shape[0] * pair_list.shape[1])
    weights_shape = (NC, peers * LANES + face_points.shape[0] * face_points.shape[1])
    sent_rows = (groups * peers * ROWS, LANES)
    points = (pair_list, shared_slots, face_points)
    derivatives = (t["first"], t["first_back"], t["inner"], t["inner_back"])

    def exchange(sent):
        rows = sent.reshape(groups * peers, 1, -1)
        return lax.all_to_all(rows, ("grp", "sub"), 0, 0, tiled=True).reshape(sent.shape)

    (sent,) = call(
        first_kernel, [(groups * peers * FIRST_ROWS, LANES)],
        right_side, jacobi, coarse_inverse, coarse_map, shared_slots, face_points, copied=True,
    )
    smoothed, weights, back, near, sent = call(
        start_kernel, [field, weights_shape, field, local, sent_rows],
        exchange(sent), right_side, jacobi, metric, helmholtz, coarse_map, *points, *derivatives,
    )
    image, resid, scalars, sent = call(
        middle_kernel, [field, field, (1, LANES), sent_rows],
        exchange(sent), right_side, jacobi, helmholtz, coarse_map, coarse_inverse,
        smoothed, back, near, *points,
    )
    second, back, near, sent = call(
        second_kernel, [field, field, local, sent_rows],
        exchange(sent), resid, image, weights, jacobi, metric, helmholtz, coarse_map,
        *points, *derivatives,
    )
    return tuple(
        call(
            final_kernel, [right_side.shape, right_side.shape],
            exchange(sent), smoothed, second, resid, image, scalars, back, near, helmholtz, *points,
        )
    )


def solution(mesh):
    in_specs = (
        P(("grp", "sub"), None),
        P(("grp", "sub"), None),
        P(("grp", "sub"), None),
        P(("grp", "sub"), None),
        P(None, ("grp", "sub")),
        P(("grp", "sub"), None, None),
        P(None, ("grp", "sub")),
        P(None, ("grp", "sub")),
        P("grp", None, None),
    )
    out_specs = (P(("grp", "sub"), None), P(("grp", "sub"), None))
    return jax.shard_map(body, mesh=mesh, in_specs=in_specs, out_specs=out_specs, check_vma=False)
```

```python
import jax
import jax.numpy as jnp
import ml_dtypes
import numpy as np
from jax import lax
from jax.experimental import pallas as pl
from jax.experimental.pallas import tpu as pltpu
from jax.sharding import PartitionSpec as P

NC = 64
POINTS = 512
LANES = 128
STEP = 256
FACE_ROWS = 4
ROWS = 2
FIRST_ROWS = 4
F32 = jnp.float32
BF16 = jnp.bfloat16
NT = (((1,), (1,)), ((), ()))


def split_constant(array):
    high = array.astype(ml_dtypes.bfloat16)
    low = (array - high.astype(np.float64)).astype(ml_dtypes.bfloat16)
    return high, low


def tables():
    order_index = np.arange(8)
    colloc = np.cos(np.pi * order_index / 7.0)
    end_weights = (
        np.where((order_index == 0) | (order_index == 7), 2.0, 1.0) * (-1.0) ** order_index
    )
    spacing = colloc[:, None] - colloc[None, :] + np.eye(8)
    raw_matrix = np.outer(end_weights, 1.0 / end_weights) / spacing
    off_part = raw_matrix * (1.0 - np.eye(8))
    derivative = 0.25 * (off_part - np.eye(8) * off_part.sum(axis=1)[:, None])
    along_inner = np.concatenate(
        [np.kron(np.eye(2), np.kron(derivative, np.eye(8))).T, np.kron(np.eye(16), derivative).T],
        axis=1,
    )
    high, low = split_constant(along_inner)
    inner = np.concatenate([high, low], axis=0)

    half = np.arange(LANES) // 64

    def first_rows(matrix):
        rows = []
        for to in range(4):
            for at in range(4):
                rows.append(matrix[2 * to + half, 2 * at + half])
                rows.append(matrix[2 * to + half, 2 * at + 1 - half])
        return np.stack(rows).astype(np.float32)

    return {
        "inner": inner,
        "first": np.concatenate([first_rows(derivative), first_rows(derivative.T)], axis=0),
    }


def split(value):
    high = value.astype(BF16)
    return high, (value - high.astype(F32)).astype(BF16)


def rows_of(wide):
    return jnp.concatenate([wide[:, LANES * c : LANES * (c + 1)] for c in range(4)], axis=0)


def wide_of(rows):
    elements = rows.shape[0] // 4
    return jnp.concatenate([rows[c * elements : (c + 1) * elements] for c in range(4)], axis=1)


def locate(points, elements):
    element = points >> 9
    chunk = (points >> 7) & 3
    row = jnp.where(points < elements * POINTS, chunk * elements + element, 4 * elements)
    return row, points & (LANES - 1)


def one_hot(index, count):
    steps = lax.broadcasted_iota(jnp.int32, (count, index.shape[1]), 0)
    return steps == index


def gather(field, chunks):
    high, low = split(field)
    both = jnp.concatenate([high, low], axis=1)
    out = []
    for row, lane in chunks:
        lanes = one_hot(lane, LANES).astype(F32).astype(BF16)
        picked = jnp.dot(
            both, jnp.concatenate([lanes, lanes], axis=0), preferred_element_type=F32
        )
        out.append(
            jnp.sum(
                jnp.where(one_hot(row, field.shape[0]), picked, 0.0), axis=0, keepdims=True
            )
        )
    return out


def scatter(rows, chunks, values):
    total = jnp.zeros((2 * rows, LANES), F32)
    for (row, lane), value in zip(chunks, values):
        lanes = one_hot(lane, LANES).astype(F32).astype(BF16)
        high, low = split(jnp.where(one_hot(row, rows), value, 0.0))
        total = total + lax.dot_general(
            jnp.concatenate([high, low], axis=0), lanes, NT, preferred_element_type=F32
        )
    return total[:rows] + total[rows:]


def chunked(row, lane):
    return [
        (row[:, at : at + STEP], lane[:, at : at + STEP]) for at in range(0, row.shape[1], STEP)
    ]


def cut(row):
    return [row[:, at : at + STEP] for at in range(0, row.shape[1], STEP)]


def pair_chunks(pair_ref, elements):
    row, lane = locate(pair_ref[...], elements)
    return chunked(row[0:1], lane[0:1]) + chunked(row[1:2], lane[1:2])


def joined(rows):
    return [
        jnp.concatenate([rows[at : at + 1], rows[at + 1 : at + 2]], axis=1)
        for at in range(0, rows.shape[0], 2)
    ]


def far_chunks(points, elements):
    row, lane = locate(points, elements)
    return list(zip(joined(row), joined(lane)))


def halves(wide):
    return [wide[:, at : at + LANES] for at in range(0, wide.shape[1], LANES)]


def own_group(devices, peers, away=0):
    shape = (devices, LANES)
    return lax.broadcasted_iota(jnp.int32, shape, 0) // peers - lax.axis_index("grp") == away


def send_shared(sent_ref, count, at, shared):
    devices = sent_ref.shape[0] // count
    copies = devices // shared.shape[0]
    sent_ref[pl.ds(at, devices, count), :] = jnp.concatenate([shared] * copies, axis=0)


def send_same(sent_ref, count, at, row):
    devices = sent_ref.shape[0] // count
    sent_ref[pl.ds(at, devices, count), :] = jnp.broadcast_to(row, (devices, LANES))


def send_values(sent_ref, faces_ref, count, values, peers):
    rows = jnp.concatenate([row for pair in values for row in halves(pair)], axis=0)
    send_shared(sent_ref, count, 0, rows[:peers])
    faces_ref[0 : 2 * FACE_ROWS, :] = rows[peers:]


def get(received_ref, count, at):
    return received_ref[pl.ds(at, received_ref.shape[0] // count, count), :]


def get_shared(received_ref, count, at, peers):
    rows = get(received_ref, count, at)
    mine = jnp.where(own_group(rows.shape[0], peers), rows, 0.0)
    shared = mine[:peers]
    for g in range(1, rows.shape[0] // peers):
        shared = shared + mine[g * peers : (g + 1) * peers]
    return shared


def get_row(rows, peers, away):
    here = lax.axis_index("grp") * peers + lax.axis_index("sub")
    source = lax.broadcasted_iota(jnp.int32, rows.shape, 0) - here == away * peers
    return jnp.sum(jnp.where(source, rows, 0.0), axis=0, keepdims=True)


def get_faces(gathered_ref, at, groups):
    count = gathered_ref.shape[0] // groups
    group = lax.axis_index("grp")
    below, above = 0.0, 0.0
    for g in range(groups):
        rows = gathered_ref[g * count + at : g * count + at + 2 * FACE_ROWS, :]
        below = below + jnp.where(group == g + 1, rows[FACE_ROWS:], 0.0)
        above = above + jnp.where(group == g - 1, rows[:FACE_ROWS], 0.0)
    return jnp.concatenate([below, above], axis=0)


def swapped(values):
    count = len(values) // 2
    return values[count:] + values[:count]


def along_first(field, table_ref, base):
    elements = field.shape[0] // 4
    turned = pltpu.roll(field, 64, axis=1)
    out = []
    for to in range(4):
        total = None
        for at in range(4):
            place = base + 2 * (4 * to + at)
            rows = slice(at * elements, (at + 1) * elements)
            term = (
                table_ref[place : place + 1, :] * field[rows]
                + table_ref[place + 1 : place + 2, :] * turned[rows]
            )
            total = term if total is None else total + term
        out.append(total)
    return jnp.concatenate(out, axis=0)


def stiffness(field, metric_ref, first_ref, inner_ref):
    metric = [rows_of(metric_ref[:, POINTS * d : POINTS * (d + 1)]) for d in range(3)]
    count = field.shape[0]
    grad_first = along_first(field, first_ref, 0)
    high, low = split(field)
    both = jnp.dot(
        jnp.concatenate([high, low], axis=0), inner_ref[:LANES], preferred_element_type=F32
    )
    inner = both[:count] + both[count:]
    inner = inner + jnp.dot(high, inner_ref[LANES:], preferred_element_type=F32)
    flux_first = metric[0] * grad_first
    flux = jnp.concatenate([metric[1], metric[2]], axis=1) * inner
    high, low = split(flux)
    both = lax.dot_general(
        jnp.concatenate([high, low], axis=0), inner_ref[:LANES], NT, preferred_element_type=F32
    )
    back = both[:count] + both[count:]
    back = back + lax.dot_general(high, inner_ref[LANES:], NT, preferred_element_type=F32)
    back = back + along_first(flux_first, first_ref, 32)
    energy = flux * inner
    return back, flux_first * grad_first + energy[:, :LANES] + energy[:, LANES:]


def factors(points):
    nodes = 0.5 * (1.0 + np.cos(np.pi * np.arange(8) / 7.0))
    out = []
    for shift in (6, 3, 0):
        index = (points >> shift) & 7
        near = jnp.full(points.shape, nodes[7], F32)
        far = jnp.full(points.shape, nodes[0], F32)
        for m in range(7):
            near = jnp.where(index == m, float(nodes[m]), near)
            far = jnp.where(index == m, float(nodes[7 - m]), far)
        out.append((near, far))
    return out


def corners(points):
    first, second, third = factors(points)
    return [
        first[q >> 2 & 1] * (second[q >> 1 & 1] * third[q & 1]) for q in range(8)
    ]


def own_corners():
    return corners(lax.broadcasted_iota(jnp.int32, (1, POINTS), 1))


def flat_map(mapped):
    elements = mapped.shape[1]
    width = 8 * elements
    own = own_element(elements, width)
    place = lax.broadcasted_iota(jnp.int32, (8, width), 1) // elements
    spread = jnp.where(own, 1.0, 0.0).astype(BF16)
    wide = jnp.dot(mapped.astype(F32).astype(BF16), spread, preferred_element_type=F32)
    keep = lax.broadcasted_iota(jnp.int32, (8, width), 0) == place
    return jnp.sum(jnp.where(keep, wide, 0.0), axis=0, keepdims=True)


def one_vertex(flat):
    return jnp.where(one_hot(whole(flat), NC), 1.0, 0.0)


def whole(values):
    return (values + 0.5).astype(jnp.int32)


def own_element(elements, width):
    shape = (elements, width)
    return lax.broadcasted_iota(jnp.int32, shape, 0) == (
        lax.broadcasted_iota(jnp.int32, shape, 1) % elements
    )


def own_place(elements, q):
    shape = (elements, 8 * elements)
    lane = lax.broadcasted_iota(jnp.int32, shape, 1)
    return lane == lax.broadcasted_iota(jnp.int32, shape, 0) + q * elements


def coarse_part(field, vertices, inverse):
    elements = field.shape[0] // 4
    flat = jnp.zeros((elements, 8 * elements), F32)
    for q, corner in enumerate(own_corners()):
        inner = None
        for c in range(4):
            term = field[c * elements : (c + 1) * elements] * corner[:, c * LANES : (c + 1) * LANES]
            inner = term if inner is None else inner + term
        flat = jnp.where(own_place(elements, q), jnp.sum(inner, axis=1, keepdims=True), flat)
    flat = jnp.sum(flat, axis=0, keepdims=True)
    part = jnp.sum(vertices * flat, axis=1, keepdims=True)
    part = jnp.sum(inverse * part, axis=0, keepdims=True)
    return jnp.concatenate([part, jnp.zeros((1, LANES - NC), F32)], axis=1)


def column(row):
    shape = (NC, LANES)
    keep = lax.broadcasted_iota(jnp.int32, shape, 0) == lax.broadcasted_iota(jnp.int32, shape, 1)
    return jnp.sum(jnp.where(keep, row, 0.0), axis=1, keepdims=True)


def get_solved(received_ref, count, peers):
    rows = get(received_ref, count, 1)
    return [
        column(
            jnp.sum(
                jnp.where(own_group(rows.shape[0], peers, away), rows, 0.0), axis=0, keepdims=True
            )
        )
        for away in (0, -1, 1)
    ]


def prolonged(solved, vertices, elements):
    flat = jnp.sum(vertices * solved, axis=0, keepdims=True)
    out = [None] * 4
    for q, corner in enumerate(own_corners()):
        value = jnp.sum(jnp.where(own_place(elements, q), flat, 0.0), axis=1, keepdims=True)
        for c in range(4):
            term = value * corner[:, c * LANES : (c + 1) * LANES]
            out[c] = term if out[c] is None else out[c] + term
    return jnp.concatenate(out, axis=0)


def prolong_at(points, vertices, elements):
    mine = lax.broadcasted_iota(jnp.int32, (elements, points.shape[1]), 0) == points >> 9
    weights = jnp.concatenate([jnp.where(mine, corner, 0.0) for corner in corners(points)], axis=0)
    high, low = split(weights)
    both = jnp.dot(
        vertices.astype(BF16),
        jnp.concatenate([high, low], axis=1),
        preferred_element_type=F32,
    )
    return both[:, : points.shape[1]] + both[:, points.shape[1] :]


def total_of(array):
    return jnp.sum(jnp.sum(array, axis=0, keepdims=True), axis=1, keepdims=True)


def packed(values):
    lane = lax.broadcasted_iota(jnp.int32, (1, LANES), 1)
    out = jnp.zeros((1, LANES), F32)
    for k, value in enumerate(values):
        out = jnp.where(lane == k, value, out)
    return out


def unpacked(row, count):
    lane = lax.broadcasted_iota(jnp.int32, row.shape, 1)
    return [
        jnp.sum(jnp.where(lane == k, row, 0.0), axis=1, keepdims=True) for k in range(count)
    ]


def first_kernel(
    right_hbm, jacobi_hbm, inverse_hbm, map_hbm, slot_hbm, face_hbm,
    sent_ref, faces_ref, fields_ref, points_ref,
    right_ref, jacobi_ref, inverse_ref, map_ref, slot_ref, face_ref, sems,
):
    copies = []
    for k, (source, target) in enumerate(
        (
            (face_hbm, face_ref),
            (slot_hbm, slot_ref),
            (right_hbm, right_ref),
            (jacobi_hbm, jacobi_ref),
            (map_hbm, map_ref),
            (inverse_hbm, inverse_ref),
        )
    ):
        copy = pltpu.make_async_copy(source, target, sems.at[k])
        copy.start()
        copies.append(copy)
    for copy in copies:
        copy.wait()
    elements = right_ref.shape[0]
    peers = slot_ref.shape[1]
    faces = face_ref[...]
    faces = jnp.concatenate(halves(faces[0:1]) + halves(faces[1:2]), axis=0)
    points = jnp.concatenate([slot_ref[0], faces], axis=0)
    points_ref[...] = points
    resid = rows_of(right_ref[...])
    flat = flat_map(map_ref[...])
    smoothed = rows_of(jacobi_ref[...]) * resid
    fields_ref[0 : 4 * elements, :] = resid
    fields_ref[4 * elements : 8 * elements, :] = smoothed
    fields_ref[8 * elements :, :] = jnp.broadcast_to(flat, (8, LANES))
    part = coarse_part(resid, one_vertex(flat), inverse_ref[0])
    values = gather(smoothed, far_chunks(points, elements))
    send_values(sent_ref, faces_ref, FIRST_ROWS, values, peers)
    send_same(sent_ref, FIRST_ROWS, 1, part)
    send_same(sent_ref, FIRST_ROWS, 2, flat)
    points = points.astype(F32)
    send_shared(sent_ref, FIRST_ROWS, 3, points[:peers])
    faces_ref[2 * FACE_ROWS :, :] = points[peers:]


def static_of(received_ref, gathered_ref, peers, elements):
    maps = get(received_ref, FIRST_ROWS, 2)
    own = get_shared(received_ref, FIRST_ROWS, 2, peers)
    shared = whole(get_shared(received_ref, FIRST_ROWS, 3, peers))
    out = [
        prolong_at(shared[b : b + 1], one_vertex(own[b : b + 1]), elements) for b in range(peers)
    ]
    faces = whole(get_faces(gathered_ref, 2 * FACE_ROWS, maps.shape[0] // peers))
    faces = joined(faces)
    for k, points in enumerate(faces):
        away = -1 if k < len(faces) // 2 else 1
        out.append(prolong_at(points, one_vertex(get_row(maps, peers, away)), elements))
    return jnp.concatenate(out, axis=1)


def get_far(received_ref, gathered_ref, count, peers):
    groups = received_ref.shape[0] // (count * peers)
    return jnp.concatenate(
        [get_shared(received_ref, count, 0, peers), get_faces(gathered_ref, 0, groups)], axis=0
    )


def apply(
    smoothed, count, received_ref, gathered_ref, weights, solved, metric_ref, helmholtz_ref,
    first_ref, inner_ref, pair_ref, points_ref, dots, back_ref, local_ref, sent_ref, faces_ref,
):
    elements = smoothed.shape[0] // 4
    peers = points_ref.shape[0] - 2 * FACE_ROWS
    pairs = pair_chunks(pair_ref, elements)
    far = far_chunks(points_ref[...], elements)
    ends = [LANES * k for k in (0, peers, peers + FACE_ROWS, peers + 2 * FACE_ROWS)]
    coarse = []
    for k in range(3):
        coarse += halves(
            jnp.sum(weights[:, ends[k] : ends[k + 1]] * solved[k], axis=0, keepdims=True)
        )
    incoming = get_far(received_ref, gathered_ref, count, peers) + jnp.concatenate(coarse, axis=0)
    values = swapped(gather(smoothed, pairs)) + joined(incoming)
    summed = smoothed + scatter(smoothed.shape[0], pairs + far, values)
    back, energy = stiffness(summed, metric_ref, first_ref, inner_ref)
    energy = energy + rows_of(helmholtz_ref[...]) * smoothed * smoothed
    back_ref[...] = back
    values = gather(back, pairs + far)
    near = swapped(values[: len(pairs)])
    for k, value in enumerate(near):
        local_ref[0:1, k * STEP : (k + 1) * STEP] = value
    send_values(sent_ref, faces_ref, ROWS, values[len(pairs) :], peers)
    send_same(sent_ref, ROWS, 1, packed(dots + [total_of(energy)]))


def image_of(
    field_ref, back_ref, local_ref, received_ref, gathered_ref, helmholtz_ref, pair_ref, points_ref
):
    elements = field_ref.shape[0] // 4
    peers = points_ref.shape[0] - 2 * FACE_ROWS
    chunks = pair_chunks(pair_ref, elements) + far_chunks(points_ref[...], elements)
    values = cut(local_ref[...]) + joined(get_far(received_ref, gathered_ref, ROWS, peers))
    summed = back_ref[...] + scatter(field_ref.shape[0], chunks, values)
    return summed + rows_of(helmholtz_ref[...]) * field_ref[...]


def start_kernel(
    received_ref, gathered_ref, fields_ref, points_ref, pair_ref, metric_ref, helmholtz_ref,
    first_ref, inner_ref,
    smoothed_ref, weights_ref, back_ref, local_ref, sent_ref, faces_ref,
):
    elements = helmholtz_ref.shape[0]
    peers = points_ref.shape[0] - 2 * FACE_ROWS
    solved = get_solved(received_ref, FIRST_ROWS, peers)
    resid = fields_ref[0 : 4 * elements, :]
    vertices = one_vertex(fields_ref[8 * elements : 8 * elements + 1, :])
    smoothed = fields_ref[4 * elements : 8 * elements, :]
    smoothed = smoothed + prolonged(solved[0], vertices, elements)
    smoothed_ref[...] = smoothed
    weights = static_of(received_ref, gathered_ref, peers, elements)
    weights_ref[...] = weights
    apply(
        smoothed, FIRST_ROWS, received_ref, gathered_ref, weights, solved, metric_ref,
        helmholtz_ref, first_ref, inner_ref, pair_ref, points_ref,
        [total_of(resid * smoothed)], back_ref, local_ref, sent_ref, faces_ref,
    )


def middle_kernel(
    received_ref, gathered_ref, fields_ref, points_ref, pair_ref, jacobi_ref, helmholtz_ref,
    inverse_ref, smoothed_ref, back_ref, local_ref,
    image_ref, resid_ref, scalars_ref, sent_ref, faces_ref,
):
    elements = helmholtz_ref.shape[0]
    peers = points_ref.shape[0] - 2 * FACE_ROWS
    dots = jnp.sum(get(received_ref, ROWS, 1), axis=0, keepdims=True)
    scalars_ref[...] = dots
    values = unpacked(dots, 2)
    alpha = values[0] / values[1]
    image = image_of(
        smoothed_ref, back_ref, local_ref, received_ref, gathered_ref, helmholtz_ref, pair_ref,
        points_ref,
    )
    image_ref[...] = image
    resid = fields_ref[0 : 4 * elements, :] - alpha * image
    resid_ref[...] = resid
    vertices = one_vertex(fields_ref[8 * elements : 8 * elements + 1, :])
    part = coarse_part(resid, vertices, inverse_ref[0])
    values = gather(rows_of(jacobi_ref[...]) * resid, far_chunks(points_ref[...], elements))
    send_values(sent_ref, faces_ref, ROWS, values, peers)
    send_same(sent_ref, ROWS, 1, part)


def second_kernel(
    received_ref, gathered_ref, fields_ref, points_ref, pair_ref, resid_ref, image_ref,
    weights_ref, jacobi_ref, metric_ref, helmholtz_ref, first_ref, inner_ref,
    smoothed_ref, back_ref, local_ref, sent_ref, faces_ref,
):
    elements = helmholtz_ref.shape[0]
    peers = points_ref.shape[0] - 2 * FACE_ROWS
    solved = get_solved(received_ref, ROWS, peers)
    resid = resid_ref[...]
    vertices = one_vertex(fields_ref[8 * elements : 8 * elements + 1, :])
    smoothed = rows_of(jacobi_ref[...]) * resid + prolonged(solved[0], vertices, elements)
    smoothed_ref[...] = smoothed
    apply(
        smoothed, ROWS, received_ref, gathered_ref, weights_ref[...], solved, metric_ref,
        helmholtz_ref, first_ref, inner_ref, pair_ref, points_ref,
        [total_of(resid * smoothed), total_of(image_ref[...] * smoothed)],
        back_ref, local_ref, sent_ref, faces_ref,
    )


def final_kernel(
    received_ref, gathered_ref, points_ref, pair_ref, old_ref, field_ref, resid_ref, old_image_ref,
    scalars_ref, back_ref, local_ref, helmholtz_ref,
    solution_ref, residual_ref,
):
    before = unpacked(scalars_ref[...], 2)
    now = unpacked(jnp.sum(get(received_ref, ROWS, 1), axis=0, keepdims=True), 3)
    alpha = before[0] / before[1]
    beta = now[0] / before[0]
    curved = now[2] + beta * (2.0 * now[1] + beta * before[1])
    step = now[0] / curved
    old = old_ref[...]
    direction = field_ref[...] + beta * old
    solution_ref[...] = wide_of(alpha * old + step * direction)
    image = image_of(
        field_ref, back_ref, local_ref, received_ref, gathered_ref, helmholtz_ref, pair_ref,
        points_ref,
    )
    image = image + beta * old_image_ref[...]
    residual_ref[...] = wide_of(resid_ref[...] - step * image)


def call(kernel, outs, *args, copied=False):
    space = pl.ANY if copied else pltpu.VMEM
    scratch = [pltpu.VMEM(arg.shape, arg.dtype) for arg in args] if copied else []
    return pl.pallas_call(
        kernel,
        out_shape=[jax.ShapeDtypeStruct(*out) if isinstance(out[0], tuple) else jax.ShapeDtypeStruct(out, F32) for out in outs],
        in_specs=[pl.BlockSpec(memory_space=space)] * len(args),
        out_specs=[pl.BlockSpec(memory_space=pltpu.VMEM)] * len(outs),
        scratch_shapes=scratch + ([pltpu.SemaphoreType.DMA((len(args),))] if copied else []),
        compiler_params=pltpu.CompilerParams(vmem_limit_bytes=(60 if copied else 24) * 1024 * 1024),
    )(*args)


def body(
    right_side,
    metric,
    helmholtz,
    jacobi,
    pair_list,
    shared_slots,
    face_points,
    coarse_map,
    coarse_inverse,
):
    peers = lax.axis_size("sub")
    groups = lax.axis_size("grp")
    t = {name: jnp.asarray(value) for name, value in tables().items()}
    elements = right_side.shape[0]
    field = (4 * elements, LANES)
    local = (1, pair_list.shape[0] * pair_list.shape[1])
    points_shape = (peers + 2 * FACE_ROWS, LANES)
    outs = [(groups * peers * ROWS, LANES), (2 * FACE_ROWS, LANES)]

    def exchange(sent, faces):
        gathered = lax.all_gather(faces, "grp", axis=0, tiled=True)
        rows = sent.reshape(groups * peers, 1, -1)
        received = lax.all_to_all(rows, ("grp", "sub"), 0, 0, tiled=True)
        return received.reshape(sent.shape), gathered

    sent, faces, fields, points = call(
        first_kernel,
        [
            (groups * peers * FIRST_ROWS, LANES),
            (4 * FACE_ROWS, LANES),
            (8 * elements + 8, LANES),
            (points_shape, jnp.int32),
        ],
        right_side, jacobi, coarse_inverse, coarse_map, shared_slots, face_points, copied=True,
    )
    smoothed, weights, back, near, sent, faces = call(
        start_kernel,
        [field, (NC, points_shape[0] * LANES), field, local, *outs],
        *exchange(sent, faces), fields, points, pair_list, metric, helmholtz,
        t["first"], t["inner"],
    )
    image, resid, scalars, sent, faces = call(
        middle_kernel, [field, field, (1, LANES), *outs],
        *exchange(sent, faces), fields, points, pair_list, jacobi, helmholtz, coarse_inverse,
        smoothed, back, near,
    )
    second, back, near, sent, faces = call(
        second_kernel, [field, field, local, *outs],
        *exchange(sent, faces), fields, points, pair_list, resid, image, weights, jacobi,
        metric, helmholtz, t["first"], t["inner"],
    )
    return tuple(
        call(
            final_kernel, [right_side.shape, right_side.shape],
            *exchange(sent, faces), points, pair_list, smoothed, second, resid, image, scalars,
            back, near, helmholtz,
        )
    )


def solution(mesh):
    in_specs = (
        P(("grp", "sub"), None),
        P(("grp", "sub"), None),
        P(("grp", "sub"), None),
        P(("grp", "sub"), None),
        P(None, ("grp", "sub")),
        P(("grp", "sub"), None, None),
        P(None, ("grp", "sub")),
        P(None, ("grp", "sub")),
        P("grp", None, None),
    )
    out_specs = (P(("grp", "sub"), None), P(("grp", "sub"), None))
    return jax.shard_map(body, mesh=mesh, in_specs=in_specs, out_specs=out_specs, check_vma=False)
```

```python
import jax
import jax.numpy as jnp
import ml_dtypes
import numpy as np
from jax import lax
from jax.experimental import pallas as pl
from jax.experimental.pallas import tpu as pltpu
from jax.sharding import PartitionSpec as P

NC = 64
POINTS = 512
LANES = 128
STEP = 256
FACE_ROWS = 4
ROWS = 8
FIRST_ROWS = 16
TERMS = FACE_ROWS
F32 = jnp.float32
BF16 = jnp.bfloat16
NT = (((1,), (1,)), ((), ()))


def split_constant(array):
    high = array.astype(ml_dtypes.bfloat16)
    low = (array - high.astype(np.float64)).astype(ml_dtypes.bfloat16)
    return high, low


def tables():
    order_index = np.arange(8)
    colloc = np.cos(np.pi * order_index / 7.0)
    end_weights = (
        np.where((order_index == 0) | (order_index == 7), 2.0, 1.0) * (-1.0) ** order_index
    )
    spacing = colloc[:, None] - colloc[None, :] + np.eye(8)
    raw_matrix = np.outer(end_weights, 1.0 / end_weights) / spacing
    off_part = raw_matrix * (1.0 - np.eye(8))
    derivative = 0.25 * (off_part - np.eye(8) * off_part.sum(axis=1)[:, None])
    along_inner = np.concatenate(
        [np.kron(np.eye(2), np.kron(derivative, np.eye(8))).T, np.kron(np.eye(16), derivative).T],
        axis=1,
    )
    high, low = split_constant(along_inner)
    inner = np.concatenate([high, low], axis=0)

    half = np.arange(LANES) // 64

    def first_rows(matrix):
        rows = []
        for to in range(4):
            for at in range(4):
                rows.append(matrix[2 * to + half, 2 * at + half])
                rows.append(matrix[2 * to + half, 2 * at + 1 - half])
        return np.stack(rows).astype(np.float32)

    return {
        "inner": inner,
        "first": np.concatenate([first_rows(derivative), first_rows(derivative.T)], axis=0),
    }


def split(value):
    high = value.astype(BF16)
    return high, (value - high.astype(F32)).astype(BF16)


def rows_of(wide):
    return jnp.concatenate([wide[:, LANES * c : LANES * (c + 1)] for c in range(4)], axis=0)


def wide_of(rows):
    elements = rows.shape[0] // 4
    return jnp.concatenate([rows[c * elements : (c + 1) * elements] for c in range(4)], axis=1)


def locate(points, elements):
    element = points >> 9
    chunk = (points >> 7) & 3
    row = jnp.where(points < elements * POINTS, chunk * elements + element, 4 * elements)
    return row, points & (LANES - 1)


def one_hot(index, count):
    steps = lax.broadcasted_iota(jnp.int32, (count, index.shape[1]), 0)
    return steps == index


def gather(field, chunks):
    high, low = split(field)
    both = jnp.concatenate([high, low], axis=1)
    out = []
    for row, lane in chunks:
        lanes = one_hot(lane, LANES).astype(F32).astype(BF16)
        picked = jnp.dot(
            both, jnp.concatenate([lanes, lanes], axis=0), preferred_element_type=F32
        )
        out.append(
            jnp.sum(
                jnp.where(one_hot(row, field.shape[0]), picked, 0.0), axis=0, keepdims=True
            )
        )
    return out


def scatter(rows, chunks, values):
    total = jnp.zeros((2 * rows, LANES), F32)
    for (row, lane), value in zip(chunks, values):
        lanes = one_hot(lane, LANES).astype(F32).astype(BF16)
        high, low = split(jnp.where(one_hot(row, rows), value, 0.0))
        total = total + lax.dot_general(
            jnp.concatenate([high, low], axis=0), lanes, NT, preferred_element_type=F32
        )
    return total[:rows] + total[rows:]


def chunked(row, lane):
    return [
        (row[:, at : at + STEP], lane[:, at : at + STEP]) for at in range(0, row.shape[1], STEP)
    ]


def cut(row):
    return [row[:, at : at + STEP] for at in range(0, row.shape[1], STEP)]


def pair_chunks(pair_ref, elements):
    row, lane = locate(pair_ref[...], elements)
    return chunked(row[0:1], lane[0:1]) + chunked(row[1:2], lane[1:2])


def joined(rows):
    return [
        jnp.concatenate([rows[at : at + 1], rows[at + 1 : at + 2]], axis=1)
        for at in range(0, rows.shape[0], 2)
    ]


def far_chunks(points, elements):
    row, lane = locate(points, elements)
    return list(zip(joined(row), joined(lane)))


def halves(wide):
    return [wide[:, at : at + LANES] for at in range(0, wide.shape[1], LANES)]


def own_group(devices, peers, away=0):
    shape = (devices, LANES)
    return lax.broadcasted_iota(jnp.int32, shape, 0) // peers - lax.axis_index("grp") == away


def send_rows(sent_ref, count, at, rows, peers):
    devices = sent_ref.shape[0] // count
    above = own_group(devices, peers, 1)
    shared = jnp.concatenate([rows[:peers]] * (devices // peers), axis=0)
    for r in range(FACE_ROWS):
        down = rows[peers + r : peers + r + 1]
        up = rows[peers + FACE_ROWS + r : peers + FACE_ROWS + r + 1]
        out = jnp.where(above, up, down)
        if r == 0:
            out = jnp.where(own_group(devices, peers), shared, out)
        sent_ref[pl.ds(at + r, devices, count), :] = out


def send_same(sent_ref, count, at, row):
    devices = sent_ref.shape[0] // count
    sent_ref[pl.ds(at, devices, count), :] = jnp.broadcast_to(row, (devices, LANES))


def send_values(sent_ref, count, values, peers):
    rows = jnp.concatenate([row for pair in values for row in halves(pair)], axis=0)
    send_rows(sent_ref, count, 0, rows, peers)


def get(received_ref, count, at):
    return received_ref[pl.ds(at, received_ref.shape[0] // count, count), :]


def get_shared(rows, peers):
    mine = jnp.where(own_group(rows.shape[0], peers), rows, 0.0)
    shared = mine[:peers]
    for g in range(1, rows.shape[0] // peers):
        shared = shared + mine[g * peers : (g + 1) * peers]
    return shared


def get_row(rows, peers, away):
    here = lax.axis_index("grp") * peers + lax.axis_index("sub")
    source = lax.broadcasted_iota(jnp.int32, rows.shape, 0) - here == away * peers
    return jnp.sum(jnp.where(source, rows, 0.0), axis=0, keepdims=True)


def get_rows(received_ref, count, at, peers):
    rows = [get(received_ref, count, at + r) for r in range(FACE_ROWS)]
    faces = [get_row(part, peers, away) for away in (-1, 1) for part in rows]
    return jnp.concatenate([get_shared(rows[0], peers)] + faces, axis=0)


def swapped(values):
    count = len(values) // 2
    return values[count:] + values[:count]


def along_first(field, table_ref, base):
    elements = field.shape[0] // 4
    turned = pltpu.roll(field, 64, axis=1)
    out = []
    for to in range(4):
        total = None
        for at in range(4):
            place = base + 2 * (4 * to + at)
            rows = slice(at * elements, (at + 1) * elements)
            term = (
                table_ref[place : place + 1, :] * field[rows]
                + table_ref[place + 1 : place + 2, :] * turned[rows]
            )
            total = term if total is None else total + term
        out.append(total)
    return jnp.concatenate(out, axis=0)


def stiffness(field, metric_ref, first_ref, inner_ref):
    metric = [rows_of(metric_ref[:, POINTS * d : POINTS * (d + 1)]) for d in range(3)]
    count = field.shape[0]
    grad_first = along_first(field, first_ref, 0)
    high, low = split(field)
    both = jnp.dot(
        jnp.concatenate([high, low], axis=0), inner_ref[:LANES], preferred_element_type=F32
    )
    inner = both[:count] + both[count:]
    inner = inner + jnp.dot(high, inner_ref[LANES:], preferred_element_type=F32)
    flux_first = metric[0] * grad_first
    flux = jnp.concatenate([metric[1], metric[2]], axis=1) * inner
    high, low = split(flux)
    both = lax.dot_general(
        jnp.concatenate([high, low], axis=0), inner_ref[:LANES], NT, preferred_element_type=F32
    )
    back = both[:count] + both[count:]
    back = back + lax.dot_general(high, inner_ref[LANES:], NT, preferred_element_type=F32)
    back = back + along_first(flux_first, first_ref, 32)
    energy = flux * inner
    return back, flux_first * grad_first + energy[:, :LANES] + energy[:, LANES:]


def factors(points):
    nodes = 0.5 * (1.0 + np.cos(np.pi * np.arange(8) / 7.0))
    out = []
    for shift in (6, 3, 0):
        index = (points >> shift) & 7
        near = jnp.full(points.shape, nodes[7], F32)
        far = jnp.full(points.shape, nodes[0], F32)
        for m in range(7):
            near = jnp.where(index == m, float(nodes[m]), near)
            far = jnp.where(index == m, float(nodes[7 - m]), far)
        out.append((near, far))
    return out


def corners(points):
    first, second, third = factors(points)
    return [
        first[q >> 2 & 1] * (second[q >> 1 & 1] * third[q & 1]) for q in range(8)
    ]


def own_corners():
    return corners(lax.broadcasted_iota(jnp.int32, (1, POINTS), 1))


def flat_map(mapped):
    elements = mapped.shape[1]
    width = 8 * elements
    own = own_element(elements, width)
    place = lax.broadcasted_iota(jnp.int32, (8, width), 1) // elements
    spread = jnp.where(own, 1.0, 0.0).astype(BF16)
    wide = jnp.dot(mapped.astype(F32).astype(BF16), spread, preferred_element_type=F32)
    keep = lax.broadcasted_iota(jnp.int32, (8, width), 0) == place
    return jnp.sum(jnp.where(keep, wide, 0.0), axis=0, keepdims=True)


def one_vertex(flat):
    return jnp.where(one_hot(whole(flat), NC), 1.0, 0.0)


def whole(values):
    return (values + 0.5).astype(jnp.int32)


def own_element(elements, width):
    shape = (elements, width)
    return lax.broadcasted_iota(jnp.int32, shape, 0) == (
        lax.broadcasted_iota(jnp.int32, shape, 1) % elements
    )


def own_place(elements, q):
    shape = (elements, 8 * elements)
    lane = lax.broadcasted_iota(jnp.int32, shape, 1)
    return lane == lax.broadcasted_iota(jnp.int32, shape, 0) + q * elements


def coarse_part(field, vertices, inverse):
    elements = field.shape[0] // 4
    flat = jnp.zeros((elements, 8 * elements), F32)
    for q, corner in enumerate(own_corners()):
        inner = None
        for c in range(4):
            term = field[c * elements : (c + 1) * elements] * corner[:, c * LANES : (c + 1) * LANES]
            inner = term if inner is None else inner + term
        flat = jnp.where(own_place(elements, q), jnp.sum(inner, axis=1, keepdims=True), flat)
    flat = jnp.sum(flat, axis=0, keepdims=True)
    part = jnp.sum(vertices * flat, axis=1, keepdims=True)
    part = jnp.sum(inverse * part, axis=0, keepdims=True)
    return jnp.concatenate([part, jnp.zeros((1, LANES - NC), F32)], axis=1)


def column(row):
    shape = (NC, LANES)
    keep = lax.broadcasted_iota(jnp.int32, shape, 0) == lax.broadcasted_iota(jnp.int32, shape, 1)
    return jnp.sum(jnp.where(keep, row, 0.0), axis=1, keepdims=True)


def get_solved(received_ref, count, peers):
    rows = get(received_ref, count, TERMS)
    return [
        column(
            jnp.sum(
                jnp.where(own_group(rows.shape[0], peers, away), rows, 0.0), axis=0, keepdims=True
            )
        )
        for away in (0, -1, 1)
    ]


def prolonged(solved, vertices, elements):
    flat = jnp.sum(vertices * solved, axis=0, keepdims=True)
    out = [None] * 4
    for q, corner in enumerate(own_corners()):
        value = jnp.sum(jnp.where(own_place(elements, q), flat, 0.0), axis=1, keepdims=True)
        for c in range(4):
            term = value * corner[:, c * LANES : (c + 1) * LANES]
            out[c] = term if out[c] is None else out[c] + term
    return jnp.concatenate(out, axis=0)


def prolong_at(points, vertices, elements):
    mine = lax.broadcasted_iota(jnp.int32, (elements, points.shape[1]), 0) == points >> 9
    weights = jnp.concatenate([jnp.where(mine, corner, 0.0) for corner in corners(points)], axis=0)
    high, low = split(weights)
    both = jnp.dot(
        vertices.astype(BF16),
        jnp.concatenate([high, low], axis=1),
        preferred_element_type=F32,
    )
    return both[:, : points.shape[1]] + both[:, points.shape[1] :]


def total_of(array):
    return jnp.sum(jnp.sum(array, axis=0, keepdims=True), axis=1, keepdims=True)


def packed(values):
    lane = lax.broadcasted_iota(jnp.int32, (1, LANES), 1)
    out = jnp.zeros((1, LANES), F32)
    for k, value in enumerate(values):
        out = jnp.where(lane == k, value, out)
    return out


def unpacked(row, count):
    lane = lax.broadcasted_iota(jnp.int32, row.shape, 1)
    return [
        jnp.sum(jnp.where(lane == k, row, 0.0), axis=1, keepdims=True) for k in range(count)
    ]


def first_kernel(
    right_hbm, jacobi_hbm, inverse_hbm, map_hbm, slot_hbm, face_hbm,
    sent_ref, fields_ref, points_ref,
    right_ref, jacobi_ref, inverse_ref, map_ref, slot_ref, face_ref, sems,
):
    copies = []
    for k, (source, target) in enumerate(
        (
            (face_hbm, face_ref),
            (slot_hbm, slot_ref),
            (right_hbm, right_ref),
            (jacobi_hbm, jacobi_ref),
            (map_hbm, map_ref),
            (inverse_hbm, inverse_ref),
        )
    ):
        copy = pltpu.make_async_copy(source, target, sems.at[k])
        copy.start()
        copies.append(copy)
    for copy in copies:
        copy.wait()
    elements = right_ref.shape[0]
    peers = slot_ref.shape[1]
    faces = face_ref[...]
    faces = jnp.concatenate(halves(faces[0:1]) + halves(faces[1:2]), axis=0)
    points = jnp.concatenate([slot_ref[0], faces], axis=0)
    points_ref[...] = points
    resid = rows_of(right_ref[...])
    flat = flat_map(map_ref[...])
    smoothed = rows_of(jacobi_ref[...]) * resid
    fields_ref[0 : 4 * elements, :] = resid
    fields_ref[4 * elements : 8 * elements, :] = smoothed
    fields_ref[8 * elements :, :] = jnp.broadcast_to(flat, (8, LANES))
    part = coarse_part(resid, one_vertex(flat), inverse_ref[0])
    values = gather(smoothed, far_chunks(points, elements))
    send_values(sent_ref, FIRST_ROWS, values, peers)
    send_same(sent_ref, FIRST_ROWS, TERMS, part)
    send_same(sent_ref, FIRST_ROWS, TERMS + 1, flat)
    send_rows(sent_ref, FIRST_ROWS, TERMS + 2, points.astype(F32), peers)


def static_of(received_ref, peers, elements):
    maps = get(received_ref, FIRST_ROWS, TERMS + 1)
    own = get_shared(maps, peers)
    points = whole(get_rows(received_ref, FIRST_ROWS, TERMS + 2, peers))
    out = [
        prolong_at(points[b : b + 1], one_vertex(own[b : b + 1]), elements) for b in range(peers)
    ]
    for k, pair in enumerate(joined(points[peers:])):
        away = -1 if 2 * k < FACE_ROWS else 1
        out.append(prolong_at(pair, one_vertex(get_row(maps, peers, away)), elements))
    return jnp.concatenate(out, axis=1)


def apply(
    smoothed, count, received_ref, weights, solved, metric_ref, helmholtz_ref,
    first_ref, inner_ref, pair_ref, points_ref, dots, back_ref, local_ref, sent_ref,
):
    elements = smoothed.shape[0] // 4
    peers = points_ref.shape[0] - 2 * FACE_ROWS
    pairs = pair_chunks(pair_ref, elements)
    far = far_chunks(points_ref[...], elements)
    ends = [LANES * k for k in (0, peers, peers + FACE_ROWS, peers + 2 * FACE_ROWS)]
    coarse = []
    for k in range(3):
        coarse += halves(
            jnp.sum(weights[:, ends[k] : ends[k + 1]] * solved[k], axis=0, keepdims=True)
        )
    incoming = get_rows(received_ref, count, 0, peers) + jnp.concatenate(coarse, axis=0)
    values = swapped(gather(smoothed, pairs)) + joined(incoming)
    summed = smoothed + scatter(smoothed.shape[0], pairs + far, values)
    back, energy = stiffness(summed, metric_ref, first_ref, inner_ref)
    energy = energy + rows_of(helmholtz_ref[...]) * smoothed * smoothed
    back_ref[...] = back
    values = gather(back, pairs + far)
    near = swapped(values[: len(pairs)])
    for k, value in enumerate(near):
        local_ref[0:1, k * STEP : (k + 1) * STEP] = value
    send_values(sent_ref, ROWS, values[len(pairs) :], peers)
    send_same(sent_ref, ROWS, TERMS, packed(dots + [total_of(energy)]))


def image_of(
    field_ref, back_ref, local_ref, received_ref, helmholtz_ref, pair_ref, points_ref
):
    elements = field_ref.shape[0] // 4
    peers = points_ref.shape[0] - 2 * FACE_ROWS
    chunks = pair_chunks(pair_ref, elements) + far_chunks(points_ref[...], elements)
    values = cut(local_ref[...]) + joined(get_rows(received_ref, ROWS, 0, peers))
    summed = back_ref[...] + scatter(field_ref.shape[0], chunks, values)
    return summed + rows_of(helmholtz_ref[...]) * field_ref[...]


def start_kernel(
    received_ref, fields_ref, points_ref, pair_ref, metric_ref, helmholtz_ref,
    first_ref, inner_ref,
    smoothed_ref, weights_ref, back_ref, local_ref, sent_ref,
):
    elements = helmholtz_ref.shape[0]
    peers = points_ref.shape[0] - 2 * FACE_ROWS
    solved = get_solved(received_ref, FIRST_ROWS, peers)
    resid = fields_ref[0 : 4 * elements, :]
    vertices = one_vertex(fields_ref[8 * elements : 8 * elements + 1, :])
    smoothed = fields_ref[4 * elements : 8 * elements, :]
    smoothed = smoothed + prolonged(solved[0], vertices, elements)
    smoothed_ref[...] = smoothed
    weights = static_of(received_ref, peers, elements)
    weights_ref[...] = weights
    apply(
        smoothed, FIRST_ROWS, received_ref, weights, solved, metric_ref,
        helmholtz_ref, first_ref, inner_ref, pair_ref, points_ref,
        [total_of(resid * smoothed)], back_ref, local_ref, sent_ref,
    )


def middle_kernel(
    received_ref, fields_ref, points_ref, pair_ref, jacobi_ref, helmholtz_ref,
    inverse_ref, smoothed_ref, back_ref, local_ref,
    image_ref, resid_ref, scalars_ref, sent_ref,
):
    elements = helmholtz_ref.shape[0]
    peers = points_ref.shape[0] - 2 * FACE_ROWS
    dots = jnp.sum(get(received_ref, ROWS, TERMS), axis=0, keepdims=True)
    scalars_ref[...] = dots
    values = unpacked(dots, 2)
    alpha = values[0] / values[1]
    image = image_of(
        smoothed_ref, back_ref, local_ref, received_ref, helmholtz_ref, pair_ref,
        points_ref,
    )
    image_ref[...] = image
    resid = fields_ref[0 : 4 * elements, :] - alpha * image
    resid_ref[...] = resid
    vertices = one_vertex(fields_ref[8 * elements : 8 * elements + 1, :])
    part = coarse_part(resid, vertices, inverse_ref[0])
    values = gather(rows_of(jacobi_ref[...]) * resid, far_chunks(points_ref[...], elements))
    send_values(sent_ref, ROWS, values, peers)
    send_same(sent_ref, ROWS, TERMS, part)


def second_kernel(
    received_ref, fields_ref, points_ref, pair_ref, resid_ref, image_ref,
    weights_ref, jacobi_ref, metric_ref, helmholtz_ref, first_ref, inner_ref,
    smoothed_ref, back_ref, local_ref, sent_ref,
):
    elements = helmholtz_ref.shape[0]
    peers = points_ref.shape[0] - 2 * FACE_ROWS
    solved = get_solved(received_ref, ROWS, peers)
    resid = resid_ref[...]
    vertices = one_vertex(fields_ref[8 * elements : 8 * elements + 1, :])
    smoothed = rows_of(jacobi_ref[...]) * resid + prolonged(solved[0], vertices, elements)
    smoothed_ref[...] = smoothed
    apply(
        smoothed, ROWS, received_ref, weights_ref[...], solved, metric_ref,
        helmholtz_ref, first_ref, inner_ref, pair_ref, points_ref,
        [total_of(resid * smoothed), total_of(image_ref[...] * smoothed)],
        back_ref, local_ref, sent_ref,
    )


def final_kernel(
    received_ref, points_ref, pair_ref, old_ref, field_ref, resid_ref, old_image_ref,
    scalars_ref, back_ref, local_ref, helmholtz_ref,
    solution_ref, residual_ref,
):
    before = unpacked(scalars_ref[...], 2)
    now = unpacked(jnp.sum(get(received_ref, ROWS, TERMS), axis=0, keepdims=True), 3)
    alpha = before[0] / before[1]
    beta = now[0] / before[0]
    curved = now[2] + beta * (2.0 * now[1] + beta * before[1])
    step = now[0] / curved
    old = old_ref[...]
    direction = field_ref[...] + beta * old
    solution_ref[...] = wide_of(alpha * old + step * direction)
    image = image_of(
        field_ref, back_ref, local_ref, received_ref, helmholtz_ref, pair_ref,
        points_ref,
    )
    image = image + beta * old_image_ref[...]
    residual_ref[...] = wide_of(resid_ref[...] - step * image)


def call(kernel, outs, *args, copied=False):
    space = pl.ANY if copied else pltpu.VMEM
    scratch = [pltpu.VMEM(arg.shape, arg.dtype) for arg in args] if copied else []
    return pl.pallas_call(
        kernel,
        out_shape=[
            jax.ShapeDtypeStruct(*(out if isinstance(out[0], tuple) else (out, F32))) for out in outs
        ],
        in_specs=[pl.BlockSpec(memory_space=space)] * len(args),
        out_specs=[pl.BlockSpec(memory_space=pltpu.VMEM)] * len(outs),
        scratch_shapes=scratch + ([pltpu.SemaphoreType.DMA((len(args),))] if copied else []),
        compiler_params=pltpu.CompilerParams(vmem_limit_bytes=(60 if copied else 24) * 1024 * 1024),
    )(*args)


def body(
    right_side,
    metric,
    helmholtz,
    jacobi,
    pair_list,
    shared_slots,
    face_points,
    coarse_map,
    coarse_inverse,
):
    peers = lax.axis_size("sub")
    groups = lax.axis_size("grp")
    t = {name: jnp.asarray(value) for name, value in tables().items()}
    elements = right_side.shape[0]
    field = (4 * elements, LANES)
    local = (1, pair_list.shape[0] * pair_list.shape[1])
    points_shape = (peers + 2 * FACE_ROWS, LANES)
    sent_shape = (groups * peers * ROWS, LANES)

    def exchange(sent):
        rows = sent.reshape(groups * peers, -1, LANES)
        return lax.all_to_all(rows, ("grp", "sub"), 0, 0, tiled=True).reshape(sent.shape)

    sent, fields, points = call(
        first_kernel,
        [
            (groups * peers * FIRST_ROWS, LANES),
            (8 * elements + 8, LANES),
            (points_shape, jnp.int32),
        ],
        right_side, jacobi, coarse_inverse, coarse_map, shared_slots, face_points, copied=True,
    )
    smoothed, weights, back, near, sent = call(
        start_kernel,
        [field, (NC, points_shape[0] * LANES), field, local, sent_shape],
        exchange(sent), fields, points, pair_list, metric, helmholtz,
        t["first"], t["inner"],
    )
    image, resid, scalars, sent = call(
        middle_kernel, [field, field, (1, LANES), sent_shape],
        exchange(sent), fields, points, pair_list, jacobi, helmholtz, coarse_inverse,
        smoothed, back, near,
    )
    second, back, near, sent = call(
        second_kernel, [field, field, local, sent_shape],
        exchange(sent), fields, points, pair_list, resid, image, weights, jacobi,
        metric, helmholtz, t["first"], t["inner"],
    )
    return tuple(
        call(
            final_kernel, [right_side.shape, right_side.shape],
            exchange(sent), points, pair_list, smoothed, second, resid, image, scalars,
            back, near, helmholtz,
        )
    )


def solution(mesh):
    in_specs = (
        P(("grp", "sub"), None),
        P(("grp", "sub"), None),
        P(("grp", "sub"), None),
        P(("grp", "sub"), None),
        P(None, ("grp", "sub")),
        P(("grp", "sub"), None, None),
        P(None, ("grp", "sub")),
        P(None, ("grp", "sub")),
        P("grp", None, None),
    )
    out_specs = (P(("grp", "sub"), None), P(("grp", "sub"), None))
    return jax.shard_map(body, mesh=mesh, in_specs=in_specs, out_specs=out_specs, check_vma=False)
```

```python
import jax
import jax.numpy as jnp
import ml_dtypes
import numpy as np
from jax import lax
from jax.experimental import pallas as pl
from jax.experimental.pallas import tpu as pltpu
from jax.sharding import PartitionSpec as P

NC = 64
POINTS = 512
LANES = 128
STEP = 256
FACE_ROWS = 4
ROWS = 5
FIRST_ROWS = 10
TERMS = FACE_ROWS
F32 = jnp.float32
BF16 = jnp.bfloat16
NT = (((1,), (1,)), ((), ()))


def split_constant(array):
    high = array.astype(ml_dtypes.bfloat16)
    low = (array - high.astype(np.float64)).astype(ml_dtypes.bfloat16)
    return high, low


def tables():
    order_index = np.arange(8)
    colloc = np.cos(np.pi * order_index / 7.0)
    end_weights = (
        np.where((order_index == 0) | (order_index == 7), 2.0, 1.0) * (-1.0) ** order_index
    )
    spacing = colloc[:, None] - colloc[None, :] + np.eye(8)
    raw_matrix = np.outer(end_weights, 1.0 / end_weights) / spacing
    off_part = raw_matrix * (1.0 - np.eye(8))
    derivative = 0.25 * (off_part - np.eye(8) * off_part.sum(axis=1)[:, None])
    along_inner = np.concatenate(
        [np.kron(np.eye(2), np.kron(derivative, np.eye(8))).T, np.kron(np.eye(16), derivative).T],
        axis=1,
    )
    high, low = split_constant(along_inner)
    inner = np.concatenate([high, low], axis=0)

    half = np.arange(LANES) // 64

    def first_rows(matrix):
        rows = []
        for to in range(4):
            for at in range(4):
                rows.append(matrix[2 * to + half, 2 * at + half])
                rows.append(matrix[2 * to + half, 2 * at + 1 - half])
        return np.stack(rows).astype(np.float32)

    return {
        "inner": inner,
        "first": np.concatenate([first_rows(derivative), first_rows(derivative.T)], axis=0),
    }


def split(value):
    high = value.astype(BF16)
    return high, (value - high.astype(F32)).astype(BF16)


def rows_of(wide):
    return jnp.concatenate([wide[:, LANES * c : LANES * (c + 1)] for c in range(4)], axis=0)


def wide_of(rows):
    elements = rows.shape[0] // 4
    return jnp.concatenate([rows[c * elements : (c + 1) * elements] for c in range(4)], axis=1)


def locate(points, elements):
    element = points >> 9
    chunk = (points >> 7) & 3
    row = jnp.where(points < elements * POINTS, chunk * elements + element, 4 * elements)
    return row, points & (LANES - 1)


def one_hot(index, count):
    steps = lax.broadcasted_iota(jnp.int32, (count, index.shape[1]), 0)
    return steps == index


def lane_hot(lane):
    steps = lax.broadcasted_iota(jnp.int32, (LANES, lane.shape[1]), 0).astype(F32).astype(BF16)
    one = jnp.ones(steps.shape, BF16)
    return jnp.where(steps == lane.astype(F32).astype(BF16), one, jnp.zeros_like(one))


def gather(field, chunks):
    high, low = split(field)
    both = jnp.concatenate([high, low], axis=1)
    out = []
    for row, lane in chunks:
        lanes = lane_hot(lane)
        picked = jnp.dot(
            both, jnp.concatenate([lanes, lanes], axis=0), preferred_element_type=F32
        )
        out.append(
            jnp.sum(
                jnp.where(one_hot(row, field.shape[0]), picked, 0.0), axis=0, keepdims=True
            )
        )
    return out


def scatter(rows, chunks, values):
    total = jnp.zeros((2 * rows, LANES), F32)
    for (row, lane), value in zip(chunks, values):
        steps = lax.broadcasted_iota(jnp.int32, (rows, row.shape[1]), 0).astype(F32).astype(BF16)
        mine = steps == row.astype(F32).astype(BF16)
        parts = [jnp.where(mine, part, jnp.zeros_like(steps)) for part in split(value)]
        total = total + lax.dot_general(
            jnp.concatenate(parts, axis=0), lane_hot(lane), NT, preferred_element_type=F32
        )
    return total[:rows] + total[rows:]


def chunked(row, lane):
    return [
        (row[:, at : at + STEP], lane[:, at : at + STEP]) for at in range(0, row.shape[1], STEP)
    ]


def cut(row):
    return [row[:, at : at + STEP] for at in range(0, row.shape[1], STEP)]


def pair_chunks(pair_ref, elements):
    row, lane = locate(pair_ref[...], elements)
    return chunked(row[0:1], lane[0:1]) + chunked(row[1:2], lane[1:2])


def joined(rows):
    return [
        jnp.concatenate([rows[at : at + 1], rows[at + 1 : at + 2]], axis=1)
        for at in range(0, rows.shape[0], 2)
    ]


def far_chunks(points, elements):
    row, lane = locate(points, elements)
    return list(zip(joined(row), joined(lane)))


def halves(wide):
    return [wide[:, at : at + LANES] for at in range(0, wide.shape[1], LANES)]


def own_group(devices, peers, away=0):
    shape = (devices, LANES)
    return lax.broadcasted_iota(jnp.int32, shape, 0) // peers - lax.axis_index("grp") == away


def send_rows(sent_ref, count, at, rows, peers):
    devices = sent_ref.shape[0] // count
    above = own_group(devices, peers, 1)
    shared = jnp.concatenate([rows[:peers]] * (devices // peers), axis=0)
    for r in range(FACE_ROWS):
        down = rows[peers + r : peers + r + 1]
        up = rows[peers + FACE_ROWS + r : peers + FACE_ROWS + r + 1]
        out = jnp.where(above, up, down)
        if r == 0:
            out = jnp.where(own_group(devices, peers), shared, out)
        sent_ref[pl.ds(at + r, devices, count), :] = out


def send_same(sent_ref, count, at, row):
    devices = sent_ref.shape[0] // count
    sent_ref[pl.ds(at, devices, count), :] = jnp.broadcast_to(row, (devices, LANES))


def send_values(sent_ref, count, values, peers):
    rows = jnp.concatenate([row for pair in values for row in halves(pair)], axis=0)
    send_rows(sent_ref, count, 0, rows, peers)


def get(received_ref, count, at):
    return received_ref[pl.ds(at, received_ref.shape[0] // count, count), :]


def get_shared(rows, peers):
    mine = jnp.where(own_group(rows.shape[0], peers), rows, 0.0)
    shared = mine[:peers]
    for g in range(1, rows.shape[0] // peers):
        shared = shared + mine[g * peers : (g + 1) * peers]
    return shared


def get_row(rows, peers, away):
    here = lax.axis_index("grp") * peers + lax.axis_index("sub")
    source = lax.broadcasted_iota(jnp.int32, rows.shape, 0) - here == away * peers
    return jnp.sum(jnp.where(source, rows, 0.0), axis=0, keepdims=True)


def get_rows(received_ref, count, at, peers):
    rows = [get(received_ref, count, at + r) for r in range(FACE_ROWS)]
    faces = [get_row(part, peers, away) for away in (-1, 1) for part in rows]
    return jnp.concatenate([get_shared(rows[0], peers)] + faces, axis=0)


def swapped(values):
    count = len(values) // 2
    return values[count:] + values[:count]


def along_first(field, table_ref, base):
    elements = field.shape[0] // 4
    turned = pltpu.roll(field, 64, axis=1)
    out = []
    for to in range(4):
        total = None
        for at in range(4):
            place = base + 2 * (4 * to + at)
            rows = slice(at * elements, (at + 1) * elements)
            term = (
                table_ref[place : place + 1, :] * field[rows]
                + table_ref[place + 1 : place + 2, :] * turned[rows]
            )
            total = term if total is None else total + term
        out.append(total)
    return jnp.concatenate(out, axis=0)


def stiffness(field, metric_ref, first_ref, inner_ref):
    metric = [rows_of(metric_ref[:, POINTS * d : POINTS * (d + 1)]) for d in range(3)]
    count = field.shape[0]
    grad_first = along_first(field, first_ref, 0)
    high, low = split(field)
    both = jnp.dot(
        jnp.concatenate([high, low], axis=0), inner_ref[:LANES], preferred_element_type=F32
    )
    inner = both[:count] + both[count:]
    inner = inner + jnp.dot(high, inner_ref[LANES:], preferred_element_type=F32)
    flux_first = metric[0] * grad_first
    flux = jnp.concatenate([metric[1], metric[2]], axis=1) * inner
    high, low = split(flux)
    both = lax.dot_general(
        jnp.concatenate([high, low], axis=0), inner_ref[:LANES], NT, preferred_element_type=F32
    )
    back = both[:count] + both[count:]
    back = back + lax.dot_general(high, inner_ref[LANES:], NT, preferred_element_type=F32)
    back = back + along_first(flux_first, first_ref, 32)
    energy = flux * inner
    return back, flux_first * grad_first + energy[:, :LANES] + energy[:, LANES:]


def factors(points):
    nodes = 0.5 * (1.0 + np.cos(np.pi * np.arange(8) / 7.0))
    out = []
    for shift in (6, 3, 0):
        index = (points >> shift) & 7
        near = jnp.full(points.shape, nodes[7], F32)
        far = jnp.full(points.shape, nodes[0], F32)
        for m in range(7):
            near = jnp.where(index == m, float(nodes[m]), near)
            far = jnp.where(index == m, float(nodes[7 - m]), far)
        out.append((near, far))
    return out


def corners(points):
    first, second, third = factors(points)
    return [
        first[q >> 2 & 1] * (second[q >> 1 & 1] * third[q & 1]) for q in range(8)
    ]


def own_corners():
    return corners(lax.broadcasted_iota(jnp.int32, (1, POINTS), 1))


def flat_map(mapped):
    elements = mapped.shape[1]
    width = 8 * elements
    own = own_element(elements, width)
    place = lax.broadcasted_iota(jnp.int32, (8, width), 1) // elements
    spread = jnp.where(own, 1.0, 0.0).astype(BF16)
    wide = jnp.dot(mapped.astype(F32).astype(BF16), spread, preferred_element_type=F32)
    keep = lax.broadcasted_iota(jnp.int32, (8, width), 0) == place
    return jnp.sum(jnp.where(keep, wide, 0.0), axis=0, keepdims=True)


def one_vertex(flat):
    return jnp.where(one_hot(whole(flat), NC), 1.0, 0.0)


def whole(values):
    return (values + 0.5).astype(jnp.int32)


def own_element(elements, width):
    shape = (elements, width)
    return lax.broadcasted_iota(jnp.int32, shape, 0) == (
        lax.broadcasted_iota(jnp.int32, shape, 1) % elements
    )


def own_place(elements, q):
    shape = (elements, 8 * elements)
    lane = lax.broadcasted_iota(jnp.int32, shape, 1)
    return lane == lax.broadcasted_iota(jnp.int32, shape, 0) + q * elements


def coarse_part(field, vertices, inverse):
    elements = field.shape[0] // 4
    flat = jnp.zeros((elements, 8 * elements), F32)
    for q, corner in enumerate(own_corners()):
        inner = None
        for c in range(4):
            term = field[c * elements : (c + 1) * elements] * corner[:, c * LANES : (c + 1) * LANES]
            inner = term if inner is None else inner + term
        flat = jnp.where(own_place(elements, q), jnp.sum(inner, axis=1, keepdims=True), flat)
    flat = jnp.sum(flat, axis=0, keepdims=True)
    part = jnp.sum(vertices * flat, axis=1, keepdims=True)
    part = jnp.sum(inverse * part, axis=0, keepdims=True)
    return jnp.concatenate([part, jnp.zeros((1, LANES - NC), F32)], axis=1)


def column(row):
    shape = (NC, LANES)
    keep = lax.broadcasted_iota(jnp.int32, shape, 0) == lax.broadcasted_iota(jnp.int32, shape, 1)
    return jnp.sum(jnp.where(keep, row, 0.0), axis=1, keepdims=True)


def get_solved(received_ref, count, peers):
    rows = get(received_ref, count, TERMS)
    return [
        column(
            jnp.sum(
                jnp.where(own_group(rows.shape[0], peers, away), rows, 0.0), axis=0, keepdims=True
            )
        )
        for away in (0, -1, 1)
    ]


def prolonged(solved, vertices, elements):
    flat = jnp.sum(vertices * solved, axis=0, keepdims=True)
    out = [None] * 4
    for q, corner in enumerate(own_corners()):
        value = jnp.sum(jnp.where(own_place(elements, q), flat, 0.0), axis=1, keepdims=True)
        for c in range(4):
            term = value * corner[:, c * LANES : (c + 1) * LANES]
            out[c] = term if out[c] is None else out[c] + term
    return jnp.concatenate(out, axis=0)


def prolong_at(points, vertices, elements):
    mine = lax.broadcasted_iota(jnp.int32, (elements, points.shape[1]), 0) == points >> 9
    weights = jnp.concatenate([jnp.where(mine, corner, 0.0) for corner in corners(points)], axis=0)
    high, low = split(weights)
    both = jnp.dot(
        vertices.astype(BF16),
        jnp.concatenate([high, low], axis=1),
        preferred_element_type=F32,
    )
    return both[:, : points.shape[1]] + both[:, points.shape[1] :]


def total_of(array):
    return jnp.sum(jnp.sum(array, axis=0, keepdims=True), axis=1, keepdims=True)


def packed(values):
    lane = lax.broadcasted_iota(jnp.int32, (1, LANES), 1)
    out = jnp.zeros((1, LANES), F32)
    for k, value in enumerate(values):
        out = jnp.where(lane == k, value, out)
    return out


def unpacked(row, count):
    lane = lax.broadcasted_iota(jnp.int32, row.shape, 1)
    return [
        jnp.sum(jnp.where(lane == k, row, 0.0), axis=1, keepdims=True) for k in range(count)
    ]


def first_kernel(
    right_hbm, jacobi_hbm, inverse_hbm, map_hbm, slot_hbm, face_hbm,
    sent_ref, fields_ref, points_ref,
    right_ref, jacobi_ref, inverse_ref, map_ref, slot_ref, face_ref, sems,
):
    copies = []
    for k, (source, target) in enumerate(
        (
            (face_hbm, face_ref),
            (slot_hbm, slot_ref),
            (right_hbm, right_ref),
            (jacobi_hbm, jacobi_ref),
            (map_hbm, map_ref),
            (inverse_hbm, inverse_ref),
        )
    ):
        copy = pltpu.make_async_copy(source, target, sems.at[k])
        copy.start()
        copies.append(copy)
    for copy in copies:
        copy.wait()
    elements = right_ref.shape[0]
    peers = slot_ref.shape[1]
    faces = face_ref[...]
    faces = jnp.concatenate(halves(faces[0:1]) + halves(faces[1:2]), axis=0)
    points = jnp.concatenate([slot_ref[0], faces], axis=0)
    points_ref[...] = points
    resid = rows_of(right_ref[...])
    flat = flat_map(map_ref[...])
    smoothed = rows_of(jacobi_ref[...]) * resid
    fields_ref[0 : 4 * elements, :] = resid
    fields_ref[4 * elements : 8 * elements, :] = smoothed
    fields_ref[8 * elements :, :] = jnp.broadcast_to(flat, (8, LANES))
    part = coarse_part(resid, one_vertex(flat), inverse_ref[0])
    values = gather(smoothed, far_chunks(points, elements))
    send_values(sent_ref, FIRST_ROWS, values, peers)
    send_same(sent_ref, FIRST_ROWS, TERMS, part)
    send_same(sent_ref, FIRST_ROWS, TERMS + 1, flat)
    send_rows(sent_ref, FIRST_ROWS, TERMS + 2, points.astype(F32), peers)


def static_of(received_ref, peers, elements):
    maps = get(received_ref, FIRST_ROWS, TERMS + 1)
    own = get_shared(maps, peers)
    points = whole(get_rows(received_ref, FIRST_ROWS, TERMS + 2, peers))
    out = [
        prolong_at(points[b : b + 1], one_vertex(own[b : b + 1]), elements) for b in range(peers)
    ]
    for k, pair in enumerate(joined(points[peers:])):
        away = -1 if 2 * k < FACE_ROWS else 1
        out.append(prolong_at(pair, one_vertex(get_row(maps, peers, away)), elements))
    return jnp.concatenate(out, axis=1)


def apply(
    smoothed, count, received_ref, weights, solved, metric_ref, helmholtz_ref,
    first_ref, inner_ref, pair_ref, points_ref, dots, back_ref, local_ref, sent_ref,
):
    elements = smoothed.shape[0] // 4
    peers = points_ref.shape[0] - 2 * FACE_ROWS
    pairs = pair_chunks(pair_ref, elements)
    far = far_chunks(points_ref[...], elements)
    ends = [LANES * k for k in (0, peers, peers + FACE_ROWS, peers + 2 * FACE_ROWS)]
    coarse = []
    for k in range(3):
        coarse += halves(
            jnp.sum(weights[:, ends[k] : ends[k + 1]] * solved[k], axis=0, keepdims=True)
        )
    incoming = get_rows(received_ref, count, 0, peers) + jnp.concatenate(coarse, axis=0)
    values = swapped(gather(smoothed, pairs)) + joined(incoming)
    summed = smoothed + scatter(smoothed.shape[0], pairs + far, values)
    back, energy = stiffness(summed, metric_ref, first_ref, inner_ref)
    energy = energy + rows_of(helmholtz_ref[...]) * smoothed * smoothed
    back_ref[...] = back
    values = gather(back, pairs + far)
    near = swapped(values[: len(pairs)])
    for k, value in enumerate(near):
        local_ref[0:1, k * STEP : (k + 1) * STEP] = value
    send_values(sent_ref, ROWS, values[len(pairs) :], peers)
    send_same(sent_ref, ROWS, TERMS, packed(dots + [total_of(energy)]))


def image_of(
    field_ref, back_ref, local_ref, received_ref, helmholtz_ref, pair_ref, points_ref
):
    elements = field_ref.shape[0] // 4
    peers = points_ref.shape[0] - 2 * FACE_ROWS
    chunks = pair_chunks(pair_ref, elements) + far_chunks(points_ref[...], elements)
    values = cut(local_ref[...]) + joined(get_rows(received_ref, ROWS, 0, peers))
    summed = back_ref[...] + scatter(field_ref.shape[0], chunks, values)
    return summed + rows_of(helmholtz_ref[...]) * field_ref[...]


def start_kernel(
    received_ref, fields_ref, points_ref, pair_ref, metric_ref, helmholtz_ref,
    first_ref, inner_ref,
    smoothed_ref, weights_ref, back_ref, local_ref, sent_ref,
):
    elements = helmholtz_ref.shape[0]
    peers = points_ref.shape[0] - 2 * FACE_ROWS
    solved = get_solved(received_ref, FIRST_ROWS, peers)
    resid = fields_ref[0 : 4 * elements, :]
    vertices = one_vertex(fields_ref[8 * elements : 8 * elements + 1, :])
    smoothed = fields_ref[4 * elements : 8 * elements, :]
    smoothed = smoothed + prolonged(solved[0], vertices, elements)
    smoothed_ref[...] = smoothed
    weights = static_of(received_ref, peers, elements)
    weights_ref[...] = weights
    apply(
        smoothed, FIRST_ROWS, received_ref, weights, solved, metric_ref,
        helmholtz_ref, first_ref, inner_ref, pair_ref, points_ref,
        [total_of(resid * smoothed)], back_ref, local_ref, sent_ref,
    )


def middle_kernel(
    received_ref, fields_ref, points_ref, pair_ref, jacobi_ref, helmholtz_ref,
    inverse_ref, smoothed_ref, back_ref, local_ref,
    image_ref, resid_ref, scalars_ref, sent_ref,
):
    elements = helmholtz_ref.shape[0]
    peers = points_ref.shape[0] - 2 * FACE_ROWS
    dots = jnp.sum(get(received_ref, ROWS, TERMS), axis=0, keepdims=True)
    scalars_ref[...] = dots
    values = unpacked(dots, 2)
    alpha = values[0] / values[1]
    image = image_of(
        smoothed_ref, back_ref, local_ref, received_ref, helmholtz_ref, pair_ref,
        points_ref,
    )
    image_ref[...] = image
    resid = fields_ref[0 : 4 * elements, :] - alpha * image
    resid_ref[...] = resid
    vertices = one_vertex(fields_ref[8 * elements : 8 * elements + 1, :])
    part = coarse_part(resid, vertices, inverse_ref[0])
    values = gather(rows_of(jacobi_ref[...]) * resid, far_chunks(points_ref[...], elements))
    send_values(sent_ref, ROWS, values, peers)
    send_same(sent_ref, ROWS, TERMS, part)


def second_kernel(
    received_ref, fields_ref, points_ref, pair_ref, resid_ref, image_ref,
    weights_ref, jacobi_ref, metric_ref, helmholtz_ref, first_ref, inner_ref,
    smoothed_ref, back_ref, local_ref, sent_ref,
):
    elements = helmholtz_ref.shape[0]
    peers = points_ref.shape[0] - 2 * FACE_ROWS
    solved = get_solved(received_ref, ROWS, peers)
    resid = resid_ref[...]
    vertices = one_vertex(fields_ref[8 * elements : 8 * elements + 1, :])
    smoothed = rows_of(jacobi_ref[...]) * resid + prolonged(solved[0], vertices, elements)
    smoothed_ref[...] = smoothed
    apply(
        smoothed, ROWS, received_ref, weights_ref[...], solved, metric_ref,
        helmholtz_ref, first_ref, inner_ref, pair_ref, points_ref,
        [total_of(resid * smoothed), total_of(image_ref[...] * smoothed)],
        back_ref, local_ref, sent_ref,
    )


def final_kernel(
    received_ref, points_ref, pair_ref, old_ref, field_ref, resid_ref, old_image_ref,
    scalars_ref, back_ref, local_ref, helmholtz_ref,
    solution_ref, residual_ref,
):
    before = unpacked(scalars_ref[...], 2)
    now = unpacked(jnp.sum(get(received_ref, ROWS, TERMS), axis=0, keepdims=True), 3)
    alpha = before[0] / before[1]
    beta = now[0] / before[0]
    curved = now[2] + beta * (2.0 * now[1] + beta * before[1])
    step = now[0] / curved
    old = old_ref[...]
    direction = field_ref[...] + beta * old
    solution_ref[...] = wide_of(alpha * old + step * direction)
    image = image_of(
        field_ref, back_ref, local_ref, received_ref, helmholtz_ref, pair_ref,
        points_ref,
    )
    image = image + beta * old_image_ref[...]
    residual_ref[...] = wide_of(resid_ref[...] - step * image)


def call(kernel, outs, *args, copied=False):
    space = pl.ANY if copied else pltpu.VMEM
    scratch = [pltpu.VMEM(arg.shape, arg.dtype) for arg in args] if copied else []
    if copied:
        args = [pltpu.with_memory_space_constraint(arg, pltpu.HBM) for arg in args]
    return pl.pallas_call(
        kernel,
        out_shape=[
            jax.ShapeDtypeStruct(*(out if isinstance(out[0], tuple) else (out, F32))) for out in outs
        ],
        in_specs=[pl.BlockSpec(memory_space=space)] * len(args),
        out_specs=[pl.BlockSpec(memory_space=pltpu.VMEM)] * len(outs),
        scratch_shapes=scratch + ([pltpu.SemaphoreType.DMA((len(args),))] if copied else []),
        compiler_params=pltpu.CompilerParams(vmem_limit_bytes=24 * 1024 * 1024),
    )(*args)


def body(
    right_side,
    metric,
    helmholtz,
    jacobi,
    pair_list,
    shared_slots,
    face_points,
    coarse_map,
    coarse_inverse,
):
    peers = lax.axis_size("sub")
    groups = lax.axis_size("grp")
    t = {name: jnp.asarray(value) for name, value in tables().items()}
    elements = right_side.shape[0]
    field = (4 * elements, LANES)
    local = (1, pair_list.shape[0] * pair_list.shape[1])
    points_shape = (peers + 2 * FACE_ROWS, LANES)
    sent_shape = (groups * peers * ROWS, LANES)

    def exchange(sent):
        rows = sent.reshape(groups * peers, 1, -1)
        return lax.all_to_all(rows, ("grp", "sub"), 0, 0, tiled=True).reshape(sent.shape)

    sent, fields, points = call(
        first_kernel,
        [
            (groups * peers * FIRST_ROWS, LANES),
            (8 * elements + 8, LANES),
            (points_shape, jnp.int32),
        ],
        right_side, jacobi, coarse_inverse, coarse_map, shared_slots, face_points, copied=True,
    )
    smoothed, weights, back, near, sent = call(
        start_kernel,
        [field, (NC, points_shape[0] * LANES), field, local, sent_shape],
        exchange(sent), fields, points, pair_list, metric, helmholtz,
        t["first"], t["inner"],
    )
    image, resid, scalars, sent = call(
        middle_kernel, [field, field, (1, LANES), sent_shape],
        exchange(sent), fields, points, pair_list, jacobi, helmholtz, coarse_inverse,
        smoothed, back, near,
    )
    second, back, near, sent = call(
        second_kernel, [field, field, local, sent_shape],
        exchange(sent), fields, points, pair_list, resid, image, weights, jacobi,
        metric, helmholtz, t["first"], t["inner"],
    )
    return tuple(
        call(
            final_kernel, [right_side.shape, right_side.shape],
            exchange(sent), points, pair_list, smoothed, second, resid, image, scalars,
            back, near, helmholtz,
        )
    )


def solution(mesh):
    in_specs = (
        P(("grp", "sub"), None),
        P(("grp", "sub"), None),
        P(("grp", "sub"), None),
        P(("grp", "sub"), None),
        P(None, ("grp", "sub")),
        P(("grp", "sub"), None, None),
        P(None, ("grp", "sub")),
        P(None, ("grp", "sub")),
        P("grp", None, None),
    )
    out_specs = (P(("grp", "sub"), None), P(("grp", "sub"), None))
    return jax.shard_map(body, mesh=mesh, in_specs=in_specs, out_specs=out_specs, check_vma=False)
```

```python
import jax
import jax.numpy as jnp
import ml_dtypes
import numpy as np
from jax import lax
from jax.experimental import pallas as pl
from jax.experimental.pallas import tpu as pltpu
from jax.sharding import PartitionSpec as P

NC = 64
POINTS = 512
LANES = 128
FACE_ROWS = 4
ROWS = 5
FIRST_ROWS = 10
TERMS = FACE_ROWS
F32 = jnp.float32
BF16 = jnp.bfloat16
NT = (((1,), (1,)), ((), ()))


def split_constant(array):
    high = array.astype(ml_dtypes.bfloat16)
    low = (array - high.astype(np.float64)).astype(ml_dtypes.bfloat16)
    return high, low


def tables():
    order_index = np.arange(8)
    colloc = np.cos(np.pi * order_index / 7.0)
    end_weights = (
        np.where((order_index == 0) | (order_index == 7), 2.0, 1.0) * (-1.0) ** order_index
    )
    spacing = colloc[:, None] - colloc[None, :] + np.eye(8)
    raw_matrix = np.outer(end_weights, 1.0 / end_weights) / spacing
    off_part = raw_matrix * (1.0 - np.eye(8))
    derivative = 0.25 * (off_part - np.eye(8) * off_part.sum(axis=1)[:, None])
    along_inner = np.concatenate(
        [np.kron(np.eye(2), np.kron(derivative, np.eye(8))).T, np.kron(np.eye(16), derivative).T],
        axis=1,
    )
    high, low = split_constant(along_inner)
    inner = np.concatenate([high, low], axis=0)

    half = np.arange(LANES) // 64

    def first_rows(matrix):
        rows = []
        for to in range(4):
            for at in range(4):
                rows.append(matrix[2 * to + half, 2 * at + half])
                rows.append(matrix[2 * to + half, 2 * at + 1 - half])
        return np.stack(rows).astype(np.float32)

    return {
        "inner": inner,
        "first": np.concatenate([first_rows(derivative), first_rows(derivative.T)], axis=0),
    }


def split(value):
    high = value.astype(BF16)
    return high, (value - high.astype(F32)).astype(BF16)


def rows_of(wide):
    return jnp.concatenate([wide[:, LANES * c : LANES * (c + 1)] for c in range(4)], axis=0)


def wide_of(rows):
    elements = rows.shape[0] // 4
    return jnp.concatenate([rows[c * elements : (c + 1) * elements] for c in range(4)], axis=1)


def locate(points, elements):
    element = points >> 9
    chunk = (points >> 7) & 3
    row = jnp.where(points < elements * POINTS, chunk * elements + element, 4 * elements)
    return row, points & (LANES - 1)


def one_hot(index, count):
    steps = lax.broadcasted_iota(jnp.int32, (count, index.shape[1]), 0)
    return steps == index


def lane_hot(lane):
    steps = lax.broadcasted_iota(jnp.int32, (LANES, lane.shape[1]), 0).astype(F32).astype(BF16)
    one = jnp.ones(steps.shape, BF16)
    return jnp.where(steps == lane.astype(F32).astype(BF16), one, jnp.zeros_like(one))


def take(values, lanes):
    return jnp.take_along_axis(values, lanes, axis=1, mode="promise_in_bounds")


def gather(field_ref, points):
    row, lane = locate(points, field_ref.shape[0] // 4)
    out = jnp.zeros(points.shape, F32)
    for h in range(field_ref.shape[0]):
        spread = jnp.broadcast_to(field_ref[h : h + 1, :], points.shape)
        out = jnp.where(row == h, take(spread, lane), out)
    return out


def joined(rows):
    return [
        jnp.concatenate([rows[at : at + 1], rows[at + 1 : at + 2]], axis=1)
        for at in range(0, rows.shape[0], 2)
    ]


def scatter(count, points, values):
    total = jnp.zeros((2 * count, LANES), F32)
    rows, lanes = locate(points, count // 4)
    for row, lane, value in zip(joined(rows), joined(lanes), joined(values)):
        steps = lax.broadcasted_iota(jnp.int32, (count, row.shape[1]), 0).astype(F32).astype(BF16)
        mine = steps == row.astype(F32).astype(BF16)
        parts = [jnp.where(mine, part, jnp.zeros_like(steps)) for part in split(value)]
        total = total + lax.dot_general(
            jnp.concatenate(parts, axis=0), lane_hot(lane), NT, preferred_element_type=F32
        )
    return total[:count] + total[count:]


def halves(wide):
    return [wide[:, at : at + LANES] for at in range(0, wide.shape[1], LANES)]


def own_group(devices, peers, away=0):
    shape = (devices, LANES)
    return lax.broadcasted_iota(jnp.int32, shape, 0) // peers - lax.axis_index("grp") == away


def send_rows(sent_ref, count, at, rows, peers):
    devices = sent_ref.shape[0] // count
    above = own_group(devices, peers, 1)
    shared = jnp.concatenate([rows[:peers]] * (devices // peers), axis=0)
    for r in range(FACE_ROWS):
        down = rows[peers + r : peers + r + 1]
        up = rows[peers + FACE_ROWS + r : peers + FACE_ROWS + r + 1]
        out = jnp.where(above, up, down)
        if r == 0:
            out = jnp.where(own_group(devices, peers), shared, out)
        sent_ref[pl.ds(at + r, devices, count), :] = out


def send_same(sent_ref, count, at, row):
    devices = sent_ref.shape[0] // count
    sent_ref[pl.ds(at, devices, count), :] = jnp.broadcast_to(row, (devices, LANES))


def get(received_ref, count, at):
    return received_ref[pl.ds(at, received_ref.shape[0] // count, count), :]


def get_shared(rows, peers):
    mine = jnp.where(own_group(rows.shape[0], peers), rows, 0.0)
    shared = mine[:peers]
    for g in range(1, rows.shape[0] // peers):
        shared = shared + mine[g * peers : (g + 1) * peers]
    return shared


def get_row(rows, peers, away):
    here = lax.axis_index("grp") * peers + lax.axis_index("sub")
    source = lax.broadcasted_iota(jnp.int32, rows.shape, 0) - here == away * peers
    return jnp.sum(jnp.where(source, rows, 0.0), axis=0, keepdims=True)


def get_rows(received_ref, count, at, peers):
    rows = [get(received_ref, count, at + r) for r in range(FACE_ROWS)]
    faces = [get_row(part, peers, away) for away in (-1, 1) for part in rows]
    return jnp.concatenate([get_shared(rows[0], peers)] + faces, axis=0)


def swapped(values):
    count = values.shape[0] // 2
    return jnp.concatenate([values[count:], values[:count]], axis=0)


def along_first(field, table_ref, base):
    elements = field.shape[0] // 4
    turned = pltpu.roll(field, 64, axis=1)
    out = []
    for to in range(4):
        total = None
        for at in range(4):
            place = base + 2 * (4 * to + at)
            rows = slice(at * elements, (at + 1) * elements)
            term = (
                table_ref[place : place + 1, :] * field[rows]
                + table_ref[place + 1 : place + 2, :] * turned[rows]
            )
            total = term if total is None else total + term
        out.append(total)
    return jnp.concatenate(out, axis=0)


def stiffness(field, metric_ref, first_ref, inner_ref):
    metric = [rows_of(metric_ref[:, POINTS * d : POINTS * (d + 1)]) for d in range(3)]
    count = field.shape[0]
    grad_first = along_first(field, first_ref, 0)
    high, low = split(field)
    both = jnp.dot(
        jnp.concatenate([high, low], axis=0), inner_ref[:LANES], preferred_element_type=F32
    )
    inner = both[:count] + both[count:]
    inner = inner + jnp.dot(high, inner_ref[LANES:], preferred_element_type=F32)
    flux_first = metric[0] * grad_first
    flux = jnp.concatenate([metric[1], metric[2]], axis=1) * inner
    high, low = split(flux)
    both = lax.dot_general(
        jnp.concatenate([high, low], axis=0), inner_ref[:LANES], NT, preferred_element_type=F32
    )
    back = both[:count] + both[count:]
    back = back + lax.dot_general(high, inner_ref[LANES:], NT, preferred_element_type=F32)
    back = back + along_first(flux_first, first_ref, 32)
    energy = flux * inner
    return back, flux_first * grad_first + energy[:, :LANES] + energy[:, LANES:]


def factors(points):
    nodes = 0.5 * (1.0 + np.cos(np.pi * np.arange(8) / 7.0))
    out = []
    for shift in (6, 3, 0):
        index = (points >> shift) & 7
        near = jnp.full(points.shape, nodes[7], F32)
        far = jnp.full(points.shape, nodes[0], F32)
        for m in range(7):
            near = jnp.where(index == m, float(nodes[m]), near)
            far = jnp.where(index == m, float(nodes[7 - m]), far)
        out.append((near, far))
    return out


def corners(points):
    first, second, third = factors(points)
    return [first[q >> 2 & 1] * (second[q >> 1 & 1] * third[q & 1]) for q in range(8)]


def own_corners():
    return corners(lax.broadcasted_iota(jnp.int32, (1, POINTS), 1))


def flat_map(mapped):
    elements = mapped.shape[1]
    width = 8 * elements
    own = own_element(elements, width)
    place = lax.broadcasted_iota(jnp.int32, (8, width), 1) // elements
    spread = jnp.where(own, 1.0, 0.0).astype(BF16)
    wide = jnp.dot(mapped.astype(F32).astype(BF16), spread, preferred_element_type=F32)
    keep = lax.broadcasted_iota(jnp.int32, (8, width), 0) == place
    return jnp.sum(jnp.where(keep, wide, 0.0), axis=0, keepdims=True)


def one_vertex(flat):
    return jnp.where(one_hot(flat, NC), 1.0, 0.0)


def whole(values):
    return (values + 0.5).astype(jnp.int32)


def own_element(elements, width):
    shape = (elements, width)
    return lax.broadcasted_iota(jnp.int32, shape, 0) == (
        lax.broadcasted_iota(jnp.int32, shape, 1) % elements
    )


def own_place(elements, q):
    shape = (elements, 8 * elements)
    lane = lax.broadcasted_iota(jnp.int32, shape, 1)
    return lane == lax.broadcasted_iota(jnp.int32, shape, 0) + q * elements


def coarse_part(field, vertices, inverse):
    elements = field.shape[0] // 4
    flat = jnp.zeros((elements, 8 * elements), F32)
    for q, corner in enumerate(own_corners()):
        inner = None
        for c in range(4):
            term = field[c * elements : (c + 1) * elements] * corner[:, c * LANES : (c + 1) * LANES]
            inner = term if inner is None else inner + term
        flat = jnp.where(own_place(elements, q), jnp.sum(inner, axis=1, keepdims=True), flat)
    flat = jnp.sum(flat, axis=0, keepdims=True)
    part = jnp.sum(vertices * flat, axis=1, keepdims=True)
    part = jnp.sum(inverse * part, axis=0, keepdims=True)
    return jnp.concatenate([part, jnp.zeros((1, LANES - NC), F32)], axis=1)


def get_solved(received_ref, count, peers):
    rows = get(received_ref, count, TERMS)
    return [
        jnp.sum(jnp.where(own_group(rows.shape[0], peers, away), rows, 0.0), axis=0, keepdims=True)
        for away in (0, -1, 1)
    ]


def prolonged(solved, flat, elements):
    shape = (elements, LANES)
    element = lax.broadcasted_iota(jnp.int32, shape, 0)
    at_corner = take(jnp.broadcast_to(solved, shape), jnp.broadcast_to(flat, shape))
    out = [None] * 4
    for q, corner in enumerate(own_corners()):
        value = take(at_corner, element + q * elements)
        for c in range(4):
            term = value * corner[:, c * LANES : (c + 1) * LANES]
            out[c] = term if out[c] is None else out[c] + term
    return jnp.concatenate(out, axis=0)


def prolonged_far(solved, maps, points, elements):
    peers = points.shape[0] - 2 * FACE_ROWS
    counts = (peers, FACE_ROWS, FACE_ROWS)
    spread = [jnp.broadcast_to(part, (n, LANES)) for part, n in zip(solved, counts)]
    at_corner = take(jnp.concatenate(spread, axis=0), maps)
    element = (points >> 9) & (elements - 1)
    total = jnp.zeros(points.shape, F32)
    for q, corner in enumerate(corners(points)):
        total = total + corner * take(at_corner, element + q * elements)
    return total


def total_of(array):
    return jnp.sum(jnp.sum(array, axis=0, keepdims=True), axis=1, keepdims=True)


def packed(values):
    lane = lax.broadcasted_iota(jnp.int32, (1, LANES), 1)
    out = jnp.zeros((1, LANES), F32)
    for k, value in enumerate(values):
        out = jnp.where(lane == k, value, out)
    return out


def unpacked(row, count):
    lane = lax.broadcasted_iota(jnp.int32, row.shape, 1)
    return [
        jnp.sum(jnp.where(lane == k, row, 0.0), axis=1, keepdims=True) for k in range(count)
    ]


def first_kernel(
    right_hbm, jacobi_hbm, inverse_hbm, map_hbm, slot_hbm, face_hbm, pair_hbm,
    sent_ref, fields_ref, points_ref, flat_ref,
    right_ref, jacobi_ref, inverse_ref, map_ref, slot_ref, face_ref, pair_ref, sems,
):
    copies = []
    for k, (source, target) in enumerate(
        (
            (face_hbm, face_ref),
            (slot_hbm, slot_ref),
            (right_hbm, right_ref),
            (jacobi_hbm, jacobi_ref),
            (map_hbm, map_ref),
            (inverse_hbm, inverse_ref),
            (pair_hbm, pair_ref),
        )
    ):
        copy = pltpu.make_async_copy(source, target, sems.at[k])
        copy.start()
        copies.append(copy)
    for copy in copies:
        copy.wait()
    elements = right_ref.shape[0]
    peers = slot_ref.shape[1]
    far = peers + 2 * FACE_ROWS
    faces = face_ref[...]
    pairs = pair_ref[...]
    points_ref[0:peers, :] = slot_ref[0]
    points_ref[peers:far, :] = jnp.concatenate(halves(faces[0:1]) + halves(faces[1:2]), axis=0)
    points_ref[far:, :] = jnp.concatenate(halves(pairs[0:1]) + halves(pairs[1:2]), axis=0)
    points = points_ref[0:far, :]
    resid = rows_of(right_ref[...])
    flat = flat_map(map_ref[...])
    flat_ref[...] = whole(flat)
    fields_ref[0 : 4 * elements, :] = resid
    fields_ref[4 * elements :, :] = rows_of(jacobi_ref[...]) * resid
    part = coarse_part(resid, one_vertex(whole(flat)), inverse_ref[0])
    values = gather(fields_ref.at[4 * elements : 8 * elements], points)
    send_rows(sent_ref, FIRST_ROWS, 0, values, peers)
    send_same(sent_ref, FIRST_ROWS, TERMS, part)
    send_same(sent_ref, FIRST_ROWS, TERMS + 1, flat)
    send_rows(sent_ref, FIRST_ROWS, TERMS + 2, points.astype(F32), peers)


def far_maps(received_ref, peers):
    maps = get(received_ref, FIRST_ROWS, TERMS + 1)
    sides = [
        jnp.broadcast_to(get_row(maps, peers, away), (FACE_ROWS, LANES)) for away in (-1, 1)
    ]
    return whole(jnp.concatenate([get_shared(maps, peers)] + sides, axis=0))


def apply(
    smoothed_ref, count, received_ref, maps, far_points, solved, metric_ref, helmholtz_ref,
    first_ref, inner_ref, points_ref, dots, back_ref, local_ref, sent_ref,
):
    elements = smoothed_ref.shape[0] // 4
    far = far_points.shape[0]
    peers = far - 2 * FACE_ROWS
    points = points_ref[...]
    incoming = get_rows(received_ref, count, 0, peers)
    incoming = incoming + prolonged_far(solved, maps, far_points, elements)
    near = swapped(gather(smoothed_ref, points[far:]))
    smoothed = smoothed_ref[...]
    summed = smoothed + scatter(
        4 * elements, points, jnp.concatenate([incoming, near], axis=0)
    )
    back, energy = stiffness(summed, metric_ref, first_ref, inner_ref)
    energy = energy + rows_of(helmholtz_ref[...]) * smoothed * smoothed
    back_ref[...] = back
    values = gather(back_ref, points)
    local_ref[...] = swapped(values[far:])
    send_rows(sent_ref, ROWS, 0, values[:far], peers)
    send_same(sent_ref, ROWS, TERMS, packed(dots + [total_of(energy)]))


def image_of(field_ref, back_ref, local_ref, received_ref, helmholtz_ref, points_ref):
    peers = points_ref.shape[0] - local_ref.shape[0] - 2 * FACE_ROWS
    incoming = get_rows(received_ref, ROWS, 0, peers)
    values = jnp.concatenate([incoming, local_ref[...]], axis=0)
    summed = back_ref[...] + scatter(field_ref.shape[0], points_ref[...], values)
    return summed + rows_of(helmholtz_ref[...]) * field_ref[...]


def start_kernel(
    received_ref, fields_ref, points_ref, flat_ref, metric_ref, helmholtz_ref, first_ref, inner_ref,
    smoothed_ref, maps_ref, far_points_ref, back_ref, local_ref, sent_ref,
):
    elements = helmholtz_ref.shape[0]
    peers = maps_ref.shape[0] - 2 * FACE_ROWS
    solved = get_solved(received_ref, FIRST_ROWS, peers)
    resid = fields_ref[0 : 4 * elements, :]
    smoothed = fields_ref[4 * elements :, :] + prolonged(solved[0], flat_ref[...], elements)
    smoothed_ref[...] = smoothed
    maps = far_maps(received_ref, peers)
    maps_ref[...] = maps
    far_points = whole(get_rows(received_ref, FIRST_ROWS, TERMS + 2, peers))
    far_points_ref[...] = far_points
    apply(
        smoothed_ref, FIRST_ROWS, received_ref, maps, far_points, solved, metric_ref,
        helmholtz_ref, first_ref, inner_ref, points_ref,
        [total_of(resid * smoothed)], back_ref, local_ref, sent_ref,
    )


def middle_kernel(
    received_ref, fields_ref, points_ref, flat_ref, jacobi_ref, helmholtz_ref, inverse_ref,
    smoothed_ref, back_ref, local_ref,
    image_ref, resid_ref, rough_ref, scalars_ref, sent_ref,
):
    elements = helmholtz_ref.shape[0]
    far = points_ref.shape[0] - local_ref.shape[0]
    dots = jnp.sum(get(received_ref, ROWS, TERMS), axis=0, keepdims=True)
    scalars_ref[...] = dots
    values = unpacked(dots, 2)
    alpha = values[0] / values[1]
    image = image_of(smoothed_ref, back_ref, local_ref, received_ref, helmholtz_ref, points_ref)
    image_ref[...] = image
    resid = fields_ref[0 : 4 * elements, :] - alpha * image
    resid_ref[...] = resid
    rough_ref[...] = rows_of(jacobi_ref[...]) * resid
    part = coarse_part(resid, one_vertex(flat_ref[...]), inverse_ref[0])
    values = gather(rough_ref, points_ref[0:far, :])
    send_rows(sent_ref, ROWS, 0, values, far - 2 * FACE_ROWS)
    send_same(sent_ref, ROWS, TERMS, part)


def second_kernel(
    received_ref, points_ref, flat_ref, maps_ref, far_points_ref, resid_ref, rough_ref, image_ref,
    metric_ref, helmholtz_ref, first_ref, inner_ref,
    smoothed_ref, back_ref, local_ref, sent_ref,
):
    elements = helmholtz_ref.shape[0]
    solved = get_solved(received_ref, ROWS, maps_ref.shape[0] - 2 * FACE_ROWS)
    resid = resid_ref[...]
    smoothed = rough_ref[...] + prolonged(solved[0], flat_ref[...], elements)
    smoothed_ref[...] = smoothed
    apply(
        smoothed_ref, ROWS, received_ref, maps_ref[...], far_points_ref[...], solved, metric_ref,
        helmholtz_ref, first_ref, inner_ref, points_ref,
        [total_of(resid * smoothed), total_of(image_ref[...] * smoothed)],
        back_ref, local_ref, sent_ref,
    )


def final_kernel(
    received_ref, points_ref, old_ref, field_ref, resid_ref, old_image_ref,
    scalars_ref, back_ref, local_ref, helmholtz_ref,
    solution_ref, residual_ref,
):
    before = unpacked(scalars_ref[...], 2)
    now = unpacked(jnp.sum(get(received_ref, ROWS, TERMS), axis=0, keepdims=True), 3)
    alpha = before[0] / before[1]
    beta = now[0] / before[0]
    curved = now[2] + beta * (2.0 * now[1] + beta * before[1])
    step = now[0] / curved
    old = old_ref[...]
    direction = field_ref[...] + beta * old
    solution_ref[...] = wide_of(alpha * old + step * direction)
    image = image_of(field_ref, back_ref, local_ref, received_ref, helmholtz_ref, points_ref)
    image = image + beta * old_image_ref[...]
    residual_ref[...] = wide_of(resid_ref[...] - step * image)


def call(kernel, outs, *args, copied=False):
    space = pl.ANY if copied else pltpu.VMEM
    scratch = [pltpu.VMEM(arg.shape, arg.dtype) for arg in args] if copied else []
    if copied:
        args = [pltpu.with_memory_space_constraint(arg, pltpu.HBM) for arg in args]
    return pl.pallas_call(
        kernel,
        out_shape=[
            jax.ShapeDtypeStruct(*(out if isinstance(out[0], tuple) else (out, F32))) for out in outs
        ],
        in_specs=[pl.BlockSpec(memory_space=space)] * len(args),
        out_specs=[pl.BlockSpec(memory_space=pltpu.VMEM)] * len(outs),
        scratch_shapes=scratch + ([pltpu.SemaphoreType.DMA((len(args),))] if copied else []),
        compiler_params=pltpu.CompilerParams(vmem_limit_bytes=24 * 1024 * 1024),
    )(*args)


def body(
    right_side,
    metric,
    helmholtz,
    jacobi,
    pair_list,
    shared_slots,
    face_points,
    coarse_map,
    coarse_inverse,
):
    peers = lax.axis_size("sub")
    groups = lax.axis_size("grp")
    t = {name: jnp.asarray(value) for name, value in tables().items()}
    elements = right_side.shape[0]
    field = (4 * elements, LANES)
    far = (peers + face_points.size // LANES, LANES)
    local = (pair_list.size // LANES, LANES)
    sent_shape = (groups * peers * ROWS, LANES)

    def exchange(sent):
        rows = sent.reshape(groups * peers, 1, -1)
        return lax.all_to_all(rows, ("grp", "sub"), 0, 0, tiled=True).reshape(sent.shape)

    sent, fields, points, flat = call(
        first_kernel,
        [
            (groups * peers * FIRST_ROWS, LANES),
            (8 * elements, LANES),
            ((far[0] + local[0], LANES), jnp.int32),
            ((1, LANES), jnp.int32),
        ],
        right_side, jacobi, coarse_inverse, coarse_map, shared_slots, face_points, pair_list,
        copied=True,
    )
    smoothed, maps, far_points, back, near, sent = call(
        start_kernel,
        [field, (far, jnp.int32), (far, jnp.int32), field, local, sent_shape],
        exchange(sent), fields, points, flat, metric, helmholtz, t["first"], t["inner"],
    )
    image, resid, rough, scalars, sent = call(
        middle_kernel, [field, field, field, (1, LANES), sent_shape],
        exchange(sent), fields, points, flat, jacobi, helmholtz, coarse_inverse,
        smoothed, back, near,
    )
    second, back, near, sent = call(
        second_kernel, [field, field, local, sent_shape],
        exchange(sent), points, flat, maps, far_points, resid, rough, image,
        metric, helmholtz, t["first"], t["inner"],
    )
    return tuple(
        call(
            final_kernel, [right_side.shape, right_side.shape],
            exchange(sent), points, smoothed, second, resid, image, scalars, back, near, helmholtz,
        )
    )


def solution(mesh):
    in_specs = (
        P(("grp", "sub"), None),
        P(("grp", "sub"), None),
        P(("grp", "sub"), None),
        P(("grp", "sub"), None),
        P(None, ("grp", "sub")),
        P(("grp", "sub"), None, None),
        P(None, ("grp", "sub")),
        P(None, ("grp", "sub")),
        P("grp", None, None),
    )
    out_specs = (P(("grp", "sub"), None), P(("grp", "sub"), None))
    return jax.shard_map(body, mesh=mesh, in_specs=in_specs, out_specs=out_specs, check_vma=False)
```

```python
import functools

import jax
import jax.numpy as jnp
import ml_dtypes
import numpy as np
from jax import lax
from jax.experimental import pallas as pl
from jax.experimental.pallas import tpu as pltpu
from jax.sharding import PartitionSpec as P

NC = 64
POINTS = 512
LANES = 128
FACE_ROWS = 4
ROWS = 5
FIRST_ROWS = 10
TERMS = FACE_ROWS
F32 = jnp.float32
BF16 = jnp.bfloat16
NT = (((1,), (1,)), ((), ()))


def split_constant(array):
    high = array.astype(ml_dtypes.bfloat16)
    low = (array - high.astype(np.float64)).astype(ml_dtypes.bfloat16)
    return high, low


def tables():
    order_index = np.arange(8)
    colloc = np.cos(np.pi * order_index / 7.0)
    end_weights = (
        np.where((order_index == 0) | (order_index == 7), 2.0, 1.0) * (-1.0) ** order_index
    )
    spacing = colloc[:, None] - colloc[None, :] + np.eye(8)
    raw_matrix = np.outer(end_weights, 1.0 / end_weights) / spacing
    off_part = raw_matrix * (1.0 - np.eye(8))
    derivative = 0.25 * (off_part - np.eye(8) * off_part.sum(axis=1)[:, None])
    along_inner = np.concatenate(
        [np.kron(np.eye(2), np.kron(derivative, np.eye(8))).T, np.kron(np.eye(16), derivative).T],
        axis=1,
    )
    high, low = split_constant(along_inner)
    inner = np.concatenate([high, low], axis=0)

    half = np.arange(LANES) // 64

    def first_rows(matrix):
        rows = []
        for to in range(4):
            for at in range(4):
                rows.append(matrix[2 * to + half, 2 * at + half])
                rows.append(matrix[2 * to + half, 2 * at + 1 - half])
        return np.stack(rows).astype(np.float32)

    return {
        "inner": inner,
        "first": np.concatenate([first_rows(derivative), first_rows(derivative.T)], axis=0),
    }


def split(value):
    high = value.astype(BF16)
    return high, (value - high.astype(F32)).astype(BF16)


def rows_of(wide):
    return jnp.concatenate([wide[:, LANES * c : LANES * (c + 1)] for c in range(4)], axis=0)


def wide_of(rows):
    elements = rows.shape[0] // 4
    return jnp.concatenate([rows[c * elements : (c + 1) * elements] for c in range(4)], axis=1)


def locate(points, elements):
    element = points >> 9
    chunk = (points >> 7) & 3
    row = jnp.where(points < elements * POINTS, chunk * elements + element, 4 * elements)
    return row, points & (LANES - 1)


def one_hot(index, count):
    steps = lax.broadcasted_iota(jnp.int32, (count, index.shape[1]), 0)
    return steps == index


def lane_hot(lane):
    steps = lax.broadcasted_iota(jnp.int32, (LANES, lane.shape[1]), 0).astype(F32).astype(BF16)
    one = jnp.ones(steps.shape, BF16)
    return jnp.where(steps == lane.astype(F32).astype(BF16), one, jnp.zeros_like(one))


def take(values, lanes):
    return jnp.take_along_axis(values, lanes, axis=1, mode="promise_in_bounds")


def joined(rows, count):
    return [
        jnp.concatenate([rows[at + k : at + k + 1] for k in range(count)], axis=1)
        for at in range(0, rows.shape[0], count)
    ]


def gather(field, points):
    rows, lanes = locate(points, field.shape[0] // 4)
    both = jnp.concatenate(split(field), axis=1)
    out = []
    for row, lane in zip(joined(rows, 2), joined(lanes, 2)):
        hot = lane_hot(lane)
        picked = jnp.dot(both, jnp.concatenate([hot, hot], axis=0), preferred_element_type=F32)
        mine = jnp.where(one_hot(row, field.shape[0]), picked, 0.0)
        out += halves(jnp.sum(mine, axis=0, keepdims=True))
    return jnp.concatenate(out, axis=0)


def scatter(count, points, values):
    total = jnp.zeros((2 * count, LANES), F32)
    rows, lanes = locate(points, count // 4)
    for row, lane, value in zip(joined(rows, 4), joined(lanes, 4), joined(values, 4)):
        steps = lax.broadcasted_iota(jnp.int32, (count, row.shape[1]), 0).astype(F32).astype(BF16)
        mine = steps == row.astype(F32).astype(BF16)
        parts = [jnp.where(mine, part, jnp.zeros_like(steps)) for part in split(value)]
        total = total + lax.dot_general(
            jnp.concatenate(parts, axis=0), lane_hot(lane), NT, preferred_element_type=F32
        )
    return total[:count] + total[count:]


def halves(wide):
    return [wide[:, at : at + LANES] for at in range(0, wide.shape[1], LANES)]


def own_group(devices, peers, away=0):
    shape = (devices, LANES)
    return lax.broadcasted_iota(jnp.int32, shape, 0) // peers - lax.axis_index("grp") == away


def send_rows(sent_ref, count, at, rows, peers):
    devices = sent_ref.shape[0] // count
    above = own_group(devices, peers, 1)
    shared = jnp.concatenate([rows[:peers]] * (devices // peers), axis=0)
    for r in range(FACE_ROWS):
        down = rows[peers + r : peers + r + 1]
        up = rows[peers + FACE_ROWS + r : peers + FACE_ROWS + r + 1]
        out = jnp.where(above, up, down)
        if r == 0:
            out = jnp.where(own_group(devices, peers), shared, out)
        sent_ref[pl.ds(at + r, devices, count), :] = out


def send_same(sent_ref, count, at, row):
    devices = sent_ref.shape[0] // count
    sent_ref[pl.ds(at, devices, count), :] = jnp.broadcast_to(row, (devices, LANES))


def get(received_ref, count, at):
    return received_ref[pl.ds(at, received_ref.shape[0] // count, count), :]


def get_shared(rows, peers):
    mine = jnp.where(own_group(rows.shape[0], peers), rows, 0.0)
    shared = mine[:peers]
    for g in range(1, rows.shape[0] // peers):
        shared = shared + mine[g * peers : (g + 1) * peers]
    return shared


def get_row(rows, peers, away):
    here = lax.axis_index("grp") * peers + lax.axis_index("sub")
    source = lax.broadcasted_iota(jnp.int32, rows.shape, 0) - here == away * peers
    return jnp.sum(jnp.where(source, rows, 0.0), axis=0, keepdims=True)


def get_rows(received_ref, count, at, peers):
    rows = [get(received_ref, count, at + r) for r in range(FACE_ROWS)]
    faces = [get_row(part, peers, away) for away in (-1, 1) for part in rows]
    return jnp.concatenate([get_shared(rows[0], peers)] + faces, axis=0)


def swapped(values):
    count = values.shape[0] // 2
    return jnp.concatenate([values[count:], values[:count]], axis=0)


def along_first(field, table_ref, base):
    elements = field.shape[0] // 4
    turned = pltpu.roll(field, 64, axis=1)
    out = []
    for to in range(4):
        total = None
        for at in range(4):
            place = base + 2 * (4 * to + at)
            rows = slice(at * elements, (at + 1) * elements)
            term = (
                table_ref[place : place + 1, :] * field[rows]
                + table_ref[place + 1 : place + 2, :] * turned[rows]
            )
            total = term if total is None else total + term
        out.append(total)
    return jnp.concatenate(out, axis=0)


def stiffness(field, metric_ref, first_ref, inner_ref):
    metric = [rows_of(metric_ref[:, POINTS * d : POINTS * (d + 1)]) for d in range(3)]
    count = field.shape[0]
    grad_first = along_first(field, first_ref, 0)
    high, low = split(field)
    both = jnp.dot(
        jnp.concatenate([high, low], axis=0), inner_ref[:LANES], preferred_element_type=F32
    )
    inner = both[:count] + both[count:]
    inner = inner + jnp.dot(high, inner_ref[LANES:], preferred_element_type=F32)
    flux_first = metric[0] * grad_first
    flux = jnp.concatenate([metric[1], metric[2]], axis=1) * inner
    high, low = split(flux)
    both = lax.dot_general(
        jnp.concatenate([high, low], axis=0), inner_ref[:LANES], NT, preferred_element_type=F32
    )
    back = both[:count] + both[count:]
    back = back + lax.dot_general(high, inner_ref[LANES:], NT, preferred_element_type=F32)
    back = back + along_first(flux_first, first_ref, 32)
    energy = flux * inner
    return back, flux_first * grad_first + energy[:, :LANES] + energy[:, LANES:]


def factors(points):
    nodes = 0.5 * (1.0 + np.cos(np.pi * np.arange(8) / 7.0))
    out = []
    for shift in (6, 3, 0):
        index = (points >> shift) & 7
        near = jnp.full(points.shape, nodes[7], F32)
        far = jnp.full(points.shape, nodes[0], F32)
        for m in range(7):
            near = jnp.where(index == m, float(nodes[m]), near)
            far = jnp.where(index == m, float(nodes[7 - m]), far)
        out.append((near, far))
    return out


def corners(points):
    first, second, third = factors(points)
    return [first[q >> 2 & 1] * (second[q >> 1 & 1] * third[q & 1]) for q in range(8)]


def own_corners():
    return corners(lax.broadcasted_iota(jnp.int32, (1, POINTS), 1))


def flat_map(mapped):
    elements = mapped.shape[1]
    width = 8 * elements
    own = own_element(elements, width)
    place = lax.broadcasted_iota(jnp.int32, (8, width), 1) // elements
    spread = jnp.where(own, 1.0, 0.0).astype(BF16)
    wide = jnp.dot(mapped.astype(F32).astype(BF16), spread, preferred_element_type=F32)
    keep = lax.broadcasted_iota(jnp.int32, (8, width), 0) == place
    return jnp.sum(jnp.where(keep, wide, 0.0), axis=0, keepdims=True)


def one_vertex(flat):
    return jnp.where(one_hot(flat, NC), 1.0, 0.0)


def whole(values):
    return (values + 0.5).astype(jnp.int32)


def own_element(elements, width):
    shape = (elements, width)
    return lax.broadcasted_iota(jnp.int32, shape, 0) == (
        lax.broadcasted_iota(jnp.int32, shape, 1) % elements
    )


def own_place(elements, q):
    shape = (elements, 8 * elements)
    lane = lax.broadcasted_iota(jnp.int32, shape, 1)
    return lane == lax.broadcasted_iota(jnp.int32, shape, 0) + q * elements


def coarse_part(field, vertices, inverse):
    elements = field.shape[0] // 4
    flat = jnp.zeros((elements, 8 * elements), F32)
    for q, corner in enumerate(own_corners()):
        inner = None
        for c in range(4):
            term = field[c * elements : (c + 1) * elements] * corner[:, c * LANES : (c + 1) * LANES]
            inner = term if inner is None else inner + term
        flat = jnp.where(own_place(elements, q), jnp.sum(inner, axis=1, keepdims=True), flat)
    flat = jnp.sum(flat, axis=0, keepdims=True)
    part = jnp.sum(vertices * flat, axis=1, keepdims=True)
    part = jnp.sum(inverse * part, axis=0, keepdims=True)
    return jnp.concatenate([part, jnp.zeros((1, LANES - NC), F32)], axis=1)


def get_solved(received_ref, count, peers):
    rows = get(received_ref, count, TERMS)
    return [
        jnp.sum(jnp.where(own_group(rows.shape[0], peers, away), rows, 0.0), axis=0, keepdims=True)
        for away in (0, -1, 1)
    ]


def prolonged(solved, flat, elements):
    shape = (elements, LANES)
    element = lax.broadcasted_iota(jnp.int32, shape, 0)
    at_corner = take(jnp.broadcast_to(solved, shape), jnp.broadcast_to(flat, shape))
    out = [None] * 4
    for q, corner in enumerate(own_corners()):
        value = take(at_corner, element + q * elements)
        for c in range(4):
            term = value * corner[:, c * LANES : (c + 1) * LANES]
            out[c] = term if out[c] is None else out[c] + term
    return jnp.concatenate(out, axis=0)


def prolonged_at(solved, maps, points, elements):
    at_corner = take(solved, maps)
    element = (points >> 9) & (elements - 1)
    total = jnp.zeros(points.shape, F32)
    for q, corner in enumerate(corners(points)):
        total = total + corner * take(at_corner, element + q * elements)
    return total


def total_of(array):
    return jnp.sum(jnp.sum(array, axis=0, keepdims=True), axis=1, keepdims=True)


def packed(values):
    lane = lax.broadcasted_iota(jnp.int32, (1, LANES), 1)
    out = jnp.zeros((1, LANES), F32)
    for k, value in enumerate(values):
        out = jnp.where(lane == k, value, out)
    return out


def unpacked(row, count):
    lane = lax.broadcasted_iota(jnp.int32, row.shape, 1)
    return [
        jnp.sum(jnp.where(lane == k, row, 0.0), axis=1, keepdims=True) for k in range(count)
    ]


def first_kernel(
    right_hbm, jacobi_hbm, inverse_hbm, map_hbm, slot_hbm, face_hbm, pair_hbm,
    sent_ref, resid_ref, rough_ref, points_ref, flat_ref,
    right_ref, jacobi_ref, inverse_ref, map_ref, slot_ref, face_ref, pair_ref, sems,
):
    copies = []
    for k, (source, target) in enumerate(
        (
            (face_hbm, face_ref),
            (slot_hbm, slot_ref),
            (right_hbm, right_ref),
            (jacobi_hbm, jacobi_ref),
            (map_hbm, map_ref),
            (inverse_hbm, inverse_ref),
            (pair_hbm, pair_ref),
        )
    ):
        copy = pltpu.make_async_copy(source, target, sems.at[k])
        copy.start()
        copies.append(copy)
    for copy in copies:
        copy.wait()
    elements = right_ref.shape[0]
    peers = slot_ref.shape[1]
    far = peers + 2 * FACE_ROWS
    faces = face_ref[...]
    pairs = pair_ref[...]
    points_ref[0:peers, :] = slot_ref[0]
    points_ref[peers:far, :] = jnp.concatenate(halves(faces[0:1]) + halves(faces[1:2]), axis=0)
    points_ref[far:, :] = jnp.concatenate(halves(pairs[0:1]) + halves(pairs[1:2]), axis=0)
    points = points_ref[0:far, :]
    resid = rows_of(right_ref[...])
    flat = flat_map(map_ref[...])
    flat_ref[...] = whole(flat)
    resid_ref[...] = resid
    rough = rows_of(jacobi_ref[...]) * resid
    rough_ref[...] = rough
    part = coarse_part(resid, one_vertex(whole(flat)), inverse_ref[0])
    values = gather(rough, points)
    send_rows(sent_ref, FIRST_ROWS, 0, values, peers)
    send_same(sent_ref, FIRST_ROWS, TERMS, part)
    send_same(sent_ref, FIRST_ROWS, TERMS + 1, flat)
    send_rows(sent_ref, FIRST_ROWS, TERMS + 2, points.astype(F32), peers)


def far_maps(received_ref, peers):
    maps = get(received_ref, FIRST_ROWS, TERMS + 1)
    sides = [
        jnp.broadcast_to(get_row(maps, peers, away), (FACE_ROWS, LANES)) for away in (-1, 1)
    ]
    return whole(jnp.concatenate([get_shared(maps, peers)] + sides, axis=0))


def apply(
    smoothed, count, received_ref, near, flat, maps, far_points, solved, metric_ref,
    helmholtz_ref, first_ref, inner_ref, points_ref, dots, back_ref, sent_ref,
):
    elements = smoothed.shape[0] // 4
    far = far_points.shape[0]
    peers = far - 2 * FACE_ROWS
    points = points_ref[...]
    counts = (peers, FACE_ROWS, FACE_ROWS, near.shape[0])
    coarse = prolonged_at(
        jnp.concatenate(
            [
                jnp.broadcast_to(part, (n, LANES))
                for part, n in zip((*solved, solved[0]), counts)
            ],
            axis=0,
        ),
        jnp.concatenate([maps, jnp.broadcast_to(flat, near.shape)], axis=0),
        jnp.concatenate([far_points, swapped(points[far:])], axis=0),
        elements,
    )
    incoming = jnp.concatenate([get_rows(received_ref, count, 0, peers), near], axis=0)
    summed = smoothed + scatter(4 * elements, points, incoming + coarse)
    back, energy = stiffness(summed, metric_ref, first_ref, inner_ref)
    energy = energy + rows_of(helmholtz_ref[...]) * smoothed * smoothed
    back_ref[...] = back
    send_rows(sent_ref, ROWS, 0, gather(back, points[:far]), peers)
    send_same(sent_ref, ROWS, TERMS, packed(dots + [total_of(energy)]))


def near_kernel(field_ref, points_ref, near_ref):
    points = points_ref[points_ref.shape[0] - near_ref.shape[0] :, :]
    near_ref[...] = swapped(gather(field_ref[...], points))


def inside_kernel(field_ref, back_ref, helmholtz_ref, points_ref, inside_ref, *, far):
    points = points_ref[far:, :]
    back = back_ref[...]
    near = scatter(back.shape[0], points, swapped(gather(back, points)))
    inside_ref[...] = back + near + rows_of(helmholtz_ref[...]) * field_ref[...]


def image_of(inside_ref, received_ref, points_ref, far):
    incoming = get_rows(received_ref, ROWS, 0, far - 2 * FACE_ROWS)
    return inside_ref[...] + scatter(inside_ref.shape[0], points_ref[0:far, :], incoming)


def start_kernel(
    received_ref, near_ref, resid_ref, rough_ref, points_ref, flat_ref, metric_ref, helmholtz_ref,
    first_ref, inner_ref,
    smoothed_ref, maps_ref, far_points_ref, back_ref, sent_ref,
):
    elements = helmholtz_ref.shape[0]
    peers = maps_ref.shape[0] - 2 * FACE_ROWS
    solved = get_solved(received_ref, FIRST_ROWS, peers)
    resid = resid_ref[...]
    smoothed = rough_ref[...] + prolonged(solved[0], flat_ref[...], elements)
    smoothed_ref[...] = smoothed
    maps = far_maps(received_ref, peers)
    maps_ref[...] = maps
    far_points = whole(get_rows(received_ref, FIRST_ROWS, TERMS + 2, peers))
    far_points_ref[...] = far_points
    apply(
        smoothed, FIRST_ROWS, received_ref, near_ref[...], flat_ref[...], maps, far_points, solved,
        metric_ref, helmholtz_ref, first_ref, inner_ref, points_ref,
        [total_of(resid * smoothed)], back_ref, sent_ref,
    )


def middle_kernel(
    received_ref, inside_ref, right_ref, points_ref, flat_ref, jacobi_ref, inverse_ref,
    image_ref, resid_ref, rough_ref, scalars_ref, sent_ref, *, far,
):
    dots = jnp.sum(get(received_ref, ROWS, TERMS), axis=0, keepdims=True)
    scalars_ref[...] = dots
    values = unpacked(dots, 2)
    alpha = values[0] / values[1]
    image = image_of(inside_ref, received_ref, points_ref, far)
    image_ref[...] = image
    resid = right_ref[...] - alpha * image
    resid_ref[...] = resid
    rough = rows_of(jacobi_ref[...]) * resid
    rough_ref[...] = rough
    part = coarse_part(resid, one_vertex(flat_ref[...]), inverse_ref[0])
    values = gather(rough, points_ref[0:far, :])
    send_rows(sent_ref, ROWS, 0, values, far - 2 * FACE_ROWS)
    send_same(sent_ref, ROWS, TERMS, part)


def second_kernel(
    received_ref, near_ref, points_ref, flat_ref, maps_ref, far_points_ref, resid_ref, rough_ref,
    image_ref, metric_ref, helmholtz_ref, first_ref, inner_ref,
    smoothed_ref, back_ref, sent_ref,
):
    elements = helmholtz_ref.shape[0]
    solved = get_solved(received_ref, ROWS, maps_ref.shape[0] - 2 * FACE_ROWS)
    resid = resid_ref[...]
    smoothed = rough_ref[...] + prolonged(solved[0], flat_ref[...], elements)
    smoothed_ref[...] = smoothed
    apply(
        smoothed, ROWS, received_ref, near_ref[...], flat_ref[...], maps_ref[...],
        far_points_ref[...], solved, metric_ref, helmholtz_ref, first_ref, inner_ref, points_ref,
        [total_of(resid * smoothed), total_of(image_ref[...] * smoothed)],
        back_ref, sent_ref,
    )


def final_kernel(
    received_ref, inside_ref, points_ref, old_ref, field_ref, resid_ref, old_image_ref, scalars_ref,
    solution_ref, residual_ref, *, far,
):
    before = unpacked(scalars_ref[...], 2)
    now = unpacked(jnp.sum(get(received_ref, ROWS, TERMS), axis=0, keepdims=True), 3)
    alpha = before[0] / before[1]
    beta = now[0] / before[0]
    curved = now[2] + beta * (2.0 * now[1] + beta * before[1])
    step = now[0] / curved
    old = old_ref[...]
    direction = field_ref[...] + beta * old
    solution_ref[...] = wide_of(alpha * old + step * direction)
    image = image_of(inside_ref, received_ref, points_ref, far)
    image = image + beta * old_image_ref[...]
    residual_ref[...] = wide_of(resid_ref[...] - step * image)


def call(kernel, outs, *args, copied=False):
    space = pl.ANY if copied else pltpu.VMEM
    scratch = [pltpu.VMEM(arg.shape, arg.dtype) for arg in args] if copied else []
    if copied:
        args = [pltpu.with_memory_space_constraint(arg, pltpu.HBM) for arg in args]
    return pl.pallas_call(
        kernel,
        out_shape=[
            jax.ShapeDtypeStruct(*(out if isinstance(out[0], tuple) else (out, F32))) for out in outs
        ],
        in_specs=[pl.BlockSpec(memory_space=space)] * len(args),
        out_specs=[pl.BlockSpec(memory_space=pltpu.VMEM)] * len(outs),
        scratch_shapes=scratch + ([pltpu.SemaphoreType.DMA((len(args),))] if copied else []),
        compiler_params=pltpu.CompilerParams(vmem_limit_bytes=24 * 1024 * 1024),
    )(*args)


def body(
    right_side,
    metric,
    helmholtz,
    jacobi,
    pair_list,
    shared_slots,
    face_points,
    coarse_map,
    coarse_inverse,
):
    peers = lax.axis_size("sub")
    groups = lax.axis_size("grp")
    t = {name: jnp.asarray(value) for name, value in tables().items()}
    elements = right_side.shape[0]
    field = (4 * elements, LANES)
    far = (peers + face_points.size // LANES, LANES)
    local = (pair_list.size // LANES, LANES)
    sent_shape = (groups * peers * ROWS, LANES)
    inside_part, middle, final = [
        functools.partial(kernel, far=far[0])
        for kernel in (inside_kernel, middle_kernel, final_kernel)
    ]

    def exchange(sent):
        rows = sent.reshape(groups * peers, 1, -1)
        return lax.all_to_all(rows, ("grp", "sub"), 0, 0, tiled=True).reshape(sent.shape)

    sent, resid, rough, points, flat = call(
        first_kernel,
        [
            (groups * peers * FIRST_ROWS, LANES),
            field,
            field,
            ((far[0] + local[0], LANES), jnp.int32),
            ((1, LANES), jnp.int32),
        ],
        right_side, jacobi, coarse_inverse, coarse_map, shared_slots, face_points, pair_list,
        copied=True,
    )
    received = exchange(sent)
    (near,) = call(near_kernel, [local], rough, points)
    smoothed, maps, far_points, back, sent = call(
        start_kernel,
        [field, (far, jnp.int32), (far, jnp.int32), field, sent_shape],
        received, near, resid, rough, points, flat, metric, helmholtz, t["first"], t["inner"],
    )
    received = exchange(sent)
    (inside,) = call(inside_part, [field], smoothed, back, helmholtz, points)
    image, resid, rough, scalars, sent = call(
        middle, [field, field, field, (1, LANES), sent_shape],
        received, inside, resid, points, flat, jacobi, coarse_inverse,
    )
    received = exchange(sent)
    (near,) = call(near_kernel, [local], rough, points)
    second, back, sent = call(
        second_kernel, [field, field, sent_shape],
        received, near, points, flat, maps, far_points, resid, rough, image,
        metric, helmholtz, t["first"], t["inner"],
    )
    received = exchange(sent)
    (inside,) = call(inside_part, [field], second, back, helmholtz, points)
    return tuple(
        call(
            final, [right_side.shape, right_side.shape],
            received, inside, points, smoothed, second, resid, image, scalars,
        )
    )


def solution(mesh):
    in_specs = (
        P(("grp", "sub"), None),
        P(("grp", "sub"), None),
        P(("grp", "sub"), None),
        P(("grp", "sub"), None),
        P(None, ("grp", "sub")),
        P(("grp", "sub"), None, None),
        P(None, ("grp", "sub")),
        P(None, ("grp", "sub")),
        P("grp", None, None),
    )
    out_specs = (P(("grp", "sub"), None), P(("grp", "sub"), None))
    return jax.shard_map(body, mesh=mesh, in_specs=in_specs, out_specs=out_specs, check_vma=False)
```

```python
import jax
import jax.numpy as jnp
import ml_dtypes
import numpy as np
from jax import lax
from jax.experimental import pallas as pl
from jax.experimental.pallas import tpu as pltpu
from jax.sharding import PartitionSpec as P

NC = 64
POINTS = 512
LANES = 128
STEP = 256
FACE_ROWS = 4
ROWS = 5
FIRST_ROWS = 10
TERMS = FACE_ROWS
F32 = jnp.float32
BF16 = jnp.bfloat16
NT = (((1,), (1,)), ((), ()))


def split_constant(array):
    high = array.astype(ml_dtypes.bfloat16)
    low = (array - high.astype(np.float64)).astype(ml_dtypes.bfloat16)
    return high, low


def tables():
    order_index = np.arange(8)
    colloc = np.cos(np.pi * order_index / 7.0)
    end_weights = (
        np.where((order_index == 0) | (order_index == 7), 2.0, 1.0) * (-1.0) ** order_index
    )
    spacing = colloc[:, None] - colloc[None, :] + np.eye(8)
    raw_matrix = np.outer(end_weights, 1.0 / end_weights) / spacing
    off_part = raw_matrix * (1.0 - np.eye(8))
    derivative = 0.25 * (off_part - np.eye(8) * off_part.sum(axis=1)[:, None])
    along_inner = np.concatenate(
        [np.kron(np.eye(2), np.kron(derivative, np.eye(8))).T, np.kron(np.eye(16), derivative).T],
        axis=1,
    )
    high, low = split_constant(along_inner)
    inner = np.concatenate([high, low], axis=0)

    half = np.arange(LANES) // 64

    def first_rows(matrix):
        rows = []
        for to in range(4):
            for at in range(4):
                rows.append(matrix[2 * to + half, 2 * at + half])
                rows.append(matrix[2 * to + half, 2 * at + 1 - half])
        return np.stack(rows).astype(np.float32)

    return {
        "inner": inner,
        "first": np.concatenate([first_rows(derivative), first_rows(derivative.T)], axis=0),
    }


def split(value):
    high = value.astype(BF16)
    return high, (value - high.astype(F32)).astype(BF16)


def rows_of(wide):
    return jnp.concatenate([wide[:, LANES * c : LANES * (c + 1)] for c in range(4)], axis=0)


def wide_of(rows):
    elements = rows.shape[0] // 4
    return jnp.concatenate([rows[c * elements : (c + 1) * elements] for c in range(4)], axis=1)


def locate(points, elements):
    element = points >> 9
    chunk = (points >> 7) & 3
    row = jnp.where(points < elements * POINTS, chunk * elements + element, 4 * elements)
    return row, points & (LANES - 1)


def one_hot(index, count):
    steps = lax.broadcasted_iota(jnp.int32, (count, index.shape[1]), 0)
    return steps == index


def lane_hot(lane):
    steps = lax.broadcasted_iota(jnp.int32, (LANES, lane.shape[1]), 0).astype(F32).astype(BF16)
    one = jnp.ones(steps.shape, BF16)
    return jnp.where(steps == lane.astype(F32).astype(BF16), one, jnp.zeros_like(one))


def take(values, lanes):
    return jnp.take_along_axis(values, lanes, axis=1, mode="promise_in_bounds")


def gather(field, chunks):
    count = field.shape[0]
    both = jnp.concatenate(split(field), axis=0)
    out = []
    for row, lane in chunks:
        picked = jnp.dot(both, lane_hot(lane), preferred_element_type=F32)
        mine = jnp.where(one_hot(row, count), picked[:count] + picked[count:], 0.0)
        out.append(jnp.sum(mine, axis=0, keepdims=True))
    return out


def scatter(rows, chunks, values):
    total = jnp.zeros((2 * rows, LANES), F32)
    for (row, lane), value in zip(chunks, values):
        steps = lax.broadcasted_iota(jnp.int32, (rows, row.shape[1]), 0).astype(F32).astype(BF16)
        mine = steps == row.astype(F32).astype(BF16)
        parts = [jnp.where(mine, part, jnp.zeros_like(steps)) for part in split(value)]
        total = total + lax.dot_general(
            jnp.concatenate(parts, axis=0), lane_hot(lane), NT, preferred_element_type=F32
        )
    return total[:rows] + total[rows:]


def chunked(row, lane):
    return [
        (row[:, at : at + STEP], lane[:, at : at + STEP]) for at in range(0, row.shape[1], STEP)
    ]


def cut(row):
    return [row[:, at : at + STEP] for at in range(0, row.shape[1], STEP)]


def pair_chunks(pair_ref, elements):
    row, lane = locate(pair_ref[...], elements)
    return chunked(row[0:1], lane[0:1]) + chunked(row[1:2], lane[1:2])


def joined(rows):
    return [
        jnp.concatenate([rows[at : at + 1], rows[at + 1 : at + 2]], axis=1)
        for at in range(0, rows.shape[0], 2)
    ]


def far_chunks(points, elements):
    row, lane = locate(points, elements)
    return list(zip(joined(row), joined(lane)))


def halves(wide):
    return [wide[:, at : at + LANES] for at in range(0, wide.shape[1], LANES)]


def own_group(devices, peers, away=0):
    shape = (devices, LANES)
    return lax.broadcasted_iota(jnp.int32, shape, 0) // peers - lax.axis_index("grp") == away


def send_rows(sent_ref, count, at, rows, peers):
    devices = sent_ref.shape[0] // count
    above = own_group(devices, peers, 1)
    shared = jnp.concatenate([rows[:peers]] * (devices // peers), axis=0)
    for r in range(FACE_ROWS):
        down = rows[peers + r : peers + r + 1]
        up = rows[peers + FACE_ROWS + r : peers + FACE_ROWS + r + 1]
        out = jnp.where(above, up, down)
        if r == 0:
            out = jnp.where(own_group(devices, peers), shared, out)
        sent_ref[pl.ds(at + r, devices, count), :] = out


def send_same(sent_ref, count, at, row):
    devices = sent_ref.shape[0] // count
    sent_ref[pl.ds(at, devices, count), :] = jnp.broadcast_to(row, (devices, LANES))


def send_values(sent_ref, count, values, peers):
    rows = jnp.concatenate([row for pair in values for row in halves(pair)], axis=0)
    send_rows(sent_ref, count, 0, rows, peers)


def get(received_ref, count, at):
    return received_ref[pl.ds(at, received_ref.shape[0] // count, count), :]


def get_shared(rows, peers):
    mine = jnp.where(own_group(rows.shape[0], peers), rows, 0.0)
    shared = mine[:peers]
    for g in range(1, rows.shape[0] // peers):
        shared = shared + mine[g * peers : (g + 1) * peers]
    return shared


def get_row(rows, peers, away):
    here = lax.axis_index("grp") * peers + lax.axis_index("sub")
    source = lax.broadcasted_iota(jnp.int32, rows.shape, 0) - here == away * peers
    return jnp.sum(jnp.where(source, rows, 0.0), axis=0, keepdims=True)


def get_rows(received_ref, count, at, peers):
    rows = [get(received_ref, count, at + r) for r in range(FACE_ROWS)]
    faces = [get_row(part, peers, away) for away in (-1, 1) for part in rows]
    return jnp.concatenate([get_shared(rows[0], peers)] + faces, axis=0)


def swapped(values):
    count = len(values) // 2
    return values[count:] + values[:count]


def along_first(field, table_ref, base):
    elements = field.shape[0] // 4
    turned = pltpu.roll(field, 64, axis=1)
    out = []
    for to in range(4):
        total = None
        for at in range(4):
            place = base + 2 * (4 * to + at)
            rows = slice(at * elements, (at + 1) * elements)
            term = (
                table_ref[place : place + 1, :] * field[rows]
                + table_ref[place + 1 : place + 2, :] * turned[rows]
            )
            total = term if total is None else total + term
        out.append(total)
    return jnp.concatenate(out, axis=0)


def stiffness(field, metric_ref, first_ref, inner_ref):
    metric = [rows_of(metric_ref[:, POINTS * d : POINTS * (d + 1)]) for d in range(3)]
    count = field.shape[0]
    grad_first = along_first(field, first_ref, 0)
    high, low = split(field)
    both = jnp.dot(
        jnp.concatenate([high, low], axis=0), inner_ref[:LANES], preferred_element_type=F32
    )
    inner = both[:count] + both[count:]
    inner = inner + jnp.dot(high, inner_ref[LANES:], preferred_element_type=F32)
    flux_first = metric[0] * grad_first
    flux = jnp.concatenate([metric[1], metric[2]], axis=1) * inner
    high, low = split(flux)
    both = lax.dot_general(
        jnp.concatenate([high, low], axis=0), inner_ref[:LANES], NT, preferred_element_type=F32
    )
    back = both[:count] + both[count:]
    back = back + lax.dot_general(high, inner_ref[LANES:], NT, preferred_element_type=F32)
    back = back + along_first(flux_first, first_ref, 32)
    energy = flux * inner
    return back, flux_first * grad_first + energy[:, :LANES] + energy[:, LANES:]


def factors(points):
    nodes = 0.5 * (1.0 + np.cos(np.pi * np.arange(8) / 7.0))
    out = []
    for shift in (6, 3, 0):
        index = (points >> shift) & 7
        near = jnp.full(points.shape, nodes[7], F32)
        far = jnp.full(points.shape, nodes[0], F32)
        for m in range(7):
            near = jnp.where(index == m, float(nodes[m]), near)
            far = jnp.where(index == m, float(nodes[7 - m]), far)
        out.append((near, far))
    return out


def corners(points):
    first, second, third = factors(points)
    return [
        first[q >> 2 & 1] * (second[q >> 1 & 1] * third[q & 1]) for q in range(8)
    ]


def own_corners():
    return corners(lax.broadcasted_iota(jnp.int32, (1, POINTS), 1))


def flat_map(mapped):
    elements = mapped.shape[1]
    width = 8 * elements
    own = own_element(elements, width)
    place = lax.broadcasted_iota(jnp.int32, (8, width), 1) // elements
    spread = jnp.where(own, 1.0, 0.0).astype(BF16)
    wide = jnp.dot(mapped.astype(F32).astype(BF16), spread, preferred_element_type=F32)
    keep = lax.broadcasted_iota(jnp.int32, (8, width), 0) == place
    return jnp.sum(jnp.where(keep, wide, 0.0), axis=0, keepdims=True)


def one_vertex(flat):
    return jnp.where(one_hot(whole(flat), NC), 1.0, 0.0)


def whole(values):
    return (values + 0.5).astype(jnp.int32)


def own_element(elements, width):
    shape = (elements, width)
    return lax.broadcasted_iota(jnp.int32, shape, 0) == (
        lax.broadcasted_iota(jnp.int32, shape, 1) % elements
    )


def own_place(elements, q):
    shape = (elements, 8 * elements)
    lane = lax.broadcasted_iota(jnp.int32, shape, 1)
    return lane == lax.broadcasted_iota(jnp.int32, shape, 0) + q * elements


def coarse_part(field, vertices, inverse):
    elements = field.shape[0] // 4
    flat = jnp.zeros((elements, 8 * elements), F32)
    for q, corner in enumerate(own_corners()):
        inner = None
        for c in range(4):
            term = field[c * elements : (c + 1) * elements] * corner[:, c * LANES : (c + 1) * LANES]
            inner = term if inner is None else inner + term
        flat = jnp.where(own_place(elements, q), jnp.sum(inner, axis=1, keepdims=True), flat)
    flat = jnp.sum(flat, axis=0, keepdims=True)
    part = jnp.sum(vertices * flat, axis=1, keepdims=True)
    part = jnp.sum(inverse * part, axis=0, keepdims=True)
    return jnp.concatenate([part, jnp.zeros((1, LANES - NC), F32)], axis=1)


def get_solved(received_ref, count, peers):
    rows = get(received_ref, count, TERMS)
    return [
        jnp.sum(jnp.where(own_group(rows.shape[0], peers, away), rows, 0.0), axis=0, keepdims=True)
        for away in (0, -1, 1)
    ]


def prolonged(solved, flat, elements):
    shape = (elements, LANES)
    element = lax.broadcasted_iota(jnp.int32, shape, 0)
    at_corner = take(jnp.broadcast_to(solved, shape), jnp.broadcast_to(flat, shape))
    out = [None] * 4
    for q, corner in enumerate(own_corners()):
        value = take(at_corner, element + q * elements)
        for c in range(4):
            term = value * corner[:, c * LANES : (c + 1) * LANES]
            out[c] = term if out[c] is None else out[c] + term
    return jnp.concatenate(out, axis=0)


def prolonged_at(solved, maps, points, elements):
    at_corner = take(solved, maps)
    element = (points >> 9) & (elements - 1)
    total = jnp.zeros(points.shape, F32)
    for q, corner in enumerate(corners(points)):
        total = total + corner * take(at_corner, element + q * elements)
    return total


def total_of(array):
    return jnp.sum(jnp.sum(array, axis=0, keepdims=True), axis=1, keepdims=True)


def packed(values):
    lane = lax.broadcasted_iota(jnp.int32, (1, LANES), 1)
    out = jnp.zeros((1, LANES), F32)
    for k, value in enumerate(values):
        out = jnp.where(lane == k, value, out)
    return out


def unpacked(row, count):
    lane = lax.broadcasted_iota(jnp.int32, row.shape, 1)
    return [
        jnp.sum(jnp.where(lane == k, row, 0.0), axis=1, keepdims=True) for k in range(count)
    ]


def first_kernel(
    right_hbm, jacobi_hbm, inverse_hbm, map_hbm, slot_hbm, face_hbm,
    sent_ref, fields_ref, points_ref,
    right_ref, jacobi_ref, inverse_ref, map_ref, slot_ref, face_ref, sems,
):
    copies = []
    for k, (source, target) in enumerate(
        (
            (face_hbm, face_ref),
            (slot_hbm, slot_ref),
            (right_hbm, right_ref),
            (jacobi_hbm, jacobi_ref),
            (map_hbm, map_ref),
            (inverse_hbm, inverse_ref),
        )
    ):
        copy = pltpu.make_async_copy(source, target, sems.at[k])
        copy.start()
        copies.append(copy)
    for copy in copies:
        copy.wait()
    elements = right_ref.shape[0]
    peers = slot_ref.shape[1]
    faces = face_ref[...]
    faces = jnp.concatenate(halves(faces[0:1]) + halves(faces[1:2]), axis=0)
    points = jnp.concatenate([slot_ref[0], faces], axis=0)
    points_ref[...] = points
    resid = rows_of(right_ref[...])
    flat = flat_map(map_ref[...])
    smoothed = rows_of(jacobi_ref[...]) * resid
    fields_ref[0 : 4 * elements, :] = resid
    fields_ref[4 * elements : 8 * elements, :] = smoothed
    fields_ref[8 * elements :, :] = jnp.broadcast_to(flat, (8, LANES))
    part = coarse_part(resid, one_vertex(flat), inverse_ref[0])
    values = gather(smoothed, far_chunks(points, elements))
    send_values(sent_ref, FIRST_ROWS, values, peers)
    send_same(sent_ref, FIRST_ROWS, TERMS, part)
    send_same(sent_ref, FIRST_ROWS, TERMS + 1, flat)
    send_rows(sent_ref, FIRST_ROWS, TERMS + 2, points.astype(F32), peers)


def far_maps(received_ref, peers):
    maps = get(received_ref, FIRST_ROWS, TERMS + 1)
    sides = [
        jnp.broadcast_to(get_row(maps, peers, away), (FACE_ROWS, LANES)) for away in (-1, 1)
    ]
    return whole(jnp.concatenate([get_shared(maps, peers)] + sides, axis=0))


def apply(
    smoothed, count, received_ref, maps, far_points, solved, metric_ref, helmholtz_ref,
    first_ref, inner_ref, pair_ref, points_ref, dots, back_ref, local_ref, sent_ref,
):
    elements = smoothed.shape[0] // 4
    peers = points_ref.shape[0] - 2 * FACE_ROWS
    pairs = pair_chunks(pair_ref, elements)
    far = far_chunks(points_ref[...], elements)
    counts = (peers, FACE_ROWS, FACE_ROWS)
    spread = [jnp.broadcast_to(part, (n, LANES)) for part, n in zip(solved, counts)]
    incoming = get_rows(received_ref, count, 0, peers) + prolonged_at(
        jnp.concatenate(spread, axis=0), maps, far_points, elements
    )
    values = swapped(gather(smoothed, pairs)) + joined(incoming)
    summed = smoothed + scatter(smoothed.shape[0], pairs + far, values)
    back, energy = stiffness(summed, metric_ref, first_ref, inner_ref)
    energy = energy + rows_of(helmholtz_ref[...]) * smoothed * smoothed
    back_ref[...] = back
    values = gather(back, pairs + far)
    near = swapped(values[: len(pairs)])
    for k, value in enumerate(near):
        local_ref[0:1, k * STEP : (k + 1) * STEP] = value
    send_values(sent_ref, ROWS, values[len(pairs) :], peers)
    send_same(sent_ref, ROWS, TERMS, packed(dots + [total_of(energy)]))


def image_of(
    field_ref, back_ref, local_ref, received_ref, helmholtz_ref, pair_ref, points_ref
):
    elements = field_ref.shape[0] // 4
    peers = points_ref.shape[0] - 2 * FACE_ROWS
    chunks = pair_chunks(pair_ref, elements) + far_chunks(points_ref[...], elements)
    values = cut(local_ref[...]) + joined(get_rows(received_ref, ROWS, 0, peers))
    summed = back_ref[...] + scatter(field_ref.shape[0], chunks, values)
    return summed + rows_of(helmholtz_ref[...]) * field_ref[...]


def start_kernel(
    received_ref, fields_ref, points_ref, pair_ref, metric_ref, helmholtz_ref,
    first_ref, inner_ref,
    smoothed_ref, maps_ref, far_points_ref, back_ref, local_ref, sent_ref,
):
    elements = helmholtz_ref.shape[0]
    peers = points_ref.shape[0] - 2 * FACE_ROWS
    solved = get_solved(received_ref, FIRST_ROWS, peers)
    resid = fields_ref[0 : 4 * elements, :]
    flat = whole(fields_ref[8 * elements : 8 * elements + 1, :])
    smoothed = fields_ref[4 * elements : 8 * elements, :]
    smoothed = smoothed + prolonged(solved[0], flat, elements)
    smoothed_ref[...] = smoothed
    maps = far_maps(received_ref, peers)
    maps_ref[...] = maps
    far_points = whole(get_rows(received_ref, FIRST_ROWS, TERMS + 2, peers))
    far_points_ref[...] = far_points
    apply(
        smoothed, FIRST_ROWS, received_ref, maps, far_points, solved, metric_ref,
        helmholtz_ref, first_ref, inner_ref, pair_ref, points_ref,
        [total_of(resid * smoothed)], back_ref, local_ref, sent_ref,
    )


def middle_kernel(
    received_ref, fields_ref, points_ref, pair_ref, jacobi_ref, helmholtz_ref,
    inverse_ref, smoothed_ref, back_ref, local_ref,
    image_ref, resid_ref, scalars_ref, sent_ref,
):
    elements = helmholtz_ref.shape[0]
    peers = points_ref.shape[0] - 2 * FACE_ROWS
    dots = jnp.sum(get(received_ref, ROWS, TERMS), axis=0, keepdims=True)
    scalars_ref[...] = dots
    values = unpacked(dots, 2)
    alpha = values[0] / values[1]
    image = image_of(
        smoothed_ref, back_ref, local_ref, received_ref, helmholtz_ref, pair_ref,
        points_ref,
    )
    image_ref[...] = image
    resid = fields_ref[0 : 4 * elements, :] - alpha * image
    resid_ref[...] = resid
    vertices = one_vertex(fields_ref[8 * elements : 8 * elements + 1, :])
    part = coarse_part(resid, vertices, inverse_ref[0])
    values = gather(rows_of(jacobi_ref[...]) * resid, far_chunks(points_ref[...], elements))
    send_values(sent_ref, ROWS, values, peers)
    send_same(sent_ref, ROWS, TERMS, part)


def second_kernel(
    received_ref, fields_ref, points_ref, pair_ref, resid_ref, image_ref,
    maps_ref, far_points_ref, jacobi_ref, metric_ref, helmholtz_ref, first_ref, inner_ref,
    smoothed_ref, back_ref, local_ref, sent_ref,
):
    elements = helmholtz_ref.shape[0]
    peers = points_ref.shape[0] - 2 * FACE_ROWS
    solved = get_solved(received_ref, ROWS, peers)
    resid = resid_ref[...]
    flat = whole(fields_ref[8 * elements : 8 * elements + 1, :])
    smoothed = rows_of(jacobi_ref[...]) * resid + prolonged(solved[0], flat, elements)
    smoothed_ref[...] = smoothed
    apply(
        smoothed, ROWS, received_ref, maps_ref[...], far_points_ref[...], solved, metric_ref,
        helmholtz_ref, first_ref, inner_ref, pair_ref, points_ref,
        [total_of(resid * smoothed), total_of(image_ref[...] * smoothed)],
        back_ref, local_ref, sent_ref,
    )


def final_kernel(
    received_ref, points_ref, pair_ref, old_ref, field_ref, resid_ref, old_image_ref,
    scalars_ref, back_ref, local_ref, helmholtz_ref,
    solution_ref, residual_ref,
):
    before = unpacked(scalars_ref[...], 2)
    now = unpacked(jnp.sum(get(received_ref, ROWS, TERMS), axis=0, keepdims=True), 3)
    alpha = before[0] / before[1]
    beta = now[0] / before[0]
    curved = now[2] + beta * (2.0 * now[1] + beta * before[1])
    step = now[0] / curved
    old = old_ref[...]
    direction = field_ref[...] + beta * old
    solution_ref[...] = wide_of(alpha * old + step * direction)
    image = image_of(
        field_ref, back_ref, local_ref, received_ref, helmholtz_ref, pair_ref,
        points_ref,
    )
    image = image + beta * old_image_ref[...]
    residual_ref[...] = wide_of(resid_ref[...] - step * image)


def call(kernel, outs, *args, copied=False):
    space = pl.ANY if copied else pltpu.VMEM
    scratch = [pltpu.VMEM(arg.shape, arg.dtype) for arg in args] if copied else []
    if copied:
        args = [pltpu.with_memory_space_constraint(arg, pltpu.HBM) for arg in args]
    return pl.pallas_call(
        kernel,
        out_shape=[
            jax.ShapeDtypeStruct(*(out if isinstance(out[0], tuple) else (out, F32))) for out in outs
        ],
        in_specs=[pl.BlockSpec(memory_space=space)] * len(args),
        out_specs=[pl.BlockSpec(memory_space=pltpu.VMEM)] * len(outs),
        scratch_shapes=scratch + ([pltpu.SemaphoreType.DMA((len(args),))] if copied else []),
        compiler_params=pltpu.CompilerParams(vmem_limit_bytes=24 * 1024 * 1024),
    )(*args)


def body(
    right_side,
    metric,
    helmholtz,
    jacobi,
    pair_list,
    shared_slots,
    face_points,
    coarse_map,
    coarse_inverse,
):
    peers = lax.axis_size("sub")
    groups = lax.axis_size("grp")
    t = {name: jnp.asarray(value) for name, value in tables().items()}
    elements = right_side.shape[0]
    field = (4 * elements, LANES)
    local = (1, pair_list.shape[0] * pair_list.shape[1])
    points_shape = (peers + 2 * FACE_ROWS, LANES)
    sent_shape = (groups * peers * ROWS, LANES)

    def exchange(sent):
        rows = sent.reshape(groups * peers, 1, -1)
        return lax.all_to_all(rows, ("grp", "sub"), 0, 0, tiled=True).reshape(sent.shape)

    sent, fields, points = call(
        first_kernel,
        [
            (groups * peers * FIRST_ROWS, LANES),
            (8 * elements + 8, LANES),
            (points_shape, jnp.int32),
        ],
        right_side, jacobi, coarse_inverse, coarse_map, shared_slots, face_points, copied=True,
    )
    smoothed, maps, far_points, back, near, sent = call(
        start_kernel,
        [field, (points_shape, jnp.int32), (points_shape, jnp.int32), field, local, sent_shape],
        exchange(sent), fields, points, pair_list, metric, helmholtz,
        t["first"], t["inner"],
    )
    image, resid, scalars, sent = call(
        middle_kernel, [field, field, (1, LANES), sent_shape],
        exchange(sent), fields, points, pair_list, jacobi, helmholtz, coarse_inverse,
        smoothed, back, near,
    )
    second, back, near, sent = call(
        second_kernel, [field, field, local, sent_shape],
        exchange(sent), fields, points, pair_list, resid, image, maps, far_points, jacobi,
        metric, helmholtz, t["first"], t["inner"],
    )
    return tuple(
        call(
            final_kernel, [right_side.shape, right_side.shape],
            exchange(sent), points, pair_list, smoothed, second, resid, image, scalars,
            back, near, helmholtz,
        )
    )


def solution(mesh):
    in_specs = (
        P(("grp", "sub"), None),
        P(("grp", "sub"), None),
        P(("grp", "sub"), None),
        P(("grp", "sub"), None),
        P(None, ("grp", "sub")),
        P(("grp", "sub"), None, None),
        P(None, ("grp", "sub")),
        P(None, ("grp", "sub")),
        P("grp", None, None),
    )
    out_specs = (P(("grp", "sub"), None), P(("grp", "sub"), None))
    return jax.shard_map(body, mesh=mesh, in_specs=in_specs, out_specs=out_specs, check_vma=False)
```

```python
import jax
import jax.numpy as jnp
import ml_dtypes
import numpy as np
from jax import lax
from jax.experimental import pallas as pl
from jax.experimental.pallas import tpu as pltpu
from jax.sharding import PartitionSpec as P

NC = 64
POINTS = 512
LANES = 128
STEP = 256
FACE_ROWS = 4
ROWS = 5
FIRST_ROWS = 10
TERMS = FACE_ROWS
F32 = jnp.float32
BF16 = jnp.bfloat16
NT = (((1,), (1,)), ((), ()))


def split_constant(array):
    high = array.astype(ml_dtypes.bfloat16)
    low = (array - high.astype(np.float64)).astype(ml_dtypes.bfloat16)
    return high, low


def tables():
    order_index = np.arange(8)
    colloc = np.cos(np.pi * order_index / 7.0)
    end_weights = (
        np.where((order_index == 0) | (order_index == 7), 2.0, 1.0) * (-1.0) ** order_index
    )
    spacing = colloc[:, None] - colloc[None, :] + np.eye(8)
    raw_matrix = np.outer(end_weights, 1.0 / end_weights) / spacing
    off_part = raw_matrix * (1.0 - np.eye(8))
    derivative = 0.25 * (off_part - np.eye(8) * off_part.sum(axis=1)[:, None])
    along_inner = np.concatenate(
        [np.kron(np.eye(2), np.kron(derivative, np.eye(8))).T, np.kron(np.eye(16), derivative).T],
        axis=1,
    )
    high, low = split_constant(along_inner)
    inner = np.concatenate([high, low], axis=0)

    half = np.arange(LANES) // 64

    def first_rows(matrix):
        rows = []
        for to in range(4):
            for at in range(4):
                rows.append(matrix[2 * to + half, 2 * at + half])
                rows.append(matrix[2 * to + half, 2 * at + 1 - half])
        return np.stack(rows).astype(np.float32)

    return {
        "inner": inner,
        "first": np.concatenate([first_rows(derivative), first_rows(derivative.T)], axis=0),
    }


def split(value):
    high = value.astype(BF16)
    return high, (value - high.astype(F32)).astype(BF16)


def rows_of(wide):
    return jnp.concatenate([wide[:, LANES * c : LANES * (c + 1)] for c in range(4)], axis=0)


def wide_of(rows):
    elements = rows.shape[0] // 4
    return jnp.concatenate([rows[c * elements : (c + 1) * elements] for c in range(4)], axis=1)


def locate(points, elements):
    element = points >> 9
    chunk = (points >> 7) & 3
    row = jnp.where(points < elements * POINTS, chunk * elements + element, 4 * elements)
    return row, points & (LANES - 1)


def one_hot(index, count):
    steps = lax.broadcasted_iota(jnp.int32, (count, index.shape[1]), 0)
    return steps == index


def lane_hot(lane):
    steps = lax.broadcasted_iota(jnp.int32, (LANES, lane.shape[1]), 0).astype(F32).astype(BF16)
    one = jnp.ones(steps.shape, BF16)
    return jnp.where(steps == lane.astype(F32).astype(BF16), one, jnp.zeros_like(one))


def take(values, lanes):
    return jnp.take_along_axis(values, lanes, axis=1, mode="promise_in_bounds")


def gather(field, chunks):
    count = field.shape[0]
    both = jnp.concatenate(split(field), axis=0)
    out = []
    for row, lane in chunks:
        picked = jnp.dot(both, lane_hot(lane), preferred_element_type=F32)
        mine = jnp.where(one_hot(row, count), picked[:count] + picked[count:], 0.0)
        out.append(jnp.sum(mine, axis=0, keepdims=True))
    return out


def scatter(rows, chunks, values):
    total = jnp.zeros((2 * rows, LANES), F32)
    for (row, lane), value in zip(chunks, values):
        steps = lax.broadcasted_iota(jnp.int32, (rows, row.shape[1]), 0).astype(F32).astype(BF16)
        mine = steps == row.astype(F32).astype(BF16)
        parts = [jnp.where(mine, part, jnp.zeros_like(steps)) for part in split(value)]
        total = total + lax.dot_general(
            jnp.concatenate(parts, axis=0), lane_hot(lane), NT, preferred_element_type=F32
        )
    return total[:rows] + total[rows:]


def chunked(row, lane):
    return [
        (row[:, at : at + STEP], lane[:, at : at + STEP]) for at in range(0, row.shape[1], STEP)
    ]


def cut(row):
    return [row[:, at : at + STEP] for at in range(0, row.shape[1], STEP)]


def pair_chunks(pair_ref, elements):
    row, lane = locate(pair_ref[...], elements)
    return chunked(row[0:1], lane[0:1]) + chunked(row[1:2], lane[1:2])


def joined(rows):
    return [
        jnp.concatenate([rows[at : at + 1], rows[at + 1 : at + 2]], axis=1)
        for at in range(0, rows.shape[0], 2)
    ]


def far_chunks(points, elements):
    row, lane = locate(points, elements)
    return list(zip(joined(row), joined(lane)))


def halves(wide):
    return [wide[:, at : at + LANES] for at in range(0, wide.shape[1], LANES)]


def own_group(devices, peers, away=0):
    shape = (devices, LANES)
    return lax.broadcasted_iota(jnp.int32, shape, 0) // peers - lax.axis_index("grp") == away


def send_rows(sent_ref, count, at, rows, peers):
    devices = sent_ref.shape[0] // count
    above = own_group(devices, peers, 1)
    shared = jnp.concatenate([rows[:peers]] * (devices // peers), axis=0)
    for r in range(FACE_ROWS):
        down = rows[peers + r : peers + r + 1]
        up = rows[peers + FACE_ROWS + r : peers + FACE_ROWS + r + 1]
        out = jnp.where(above, up, down)
        if r == 0:
            out = jnp.where(own_group(devices, peers), shared, out)
        sent_ref[pl.ds(at + r, devices, count), :] = out


def send_same(sent_ref, count, at, row):
    devices = sent_ref.shape[0] // count
    sent_ref[pl.ds(at, devices, count), :] = jnp.broadcast_to(row, (devices, LANES))


def send_values(sent_ref, count, values, peers):
    rows = jnp.concatenate([row for pair in values for row in halves(pair)], axis=0)
    send_rows(sent_ref, count, 0, rows, peers)


def get(received_ref, count, at):
    return received_ref[pl.ds(at, received_ref.shape[0] // count, count), :]


def get_shared(rows, peers):
    mine = jnp.where(own_group(rows.shape[0], peers), rows, 0.0)
    shared = mine[:peers]
    for g in range(1, rows.shape[0] // peers):
        shared = shared + mine[g * peers : (g + 1) * peers]
    return shared


def get_row(rows, peers, away):
    here = lax.axis_index("grp") * peers + lax.axis_index("sub")
    source = lax.broadcasted_iota(jnp.int32, rows.shape, 0) - here == away * peers
    return jnp.sum(jnp.where(source, rows, 0.0), axis=0, keepdims=True)


def get_rows(received_ref, count, at, peers):
    rows = [get(received_ref, count, at + r) for r in range(FACE_ROWS)]
    faces = [get_row(part, peers, away) for away in (-1, 1) for part in rows]
    return jnp.concatenate([get_shared(rows[0], peers)] + faces, axis=0)


def swapped(values):
    count = len(values) // 2
    return values[count:] + values[:count]


def along_first(field, table_ref, base):
    elements = field.shape[0] // 4
    turned = pltpu.roll(field, 64, axis=1)
    out = []
    for to in range(4):
        total = None
        for at in range(4):
            place = base + 2 * (4 * to + at)
            rows = slice(at * elements, (at + 1) * elements)
            term = (
                table_ref[place : place + 1, :] * field[rows]
                + table_ref[place + 1 : place + 2, :] * turned[rows]
            )
            total = term if total is None else total + term
        out.append(total)
    return jnp.concatenate(out, axis=0)


def stiffness(field, metric_ref, first_ref, inner_ref):
    metric = [rows_of(metric_ref[:, POINTS * d : POINTS * (d + 1)]) for d in range(3)]
    count = field.shape[0]
    grad_first = along_first(field, first_ref, 0)
    high, low = split(field)
    both = jnp.dot(
        jnp.concatenate([high, low], axis=0), inner_ref[:LANES], preferred_element_type=F32
    )
    inner = both[:count] + both[count:]
    inner = inner + jnp.dot(high, inner_ref[LANES:], preferred_element_type=F32)
    flux_first = metric[0] * grad_first
    flux = jnp.concatenate([metric[1], metric[2]], axis=1) * inner
    high, low = split(flux)
    both = lax.dot_general(
        jnp.concatenate([high, low], axis=0), inner_ref[:LANES], NT, preferred_element_type=F32
    )
    back = both[:count] + both[count:]
    back = back + lax.dot_general(high, inner_ref[LANES:], NT, preferred_element_type=F32)
    back = back + along_first(flux_first, first_ref, 32)
    energy = flux * inner
    return back, flux_first * grad_first + energy[:, :LANES] + energy[:, LANES:]


def factors(points):
    nodes = 0.5 * (1.0 + np.cos(np.pi * np.arange(8) / 7.0))
    out = []
    for shift in (6, 3, 0):
        index = (points >> shift) & 7
        near = jnp.full(points.shape, nodes[7], F32)
        far = jnp.full(points.shape, nodes[0], F32)
        for m in range(7):
            near = jnp.where(index == m, float(nodes[m]), near)
            far = jnp.where(index == m, float(nodes[7 - m]), far)
        out.append((near, far))
    return out


def corners(points):
    first, second, third = factors(points)
    return [
        first[q >> 2 & 1] * (second[q >> 1 & 1] * third[q & 1]) for q in range(8)
    ]


def own_corners():
    return corners(lax.broadcasted_iota(jnp.int32, (1, POINTS), 1))


def flat_map(mapped):
    elements = mapped.shape[1]
    shape = (8, 8 * elements)
    lane = lax.broadcasted_iota(jnp.int32, shape, 1)
    padded = jnp.concatenate(
        [mapped.astype(F32), jnp.zeros((8, shape[1] - elements), F32)], axis=1
    )
    wide = take(padded, lane & (elements - 1))
    keep = lax.broadcasted_iota(jnp.int32, shape, 0) == lane // elements
    return jnp.sum(jnp.where(keep, wide, 0.0), axis=0, keepdims=True)


def one_vertex(flat):
    return jnp.where(one_hot(whole(flat), NC), 1.0, 0.0)


def whole(values):
    return (values + 0.5).astype(jnp.int32)


def own_element(elements, width):
    shape = (elements, width)
    return lax.broadcasted_iota(jnp.int32, shape, 0) == (
        lax.broadcasted_iota(jnp.int32, shape, 1) % elements
    )


def own_place(elements, q):
    shape = (elements, 8 * elements)
    lane = lax.broadcasted_iota(jnp.int32, shape, 1)
    return lane == lax.broadcasted_iota(jnp.int32, shape, 0) + q * elements


def coarse_part(field, vertices, inverse):
    elements = field.shape[0] // 4
    flat = jnp.zeros((elements, 8 * elements), F32)
    for q, corner in enumerate(own_corners()):
        inner = None
        for c in range(4):
            term = field[c * elements : (c + 1) * elements] * corner[:, c * LANES : (c + 1) * LANES]
            inner = term if inner is None else inner + term
        flat = jnp.where(own_place(elements, q), jnp.sum(inner, axis=1, keepdims=True), flat)
    flat = jnp.sum(flat, axis=0, keepdims=True)
    part = jnp.sum(vertices * flat, axis=1, keepdims=True)
    part = jnp.sum(inverse * part, axis=0, keepdims=True)
    return jnp.concatenate([part, jnp.zeros((1, LANES - NC), F32)], axis=1)


def get_solved(received_ref, count, peers):
    rows = get(received_ref, count, TERMS)
    return [
        jnp.sum(jnp.where(own_group(rows.shape[0], peers, away), rows, 0.0), axis=0, keepdims=True)
        for away in (0, -1, 1)
    ]


def prolonged(solved, flat, elements):
    shape = (elements, LANES)
    element = lax.broadcasted_iota(jnp.int32, shape, 0)
    at_corner = take(jnp.broadcast_to(solved, shape), jnp.broadcast_to(flat, shape))
    out = [None] * 4
    for q, corner in enumerate(own_corners()):
        value = take(at_corner, element + q * elements)
        for c in range(4):
            term = value * corner[:, c * LANES : (c + 1) * LANES]
            out[c] = term if out[c] is None else out[c] + term
    return jnp.concatenate(out, axis=0)


def prolonged_at(solved, maps, points, elements):
    at_corner = take(solved, maps)
    element = (points >> 9) & (elements - 1)
    total = jnp.zeros(points.shape, F32)
    for q, corner in enumerate(corners(points)):
        total = total + corner * take(at_corner, element + q * elements)
    return total


def total_of(array):
    return jnp.sum(jnp.sum(array, axis=0, keepdims=True), axis=1, keepdims=True)


def packed(values):
    lane = lax.broadcasted_iota(jnp.int32, (1, LANES), 1)
    out = jnp.zeros((1, LANES), F32)
    for k, value in enumerate(values):
        out = jnp.where(lane == k, value, out)
    return out


def unpacked(row, count):
    lane = lax.broadcasted_iota(jnp.int32, row.shape, 1)
    return [
        jnp.sum(jnp.where(lane == k, row, 0.0), axis=1, keepdims=True) for k in range(count)
    ]


def first_kernel(
    right_hbm, jacobi_hbm, inverse_hbm, map_hbm, slot_hbm, face_hbm,
    sent_ref, fields_ref, points_ref,
    right_ref, jacobi_ref, inverse_ref, map_ref, slot_ref, face_ref, sems,
):
    copies = []
    for k, (source, target) in enumerate(
        (
            (face_hbm, face_ref),
            (slot_hbm, slot_ref),
            (right_hbm, right_ref),
            (jacobi_hbm, jacobi_ref),
            (map_hbm, map_ref),
            (inverse_hbm, inverse_ref),
        )
    ):
        copy = pltpu.make_async_copy(source, target, sems.at[k])
        copy.start()
        copies.append(copy)
    for copy in copies:
        copy.wait()
    elements = right_ref.shape[0]
    peers = slot_ref.shape[1]
    faces = face_ref[...]
    faces = jnp.concatenate(halves(faces[0:1]) + halves(faces[1:2]), axis=0)
    points = jnp.concatenate([slot_ref[0], faces], axis=0)
    points_ref[...] = points
    resid = rows_of(right_ref[...])
    flat = flat_map(map_ref[...])
    smoothed = rows_of(jacobi_ref[...]) * resid
    fields_ref[0 : 4 * elements, :] = resid
    fields_ref[4 * elements : 8 * elements, :] = smoothed
    fields_ref[8 * elements :, :] = jnp.broadcast_to(flat, (8, LANES))
    part = coarse_part(resid, one_vertex(flat), inverse_ref[0])
    values = gather(smoothed, far_chunks(points, elements))
    send_values(sent_ref, FIRST_ROWS, values, peers)
    send_same(sent_ref, FIRST_ROWS, TERMS, part)
    send_same(sent_ref, FIRST_ROWS, TERMS + 1, flat)
    send_rows(sent_ref, FIRST_ROWS, TERMS + 2, points.astype(F32), peers)


def far_maps(received_ref, peers):
    maps = get(received_ref, FIRST_ROWS, TERMS + 1)
    sides = [
        jnp.broadcast_to(get_row(maps, peers, away), (FACE_ROWS, LANES)) for away in (-1, 1)
    ]
    return whole(jnp.concatenate([get_shared(maps, peers)] + sides, axis=0))


def apply(
    rough, smoothed, count, received_ref, flat, maps, far_points, solved, metric_ref, helmholtz_ref,
    first_ref, inner_ref, pair_ref, points_ref, dots, back_ref, local_ref, sent_ref,
):
    elements = smoothed.shape[0] // 4
    peers = points_ref.shape[0] - 2 * FACE_ROWS
    pairs = pair_chunks(pair_ref, elements)
    far = far_chunks(points_ref[...], elements)
    near = gather(rough, pairs)
    partners = pair_ref[...]
    partners = jnp.concatenate(halves(partners[1:2]) + halves(partners[0:1]), axis=0)
    counts = (peers, FACE_ROWS, FACE_ROWS, partners.shape[0])
    spread = [
        jnp.broadcast_to(part, (n, LANES)) for part, n in zip((*solved, solved[0]), counts)
    ]
    coarse = prolonged_at(
        jnp.concatenate(spread, axis=0),
        jnp.concatenate([maps, jnp.broadcast_to(flat, partners.shape)], axis=0),
        jnp.concatenate([far_points, partners], axis=0),
        elements,
    )
    split_at = points_ref.shape[0]
    incoming = get_rows(received_ref, count, 0, peers) + coarse[:split_at]
    values = [value + more for value, more in zip(swapped(near), joined(coarse[split_at:]))]
    values = values + joined(incoming)
    summed = smoothed + scatter(smoothed.shape[0], pairs + far, values)
    back, energy = stiffness(summed, metric_ref, first_ref, inner_ref)
    energy = energy + rows_of(helmholtz_ref[...]) * smoothed * smoothed
    back_ref[...] = back
    values = gather(back, pairs + far)
    near = swapped(values[: len(pairs)])
    for k, value in enumerate(near):
        local_ref[0:1, k * STEP : (k + 1) * STEP] = value
    send_values(sent_ref, ROWS, values[len(pairs) :], peers)
    send_same(sent_ref, ROWS, TERMS, packed(dots + [total_of(energy)]))


def image_of(
    field_ref, back_ref, local_ref, received_ref, helmholtz_ref, pair_ref, points_ref
):
    elements = field_ref.shape[0] // 4
    peers = points_ref.shape[0] - 2 * FACE_ROWS
    chunks = pair_chunks(pair_ref, elements) + far_chunks(points_ref[...], elements)
    values = cut(local_ref[...]) + joined(get_rows(received_ref, ROWS, 0, peers))
    summed = back_ref[...] + scatter(field_ref.shape[0], chunks, values)
    return summed + rows_of(helmholtz_ref[...]) * field_ref[...]


def start_kernel(
    received_ref, fields_ref, points_ref, pair_ref, metric_ref, helmholtz_ref,
    first_ref, inner_ref,
    smoothed_ref, maps_ref, far_points_ref, back_ref, local_ref, sent_ref,
):
    elements = helmholtz_ref.shape[0]
    peers = points_ref.shape[0] - 2 * FACE_ROWS
    solved = get_solved(received_ref, FIRST_ROWS, peers)
    resid = fields_ref[0 : 4 * elements, :]
    flat = whole(fields_ref[8 * elements : 8 * elements + 1, :])
    rough = fields_ref[4 * elements : 8 * elements, :]
    smoothed = rough + prolonged(solved[0], flat, elements)
    smoothed_ref[...] = smoothed
    maps = far_maps(received_ref, peers)
    maps_ref[...] = maps
    far_points = whole(get_rows(received_ref, FIRST_ROWS, TERMS + 2, peers))
    far_points_ref[...] = far_points
    apply(
        rough, smoothed, FIRST_ROWS, received_ref, flat, maps, far_points, solved, metric_ref,
        helmholtz_ref, first_ref, inner_ref, pair_ref, points_ref,
        [total_of(resid * smoothed)], back_ref, local_ref, sent_ref,
    )


def middle_kernel(
    received_ref, fields_ref, points_ref, pair_ref, jacobi_ref, helmholtz_ref,
    inverse_ref, smoothed_ref, back_ref, local_ref,
    image_ref, resid_ref, scalars_ref, sent_ref,
):
    elements = helmholtz_ref.shape[0]
    peers = points_ref.shape[0] - 2 * FACE_ROWS
    dots = jnp.sum(get(received_ref, ROWS, TERMS), axis=0, keepdims=True)
    scalars_ref[...] = dots
    values = unpacked(dots, 2)
    alpha = values[0] / values[1]
    image = image_of(
        smoothed_ref, back_ref, local_ref, received_ref, helmholtz_ref, pair_ref,
        points_ref,
    )
    image_ref[...] = image
    resid = fields_ref[0 : 4 * elements, :] - alpha * image
    resid_ref[...] = resid
    vertices = one_vertex(fields_ref[8 * elements : 8 * elements + 1, :])
    part = coarse_part(resid, vertices, inverse_ref[0])
    values = gather(rows_of(jacobi_ref[...]) * resid, far_chunks(points_ref[...], elements))
    send_values(sent_ref, ROWS, values, peers)
    send_same(sent_ref, ROWS, TERMS, part)


def second_kernel(
    received_ref, fields_ref, points_ref, pair_ref, resid_ref, image_ref,
    maps_ref, far_points_ref, jacobi_ref, metric_ref, helmholtz_ref, first_ref, inner_ref,
    smoothed_ref, back_ref, local_ref, sent_ref,
):
    elements = helmholtz_ref.shape[0]
    peers = points_ref.shape[0] - 2 * FACE_ROWS
    solved = get_solved(received_ref, ROWS, peers)
    resid = resid_ref[...]
    flat = whole(fields_ref[8 * elements : 8 * elements + 1, :])
    rough = rows_of(jacobi_ref[...]) * resid
    smoothed = rough + prolonged(solved[0], flat, elements)
    smoothed_ref[...] = smoothed
    apply(
        rough, smoothed, ROWS, received_ref, flat, maps_ref[...], far_points_ref[...], solved, metric_ref,
        helmholtz_ref, first_ref, inner_ref, pair_ref, points_ref,
        [total_of(resid * smoothed), total_of(image_ref[...] * smoothed)],
        back_ref, local_ref, sent_ref,
    )


def final_kernel(
    received_ref, points_ref, pair_ref, old_ref, field_ref, resid_ref, old_image_ref,
    scalars_ref, back_ref, local_ref, helmholtz_ref,
    solution_ref, residual_ref,
):
    before = unpacked(scalars_ref[...], 2)
    now = unpacked(jnp.sum(get(received_ref, ROWS, TERMS), axis=0, keepdims=True), 3)
    alpha = before[0] / before[1]
    beta = now[0] / before[0]
    curved = now[2] + beta * (2.0 * now[1] + beta * before[1])
    step = now[0] / curved
    old = old_ref[...]
    direction = field_ref[...] + beta * old
    solution_ref[...] = wide_of(alpha * old + step * direction)
    image = image_of(
        field_ref, back_ref, local_ref, received_ref, helmholtz_ref, pair_ref,
        points_ref,
    )
    image = image + beta * old_image_ref[...]
    residual_ref[...] = wide_of(resid_ref[...] - step * image)


def call(kernel, outs, *args, copied=False):
    space = pl.ANY if copied else pltpu.VMEM
    scratch = [pltpu.VMEM(arg.shape, arg.dtype) for arg in args] if copied else []
    if copied:
        args = [pltpu.with_memory_space_constraint(arg, pltpu.HBM) for arg in args]
    return pl.pallas_call(
        kernel,
        out_shape=[
            jax.ShapeDtypeStruct(*(out if isinstance(out[0], tuple) else (out, F32))) for out in outs
        ],
        in_specs=[pl.BlockSpec(memory_space=space)] * len(args),
        out_specs=[pl.BlockSpec(memory_space=pltpu.VMEM)] * len(outs),
        scratch_shapes=scratch + ([pltpu.SemaphoreType.DMA((len(args),))] if copied else []),
        compiler_params=pltpu.CompilerParams(vmem_limit_bytes=24 * 1024 * 1024),
    )(*args)


def body(
    right_side,
    metric,
    helmholtz,
    jacobi,
    pair_list,
    shared_slots,
    face_points,
    coarse_map,
    coarse_inverse,
):
    peers = lax.axis_size("sub")
    groups = lax.axis_size("grp")
    t = {name: jnp.asarray(value) for name, value in tables().items()}
    elements = right_side.shape[0]
    field = (4 * elements, LANES)
    local = (1, pair_list.shape[0] * pair_list.shape[1])
    points_shape = (peers + 2 * FACE_ROWS, LANES)
    sent_shape = (groups * peers * ROWS, LANES)

    def exchange(sent):
        rows = sent.reshape(groups * peers, 1, -1)
        return lax.all_to_all(rows, ("grp", "sub"), 0, 0, tiled=True).reshape(sent.shape)

    sent, fields, points = call(
        first_kernel,
        [
            (groups * peers * FIRST_ROWS, LANES),
            (8 * elements + 8, LANES),
            (points_shape, jnp.int32),
        ],
        right_side, jacobi, coarse_inverse, coarse_map, shared_slots, face_points, copied=True,
    )
    smoothed, maps, far_points, back, near, sent = call(
        start_kernel,
        [field, (points_shape, jnp.int32), (points_shape, jnp.int32), field, local, sent_shape],
        exchange(sent), fields, points, pair_list, metric, helmholtz,
        t["first"], t["inner"],
    )
    image, resid, scalars, sent = call(
        middle_kernel, [field, field, (1, LANES), sent_shape],
        exchange(sent), fields, points, pair_list, jacobi, helmholtz, coarse_inverse,
        smoothed, back, near,
    )
    second, back, near, sent = call(
        second_kernel, [field, field, local, sent_shape],
        exchange(sent), fields, points, pair_list, resid, image, maps, far_points, jacobi,
        metric, helmholtz, t["first"], t["inner"],
    )
    return tuple(
        call(
            final_kernel, [right_side.shape, right_side.shape],
            exchange(sent), points, pair_list, smoothed, second, resid, image, scalars,
            back, near, helmholtz,
        )
    )


def solution(mesh):
    in_specs = (
        P(("grp", "sub"), None),
        P(("grp", "sub"), None),
        P(("grp", "sub"), None),
        P(("grp", "sub"), None),
        P(None, ("grp", "sub")),
        P(("grp", "sub"), None, None),
        P(None, ("grp", "sub")),
        P(None, ("grp", "sub")),
        P("grp", None, None),
    )
    out_specs = (P(("grp", "sub"), None), P(("grp", "sub"), None))
    return jax.shard_map(body, mesh=mesh, in_specs=in_specs, out_specs=out_specs, check_vma=False)
```

```python
import jax
import jax.numpy as jnp
import ml_dtypes
import numpy as np
from jax import lax
from jax.experimental import pallas as pl
from jax.experimental.pallas import tpu as pltpu
from jax.sharding import PartitionSpec as P

NC = 64
POINTS = 512
LANES = 128
STEP = 256
FACE_ROWS = 4
ROWS = 5
FIRST_ROWS = 10
TERMS = FACE_ROWS
F32 = jnp.float32
BF16 = jnp.bfloat16
NT = (((1,), (1,)), ((), ()))


def split_constant(array):
    high = array.astype(ml_dtypes.bfloat16)
    low = (array - high.astype(np.float64)).astype(ml_dtypes.bfloat16)
    return high, low


def tables():
    order_index = np.arange(8)
    colloc = np.cos(np.pi * order_index / 7.0)
    end_weights = (
        np.where((order_index == 0) | (order_index == 7), 2.0, 1.0) * (-1.0) ** order_index
    )
    spacing = colloc[:, None] - colloc[None, :] + np.eye(8)
    raw_matrix = np.outer(end_weights, 1.0 / end_weights) / spacing
    off_part = raw_matrix * (1.0 - np.eye(8))
    derivative = 0.25 * (off_part - np.eye(8) * off_part.sum(axis=1)[:, None])
    along_inner = np.concatenate(
        [np.kron(np.eye(2), np.kron(derivative, np.eye(8))).T, np.kron(np.eye(16), derivative).T],
        axis=1,
    )
    high, low = split_constant(along_inner)
    inner = np.concatenate([high, low], axis=0)

    half = np.arange(LANES) // 64

    def first_rows(matrix):
        rows = []
        for to in range(4):
            for at in range(4):
                rows.append(matrix[2 * to + half, 2 * at + half])
                rows.append(matrix[2 * to + half, 2 * at + 1 - half])
        return np.stack(rows).astype(np.float32)

    return {
        "inner": inner,
        "first": np.concatenate([first_rows(derivative), first_rows(derivative.T)], axis=0),
    }


def split(value):
    high = value.astype(BF16)
    return high, (value - high.astype(F32)).astype(BF16)


def rows_of(wide):
    return jnp.concatenate([wide[:, LANES * c : LANES * (c + 1)] for c in range(4)], axis=0)


def wide_of(rows):
    elements = rows.shape[0] // 4
    return jnp.concatenate([rows[c * elements : (c + 1) * elements] for c in range(4)], axis=1)


def locate(points, elements):
    element = points >> 9
    chunk = (points >> 7) & 3
    row = jnp.where(points < elements * POINTS, chunk * elements + element, 4 * elements)
    return row, points & (LANES - 1)


def one_hot(index, count):
    steps = lax.broadcasted_iota(jnp.int32, (count, index.shape[1]), 0)
    return steps == index


def lane_hot(lane):
    steps = lax.broadcasted_iota(jnp.int32, (LANES, lane.shape[1]), 0).astype(F32).astype(BF16)
    one = jnp.ones(steps.shape, BF16)
    return jnp.where(steps == lane.astype(F32).astype(BF16), one, jnp.zeros_like(one))


def take(values, lanes):
    return jnp.take_along_axis(values, lanes, axis=1, mode="promise_in_bounds")


def gather(field, chunks):
    count = field.shape[0]
    both = jnp.concatenate(split(field), axis=0)
    out = []
    for row, lane in chunks:
        picked = jnp.dot(both, lane_hot(lane), preferred_element_type=F32)
        mine = jnp.where(one_hot(row, count), picked[:count] + picked[count:], 0.0)
        out.append(jnp.sum(mine, axis=0, keepdims=True))
    return out


def scatter(rows, chunks, values):
    total = jnp.zeros((2 * rows, LANES), F32)
    for (row, lane), value in zip(chunks, values):
        steps = lax.broadcasted_iota(jnp.int32, (rows, row.shape[1]), 0).astype(F32).astype(BF16)
        mine = steps == row.astype(F32).astype(BF16)
        parts = [jnp.where(mine, part, jnp.zeros_like(steps)) for part in split(value)]
        total = total + lax.dot_general(
            jnp.concatenate(parts, axis=0), lane_hot(lane), NT, preferred_element_type=F32
        )
    return total[:rows] + total[rows:]


def chunked(row, lane):
    return [
        (row[:, at : at + STEP], lane[:, at : at + STEP]) for at in range(0, row.shape[1], STEP)
    ]


def cut(row):
    return [row[:, at : at + STEP] for at in range(0, row.shape[1], STEP)]


def pair_chunks(pair_ref, elements):
    row, lane = locate(pair_ref[...], elements)
    return chunked(row[0:1], lane[0:1]) + chunked(row[1:2], lane[1:2])


def joined(rows):
    return [
        jnp.concatenate([rows[at : at + 1], rows[at + 1 : at + 2]], axis=1)
        for at in range(0, rows.shape[0], 2)
    ]


def far_chunks(points, elements):
    row, lane = locate(points, elements)
    return list(zip(joined(row), joined(lane)))


def halves(wide):
    return [wide[:, at : at + LANES] for at in range(0, wide.shape[1], LANES)]


def owner(devices, peers):
    place = lax.broadcasted_iota(jnp.int32, (devices, LANES), 0)
    return lax.rem(place + middle_of(devices // peers) * peers, devices)


def middle_of(groups):
    return groups // 2


def own_group(devices, peers, away=0):
    return owner(devices, peers) // peers - lax.axis_index("grp") == away


def send_rows(sent_ref, count, at, rows, peers):
    devices = sent_ref.shape[0] // count
    above = own_group(devices, peers, 1)
    shared = jnp.concatenate([rows[:peers]] * (devices // peers), axis=0)
    for r in range(FACE_ROWS):
        down = rows[peers + r : peers + r + 1]
        up = rows[peers + FACE_ROWS + r : peers + FACE_ROWS + r + 1]
        out = jnp.where(above, up, down)
        if r == 0:
            out = jnp.where(own_group(devices, peers), shared, out)
        sent_ref[pl.ds(at + r, devices, count), :] = out


def send_same(sent_ref, count, at, row):
    devices = sent_ref.shape[0] // count
    sent_ref[pl.ds(at, devices, count), :] = jnp.broadcast_to(row, (devices, LANES))


def send_values(sent_ref, count, values, peers):
    rows = jnp.concatenate([row for pair in values for row in halves(pair)], axis=0)
    send_rows(sent_ref, count, 0, rows, peers)


def get(received_ref, count, at):
    return received_ref[pl.ds(at, received_ref.shape[0] // count, count), :]


def get_shared(rows, peers):
    mine = jnp.where(own_group(rows.shape[0], peers), rows, 0.0)
    shared = mine[:peers]
    for g in range(1, rows.shape[0] // peers):
        shared = shared + mine[g * peers : (g + 1) * peers]
    return shared


def get_row(rows, peers, away):
    here = lax.axis_index("grp") * peers + lax.axis_index("sub")
    source = owner(rows.shape[0], peers) - here == away * peers
    return jnp.sum(jnp.where(source, rows, 0.0), axis=0, keepdims=True)


def get_rows(received_ref, count, at, peers):
    rows = [get(received_ref, count, at + r) for r in range(FACE_ROWS)]
    faces = [get_row(part, peers, away) for away in (-1, 1) for part in rows]
    return jnp.concatenate([get_shared(rows[0], peers)] + faces, axis=0)


def swapped(values):
    count = len(values) // 2
    return values[count:] + values[:count]


def along_first(field, table_ref, base):
    elements = field.shape[0] // 4
    turned = pltpu.roll(field, 64, axis=1)
    out = []
    for to in range(4):
        total = None
        for at in range(4):
            place = base + 2 * (4 * to + at)
            rows = slice(at * elements, (at + 1) * elements)
            term = (
                table_ref[place : place + 1, :] * field[rows]
                + table_ref[place + 1 : place + 2, :] * turned[rows]
            )
            total = term if total is None else total + term
        out.append(total)
    return jnp.concatenate(out, axis=0)


def stiffness(field, metric_ref, first_ref, inner_ref):
    metric = [rows_of(metric_ref[:, POINTS * d : POINTS * (d + 1)]) for d in range(3)]
    count = field.shape[0]
    grad_first = along_first(field, first_ref, 0)
    high, low = split(field)
    both = jnp.dot(
        jnp.concatenate([high, low], axis=0), inner_ref[:LANES], preferred_element_type=F32
    )
    inner = both[:count] + both[count:]
    inner = inner + jnp.dot(high, inner_ref[LANES:], preferred_element_type=F32)
    flux_first = metric[0] * grad_first
    flux = jnp.concatenate([metric[1], metric[2]], axis=1) * inner
    high, low = split(flux)
    both = lax.dot_general(
        jnp.concatenate([high, low], axis=0), inner_ref[:LANES], NT, preferred_element_type=F32
    )
    back = both[:count] + both[count:]
    back = back + lax.dot_general(high, inner_ref[LANES:], NT, preferred_element_type=F32)
    back = back + along_first(flux_first, first_ref, 32)
    energy = flux * inner
    return back, flux_first * grad_first + energy[:, :LANES] + energy[:, LANES:]


def factors(points):
    nodes = 0.5 * (1.0 + np.cos(np.pi * np.arange(8) / 7.0))
    out = []
    for shift in (6, 3, 0):
        index = (points >> shift) & 7
        near = jnp.full(points.shape, nodes[7], F32)
        far = jnp.full(points.shape, nodes[0], F32)
        for m in range(7):
            near = jnp.where(index == m, float(nodes[m]), near)
            far = jnp.where(index == m, float(nodes[7 - m]), far)
        out.append((near, far))
    return out


def corners(points):
    first, second, third = factors(points)
    return [
        first[q >> 2 & 1] * (second[q >> 1 & 1] * third[q & 1]) for q in range(8)
    ]


def own_corners():
    return corners(lax.broadcasted_iota(jnp.int32, (1, POINTS), 1))


def flat_map(mapped):
    elements = mapped.shape[1]
    shape = (8, 8 * elements)
    lane = lax.broadcasted_iota(jnp.int32, shape, 1)
    padded = jnp.concatenate(
        [mapped.astype(F32), jnp.zeros((8, shape[1] - elements), F32)], axis=1
    )
    wide = take(padded, lane & (elements - 1))
    keep = lax.broadcasted_iota(jnp.int32, shape, 0) == lane // elements
    return jnp.sum(jnp.where(keep, wide, 0.0), axis=0, keepdims=True)


def one_vertex(flat):
    return jnp.where(one_hot(whole(flat), NC), 1.0, 0.0)


def whole(values):
    return (values + 0.5).astype(jnp.int32)


def own_element(elements, width):
    shape = (elements, width)
    return lax.broadcasted_iota(jnp.int32, shape, 0) == (
        lax.broadcasted_iota(jnp.int32, shape, 1) % elements
    )


def own_place(elements, q):
    shape = (elements, 8 * elements)
    lane = lax.broadcasted_iota(jnp.int32, shape, 1)
    return lane == lax.broadcasted_iota(jnp.int32, shape, 0) + q * elements


def coarse_part(field, vertices, inverse):
    elements = field.shape[0] // 4
    flat = jnp.zeros((elements, 8 * elements), F32)
    for q, corner in enumerate(own_corners()):
        inner = None
        for c in range(4):
            term = field[c * elements : (c + 1) * elements] * corner[:, c * LANES : (c + 1) * LANES]
            inner = term if inner is None else inner + term
        flat = jnp.where(own_place(elements, q), jnp.sum(inner, axis=1, keepdims=True), flat)
    flat = jnp.sum(flat, axis=0, keepdims=True)
    part = jnp.sum(vertices * flat, axis=1, keepdims=True)
    part = jnp.sum(inverse * part, axis=0, keepdims=True)
    return jnp.concatenate([part, jnp.zeros((1, LANES - NC), F32)], axis=1)


def get_solved(received_ref, count, peers):
    rows = get(received_ref, count, TERMS)
    return [
        jnp.sum(jnp.where(own_group(rows.shape[0], peers, away), rows, 0.0), axis=0, keepdims=True)
        for away in (0, -1, 1)
    ]


def prolonged(solved, flat, elements):
    shape = (elements, LANES)
    element = lax.broadcasted_iota(jnp.int32, shape, 0)
    at_corner = take(jnp.broadcast_to(solved, shape), jnp.broadcast_to(flat, shape))
    out = [None] * 4
    for q, corner in enumerate(own_corners()):
        value = take(at_corner, element + q * elements)
        for c in range(4):
            term = value * corner[:, c * LANES : (c + 1) * LANES]
            out[c] = term if out[c] is None else out[c] + term
    return jnp.concatenate(out, axis=0)


def prolonged_at(solved, maps, points, elements):
    at_corner = take(solved, maps)
    element = (points >> 9) & (elements - 1)
    total = jnp.zeros(points.shape, F32)
    for q, corner in enumerate(corners(points)):
        total = total + corner * take(at_corner, element + q * elements)
    return total


def total_of(array):
    return jnp.sum(jnp.sum(array, axis=0, keepdims=True), axis=1, keepdims=True)


def packed(values):
    lane = lax.broadcasted_iota(jnp.int32, (1, LANES), 1)
    out = jnp.zeros((1, LANES), F32)
    for k, value in enumerate(values):
        out = jnp.where(lane == k, value, out)
    return out


def unpacked(row, count):
    lane = lax.broadcasted_iota(jnp.int32, row.shape, 1)
    return [
        jnp.sum(jnp.where(lane == k, row, 0.0), axis=1, keepdims=True) for k in range(count)
    ]


def first_kernel(
    right_hbm, jacobi_hbm, inverse_hbm, map_hbm, slot_hbm, face_hbm,
    sent_ref, fields_ref, points_ref,
    right_ref, jacobi_ref, inverse_ref, map_ref, slot_ref, face_ref, sems,
):
    copies = []
    for k, (source, target) in enumerate(
        (
            (face_hbm, face_ref),
            (slot_hbm, slot_ref),
            (right_hbm, right_ref),
            (jacobi_hbm, jacobi_ref),
            (map_hbm, map_ref),
            (inverse_hbm, inverse_ref),
        )
    ):
        copy = pltpu.make_async_copy(source, target, sems.at[k])
        copy.start()
        copies.append(copy)
    for copy in copies:
        copy.wait()
    elements = right_ref.shape[0]
    peers = slot_ref.shape[1]
    faces = face_ref[...]
    faces = jnp.concatenate(halves(faces[0:1]) + halves(faces[1:2]), axis=0)
    points = jnp.concatenate([slot_ref[0], faces], axis=0)
    points_ref[...] = points
    resid = rows_of(right_ref[...])
    flat = flat_map(map_ref[...])
    smoothed = rows_of(jacobi_ref[...]) * resid
    fields_ref[0 : 4 * elements, :] = resid
    fields_ref[4 * elements : 8 * elements, :] = smoothed
    fields_ref[8 * elements :, :] = jnp.broadcast_to(flat, (8, LANES))
    part = coarse_part(resid, one_vertex(flat), inverse_ref[0])
    values = gather(smoothed, far_chunks(points, elements))
    send_values(sent_ref, FIRST_ROWS, values, peers)
    send_same(sent_ref, FIRST_ROWS, TERMS, part)
    send_same(sent_ref, FIRST_ROWS, TERMS + 1, flat)
    send_rows(sent_ref, FIRST_ROWS, TERMS + 2, points.astype(F32), peers)


def far_maps(received_ref, peers):
    maps = get(received_ref, FIRST_ROWS, TERMS + 1)
    sides = [
        jnp.broadcast_to(get_row(maps, peers, away), (FACE_ROWS, LANES)) for away in (-1, 1)
    ]
    return whole(jnp.concatenate([get_shared(maps, peers)] + sides, axis=0))


def apply(
    rough, smoothed, count, received_ref, flat, maps, far_points, solved, metric_ref, helmholtz_ref,
    first_ref, inner_ref, pair_ref, points_ref, dots, back_ref, local_ref, sent_ref,
):
    elements = smoothed.shape[0] // 4
    peers = points_ref.shape[0] - 2 * FACE_ROWS
    pairs = pair_chunks(pair_ref, elements)
    far = far_chunks(points_ref[...], elements)
    near = gather(rough, pairs)
    partners = pair_ref[...]
    partners = jnp.concatenate(halves(partners[1:2]) + halves(partners[0:1]), axis=0)
    counts = (peers, FACE_ROWS, FACE_ROWS, partners.shape[0])
    spread = [
        jnp.broadcast_to(part, (n, LANES)) for part, n in zip((*solved, solved[0]), counts)
    ]
    coarse = prolonged_at(
        jnp.concatenate(spread, axis=0),
        jnp.concatenate([maps, jnp.broadcast_to(flat, partners.shape)], axis=0),
        jnp.concatenate([far_points, partners], axis=0),
        elements,
    )
    split_at = points_ref.shape[0]
    incoming = get_rows(received_ref, count, 0, peers) + coarse[:split_at]
    values = [value + more for value, more in zip(swapped(near), joined(coarse[split_at:]))]
    values = values + joined(incoming)
    summed = smoothed + scatter(smoothed.shape[0], pairs + far, values)
    back, energy = stiffness(summed, metric_ref, first_ref, inner_ref)
    energy = energy + rows_of(helmholtz_ref[...]) * smoothed * smoothed
    back_ref[...] = back
    values = gather(back, pairs + far)
    near = swapped(values[: len(pairs)])
    for k, value in enumerate(near):
        local_ref[0:1, k * STEP : (k + 1) * STEP] = value
    send_values(sent_ref, ROWS, values[len(pairs) :], peers)
    send_same(sent_ref, ROWS, TERMS, packed(dots + [total_of(energy)]))


def image_of(
    field_ref, back_ref, local_ref, received_ref, helmholtz_ref, pair_ref, points_ref
):
    elements = field_ref.shape[0] // 4
    peers = points_ref.shape[0] - 2 * FACE_ROWS
    chunks = pair_chunks(pair_ref, elements) + far_chunks(points_ref[...], elements)
    values = cut(local_ref[...]) + joined(get_rows(received_ref, ROWS, 0, peers))
    summed = back_ref[...] + scatter(field_ref.shape[0], chunks, values)
    return summed + rows_of(helmholtz_ref[...]) * field_ref[...]


def start_kernel(
    received_ref, fields_ref, points_ref, pair_ref, metric_ref, helmholtz_ref,
    first_ref, inner_ref,
    smoothed_ref, maps_ref, far_points_ref, back_ref, local_ref, sent_ref,
):
    elements = helmholtz_ref.shape[0]
    peers = points_ref.shape[0] - 2 * FACE_ROWS
    solved = get_solved(received_ref, FIRST_ROWS, peers)
    resid = fields_ref[0 : 4 * elements, :]
    flat = whole(fields_ref[8 * elements : 8 * elements + 1, :])
    rough = fields_ref[4 * elements : 8 * elements, :]
    smoothed = rough + prolonged(solved[0], flat, elements)
    smoothed_ref[...] = smoothed
    maps = far_maps(received_ref, peers)
    maps_ref[...] = maps
    far_points = whole(get_rows(received_ref, FIRST_ROWS, TERMS + 2, peers))
    far_points_ref[...] = far_points
    apply(
        rough, smoothed, FIRST_ROWS, received_ref, flat, maps, far_points, solved, metric_ref,
        helmholtz_ref, first_ref, inner_ref, pair_ref, points_ref,
        [total_of(resid * smoothed)], back_ref, local_ref, sent_ref,
    )


def middle_kernel(
    received_ref, fields_ref, points_ref, pair_ref, jacobi_ref, helmholtz_ref,
    inverse_ref, smoothed_ref, back_ref, local_ref,
    image_ref, resid_ref, scalars_ref, sent_ref,
):
    elements = helmholtz_ref.shape[0]
    peers = points_ref.shape[0] - 2 * FACE_ROWS
    dots = jnp.sum(get(received_ref, ROWS, TERMS), axis=0, keepdims=True)
    scalars_ref[...] = dots
    values = unpacked(dots, 2)
    alpha = values[0] / values[1]
    image = image_of(
        smoothed_ref, back_ref, local_ref, received_ref, helmholtz_ref, pair_ref,
        points_ref,
    )
    image_ref[...] = image
    resid = fields_ref[0 : 4 * elements, :] - alpha * image
    resid_ref[...] = resid
    vertices = one_vertex(fields_ref[8 * elements : 8 * elements + 1, :])
    part = coarse_part(resid, vertices, inverse_ref[0])
    values = gather(rows_of(jacobi_ref[...]) * resid, far_chunks(points_ref[...], elements))
    send_values(sent_ref, ROWS, values, peers)
    send_same(sent_ref, ROWS, TERMS, part)


def second_kernel(
    received_ref, fields_ref, points_ref, pair_ref, resid_ref, image_ref,
    maps_ref, far_points_ref, jacobi_ref, metric_ref, helmholtz_ref, first_ref, inner_ref,
    smoothed_ref, back_ref, local_ref, sent_ref,
):
    elements = helmholtz_ref.shape[0]
    peers = points_ref.shape[0] - 2 * FACE_ROWS
    solved = get_solved(received_ref, ROWS, peers)
    resid = resid_ref[...]
    flat = whole(fields_ref[8 * elements : 8 * elements + 1, :])
    rough = rows_of(jacobi_ref[...]) * resid
    smoothed = rough + prolonged(solved[0], flat, elements)
    smoothed_ref[...] = smoothed
    apply(
        rough, smoothed, ROWS, received_ref, flat, maps_ref[...], far_points_ref[...], solved, metric_ref,
        helmholtz_ref, first_ref, inner_ref, pair_ref, points_ref,
        [total_of(resid * smoothed), total_of(image_ref[...] * smoothed)],
        back_ref, local_ref, sent_ref,
    )


def final_kernel(
    received_ref, points_ref, pair_ref, old_ref, field_ref, resid_ref, old_image_ref,
    scalars_ref, back_ref, local_ref, helmholtz_ref,
    solution_ref, residual_ref,
):
    before = unpacked(scalars_ref[...], 2)
    now = unpacked(jnp.sum(get(received_ref, ROWS, TERMS), axis=0, keepdims=True), 3)
    alpha = before[0] / before[1]
    beta = now[0] / before[0]
    curved = now[2] + beta * (2.0 * now[1] + beta * before[1])
    step = now[0] / curved
    old = old_ref[...]
    direction = field_ref[...] + beta * old
    solution_ref[...] = wide_of(alpha * old + step * direction)
    image = image_of(
        field_ref, back_ref, local_ref, received_ref, helmholtz_ref, pair_ref,
        points_ref,
    )
    image = image + beta * old_image_ref[...]
    residual_ref[...] = wide_of(resid_ref[...] - step * image)


def call(kernel, outs, *args, copied=False):
    space = pl.ANY if copied else pltpu.VMEM
    scratch = [pltpu.VMEM(arg.shape, arg.dtype) for arg in args] if copied else []
    if copied:
        args = [pltpu.with_memory_space_constraint(arg, pltpu.HBM) for arg in args]
    return pl.pallas_call(
        kernel,
        out_shape=[
            jax.ShapeDtypeStruct(*(out if isinstance(out[0], tuple) else (out, F32))) for out in outs
        ],
        in_specs=[pl.BlockSpec(memory_space=space)] * len(args),
        out_specs=[pl.BlockSpec(memory_space=pltpu.VMEM)] * len(outs),
        scratch_shapes=scratch + ([pltpu.SemaphoreType.DMA((len(args),))] if copied else []),
        compiler_params=pltpu.CompilerParams(vmem_limit_bytes=24 * 1024 * 1024),
    )(*args)


def body(
    right_side,
    metric,
    helmholtz,
    jacobi,
    pair_list,
    shared_slots,
    face_points,
    coarse_map,
    coarse_inverse,
):
    peers = lax.axis_size("sub")
    groups = lax.axis_size("grp")
    t = {name: jnp.asarray(value) for name, value in tables().items()}
    elements = right_side.shape[0]
    field = (4 * elements, LANES)
    local = (1, pair_list.shape[0] * pair_list.shape[1])
    points_shape = (peers + 2 * FACE_ROWS, LANES)
    sent_shape = (groups * peers * ROWS, LANES)

    devices = groups * peers
    order = [(d + middle_of(groups) * peers) % devices for d in range(devices)]

    def exchange(sent):
        rows = sent.reshape(groups * peers, 1, -1)
        received = lax.all_to_all(
            rows, ("grp", "sub"), 0, 0, axis_index_groups=[order], tiled=True
        )
        return received.reshape(sent.shape)

    sent, fields, points = call(
        first_kernel,
        [
            (groups * peers * FIRST_ROWS, LANES),
            (8 * elements + 8, LANES),
            (points_shape, jnp.int32),
        ],
        right_side, jacobi, coarse_inverse, coarse_map, shared_slots, face_points, copied=True,
    )
    smoothed, maps, far_points, back, near, sent = call(
        start_kernel,
        [field, (points_shape, jnp.int32), (points_shape, jnp.int32), field, local, sent_shape],
        exchange(sent), fields, points, pair_list, metric, helmholtz,
        t["first"], t["inner"],
    )
    image, resid, scalars, sent = call(
        middle_kernel, [field, field, (1, LANES), sent_shape],
        exchange(sent), fields, points, pair_list, jacobi, helmholtz, coarse_inverse,
        smoothed, back, near,
    )
    second, back, near, sent = call(
        second_kernel, [field, field, local, sent_shape],
        exchange(sent), fields, points, pair_list, resid, image, maps, far_points, jacobi,
        metric, helmholtz, t["first"], t["inner"],
    )
    return tuple(
        call(
            final_kernel, [right_side.shape, right_side.shape],
            exchange(sent), points, pair_list, smoothed, second, resid, image, scalars,
            back, near, helmholtz,
        )
    )


def solution(mesh):
    in_specs = (
        P(("grp", "sub"), None),
        P(("grp", "sub"), None),
        P(("grp", "sub"), None),
        P(("grp", "sub"), None),
        P(None, ("grp", "sub")),
        P(("grp", "sub"), None, None),
        P(None, ("grp", "sub")),
        P(None, ("grp", "sub")),
        P("grp", None, None),
    )
    out_specs = (P(("grp", "sub"), None), P(("grp", "sub"), None))
    return jax.shard_map(body, mesh=mesh, in_specs=in_specs, out_specs=out_specs, check_vma=False)
```

```python
import jax
import jax.numpy as jnp
import ml_dtypes
import numpy as np
from jax import lax
from jax.experimental import pallas as pl
from jax.experimental.pallas import tpu as pltpu
from jax.sharding import PartitionSpec as P

NC = 64
POINTS = 512
LANES = 128
STEP = 256
FACE_ROWS = 4
ROWS = 5
FIRST_ROWS = 10
TERMS = FACE_ROWS
F32 = jnp.float32
BF16 = jnp.bfloat16
NT = (((1,), (1,)), ((), ()))


def split_constant(array):
    high = array.astype(ml_dtypes.bfloat16)
    low = (array - high.astype(np.float64)).astype(ml_dtypes.bfloat16)
    return high, low


def tables():
    order_index = np.arange(8)
    colloc = np.cos(np.pi * order_index / 7.0)
    end_weights = (
        np.where((order_index == 0) | (order_index == 7), 2.0, 1.0) * (-1.0) ** order_index
    )
    spacing = colloc[:, None] - colloc[None, :] + np.eye(8)
    raw_matrix = np.outer(end_weights, 1.0 / end_weights) / spacing
    off_part = raw_matrix * (1.0 - np.eye(8))
    derivative = 0.25 * (off_part - np.eye(8) * off_part.sum(axis=1)[:, None])
    along_inner = np.concatenate(
        [np.kron(np.eye(2), np.kron(derivative, np.eye(8))).T, np.kron(np.eye(16), derivative).T],
        axis=1,
    )
    high, low = split_constant(along_inner)
    inner = np.concatenate([high, low], axis=0)

    half = np.arange(LANES) // 64

    def first_rows(matrix):
        rows = []
        for to in range(4):
            for at in range(4):
                rows.append(matrix[2 * to + half, 2 * at + half])
                rows.append(matrix[2 * to + half, 2 * at + 1 - half])
        return np.stack(rows).astype(np.float32)

    return {
        "inner": inner,
        "first": np.concatenate([first_rows(derivative), first_rows(derivative.T)], axis=0),
    }


def split(value):
    high = value.astype(BF16)
    return high, (value - high.astype(F32)).astype(BF16)


def rows_of(wide):
    return jnp.concatenate([wide[:, LANES * c : LANES * (c + 1)] for c in range(4)], axis=0)


def wide_of(rows):
    elements = rows.shape[0] // 4
    return jnp.concatenate([rows[c * elements : (c + 1) * elements] for c in range(4)], axis=1)


def locate(points, elements):
    element = points >> 9
    chunk = (points >> 7) & 3
    row = jnp.where(points < elements * POINTS, chunk * elements + element, 4 * elements)
    return row, points & (LANES - 1)


def one_hot(index, count):
    steps = lax.broadcasted_iota(jnp.int32, (count, index.shape[1]), 0)
    return steps == index


def lane_hot(lane):
    steps = lax.broadcasted_iota(jnp.int32, (LANES, lane.shape[1]), 0).astype(F32).astype(BF16)
    one = jnp.ones(steps.shape, BF16)
    return jnp.where(steps == lane.astype(F32).astype(BF16), one, jnp.zeros_like(one))


def take(values, lanes):
    return jnp.take_along_axis(values, lanes, axis=1, mode="promise_in_bounds")


def gather(field, chunks):
    count = field.shape[0]
    both = jnp.concatenate(split(field), axis=0)
    out = []
    for row, lane in chunks:
        picked = jnp.dot(both, lane_hot(lane), preferred_element_type=F32)
        mine = jnp.where(one_hot(row, count), picked[:count] + picked[count:], 0.0)
        out.append(jnp.sum(mine, axis=0, keepdims=True))
    return out


def scatter(rows, chunks, values):
    total = jnp.zeros((2 * rows, LANES), F32)
    for (row, lane), value in zip(chunks, values):
        steps = lax.broadcasted_iota(jnp.int32, (rows, row.shape[1]), 0).astype(F32).astype(BF16)
        mine = steps == row.astype(F32).astype(BF16)
        parts = [jnp.where(mine, part, jnp.zeros_like(steps)) for part in split(value)]
        total = total + lax.dot_general(
            jnp.concatenate(parts, axis=0), lane_hot(lane), NT, preferred_element_type=F32
        )
    return total[:rows] + total[rows:]


def chunked(row, lane):
    return [
        (row[:, at : at + STEP], lane[:, at : at + STEP]) for at in range(0, row.shape[1], STEP)
    ]


def pair_chunks(pair_ref, elements):
    row, lane = locate(pair_ref[...], elements)
    return chunked(row[0:1], lane[0:1]) + chunked(row[1:2], lane[1:2])


def joined(rows):
    return [
        jnp.concatenate([rows[at : at + 1], rows[at + 1 : at + 2]], axis=1)
        for at in range(0, rows.shape[0], 2)
    ]


def far_chunks(points, elements):
    row, lane = locate(points, elements)
    return list(zip(joined(row), joined(lane)))


def halves(wide):
    return [wide[:, at : at + LANES] for at in range(0, wide.shape[1], LANES)]


def own_group(devices, peers, away=0):
    shape = (devices, LANES)
    return lax.broadcasted_iota(jnp.int32, shape, 0) // peers - lax.axis_index("grp") == away


def send_rows(sent_ref, count, at, rows, peers):
    devices = sent_ref.shape[0] // count
    above = own_group(devices, peers, 1)
    shared = jnp.concatenate([rows[:peers]] * (devices // peers), axis=0)
    for r in range(FACE_ROWS):
        down = rows[peers + r : peers + r + 1]
        up = rows[peers + FACE_ROWS + r : peers + FACE_ROWS + r + 1]
        out = jnp.where(above, up, down)
        if r == 0:
            out = jnp.where(own_group(devices, peers), shared, out)
        sent_ref[pl.ds(at + r, devices, count), :] = out


def send_same(sent_ref, count, at, row):
    devices = sent_ref.shape[0] // count
    sent_ref[pl.ds(at, devices, count), :] = jnp.broadcast_to(row, (devices, LANES))


def send_values(sent_ref, count, values, peers):
    rows = jnp.concatenate([row for pair in values for row in halves(pair)], axis=0)
    send_rows(sent_ref, count, 0, rows, peers)


def get(received_ref, count, at):
    return received_ref[pl.ds(at, received_ref.shape[0] // count, count), :]


def get_shared(rows, peers):
    mine = jnp.where(own_group(rows.shape[0], peers), rows, 0.0)
    shared = mine[:peers]
    for g in range(1, rows.shape[0] // peers):
        shared = shared + mine[g * peers : (g + 1) * peers]
    return shared


def get_row(rows, peers, away):
    here = lax.axis_index("grp") * peers + lax.axis_index("sub")
    source = lax.broadcasted_iota(jnp.int32, rows.shape, 0) - here == away * peers
    return jnp.sum(jnp.where(source, rows, 0.0), axis=0, keepdims=True)


def get_rows(received_ref, count, at, peers):
    rows = [get(received_ref, count, at + r) for r in range(FACE_ROWS)]
    faces = [get_row(part, peers, away) for away in (-1, 1) for part in rows]
    return jnp.concatenate([get_shared(rows[0], peers)] + faces, axis=0)


def swapped(values):
    count = len(values) // 2
    return values[count:] + values[:count]


def along_first(field, table_ref, base):
    elements = field.shape[0] // 4
    turned = pltpu.roll(field, 64, axis=1)
    out = []
    for to in range(4):
        total = None
        for at in range(4):
            place = base + 2 * (4 * to + at)
            rows = slice(at * elements, (at + 1) * elements)
            term = (
                table_ref[place : place + 1, :] * field[rows]
                + table_ref[place + 1 : place + 2, :] * turned[rows]
            )
            total = term if total is None else total + term
        out.append(total)
    return jnp.concatenate(out, axis=0)


def stiffness(field, metric_ref, first_ref, inner_ref):
    metric = [rows_of(metric_ref[:, POINTS * d : POINTS * (d + 1)]) for d in range(3)]
    count = field.shape[0]
    grad_first = along_first(field, first_ref, 0)
    high, low = split(field)
    both = jnp.dot(
        jnp.concatenate([high, low], axis=0), inner_ref[:LANES], preferred_element_type=F32
    )
    inner = both[:count] + both[count:]
    inner = inner + jnp.dot(high, inner_ref[LANES:], preferred_element_type=F32)
    flux_first = metric[0] * grad_first
    flux = jnp.concatenate([metric[1], metric[2]], axis=1) * inner
    high, low = split(flux)
    both = lax.dot_general(
        jnp.concatenate([high, low], axis=0), inner_ref[:LANES], NT, preferred_element_type=F32
    )
    back = both[:count] + both[count:]
    back = back + lax.dot_general(high, inner_ref[LANES:], NT, preferred_element_type=F32)
    back = back + along_first(flux_first, first_ref, 32)
    energy = flux * inner
    return back, flux_first * grad_first + energy[:, :LANES] + energy[:, LANES:]


def factors(points):
    nodes = 0.5 * (1.0 + np.cos(np.pi * np.arange(8) / 7.0))
    out = []
    for shift in (6, 3, 0):
        index = (points >> shift) & 7
        near = jnp.full(points.shape, nodes[7], F32)
        far = jnp.full(points.shape, nodes[0], F32)
        for m in range(7):
            near = jnp.where(index == m, float(nodes[m]), near)
            far = jnp.where(index == m, float(nodes[7 - m]), far)
        out.append((near, far))
    return out


def corners(points):
    first, second, third = factors(points)
    return [
        first[q >> 2 & 1] * (second[q >> 1 & 1] * third[q & 1]) for q in range(8)
    ]


def own_corners():
    return corners(lax.broadcasted_iota(jnp.int32, (1, POINTS), 1))


def flat_map(mapped):
    elements = mapped.shape[1]
    shape = (8, 8 * elements)
    lane = lax.broadcasted_iota(jnp.int32, shape, 1)
    padded = jnp.concatenate(
        [mapped.astype(F32), jnp.zeros((8, shape[1] - elements), F32)], axis=1
    )
    wide = take(padded, lane & (elements - 1))
    keep = lax.broadcasted_iota(jnp.int32, shape, 0) == lane // elements
    return jnp.sum(jnp.where(keep, wide, 0.0), axis=0, keepdims=True)


def one_vertex(flat):
    return jnp.where(one_hot(whole(flat), NC), 1.0, 0.0)


def whole(values):
    return (values + 0.5).astype(jnp.int32)


def own_element(elements, width):
    shape = (elements, width)
    return lax.broadcasted_iota(jnp.int32, shape, 0) == (
        lax.broadcasted_iota(jnp.int32, shape, 1) % elements
    )


def own_place(elements, q):
    shape = (elements, 8 * elements)
    lane = lax.broadcasted_iota(jnp.int32, shape, 1)
    return lane == lax.broadcasted_iota(jnp.int32, shape, 0) + q * elements


def coarse_part(field, vertices, inverse):
    elements = field.shape[0] // 4
    flat = jnp.zeros((elements, 8 * elements), F32)
    for q, corner in enumerate(own_corners()):
        inner = None
        for c in range(4):
            term = field[c * elements : (c + 1) * elements] * corner[:, c * LANES : (c + 1) * LANES]
            inner = term if inner is None else inner + term
        flat = jnp.where(own_place(elements, q), jnp.sum(inner, axis=1, keepdims=True), flat)
    flat = jnp.sum(flat, axis=0, keepdims=True)
    part = jnp.sum(vertices * flat, axis=1, keepdims=True)
    part = jnp.sum(inverse * part, axis=0, keepdims=True)
    return jnp.concatenate([part, jnp.zeros((1, LANES - NC), F32)], axis=1)


def get_solved(received_ref, count, peers):
    rows = get(received_ref, count, TERMS)
    return [
        jnp.sum(jnp.where(own_group(rows.shape[0], peers, away), rows, 0.0), axis=0, keepdims=True)
        for away in (0, -1, 1)
    ]


def prolonged(solved, flat, elements):
    shape = (elements, LANES)
    element = lax.broadcasted_iota(jnp.int32, shape, 0)
    at_corner = take(jnp.broadcast_to(solved, shape), jnp.broadcast_to(flat, shape))
    out = [None] * 4
    for q, corner in enumerate(own_corners()):
        value = take(at_corner, element + q * elements)
        for c in range(4):
            term = value * corner[:, c * LANES : (c + 1) * LANES]
            out[c] = term if out[c] is None else out[c] + term
    return jnp.concatenate(out, axis=0)


def prolonged_at(solved, maps, points, elements):
    at_corner = take(solved, maps)
    element = (points >> 9) & (elements - 1)
    total = jnp.zeros(points.shape, F32)
    for q, corner in enumerate(corners(points)):
        total = total + corner * take(at_corner, element + q * elements)
    return total


def total_of(array):
    return jnp.sum(jnp.sum(array, axis=0, keepdims=True), axis=1, keepdims=True)


def packed(values):
    lane = lax.broadcasted_iota(jnp.int32, (1, LANES), 1)
    out = jnp.zeros((1, LANES), F32)
    for k, value in enumerate(values):
        out = jnp.where(lane == k, value, out)
    return out


def unpacked(row, count):
    lane = lax.broadcasted_iota(jnp.int32, row.shape, 1)
    return [
        jnp.sum(jnp.where(lane == k, row, 0.0), axis=1, keepdims=True) for k in range(count)
    ]


def first_kernel(
    right_hbm, jacobi_hbm, inverse_hbm, map_hbm, slot_hbm, face_hbm,
    sent_ref, fields_ref, points_ref,
    right_ref, jacobi_ref, inverse_ref, map_ref, slot_ref, face_ref, sems,
):
    copies = []
    for k, (source, target) in enumerate(
        (
            (face_hbm, face_ref),
            (slot_hbm, slot_ref),
            (right_hbm, right_ref),
            (jacobi_hbm, jacobi_ref),
            (map_hbm, map_ref),
            (inverse_hbm, inverse_ref),
        )
    ):
        copy = pltpu.make_async_copy(source, target, sems.at[k])
        copy.start()
        copies.append(copy)
    for copy in copies:
        copy.wait()
    elements = right_ref.shape[0]
    peers = slot_ref.shape[1]
    faces = face_ref[...]
    faces = jnp.concatenate(halves(faces[0:1]) + halves(faces[1:2]), axis=0)
    points = jnp.concatenate([slot_ref[0], faces], axis=0)
    points_ref[...] = points
    resid = rows_of(right_ref[...])
    flat = flat_map(map_ref[...])
    smoothed = rows_of(jacobi_ref[...]) * resid
    fields_ref[0 : 4 * elements, :] = resid
    fields_ref[4 * elements : 8 * elements, :] = smoothed
    fields_ref[8 * elements :, :] = jnp.broadcast_to(flat, (8, LANES))
    part = coarse_part(resid, one_vertex(flat), inverse_ref[0])
    values = gather(smoothed, far_chunks(points, elements))
    send_values(sent_ref, FIRST_ROWS, values, peers)
    send_same(sent_ref, FIRST_ROWS, TERMS, part)
    send_same(sent_ref, FIRST_ROWS, TERMS + 1, flat)
    send_rows(sent_ref, FIRST_ROWS, TERMS + 2, points.astype(F32), peers)


def far_maps(received_ref, peers):
    maps = get(received_ref, FIRST_ROWS, TERMS + 1)
    sides = [
        jnp.broadcast_to(get_row(maps, peers, away), (FACE_ROWS, LANES)) for away in (-1, 1)
    ]
    return whole(jnp.concatenate([get_shared(maps, peers)] + sides, axis=0))


def apply(
    rough, smoothed, count, received_ref, flat, maps, far_points, solved, metric_ref, helmholtz_ref,
    first_ref, inner_ref, pair_ref, points_ref, dots, back_ref, sent_ref,
):
    elements = smoothed.shape[0] // 4
    peers = points_ref.shape[0] - 2 * FACE_ROWS
    pairs = pair_chunks(pair_ref, elements)
    far = far_chunks(points_ref[...], elements)
    near = gather(rough, pairs)
    partners = pair_ref[...]
    partners = jnp.concatenate(halves(partners[1:2]) + halves(partners[0:1]), axis=0)
    counts = (peers, FACE_ROWS, FACE_ROWS, partners.shape[0])
    spread = [
        jnp.broadcast_to(part, (n, LANES)) for part, n in zip((*solved, solved[0]), counts)
    ]
    coarse = prolonged_at(
        jnp.concatenate(spread, axis=0),
        jnp.concatenate([maps, jnp.broadcast_to(flat, partners.shape)], axis=0),
        jnp.concatenate([far_points, partners], axis=0),
        elements,
    )
    split_at = points_ref.shape[0]
    incoming = get_rows(received_ref, count, 0, peers) + coarse[:split_at]
    values = [value + more for value, more in zip(swapped(near), joined(coarse[split_at:]))]
    values = values + joined(incoming)
    summed = smoothed + scatter(smoothed.shape[0], pairs + far, values)
    back, energy = stiffness(summed, metric_ref, first_ref, inner_ref)
    energy = energy + rows_of(helmholtz_ref[...]) * smoothed * smoothed
    back_ref[...] = back
    send_values(sent_ref, ROWS, gather(back, far), peers)
    send_same(sent_ref, ROWS, TERMS, packed(dots + [total_of(energy)]))


def image_of(
    field_ref, back_ref, received_ref, helmholtz_ref, pair_ref, points_ref
):
    elements = field_ref.shape[0] // 4
    peers = points_ref.shape[0] - 2 * FACE_ROWS
    pairs = pair_chunks(pair_ref, elements)
    back = back_ref[...]
    values = swapped(gather(back, pairs)) + joined(get_rows(received_ref, ROWS, 0, peers))
    far = far_chunks(points_ref[...], elements)
    summed = back + scatter(field_ref.shape[0], pairs + far, values)
    return summed + rows_of(helmholtz_ref[...]) * field_ref[...]


def start_kernel(
    received_ref, fields_ref, points_ref, pair_ref, metric_ref, helmholtz_ref,
    first_ref, inner_ref,
    smoothed_ref, maps_ref, far_points_ref, back_ref, sent_ref,
):
    elements = helmholtz_ref.shape[0]
    peers = points_ref.shape[0] - 2 * FACE_ROWS
    solved = get_solved(received_ref, FIRST_ROWS, peers)
    resid = fields_ref[0 : 4 * elements, :]
    flat = whole(fields_ref[8 * elements : 8 * elements + 1, :])
    rough = fields_ref[4 * elements : 8 * elements, :]
    smoothed = rough + prolonged(solved[0], flat, elements)
    smoothed_ref[...] = smoothed
    maps = far_maps(received_ref, peers)
    maps_ref[...] = maps
    far_points = whole(get_rows(received_ref, FIRST_ROWS, TERMS + 2, peers))
    far_points_ref[...] = far_points
    apply(
        rough, smoothed, FIRST_ROWS, received_ref, flat, maps, far_points, solved, metric_ref,
        helmholtz_ref, first_ref, inner_ref, pair_ref, points_ref,
        [total_of(resid * smoothed)], back_ref, sent_ref,
    )


def middle_kernel(
    received_ref, fields_ref, points_ref, pair_ref, jacobi_ref, helmholtz_ref,
    inverse_ref, smoothed_ref, back_ref,
    image_ref, resid_ref, scalars_ref, sent_ref,
):
    elements = helmholtz_ref.shape[0]
    peers = points_ref.shape[0] - 2 * FACE_ROWS
    dots = jnp.sum(get(received_ref, ROWS, TERMS), axis=0, keepdims=True)
    scalars_ref[...] = dots
    values = unpacked(dots, 2)
    alpha = values[0] / values[1]
    image = image_of(
        smoothed_ref, back_ref, received_ref, helmholtz_ref, pair_ref,
        points_ref,
    )
    image_ref[...] = image
    resid = fields_ref[0 : 4 * elements, :] - alpha * image
    resid_ref[...] = resid
    vertices = one_vertex(fields_ref[8 * elements : 8 * elements + 1, :])
    part = coarse_part(resid, vertices, inverse_ref[0])
    values = gather(rows_of(jacobi_ref[...]) * resid, far_chunks(points_ref[...], elements))
    send_values(sent_ref, ROWS, values, peers)
    send_same(sent_ref, ROWS, TERMS, part)


def second_kernel(
    received_ref, fields_ref, points_ref, pair_ref, resid_ref, image_ref,
    maps_ref, far_points_ref, jacobi_ref, metric_ref, helmholtz_ref, first_ref, inner_ref,
    smoothed_ref, back_ref, sent_ref,
):
    elements = helmholtz_ref.shape[0]
    peers = points_ref.shape[0] - 2 * FACE_ROWS
    solved = get_solved(received_ref, ROWS, peers)
    resid = resid_ref[...]
    flat = whole(fields_ref[8 * elements : 8 * elements + 1, :])
    rough = rows_of(jacobi_ref[...]) * resid
    smoothed = rough + prolonged(solved[0], flat, elements)
    smoothed_ref[...] = smoothed
    apply(
        rough, smoothed, ROWS, received_ref, flat, maps_ref[...], far_points_ref[...], solved, metric_ref,
        helmholtz_ref, first_ref, inner_ref, pair_ref, points_ref,
        [total_of(resid * smoothed), total_of(image_ref[...] * smoothed)],
        back_ref, sent_ref,
    )


def final_kernel(
    received_ref, points_ref, pair_ref, old_ref, field_ref, resid_ref, old_image_ref,
    scalars_ref, back_ref, helmholtz_ref,
    solution_ref, residual_ref,
):
    before = unpacked(scalars_ref[...], 2)
    now = unpacked(jnp.sum(get(received_ref, ROWS, TERMS), axis=0, keepdims=True), 3)
    alpha = before[0] / before[1]
    beta = now[0] / before[0]
    curved = now[2] + beta * (2.0 * now[1] + beta * before[1])
    step = now[0] / curved
    old = old_ref[...]
    direction = field_ref[...] + beta * old
    solution_ref[...] = wide_of(alpha * old + step * direction)
    image = image_of(
        field_ref, back_ref, received_ref, helmholtz_ref, pair_ref,
        points_ref,
    )
    image = image + beta * old_image_ref[...]
    residual_ref[...] = wide_of(resid_ref[...] - step * image)


def call(kernel, outs, *args, copied=False):
    space = pl.ANY if copied else pltpu.VMEM
    scratch = [pltpu.VMEM(arg.shape, arg.dtype) for arg in args] if copied else []
    if copied:
        args = [pltpu.with_memory_space_constraint(arg, pltpu.HBM) for arg in args]
    return pl.pallas_call(
        kernel,
        out_shape=[
            jax.ShapeDtypeStruct(*(out if isinstance(out[0], tuple) else (out, F32))) for out in outs
        ],
        in_specs=[pl.BlockSpec(memory_space=space)] * len(args),
        out_specs=[pl.BlockSpec(memory_space=pltpu.VMEM)] * len(outs),
        scratch_shapes=scratch + ([pltpu.SemaphoreType.DMA((len(args),))] if copied else []),
        compiler_params=pltpu.CompilerParams(vmem_limit_bytes=24 * 1024 * 1024),
    )(*args)


def body(
    right_side,
    metric,
    helmholtz,
    jacobi,
    pair_list,
    shared_slots,
    face_points,
    coarse_map,
    coarse_inverse,
):
    peers = lax.axis_size("sub")
    groups = lax.axis_size("grp")
    t = {name: jnp.asarray(value) for name, value in tables().items()}
    elements = right_side.shape[0]
    field = (4 * elements, LANES)
    points_shape = (peers + 2 * FACE_ROWS, LANES)
    sent_shape = (groups * peers * ROWS, LANES)

    def exchange(sent):
        rows = sent.reshape(groups * peers, 1, -1)
        return lax.all_to_all(rows, ("grp", "sub"), 0, 0, tiled=True).reshape(sent.shape)

    sent, fields, points = call(
        first_kernel,
        [
            (groups * peers * FIRST_ROWS, LANES),
            (8 * elements + 8, LANES),
            (points_shape, jnp.int32),
        ],
        right_side, jacobi, coarse_inverse, coarse_map, shared_slots, face_points, copied=True,
    )
    smoothed, maps, far_points, back, sent = call(
        start_kernel,
        [field, (points_shape, jnp.int32), (points_shape, jnp.int32), field, sent_shape],
        exchange(sent), fields, points, pair_list, metric, helmholtz,
        t["first"], t["inner"],
    )
    image, resid, scalars, sent = call(
        middle_kernel, [field, field, (1, LANES), sent_shape],
        exchange(sent), fields, points, pair_list, jacobi, helmholtz, coarse_inverse,
        smoothed, back,
    )
    second, back, sent = call(
        second_kernel, [field, field, sent_shape],
        exchange(sent), fields, points, pair_list, resid, image, maps, far_points, jacobi,
        metric, helmholtz, t["first"], t["inner"],
    )
    return tuple(
        call(
            final_kernel, [right_side.shape, right_side.shape],
            exchange(sent), points, pair_list, smoothed, second, resid, image, scalars,
            back, helmholtz,
        )
    )


def solution(mesh):
    in_specs = (
        P(("grp", "sub"), None),
        P(("grp", "sub"), None),
        P(("grp", "sub"), None),
        P(("grp", "sub"), None),
        P(None, ("grp", "sub")),
        P(("grp", "sub"), None, None),
        P(None, ("grp", "sub")),
        P(None, ("grp", "sub")),
        P("grp", None, None),
    )
    out_specs = (P(("grp", "sub"), None), P(("grp", "sub"), None))
    return jax.shard_map(body, mesh=mesh, in_specs=in_specs, out_specs=out_specs, check_vma=False)
```

```python
import jax
import jax.numpy as jnp
import ml_dtypes
import numpy as np
from jax import lax
from jax.experimental import pallas as pl
from jax.experimental.pallas import tpu as pltpu
from jax.sharding import PartitionSpec as P

NC = 64
POINTS = 512
LANES = 128
STEP = 256
FACE_ROWS = 4
ROWS = 5
FIRST_ROWS = 10
TERMS = FACE_ROWS
F32 = jnp.float32
BF16 = jnp.bfloat16
NT = (((1,), (1,)), ((), ()))


def split_constant(array):
    high = array.astype(ml_dtypes.bfloat16)
    low = (array - high.astype(np.float64)).astype(ml_dtypes.bfloat16)
    return high, low


def tables():
    order_index = np.arange(8)
    colloc = np.cos(np.pi * order_index / 7.0)
    end_weights = (
        np.where((order_index == 0) | (order_index == 7), 2.0, 1.0) * (-1.0) ** order_index
    )
    spacing = colloc[:, None] - colloc[None, :] + np.eye(8)
    raw_matrix = np.outer(end_weights, 1.0 / end_weights) / spacing
    off_part = raw_matrix * (1.0 - np.eye(8))
    derivative = 0.25 * (off_part - np.eye(8) * off_part.sum(axis=1)[:, None])
    along_inner = np.concatenate(
        [np.kron(np.eye(2), np.kron(derivative, np.eye(8))).T, np.kron(np.eye(16), derivative).T],
        axis=1,
    )
    high, low = split_constant(along_inner)
    inner = np.concatenate([high, low], axis=0)

    half = np.arange(LANES) // 64

    def first_rows(matrix):
        rows = []
        for to in range(4):
            for at in range(4):
                rows.append(matrix[2 * to + half, 2 * at + half])
                rows.append(matrix[2 * to + half, 2 * at + 1 - half])
        return np.stack(rows).astype(np.float32)

    return {
        "inner": inner,
        "first": np.concatenate([first_rows(derivative), first_rows(derivative.T)], axis=0),
    }


def split(value):
    high = value.astype(BF16)
    return high, (value - high.astype(F32)).astype(BF16)


def rows_of(wide):
    return jnp.concatenate([wide[:, LANES * c : LANES * (c + 1)] for c in range(4)], axis=0)


def wide_of(rows):
    elements = rows.shape[0] // 4
    return jnp.concatenate([rows[c * elements : (c + 1) * elements] for c in range(4)], axis=1)


def locate(points, elements):
    element = points >> 9
    chunk = (points >> 7) & 3
    row = jnp.where(points < elements * POINTS, chunk * elements + element, 4 * elements)
    return row, points & (LANES - 1)


def one_hot(index, count):
    steps = lax.broadcasted_iota(jnp.int32, (count, index.shape[1]), 0)
    return steps == index


def lane_hot(lane):
    steps = lax.broadcasted_iota(jnp.int32, (LANES, lane.shape[1]), 0).astype(F32).astype(BF16)
    one = jnp.ones(steps.shape, BF16)
    return jnp.where(steps == lane.astype(F32).astype(BF16), one, jnp.zeros_like(one))


def take(values, lanes):
    return jnp.take_along_axis(values, lanes, axis=1, mode="promise_in_bounds")


def gather(field, chunks):
    count = field.shape[0]
    both = jnp.concatenate(split(field), axis=0)
    out = []
    for row, hot in chunks:
        picked = jnp.dot(both, hot, preferred_element_type=F32)
        mine = jnp.where(one_hot(row, count), picked[:count] + picked[count:], 0.0)
        out.append(jnp.sum(mine, axis=0, keepdims=True))
    return out


def scatter(rows, chunks, values):
    total = jnp.zeros((2 * rows, LANES), F32)
    for (row, hot), value in zip(chunks, values):
        steps = lax.broadcasted_iota(jnp.int32, (rows, row.shape[1]), 0).astype(F32).astype(BF16)
        mine = steps == row.astype(F32).astype(BF16)
        parts = [jnp.where(mine, part, jnp.zeros_like(steps)) for part in split(value)]
        total = total + lax.dot_general(
            jnp.concatenate(parts, axis=0), hot, NT, preferred_element_type=F32
        )
    return total[:rows] + total[rows:]


def chunked(row, lane):
    return [
        (row[:, at : at + STEP], lane[:, at : at + STEP]) for at in range(0, row.shape[1], STEP)
    ]


def cut(row):
    return [row[:, at : at + STEP] for at in range(0, row.shape[1], STEP)]


def pair_places(pair_ref, elements):
    row, lane = locate(pair_ref[...], elements)
    return chunked(row[0:1], lane[0:1]) + chunked(row[1:2], lane[1:2])


def joined(rows):
    return [
        jnp.concatenate([rows[at : at + 1], rows[at + 1 : at + 2]], axis=1)
        for at in range(0, rows.shape[0], 2)
    ]


def far_places(points, elements):
    row, lane = locate(points, elements)
    return list(zip(joined(row), joined(lane)))


def built(places, hot_ref):
    out = []
    for k, (row, lane) in enumerate(places):
        hot = lane_hot(lane)
        hot_ref[k * LANES : (k + 1) * LANES, :] = hot
        out.append((row, hot))
    return out


def loaded(places, hot_ref):
    return [
        (row, hot_ref[k * LANES : (k + 1) * LANES, :]) for k, (row, lane) in enumerate(places)
    ]


def halves(wide):
    return [wide[:, at : at + LANES] for at in range(0, wide.shape[1], LANES)]


def own_group(devices, peers, away=0):
    shape = (devices, LANES)
    return lax.broadcasted_iota(jnp.int32, shape, 0) // peers - lax.axis_index("grp") == away


def send_rows(sent_ref, count, at, rows, peers):
    devices = sent_ref.shape[0] // count
    above = own_group(devices, peers, 1)
    shared = jnp.concatenate([rows[:peers]] * (devices // peers), axis=0)
    for r in range(FACE_ROWS):
        down = rows[peers + r : peers + r + 1]
        up = rows[peers + FACE_ROWS + r : peers + FACE_ROWS + r + 1]
        out = jnp.where(above, up, down)
        if r == 0:
            out = jnp.where(own_group(devices, peers), shared, out)
        sent_ref[pl.ds(at + r, devices, count), :] = out


def send_same(sent_ref, count, at, row):
    devices = sent_ref.shape[0] // count
    sent_ref[pl.ds(at, devices, count), :] = jnp.broadcast_to(row, (devices, LANES))


def send_values(sent_ref, count, values, peers):
    rows = jnp.concatenate([row for pair in values for row in halves(pair)], axis=0)
    send_rows(sent_ref, count, 0, rows, peers)


def get(received_ref, count, at):
    return received_ref[pl.ds(at, received_ref.shape[0] // count, count), :]


def get_shared(rows, peers):
    mine = jnp.where(own_group(rows.shape[0], peers), rows, 0.0)
    shared = mine[:peers]
    for g in range(1, rows.shape[0] // peers):
        shared = shared + mine[g * peers : (g + 1) * peers]
    return shared


def get_row(rows, peers, away):
    here = lax.axis_index("grp") * peers + lax.axis_index("sub")
    source = lax.broadcasted_iota(jnp.int32, rows.shape, 0) - here == away * peers
    return jnp.sum(jnp.where(source, rows, 0.0), axis=0, keepdims=True)


def get_rows(received_ref, count, at, peers):
    rows = [get(received_ref, count, at + r) for r in range(FACE_ROWS)]
    faces = [get_row(part, peers, away) for away in (-1, 1) for part in rows]
    return jnp.concatenate([get_shared(rows[0], peers)] + faces, axis=0)


def swapped(values):
    count = len(values) // 2
    return values[count:] + values[:count]


def along_first(field, table_ref, base):
    elements = field.shape[0] // 4
    turned = pltpu.roll(field, 64, axis=1)
    out = []
    for to in range(4):
        total = None
        for at in range(4):
            place = base + 2 * (4 * to + at)
            rows = slice(at * elements, (at + 1) * elements)
            term = (
                table_ref[place : place + 1, :] * field[rows]
                + table_ref[place + 1 : place + 2, :] * turned[rows]
            )
            total = term if total is None else total + term
        out.append(total)
    return jnp.concatenate(out, axis=0)


def stiffness(field, metric_ref, first_ref, inner_ref):
    metric = [rows_of(metric_ref[:, POINTS * d : POINTS * (d + 1)]) for d in range(3)]
    count = field.shape[0]
    grad_first = along_first(field, first_ref, 0)
    high, low = split(field)
    both = jnp.dot(
        jnp.concatenate([high, low], axis=0), inner_ref[:LANES], preferred_element_type=F32
    )
    inner = both[:count] + both[count:]
    inner = inner + jnp.dot(high, inner_ref[LANES:], preferred_element_type=F32)
    flux_first = metric[0] * grad_first
    flux = jnp.concatenate([metric[1], metric[2]], axis=1) * inner
    high, low = split(flux)
    both = lax.dot_general(
        jnp.concatenate([high, low], axis=0), inner_ref[:LANES], NT, preferred_element_type=F32
    )
    back = both[:count] + both[count:]
    back = back + lax.dot_general(high, inner_ref[LANES:], NT, preferred_element_type=F32)
    back = back + along_first(flux_first, first_ref, 32)
    energy = flux * inner
    return back, flux_first * grad_first + energy[:, :LANES] + energy[:, LANES:]


def factors(points):
    nodes = 0.5 * (1.0 + np.cos(np.pi * np.arange(8) / 7.0))
    out = []
    for shift in (6, 3, 0):
        index = (points >> shift) & 7
        near = jnp.full(points.shape, nodes[7], F32)
        far = jnp.full(points.shape, nodes[0], F32)
        for m in range(7):
            near = jnp.where(index == m, float(nodes[m]), near)
            far = jnp.where(index == m, float(nodes[7 - m]), far)
        out.append((near, far))
    return out


def corners(points):
    first, second, third = factors(points)
    return [
        first[q >> 2 & 1] * (second[q >> 1 & 1] * third[q & 1]) for q in range(8)
    ]


def own_corners():
    return corners(lax.broadcasted_iota(jnp.int32, (1, POINTS), 1))


def flat_map(mapped):
    elements = mapped.shape[1]
    shape = (8, 8 * elements)
    lane = lax.broadcasted_iota(jnp.int32, shape, 1)
    padded = jnp.concatenate(
        [mapped.astype(F32), jnp.zeros((8, shape[1] - elements), F32)], axis=1
    )
    wide = take(padded, lane & (elements - 1))
    keep = lax.broadcasted_iota(jnp.int32, shape, 0) == lane // elements
    return jnp.sum(jnp.where(keep, wide, 0.0), axis=0, keepdims=True)


def one_vertex(flat):
    return jnp.where(one_hot(whole(flat), NC), 1.0, 0.0)


def whole(values):
    return (values + 0.5).astype(jnp.int32)


def own_element(elements, width):
    shape = (elements, width)
    return lax.broadcasted_iota(jnp.int32, shape, 0) == (
        lax.broadcasted_iota(jnp.int32, shape, 1) % elements
    )


def own_place(elements, q):
    shape = (elements, 8 * elements)
    lane = lax.broadcasted_iota(jnp.int32, shape, 1)
    return lane == lax.broadcasted_iota(jnp.int32, shape, 0) + q * elements


def coarse_part(field, vertices, inverse):
    elements = field.shape[0] // 4
    flat = jnp.zeros((elements, 8 * elements), F32)
    for q, corner in enumerate(own_corners()):
        inner = None
        for c in range(4):
            term = field[c * elements : (c + 1) * elements] * corner[:, c * LANES : (c + 1) * LANES]
            inner = term if inner is None else inner + term
        flat = jnp.where(own_place(elements, q), jnp.sum(inner, axis=1, keepdims=True), flat)
    flat = jnp.sum(flat, axis=0, keepdims=True)
    part = jnp.sum(vertices * flat, axis=1, keepdims=True)
    part = jnp.sum(inverse * part, axis=0, keepdims=True)
    return jnp.concatenate([part, jnp.zeros((1, LANES - NC), F32)], axis=1)


def get_solved(received_ref, count, peers):
    rows = get(received_ref, count, TERMS)
    return [
        jnp.sum(jnp.where(own_group(rows.shape[0], peers, away), rows, 0.0), axis=0, keepdims=True)
        for away in (0, -1, 1)
    ]


def prolonged(solved, flat, elements):
    shape = (elements, LANES)
    element = lax.broadcasted_iota(jnp.int32, shape, 0)
    at_corner = take(jnp.broadcast_to(solved, shape), jnp.broadcast_to(flat, shape))
    out = [None] * 4
    for q, corner in enumerate(own_corners()):
        value = take(at_corner, element + q * elements)
        for c in range(4):
            term = value * corner[:, c * LANES : (c + 1) * LANES]
            out[c] = term if out[c] is None else out[c] + term
    return jnp.concatenate(out, axis=0)


def prolonged_at(solved, maps, points, elements):
    at_corner = take(solved, maps)
    element = (points >> 9) & (elements - 1)
    total = jnp.zeros(points.shape, F32)
    for q, corner in enumerate(corners(points)):
        total = total + corner * take(at_corner, element + q * elements)
    return total


def total_of(array):
    return jnp.sum(jnp.sum(array, axis=0, keepdims=True), axis=1, keepdims=True)


def packed(values):
    lane = lax.broadcasted_iota(jnp.int32, (1, LANES), 1)
    out = jnp.zeros((1, LANES), F32)
    for k, value in enumerate(values):
        out = jnp.where(lane == k, value, out)
    return out


def unpacked(row, count):
    lane = lax.broadcasted_iota(jnp.int32, row.shape, 1)
    return [
        jnp.sum(jnp.where(lane == k, row, 0.0), axis=1, keepdims=True) for k in range(count)
    ]


def first_kernel(
    right_hbm, jacobi_hbm, inverse_hbm, map_hbm, slot_hbm, face_hbm,
    sent_ref, fields_ref, points_ref, far_hot_ref,
    right_ref, jacobi_ref, inverse_ref, map_ref, slot_ref, face_ref, sems,
):
    copies = []
    for k, (source, target) in enumerate(
        (
            (face_hbm, face_ref),
            (slot_hbm, slot_ref),
            (right_hbm, right_ref),
            (jacobi_hbm, jacobi_ref),
            (map_hbm, map_ref),
            (inverse_hbm, inverse_ref),
        )
    ):
        copy = pltpu.make_async_copy(source, target, sems.at[k])
        copy.start()
        copies.append(copy)
    for copy in copies:
        copy.wait()
    elements = right_ref.shape[0]
    peers = slot_ref.shape[1]
    faces = face_ref[...]
    faces = jnp.concatenate(halves(faces[0:1]) + halves(faces[1:2]), axis=0)
    points = jnp.concatenate([slot_ref[0], faces], axis=0)
    points_ref[...] = points
    resid = rows_of(right_ref[...])
    flat = flat_map(map_ref[...])
    smoothed = rows_of(jacobi_ref[...]) * resid
    fields_ref[0 : 4 * elements, :] = resid
    fields_ref[4 * elements : 8 * elements, :] = smoothed
    fields_ref[8 * elements :, :] = jnp.broadcast_to(flat, (8, LANES))
    part = coarse_part(resid, one_vertex(flat), inverse_ref[0])
    values = gather(smoothed, built(far_places(points, elements), far_hot_ref))
    send_values(sent_ref, FIRST_ROWS, values, peers)
    send_same(sent_ref, FIRST_ROWS, TERMS, part)
    send_same(sent_ref, FIRST_ROWS, TERMS + 1, flat)
    send_rows(sent_ref, FIRST_ROWS, TERMS + 2, points.astype(F32), peers)


def far_maps(received_ref, peers):
    maps = get(received_ref, FIRST_ROWS, TERMS + 1)
    sides = [
        jnp.broadcast_to(get_row(maps, peers, away), (FACE_ROWS, LANES)) for away in (-1, 1)
    ]
    return whole(jnp.concatenate([get_shared(maps, peers)] + sides, axis=0))


def apply(
    rough, smoothed, count, received_ref, flat, maps, far_points, solved, metric_ref, helmholtz_ref,
    first_ref, inner_ref, pair_ref, pairs, points_ref, far_hot_ref, dots, back_ref, local_ref,
    sent_ref,
):
    elements = smoothed.shape[0] // 4
    peers = points_ref.shape[0] - 2 * FACE_ROWS
    far = loaded(far_places(points_ref[...], elements), far_hot_ref)
    near = gather(rough, pairs)
    partners = pair_ref[...]
    partners = jnp.concatenate(halves(partners[1:2]) + halves(partners[0:1]), axis=0)
    counts = (peers, FACE_ROWS, FACE_ROWS, partners.shape[0])
    spread = [
        jnp.broadcast_to(part, (n, LANES)) for part, n in zip((*solved, solved[0]), counts)
    ]
    coarse = prolonged_at(
        jnp.concatenate(spread, axis=0),
        jnp.concatenate([maps, jnp.broadcast_to(flat, partners.shape)], axis=0),
        jnp.concatenate([far_points, partners], axis=0),
        elements,
    )
    split_at = points_ref.shape[0]
    incoming = get_rows(received_ref, count, 0, peers) + coarse[:split_at]
    values = [value + more for value, more in zip(swapped(near), joined(coarse[split_at:]))]
    values = values + joined(incoming)
    summed = smoothed + scatter(smoothed.shape[0], pairs + far, values)
    back, energy = stiffness(summed, metric_ref, first_ref, inner_ref)
    energy = energy + rows_of(helmholtz_ref[...]) * smoothed * smoothed
    back_ref[...] = back
    values = gather(back, pairs + far)
    near = swapped(values[: len(pairs)])
    for k, value in enumerate(near):
        local_ref[0:1, k * STEP : (k + 1) * STEP] = value
    send_values(sent_ref, ROWS, values[len(pairs) :], peers)
    send_same(sent_ref, ROWS, TERMS, packed(dots + [total_of(energy)]))


def image_of(
    field_ref, back_ref, local_ref, received_ref, helmholtz_ref, pair_ref, pair_hot_ref, points_ref,
    far_hot_ref,
):
    elements = field_ref.shape[0] // 4
    peers = points_ref.shape[0] - 2 * FACE_ROWS
    chunks = loaded(pair_places(pair_ref, elements), pair_hot_ref)
    chunks = chunks + loaded(far_places(points_ref[...], elements), far_hot_ref)
    values = cut(local_ref[...]) + joined(get_rows(received_ref, ROWS, 0, peers))
    summed = back_ref[...] + scatter(field_ref.shape[0], chunks, values)
    return summed + rows_of(helmholtz_ref[...]) * field_ref[...]


def start_kernel(
    received_ref, fields_ref, points_ref, far_hot_ref, pair_ref, metric_ref, helmholtz_ref,
    first_ref, inner_ref,
    smoothed_ref, maps_ref, far_points_ref, back_ref, local_ref, sent_ref, pair_hot_ref,
):
    elements = helmholtz_ref.shape[0]
    peers = points_ref.shape[0] - 2 * FACE_ROWS
    solved = get_solved(received_ref, FIRST_ROWS, peers)
    resid = fields_ref[0 : 4 * elements, :]
    flat = whole(fields_ref[8 * elements : 8 * elements + 1, :])
    rough = fields_ref[4 * elements : 8 * elements, :]
    smoothed = rough + prolonged(solved[0], flat, elements)
    smoothed_ref[...] = smoothed
    maps = far_maps(received_ref, peers)
    maps_ref[...] = maps
    far_points = whole(get_rows(received_ref, FIRST_ROWS, TERMS + 2, peers))
    far_points_ref[...] = far_points
    apply(
        rough, smoothed, FIRST_ROWS, received_ref, flat, maps, far_points, solved, metric_ref,
        helmholtz_ref, first_ref, inner_ref, pair_ref,
        built(pair_places(pair_ref, elements), pair_hot_ref), points_ref, far_hot_ref,
        [total_of(resid * smoothed)], back_ref, local_ref, sent_ref,
    )


def middle_kernel(
    received_ref, fields_ref, points_ref, far_hot_ref, pair_ref, pair_hot_ref, jacobi_ref, helmholtz_ref,
    inverse_ref, smoothed_ref, back_ref, local_ref,
    image_ref, resid_ref, scalars_ref, sent_ref,
):
    elements = helmholtz_ref.shape[0]
    peers = points_ref.shape[0] - 2 * FACE_ROWS
    dots = jnp.sum(get(received_ref, ROWS, TERMS), axis=0, keepdims=True)
    scalars_ref[...] = dots
    values = unpacked(dots, 2)
    alpha = values[0] / values[1]
    image = image_of(
        smoothed_ref, back_ref, local_ref, received_ref, helmholtz_ref, pair_ref,
        pair_hot_ref, points_ref, far_hot_ref,
    )
    image_ref[...] = image
    resid = fields_ref[0 : 4 * elements, :] - alpha * image
    resid_ref[...] = resid
    vertices = one_vertex(fields_ref[8 * elements : 8 * elements + 1, :])
    part = coarse_part(resid, vertices, inverse_ref[0])
    values = gather(
        rows_of(jacobi_ref[...]) * resid, loaded(far_places(points_ref[...], elements), far_hot_ref),
    )
    send_values(sent_ref, ROWS, values, peers)
    send_same(sent_ref, ROWS, TERMS, part)


def second_kernel(
    received_ref, fields_ref, points_ref, far_hot_ref, pair_ref, pair_hot_ref, resid_ref, image_ref,
    maps_ref, far_points_ref, jacobi_ref, metric_ref, helmholtz_ref, first_ref, inner_ref,
    smoothed_ref, back_ref, local_ref, sent_ref,
):
    elements = helmholtz_ref.shape[0]
    peers = points_ref.shape[0] - 2 * FACE_ROWS
    solved = get_solved(received_ref, ROWS, peers)
    resid = resid_ref[...]
    flat = whole(fields_ref[8 * elements : 8 * elements + 1, :])
    rough = rows_of(jacobi_ref[...]) * resid
    smoothed = rough + prolonged(solved[0], flat, elements)
    smoothed_ref[...] = smoothed
    apply(
        rough, smoothed, ROWS, received_ref, flat, maps_ref[...], far_points_ref[...], solved, metric_ref,
        helmholtz_ref, first_ref, inner_ref, pair_ref,
        loaded(pair_places(pair_ref, elements), pair_hot_ref), points_ref, far_hot_ref,
        [total_of(resid * smoothed), total_of(image_ref[...] * smoothed)],
        back_ref, local_ref, sent_ref,
    )


def final_kernel(
    received_ref, points_ref, far_hot_ref, pair_ref, pair_hot_ref, old_ref, field_ref, resid_ref, old_image_ref,
    scalars_ref, back_ref, local_ref, helmholtz_ref,
    solution_ref, residual_ref,
):
    before = unpacked(scalars_ref[...], 2)
    now = unpacked(jnp.sum(get(received_ref, ROWS, TERMS), axis=0, keepdims=True), 3)
    alpha = before[0] / before[1]
    beta = now[0] / before[0]
    curved = now[2] + beta * (2.0 * now[1] + beta * before[1])
    step = now[0] / curved
    old = old_ref[...]
    direction = field_ref[...] + beta * old
    solution_ref[...] = wide_of(alpha * old + step * direction)
    image = image_of(
        field_ref, back_ref, local_ref, received_ref, helmholtz_ref, pair_ref,
        pair_hot_ref, points_ref, far_hot_ref,
    )
    image = image + beta * old_image_ref[...]
    residual_ref[...] = wide_of(resid_ref[...] - step * image)


def call(kernel, outs, *args, copied=False):
    space = pl.ANY if copied else pltpu.VMEM
    scratch = [pltpu.VMEM(arg.shape, arg.dtype) for arg in args] if copied else []
    if copied:
        args = [pltpu.with_memory_space_constraint(arg, pltpu.HBM) for arg in args]
    return pl.pallas_call(
        kernel,
        out_shape=[
            jax.ShapeDtypeStruct(*(out if isinstance(out[0], tuple) else (out, F32))) for out in outs
        ],
        in_specs=[pl.BlockSpec(memory_space=space)] * len(args),
        out_specs=[pl.BlockSpec(memory_space=pltpu.VMEM)] * len(outs),
        scratch_shapes=scratch + ([pltpu.SemaphoreType.DMA((len(args),))] if copied else []),
        compiler_params=pltpu.CompilerParams(vmem_limit_bytes=24 * 1024 * 1024),
    )(*args)


def body(
    right_side,
    metric,
    helmholtz,
    jacobi,
    pair_list,
    shared_slots,
    face_points,
    coarse_map,
    coarse_inverse,
):
    peers = lax.axis_size("sub")
    groups = lax.axis_size("grp")
    t = {name: jnp.asarray(value) for name, value in tables().items()}
    elements = right_side.shape[0]
    field = (4 * elements, LANES)
    local = (1, pair_list.shape[0] * pair_list.shape[1])
    points_shape = (peers + 2 * FACE_ROWS, LANES)
    sent_shape = (groups * peers * ROWS, LANES)

    def exchange(sent):
        rows = sent.reshape(groups * peers, 1, -1)
        return lax.all_to_all(rows, ("grp", "sub"), 0, 0, tiled=True).reshape(sent.shape)

    far_hot_shape = (points_shape[0] * LANES // 2, STEP)
    pair_hot_shape = (local[1] * LANES // STEP, STEP)

    sent, fields, points, far_hot = call(
        first_kernel,
        [
            (groups * peers * FIRST_ROWS, LANES),
            (8 * elements + 8, LANES),
            (points_shape, jnp.int32),
            (far_hot_shape, BF16),
        ],
        right_side, jacobi, coarse_inverse, coarse_map, shared_slots, face_points, copied=True,
    )
    smoothed, maps, far_points, back, near, sent, pair_hot = call(
        start_kernel,
        [field, (points_shape, jnp.int32), (points_shape, jnp.int32), field, local, sent_shape,
         (pair_hot_shape, BF16)],
        exchange(sent), fields, points, far_hot, pair_list, metric, helmholtz,
        t["first"], t["inner"],
    )
    image, resid, scalars, sent = call(
        middle_kernel, [field, field, (1, LANES), sent_shape],
        exchange(sent), fields, points, far_hot, pair_list, pair_hot, jacobi, helmholtz, coarse_inverse,
        smoothed, back, near,
    )
    second, back, near, sent = call(
        second_kernel, [field, field, local, sent_shape],
        exchange(sent), fields, points, far_hot, pair_list, pair_hot, resid, image, maps, far_points, jacobi,
        metric, helmholtz, t["first"], t["inner"],
    )
    return tuple(
        call(
            final_kernel, [right_side.shape, right_side.shape],
            exchange(sent), points, far_hot, pair_list, pair_hot, smoothed, second, resid, image, scalars,
            back, near, helmholtz,
        )
    )


def solution(mesh):
    in_specs = (
        P(("grp", "sub"), None),
        P(("grp", "sub"), None),
        P(("grp", "sub"), None),
        P(("grp", "sub"), None),
        P(None, ("grp", "sub")),
        P(("grp", "sub"), None, None),
        P(None, ("grp", "sub")),
        P(None, ("grp", "sub")),
        P("grp", None, None),
    )
    out_specs = (P(("grp", "sub"), None), P(("grp", "sub"), None))
    return jax.shard_map(body, mesh=mesh, in_specs=in_specs, out_specs=out_specs, check_vma=False)
```

```python
import jax
import jax.numpy as jnp
import ml_dtypes
import numpy as np
from jax import lax
from jax.experimental import pallas as pl
from jax.experimental.pallas import tpu as pltpu
from jax.sharding import PartitionSpec as P

NC = 64
POINTS = 512
LANES = 128
FACE_ROWS = 4
ROWS = 5
FIRST_ROWS = 10
TERMS = FACE_ROWS
F32 = jnp.float32
BF16 = jnp.bfloat16
NT = (((1,), (1,)), ((), ()))


def split_constant(array):
    high = array.astype(ml_dtypes.bfloat16)
    low = (array - high.astype(np.float64)).astype(ml_dtypes.bfloat16)
    return high, low


def tables():
    order_index = np.arange(8)
    colloc = np.cos(np.pi * order_index / 7.0)
    end_weights = (
        np.where((order_index == 0) | (order_index == 7), 2.0, 1.0) * (-1.0) ** order_index
    )
    spacing = colloc[:, None] - colloc[None, :] + np.eye(8)
    raw_matrix = np.outer(end_weights, 1.0 / end_weights) / spacing
    off_part = raw_matrix * (1.0 - np.eye(8))
    derivative = 0.25 * (off_part - np.eye(8) * off_part.sum(axis=1)[:, None])
    along_inner = np.concatenate(
        [np.kron(np.eye(2), np.kron(derivative, np.eye(8))).T, np.kron(np.eye(16), derivative).T],
        axis=1,
    )
    high, low = split_constant(along_inner)
    inner = np.concatenate([high, low], axis=0)

    half = np.arange(LANES) // 64

    def first_rows(matrix):
        rows = []
        for to in range(4):
            for at in range(4):
                rows.append(matrix[2 * to + half, 2 * at + half])
                rows.append(matrix[2 * to + half, 2 * at + 1 - half])
        return np.stack(rows).astype(np.float32)

    return {
        "inner": inner,
        "first": np.concatenate([first_rows(derivative), first_rows(derivative.T)], axis=0),
    }


def split(value):
    high = value.astype(BF16)
    return high, (value - high.astype(F32)).astype(BF16)


def rows_of(wide):
    return jnp.concatenate([wide[:, LANES * c : LANES * (c + 1)] for c in range(4)], axis=0)


def wide_of(rows):
    elements = rows.shape[0] // 4
    return jnp.concatenate([rows[c * elements : (c + 1) * elements] for c in range(4)], axis=1)


def locate(points, elements):
    element = points >> 9
    chunk = (points >> 7) & 3
    row = jnp.where(points < elements * POINTS, chunk * elements + element, 4 * elements)
    return row, points & (LANES - 1)


def one_hot(index, count):
    steps = lax.broadcasted_iota(jnp.int32, (count, index.shape[1]), 0)
    return steps == index


def lane_hot(lane):
    steps = lax.broadcasted_iota(jnp.int32, (LANES, lane.shape[1]), 0).astype(F32).astype(BF16)
    one = jnp.ones(steps.shape, BF16)
    return jnp.where(steps == lane.astype(F32).astype(BF16), one, jnp.zeros_like(one))


def take(values, lanes):
    return jnp.take_along_axis(values, lanes, axis=1, mode="promise_in_bounds")


def gather(field, points):
    row, hot = points
    count = field.shape[0]
    both = jnp.concatenate(split(field), axis=0)
    picked = jnp.dot(both, hot, preferred_element_type=F32)
    mine = jnp.where(one_hot(row, count), picked[:count] + picked[count:], 0.0)
    return jnp.sum(mine, axis=0, keepdims=True)


def scatter(count, points, values):
    row, hot = points
    steps = lax.broadcasted_iota(jnp.int32, (count, row.shape[1]), 0).astype(F32).astype(BF16)
    mine = steps == row.astype(F32).astype(BF16)
    parts = [jnp.where(mine, part, jnp.zeros_like(steps)) for part in split(values)]
    total = lax.dot_general(
        jnp.concatenate(parts, axis=0), hot, NT, preferred_element_type=F32
    )
    return total[:count] + total[count:]


def line(rows):
    return jnp.concatenate([rows[k : k + 1] for k in range(rows.shape[0])], axis=1)


def places_of(points, elements):
    row, lane = locate(points, elements)
    return line(row), line(lane)


def built(places, hot_ref):
    row, lane = places
    hot = lane_hot(lane)
    hot_ref[...] = hot
    return row, hot


def loaded(places, hot_ref):
    return places[0], hot_ref[...]


def halves(wide):
    return [wide[:, at : at + LANES] for at in range(0, wide.shape[1], LANES)]


def own_group(devices, peers, away=0):
    shape = (devices, LANES)
    return lax.broadcasted_iota(jnp.int32, shape, 0) // peers - lax.axis_index("grp") == away


def send_rows(sent_ref, count, at, rows, peers):
    devices = sent_ref.shape[0] // count
    above = own_group(devices, peers, 1)
    shared = jnp.concatenate([rows[:peers]] * (devices // peers), axis=0)
    for r in range(FACE_ROWS):
        down = rows[peers + r : peers + r + 1]
        up = rows[peers + FACE_ROWS + r : peers + FACE_ROWS + r + 1]
        out = jnp.where(above, up, down)
        if r == 0:
            out = jnp.where(own_group(devices, peers), shared, out)
        sent_ref[pl.ds(at + r, devices, count), :] = out


def send_same(sent_ref, count, at, row):
    devices = sent_ref.shape[0] // count
    sent_ref[pl.ds(at, devices, count), :] = jnp.broadcast_to(row, (devices, LANES))


def send_values(sent_ref, count, values, peers):
    send_rows(sent_ref, count, 0, jnp.concatenate(halves(values), axis=0), peers)


def get(received_ref, count, at):
    return received_ref[pl.ds(at, received_ref.shape[0] // count, count), :]


def get_shared(rows, peers):
    mine = jnp.where(own_group(rows.shape[0], peers), rows, 0.0)
    shared = mine[:peers]
    for g in range(1, rows.shape[0] // peers):
        shared = shared + mine[g * peers : (g + 1) * peers]
    return shared


def get_row(rows, peers, away):
    here = lax.axis_index("grp") * peers + lax.axis_index("sub")
    source = lax.broadcasted_iota(jnp.int32, rows.shape, 0) - here == away * peers
    return jnp.sum(jnp.where(source, rows, 0.0), axis=0, keepdims=True)


def get_rows(received_ref, count, at, peers):
    rows = [get(received_ref, count, at + r) for r in range(FACE_ROWS)]
    faces = [get_row(part, peers, away) for away in (-1, 1) for part in rows]
    return jnp.concatenate([get_shared(rows[0], peers)] + faces, axis=0)


def swapped(values):
    count = values.shape[1] // 2
    return jnp.concatenate([values[:, count:], values[:, :count]], axis=1)


def along_first(field, table_ref, base):
    elements = field.shape[0] // 4
    turned = pltpu.roll(field, 64, axis=1)
    out = []
    for to in range(4):
        total = None
        for at in range(4):
            place = base + 2 * (4 * to + at)
            rows = slice(at * elements, (at + 1) * elements)
            term = (
                table_ref[place : place + 1, :] * field[rows]
                + table_ref[place + 1 : place + 2, :] * turned[rows]
            )
            total = term if total is None else total + term
        out.append(total)
    return jnp.concatenate(out, axis=0)


def stiffness(field, metric_ref, first_ref, inner_ref):
    metric = [rows_of(metric_ref[:, POINTS * d : POINTS * (d + 1)]) for d in range(3)]
    count = field.shape[0]
    grad_first = along_first(field, first_ref, 0)
    high, low = split(field)
    both = jnp.dot(
        jnp.concatenate([high, low], axis=0), inner_ref[:LANES], preferred_element_type=F32
    )
    inner = both[:count] + both[count:]
    inner = inner + jnp.dot(high, inner_ref[LANES:], preferred_element_type=F32)
    flux_first = metric[0] * grad_first
    flux = jnp.concatenate([metric[1], metric[2]], axis=1) * inner
    high, low = split(flux)
    both = lax.dot_general(
        jnp.concatenate([high, low], axis=0), inner_ref[:LANES], NT, preferred_element_type=F32
    )
    back = both[:count] + both[count:]
    back = back + lax.dot_general(high, inner_ref[LANES:], NT, preferred_element_type=F32)
    back = back + along_first(flux_first, first_ref, 32)
    energy = flux * inner
    return back, flux_first * grad_first + energy[:, :LANES] + energy[:, LANES:]


def factors(points):
    nodes = 0.5 * (1.0 + np.cos(np.pi * np.arange(8) / 7.0))
    out = []
    for shift in (6, 3, 0):
        index = (points >> shift) & 7
        near = jnp.full(points.shape, nodes[7], F32)
        far = jnp.full(points.shape, nodes[0], F32)
        for m in range(7):
            near = jnp.where(index == m, float(nodes[m]), near)
            far = jnp.where(index == m, float(nodes[7 - m]), far)
        out.append((near, far))
    return out


def corners(points):
    first, second, third = factors(points)
    return [
        first[q >> 2 & 1] * (second[q >> 1 & 1] * third[q & 1]) for q in range(8)
    ]


def own_corners():
    return corners(lax.broadcasted_iota(jnp.int32, (1, POINTS), 1))


def flat_map(mapped):
    elements = mapped.shape[1]
    shape = (8, 8 * elements)
    lane = lax.broadcasted_iota(jnp.int32, shape, 1)
    padded = jnp.concatenate(
        [mapped.astype(F32), jnp.zeros((8, shape[1] - elements), F32)], axis=1
    )
    wide = take(padded, lane & (elements - 1))
    keep = lax.broadcasted_iota(jnp.int32, shape, 0) == lane // elements
    return jnp.sum(jnp.where(keep, wide, 0.0), axis=0, keepdims=True)


def one_vertex(flat):
    return jnp.where(one_hot(whole(flat), NC), 1.0, 0.0)


def whole(values):
    return (values + 0.5).astype(jnp.int32)


def own_element(elements, width):
    shape = (elements, width)
    return lax.broadcasted_iota(jnp.int32, shape, 0) == (
        lax.broadcasted_iota(jnp.int32, shape, 1) % elements
    )


def own_place(elements, q):
    shape = (elements, 8 * elements)
    lane = lax.broadcasted_iota(jnp.int32, shape, 1)
    return lane == lax.broadcasted_iota(jnp.int32, shape, 0) + q * elements


def coarse_part(field, vertices, inverse):
    elements = field.shape[0] // 4
    flat = jnp.zeros((elements, 8 * elements), F32)
    for q, corner in enumerate(own_corners()):
        inner = None
        for c in range(4):
            term = field[c * elements : (c + 1) * elements] * corner[:, c * LANES : (c + 1) * LANES]
            inner = term if inner is None else inner + term
        flat = jnp.where(own_place(elements, q), jnp.sum(inner, axis=1, keepdims=True), flat)
    flat = jnp.sum(flat, axis=0, keepdims=True)
    part = jnp.sum(vertices * flat, axis=1, keepdims=True)
    part = jnp.sum(inverse * part, axis=0, keepdims=True)
    return jnp.concatenate([part, jnp.zeros((1, LANES - NC), F32)], axis=1)


def get_solved(received_ref, count, peers):
    rows = get(received_ref, count, TERMS)
    return [
        jnp.sum(jnp.where(own_group(rows.shape[0], peers, away), rows, 0.0), axis=0, keepdims=True)
        for away in (0, -1, 1)
    ]


def prolonged(solved, flat, elements):
    shape = (elements, LANES)
    element = lax.broadcasted_iota(jnp.int32, shape, 0)
    at_corner = take(jnp.broadcast_to(solved, shape), jnp.broadcast_to(flat, shape))
    out = [None] * 4
    for q, corner in enumerate(own_corners()):
        value = take(at_corner, element + q * elements)
        for c in range(4):
            term = value * corner[:, c * LANES : (c + 1) * LANES]
            out[c] = term if out[c] is None else out[c] + term
    return jnp.concatenate(out, axis=0)


def prolonged_at(solved, maps, points, elements):
    at_corner = take(solved, maps)
    element = (points >> 9) & (elements - 1)
    total = jnp.zeros(points.shape, F32)
    for q, corner in enumerate(corners(points)):
        total = total + corner * take(at_corner, element + q * elements)
    return total


def total_of(array):
    return jnp.sum(jnp.sum(array, axis=0, keepdims=True), axis=1, keepdims=True)


def packed(values):
    lane = lax.broadcasted_iota(jnp.int32, (1, LANES), 1)
    out = jnp.zeros((1, LANES), F32)
    for k, value in enumerate(values):
        out = jnp.where(lane == k, value, out)
    return out


def unpacked(row, count):
    lane = lax.broadcasted_iota(jnp.int32, row.shape, 1)
    return [
        jnp.sum(jnp.where(lane == k, row, 0.0), axis=1, keepdims=True) for k in range(count)
    ]


def first_kernel(
    right_hbm, jacobi_hbm, inverse_hbm, map_hbm, slot_hbm, face_hbm,
    sent_ref, fields_ref, points_ref, far_hot_ref,
    right_ref, jacobi_ref, inverse_ref, map_ref, slot_ref, face_ref, sems,
):
    copies = []
    for k, (source, target) in enumerate(
        (
            (face_hbm, face_ref),
            (slot_hbm, slot_ref),
            (right_hbm, right_ref),
            (jacobi_hbm, jacobi_ref),
            (map_hbm, map_ref),
            (inverse_hbm, inverse_ref),
        )
    ):
        copy = pltpu.make_async_copy(source, target, sems.at[k])
        copy.start()
        copies.append(copy)
    for copy in copies:
        copy.wait()
    elements = right_ref.shape[0]
    peers = slot_ref.shape[1]
    faces = face_ref[...]
    faces = jnp.concatenate(halves(faces[0:1]) + halves(faces[1:2]), axis=0)
    points = jnp.concatenate([slot_ref[0], faces], axis=0)
    points_ref[...] = points
    resid = rows_of(right_ref[...])
    flat = flat_map(map_ref[...])
    smoothed = rows_of(jacobi_ref[...]) * resid
    fields_ref[0 : 4 * elements, :] = resid
    fields_ref[4 * elements : 8 * elements, :] = smoothed
    fields_ref[8 * elements :, :] = jnp.broadcast_to(flat, (8, LANES))
    part = coarse_part(resid, one_vertex(flat), inverse_ref[0])
    values = gather(smoothed, built(places_of(points, elements), far_hot_ref))
    send_values(sent_ref, FIRST_ROWS, values, peers)
    send_same(sent_ref, FIRST_ROWS, TERMS, part)
    send_same(sent_ref, FIRST_ROWS, TERMS + 1, flat)
    send_rows(sent_ref, FIRST_ROWS, TERMS + 2, points.astype(F32), peers)


def far_maps(received_ref, peers):
    maps = get(received_ref, FIRST_ROWS, TERMS + 1)
    sides = [
        jnp.broadcast_to(get_row(maps, peers, away), (FACE_ROWS, LANES)) for away in (-1, 1)
    ]
    return whole(jnp.concatenate([get_shared(maps, peers)] + sides, axis=0))


def apply(
    rough, smoothed, count, received_ref, flat, maps, far_points, solved, metric_ref, helmholtz_ref,
    first_ref, inner_ref, pair_ref, pairs, points_ref, far_hot_ref, dots, back_ref, local_ref,
    sent_ref,
):
    elements = smoothed.shape[0] // 4
    peers = points_ref.shape[0] - 2 * FACE_ROWS
    far = loaded(places_of(points_ref[...], elements), far_hot_ref)
    near = gather(rough, pairs)
    partners = pair_ref[...]
    partners = jnp.concatenate(halves(partners[1:2]) + halves(partners[0:1]), axis=0)
    counts = (peers, FACE_ROWS, FACE_ROWS, partners.shape[0])
    spread = [
        jnp.broadcast_to(part, (n, LANES)) for part, n in zip((*solved, solved[0]), counts)
    ]
    coarse = prolonged_at(
        jnp.concatenate(spread, axis=0),
        jnp.concatenate([maps, jnp.broadcast_to(flat, partners.shape)], axis=0),
        jnp.concatenate([far_points, partners], axis=0),
        elements,
    )
    split_at = points_ref.shape[0]
    incoming = get_rows(received_ref, count, 0, peers) + coarse[:split_at]
    near = swapped(near) + line(coarse[split_at:])
    count = smoothed.shape[0]
    summed = smoothed + scatter(count, pairs, near) + scatter(count, far, line(incoming))
    back, energy = stiffness(summed, metric_ref, first_ref, inner_ref)
    energy = energy + rows_of(helmholtz_ref[...]) * smoothed * smoothed
    back_ref[...] = back
    local_ref[...] = swapped(gather(back, pairs))
    send_values(sent_ref, ROWS, gather(back, far), peers)
    send_same(sent_ref, ROWS, TERMS, packed(dots + [total_of(energy)]))


def image_of(
    field_ref, back_ref, local_ref, received_ref, helmholtz_ref, pair_ref, pair_hot_ref, points_ref,
    far_hot_ref,
):
    elements = field_ref.shape[0] // 4
    peers = points_ref.shape[0] - 2 * FACE_ROWS
    pairs = loaded(places_of(pair_ref[...], elements), pair_hot_ref)
    far = loaded(places_of(points_ref[...], elements), far_hot_ref)
    incoming = line(get_rows(received_ref, ROWS, 0, peers))
    count = field_ref.shape[0]
    summed = back_ref[...] + scatter(count, pairs, local_ref[...]) + scatter(count, far, incoming)
    return summed + rows_of(helmholtz_ref[...]) * field_ref[...]


def start_kernel(
    received_ref, fields_ref, points_ref, far_hot_ref, pair_ref, metric_ref, helmholtz_ref,
    first_ref, inner_ref,
    smoothed_ref, maps_ref, far_points_ref, back_ref, local_ref, sent_ref, pair_hot_ref,
):
    elements = helmholtz_ref.shape[0]
    peers = points_ref.shape[0] - 2 * FACE_ROWS
    solved = get_solved(received_ref, FIRST_ROWS, peers)
    resid = fields_ref[0 : 4 * elements, :]
    flat = whole(fields_ref[8 * elements : 8 * elements + 1, :])
    rough = fields_ref[4 * elements : 8 * elements, :]
    smoothed = rough + prolonged(solved[0], flat, elements)
    smoothed_ref[...] = smoothed
    maps = far_maps(received_ref, peers)
    maps_ref[...] = maps
    far_points = whole(get_rows(received_ref, FIRST_ROWS, TERMS + 2, peers))
    far_points_ref[...] = far_points
    apply(
        rough, smoothed, FIRST_ROWS, received_ref, flat, maps, far_points, solved, metric_ref,
        helmholtz_ref, first_ref, inner_ref, pair_ref,
        built(places_of(pair_ref[...], elements), pair_hot_ref), points_ref, far_hot_ref,
        [total_of(resid * smoothed)], back_ref, local_ref, sent_ref,
    )


def middle_kernel(
    received_ref, fields_ref, points_ref, far_hot_ref, pair_ref, pair_hot_ref, jacobi_ref, helmholtz_ref,
    inverse_ref, smoothed_ref, back_ref, local_ref,
    image_ref, resid_ref, scalars_ref, sent_ref,
):
    elements = helmholtz_ref.shape[0]
    peers = points_ref.shape[0] - 2 * FACE_ROWS
    dots = jnp.sum(get(received_ref, ROWS, TERMS), axis=0, keepdims=True)
    scalars_ref[...] = dots
    values = unpacked(dots, 2)
    alpha = values[0] / values[1]
    image = image_of(
        smoothed_ref, back_ref, local_ref, received_ref, helmholtz_ref, pair_ref,
        pair_hot_ref, points_ref, far_hot_ref,
    )
    image_ref[...] = image
    resid = fields_ref[0 : 4 * elements, :] - alpha * image
    resid_ref[...] = resid
    vertices = one_vertex(fields_ref[8 * elements : 8 * elements + 1, :])
    part = coarse_part(resid, vertices, inverse_ref[0])
    values = gather(
        rows_of(jacobi_ref[...]) * resid, loaded(places_of(points_ref[...], elements), far_hot_ref),
    )
    send_values(sent_ref, ROWS, values, peers)
    send_same(sent_ref, ROWS, TERMS, part)


def second_kernel(
    received_ref, fields_ref, points_ref, far_hot_ref, pair_ref, pair_hot_ref, resid_ref, image_ref,
    maps_ref, far_points_ref, jacobi_ref, metric_ref, helmholtz_ref, first_ref, inner_ref,
    smoothed_ref, back_ref, local_ref, sent_ref,
):
    elements = helmholtz_ref.shape[0]
    peers = points_ref.shape[0] - 2 * FACE_ROWS
    solved = get_solved(received_ref, ROWS, peers)
    resid = resid_ref[...]
    flat = whole(fields_ref[8 * elements : 8 * elements + 1, :])
    rough = rows_of(jacobi_ref[...]) * resid
    smoothed = rough + prolonged(solved[0], flat, elements)
    smoothed_ref[...] = smoothed
    apply(
        rough, smoothed, ROWS, received_ref, flat, maps_ref[...], far_points_ref[...], solved, metric_ref,
        helmholtz_ref, first_ref, inner_ref, pair_ref,
        loaded(places_of(pair_ref[...], elements), pair_hot_ref), points_ref, far_hot_ref,
        [total_of(resid * smoothed), total_of(image_ref[...] * smoothed)],
        back_ref, local_ref, sent_ref,
    )


def final_kernel(
    received_ref, points_ref, far_hot_ref, pair_ref, pair_hot_ref, old_ref, field_ref, resid_ref, old_image_ref,
    scalars_ref, back_ref, local_ref, helmholtz_ref,
    solution_ref, residual_ref,
):
    before = unpacked(scalars_ref[...], 2)
    now = unpacked(jnp.sum(get(received_ref, ROWS, TERMS), axis=0, keepdims=True), 3)
    alpha = before[0] / before[1]
    beta = now[0] / before[0]
    curved = now[2] + beta * (2.0 * now[1] + beta * before[1])
    step = now[0] / curved
    old = old_ref[...]
    direction = field_ref[...] + beta * old
    solution_ref[...] = wide_of(alpha * old + step * direction)
    image = image_of(
        field_ref, back_ref, local_ref, received_ref, helmholtz_ref, pair_ref,
        pair_hot_ref, points_ref, far_hot_ref,
    )
    image = image + beta * old_image_ref[...]
    residual_ref[...] = wide_of(resid_ref[...] - step * image)


def call(kernel, outs, *args, copied=False):
    space = pl.ANY if copied else pltpu.VMEM
    scratch = [pltpu.VMEM(arg.shape, arg.dtype) for arg in args] if copied else []
    if copied:
        args = [pltpu.with_memory_space_constraint(arg, pltpu.HBM) for arg in args]
    return pl.pallas_call(
        kernel,
        out_shape=[
            jax.ShapeDtypeStruct(*(out if isinstance(out[0], tuple) else (out, F32))) for out in outs
        ],
        in_specs=[pl.BlockSpec(memory_space=space)] * len(args),
        out_specs=[pl.BlockSpec(memory_space=pltpu.VMEM)] * len(outs),
        scratch_shapes=scratch + ([pltpu.SemaphoreType.DMA((len(args),))] if copied else []),
        compiler_params=pltpu.CompilerParams(vmem_limit_bytes=24 * 1024 * 1024),
    )(*args)


def body(
    right_side,
    metric,
    helmholtz,
    jacobi,
    pair_list,
    shared_slots,
    face_points,
    coarse_map,
    coarse_inverse,
):
    peers = lax.axis_size("sub")
    groups = lax.axis_size("grp")
    t = {name: jnp.asarray(value) for name, value in tables().items()}
    elements = right_side.shape[0]
    field = (4 * elements, LANES)
    local = (1, pair_list.shape[0] * pair_list.shape[1])
    points_shape = (peers + 2 * FACE_ROWS, LANES)
    sent_shape = (groups * peers * ROWS, LANES)

    def exchange(sent):
        rows = sent.reshape(groups * peers, 1, -1)
        return lax.all_to_all(rows, ("grp", "sub"), 0, 0, tiled=True).reshape(sent.shape)

    far_hot_shape = (LANES, points_shape[0] * LANES)
    pair_hot_shape = (LANES, local[1])

    sent, fields, points, far_hot = call(
        first_kernel,
        [
            (groups * peers * FIRST_ROWS, LANES),
            (8 * elements + 8, LANES),
            (points_shape, jnp.int32),
            (far_hot_shape, BF16),
        ],
        right_side, jacobi, coarse_inverse, coarse_map, shared_slots, face_points, copied=True,
    )
    smoothed, maps, far_points, back, near, sent, pair_hot = call(
        start_kernel,
        [field, (points_shape, jnp.int32), (points_shape, jnp.int32), field, local, sent_shape,
         (pair_hot_shape, BF16)],
        exchange(sent), fields, points, far_hot, pair_list, metric, helmholtz,
        t["first"], t["inner"],
    )
    image, resid, scalars, sent = call(
        middle_kernel, [field, field, (1, LANES), sent_shape],
        exchange(sent), fields, points, far_hot, pair_list, pair_hot, jacobi, helmholtz, coarse_inverse,
        smoothed, back, near,
    )
    second, back, near, sent = call(
        second_kernel, [field, field, local, sent_shape],
        exchange(sent), fields, points, far_hot, pair_list, pair_hot, resid, image, maps, far_points, jacobi,
        metric, helmholtz, t["first"], t["inner"],
    )
    return tuple(
        call(
            final_kernel, [right_side.shape, right_side.shape],
            exchange(sent), points, far_hot, pair_list, pair_hot, smoothed, second, resid, image, scalars,
            back, near, helmholtz,
        )
    )


def solution(mesh):
    in_specs = (
        P(("grp", "sub"), None),
        P(("grp", "sub"), None),
        P(("grp", "sub"), None),
        P(("grp", "sub"), None),
        P(None, ("grp", "sub")),
        P(("grp", "sub"), None, None),
        P(None, ("grp", "sub")),
        P(None, ("grp", "sub")),
        P("grp", None, None),
    )
    out_specs = (P(("grp", "sub"), None), P(("grp", "sub"), None))
    return jax.shard_map(body, mesh=mesh, in_specs=in_specs, out_specs=out_specs, check_vma=False)
```

```python
import jax
import jax.numpy as jnp
import ml_dtypes
import numpy as np
from jax import lax
from jax.experimental import pallas as pl
from jax.experimental.pallas import tpu as pltpu
from jax.sharding import PartitionSpec as P

NC = 64
POINTS = 512
LANES = 128
STEP = 256
FACE_ROWS = 4
ROWS = 5
FIRST_ROWS = 10
TERMS = FACE_ROWS
F32 = jnp.float32
BF16 = jnp.bfloat16
NT = (((1,), (1,)), ((), ()))


def split_constant(array):
    high = array.astype(ml_dtypes.bfloat16)
    low = (array - high.astype(np.float64)).astype(ml_dtypes.bfloat16)
    return high, low


def tables():
    order_index = np.arange(8)
    colloc = np.cos(np.pi * order_index / 7.0)
    end_weights = (
        np.where((order_index == 0) | (order_index == 7), 2.0, 1.0) * (-1.0) ** order_index
    )
    spacing = colloc[:, None] - colloc[None, :] + np.eye(8)
    raw_matrix = np.outer(end_weights, 1.0 / end_weights) / spacing
    off_part = raw_matrix * (1.0 - np.eye(8))
    derivative = 0.25 * (off_part - np.eye(8) * off_part.sum(axis=1)[:, None])
    along_inner = np.concatenate(
        [np.kron(np.eye(2), np.kron(derivative, np.eye(8))).T, np.kron(np.eye(16), derivative).T],
        axis=1,
    )
    high, low = split_constant(along_inner)
    inner = np.concatenate([high, low], axis=0)

    half = np.arange(LANES) // 64

    def first_rows(matrix):
        rows = []
        for to in range(4):
            for at in range(4):
                rows.append(matrix[2 * to + half, 2 * at + half])
                rows.append(matrix[2 * to + half, 2 * at + 1 - half])
        return np.stack(rows).astype(np.float32)

    return {
        "inner": inner,
        "first": np.concatenate([first_rows(derivative), first_rows(derivative.T)], axis=0),
    }


def split(value):
    high = value.astype(BF16)
    return high, (value - high.astype(F32)).astype(BF16)


def rows_of(wide):
    return jnp.concatenate([wide[:, LANES * c : LANES * (c + 1)] for c in range(4)], axis=0)


def wide_of(rows):
    elements = rows.shape[0] // 4
    return jnp.concatenate([rows[c * elements : (c + 1) * elements] for c in range(4)], axis=1)


def locate(points, elements):
    element = points >> 9
    chunk = (points >> 7) & 3
    row = jnp.where(points < elements * POINTS, chunk * elements + element, 4 * elements)
    return row, points & (LANES - 1)


def one_hot(index, count):
    steps = lax.broadcasted_iota(jnp.int32, (count, index.shape[1]), 0)
    return steps == index


def lane_hot(lane):
    steps = lax.broadcasted_iota(jnp.int32, (LANES, lane.shape[1]), 0).astype(F32).astype(BF16)
    one = jnp.ones(steps.shape, BF16)
    return jnp.where(steps == lane.astype(F32).astype(BF16), one, jnp.zeros_like(one))


def take(values, lanes):
    return jnp.take_along_axis(values, lanes, axis=1, mode="promise_in_bounds")


def gather(field, chunks):
    count = field.shape[0]
    both = jnp.concatenate(split(field), axis=0)
    out = []
    for row, hot in chunks:
        picked = jnp.dot(both, hot, preferred_element_type=F32)
        mine = jnp.where(one_hot(row, count), picked[:count] + picked[count:], 0.0)
        out.append(jnp.sum(mine, axis=0, keepdims=True))
    return out


def scatter(rows, chunks, values):
    total = jnp.zeros((2 * rows, LANES), F32)
    for (row, hot), value in zip(chunks, values):
        steps = lax.broadcasted_iota(jnp.int32, (rows, row.shape[1]), 0).astype(F32).astype(BF16)
        mine = steps == row.astype(F32).astype(BF16)
        parts = [jnp.where(mine, part, jnp.zeros_like(steps)) for part in split(value)]
        total = total + jnp.dot(
            jnp.concatenate(parts, axis=0), hot, preferred_element_type=F32
        )
    return total[:rows] + total[rows:]


def chunked(row, lane):
    return [
        (row[:, at : at + STEP], lane[:, at : at + STEP]) for at in range(0, row.shape[1], STEP)
    ]


def cut(row):
    return [row[:, at : at + STEP] for at in range(0, row.shape[1], STEP)]


def pair_places(pair_ref, elements):
    row, lane = locate(pair_ref[...], elements)
    return chunked(row[0:1], lane[0:1]) + chunked(row[1:2], lane[1:2])


def joined(rows):
    return [
        jnp.concatenate([rows[at : at + 1], rows[at + 1 : at + 2]], axis=1)
        for at in range(0, rows.shape[0], 2)
    ]


def far_places(points, elements):
    row, lane = locate(points, elements)
    return list(zip(joined(row), joined(lane)))


def built(places, hot_ref):
    out = []
    for k, (row, lane) in enumerate(places):
        hot = lane_hot(lane)
        hot_ref[k * LANES : (k + 1) * LANES, :] = hot
        out.append((row, hot))
    return out


def turned(places, hot_ref):
    out = []
    for k, (row, hot) in enumerate(places):
        hot = hot.astype(F32).T.astype(BF16)
        hot_ref[k * STEP : (k + 1) * STEP, :] = hot
        out.append((row, hot))
    return out


def loaded_turned(places, hot_ref):
    return [
        (row, hot_ref[k * STEP : (k + 1) * STEP, :]) for k, (row, lane) in enumerate(places)
    ]


def loaded(places, hot_ref):
    return [
        (row, hot_ref[k * LANES : (k + 1) * LANES, :]) for k, (row, lane) in enumerate(places)
    ]


def halves(wide):
    return [wide[:, at : at + LANES] for at in range(0, wide.shape[1], LANES)]


def own_group(devices, peers, away=0):
    shape = (devices, LANES)
    return lax.broadcasted_iota(jnp.int32, shape, 0) // peers - lax.axis_index("grp") == away


def send_rows(sent_ref, count, at, rows, peers):
    devices = sent_ref.shape[0] // count
    above = own_group(devices, peers, 1)
    shared = jnp.concatenate([rows[:peers]] * (devices // peers), axis=0)
    for r in range(FACE_ROWS):
        down = rows[peers + r : peers + r + 1]
        up = rows[peers + FACE_ROWS + r : peers + FACE_ROWS + r + 1]
        out = jnp.where(above, up, down)
        if r == 0:
            out = jnp.where(own_group(devices, peers), shared, out)
        sent_ref[pl.ds(at + r, devices, count), :] = out


def send_same(sent_ref, count, at, row):
    devices = sent_ref.shape[0] // count
    sent_ref[pl.ds(at, devices, count), :] = jnp.broadcast_to(row, (devices, LANES))


def send_values(sent_ref, count, values, peers):
    rows = jnp.concatenate([row for pair in values for row in halves(pair)], axis=0)
    send_rows(sent_ref, count, 0, rows, peers)


def get(received_ref, count, at):
    return received_ref[pl.ds(at, received_ref.shape[0] // count, count), :]


def get_shared(rows, peers):
    mine = jnp.where(own_group(rows.shape[0], peers), rows, 0.0)
    shared = mine[:peers]
    for g in range(1, rows.shape[0] // peers):
        shared = shared + mine[g * peers : (g + 1) * peers]
    return shared


def get_row(rows, peers, away):
    here = lax.axis_index("grp") * peers + lax.axis_index("sub")
    source = lax.broadcasted_iota(jnp.int32, rows.shape, 0) - here == away * peers
    return jnp.sum(jnp.where(source, rows, 0.0), axis=0, keepdims=True)


def get_rows(received_ref, count, at, peers):
    rows = [get(received_ref, count, at + r) for r in range(FACE_ROWS)]
    faces = [get_row(part, peers, away) for away in (-1, 1) for part in rows]
    return jnp.concatenate([get_shared(rows[0], peers)] + faces, axis=0)


def swapped(values):
    count = len(values) // 2
    return values[count:] + values[:count]


def along_first(field, table_ref, base):
    elements = field.shape[0] // 4
    turned = pltpu.roll(field, 64, axis=1)
    out = []
    for to in range(4):
        total = None
        for at in range(4):
            place = base + 2 * (4 * to + at)
            rows = slice(at * elements, (at + 1) * elements)
            term = (
                table_ref[place : place + 1, :] * field[rows]
                + table_ref[place + 1 : place + 2, :] * turned[rows]
            )
            total = term if total is None else total + term
        out.append(total)
    return jnp.concatenate(out, axis=0)


def stiffness(field, metric_ref, first_ref, inner_ref):
    metric = [rows_of(metric_ref[:, POINTS * d : POINTS * (d + 1)]) for d in range(3)]
    count = field.shape[0]
    grad_first = along_first(field, first_ref, 0)
    high, low = split(field)
    both = jnp.dot(
        jnp.concatenate([high, low], axis=0), inner_ref[:LANES], preferred_element_type=F32
    )
    inner = both[:count] + both[count:]
    inner = inner + jnp.dot(high, inner_ref[LANES:], preferred_element_type=F32)
    flux_first = metric[0] * grad_first
    flux = jnp.concatenate([metric[1], metric[2]], axis=1) * inner
    high, low = split(flux)
    both = lax.dot_general(
        jnp.concatenate([high, low], axis=0), inner_ref[:LANES], NT, preferred_element_type=F32
    )
    back = both[:count] + both[count:]
    back = back + lax.dot_general(high, inner_ref[LANES:], NT, preferred_element_type=F32)
    back = back + along_first(flux_first, first_ref, 32)
    energy = flux * inner
    return back, flux_first * grad_first + energy[:, :LANES] + energy[:, LANES:]


def factors(points):
    nodes = 0.5 * (1.0 + np.cos(np.pi * np.arange(8) / 7.0))
    out = []
    for shift in (6, 3, 0):
        index = (points >> shift) & 7
        near = jnp.full(points.shape, nodes[7], F32)
        far = jnp.full(points.shape, nodes[0], F32)
        for m in range(7):
            near = jnp.where(index == m, float(nodes[m]), near)
            far = jnp.where(index == m, float(nodes[7 - m]), far)
        out.append((near, far))
    return out


def corners(points):
    first, second, third = factors(points)
    return [
        first[q >> 2 & 1] * (second[q >> 1 & 1] * third[q & 1]) for q in range(8)
    ]


def own_corners():
    return corners(lax.broadcasted_iota(jnp.int32, (1, POINTS), 1))


def flat_map(mapped):
    elements = mapped.shape[1]
    shape = (8, 8 * elements)
    lane = lax.broadcasted_iota(jnp.int32, shape, 1)
    padded = jnp.concatenate(
        [mapped.astype(F32), jnp.zeros((8, shape[1] - elements), F32)], axis=1
    )
    wide = take(padded, lane & (elements - 1))
    keep = lax.broadcasted_iota(jnp.int32, shape, 0) == lane // elements
    return jnp.sum(jnp.where(keep, wide, 0.0), axis=0, keepdims=True)


def one_vertex(flat):
    return jnp.where(one_hot(whole(flat), NC), 1.0, 0.0)


def whole(values):
    return (values + 0.5).astype(jnp.int32)


def own_element(elements, width):
    shape = (elements, width)
    return lax.broadcasted_iota(jnp.int32, shape, 0) == (
        lax.broadcasted_iota(jnp.int32, shape, 1) % elements
    )


def own_place(elements, q):
    shape = (elements, 8 * elements)
    lane = lax.broadcasted_iota(jnp.int32, shape, 1)
    return lane == lax.broadcasted_iota(jnp.int32, shape, 0) + q * elements


def coarse_part(field, vertices, inverse):
    elements = field.shape[0] // 4
    flat = jnp.zeros((elements, 8 * elements), F32)
    for q, corner in enumerate(own_corners()):
        inner = None
        for c in range(4):
            term = field[c * elements : (c + 1) * elements] * corner[:, c * LANES : (c + 1) * LANES]
            inner = term if inner is None else inner + term
        flat = jnp.where(own_place(elements, q), jnp.sum(inner, axis=1, keepdims=True), flat)
    flat = jnp.sum(flat, axis=0, keepdims=True)
    part = jnp.sum(vertices * flat, axis=1, keepdims=True)
    part = jnp.sum(inverse * part, axis=0, keepdims=True)
    return jnp.concatenate([part, jnp.zeros((1, LANES - NC), F32)], axis=1)


def get_solved(received_ref, count, peers):
    rows = get(received_ref, count, TERMS)
    return [
        jnp.sum(jnp.where(own_group(rows.shape[0], peers, away), rows, 0.0), axis=0, keepdims=True)
        for away in (0, -1, 1)
    ]


def prolonged(solved, flat, elements):
    shape = (elements, LANES)
    element = lax.broadcasted_iota(jnp.int32, shape, 0)
    at_corner = take(jnp.broadcast_to(solved, shape), jnp.broadcast_to(flat, shape))
    out = [None] * 4
    for q, corner in enumerate(own_corners()):
        value = take(at_corner, element + q * elements)
        for c in range(4):
            term = value * corner[:, c * LANES : (c + 1) * LANES]
            out[c] = term if out[c] is None else out[c] + term
    return jnp.concatenate(out, axis=0)


def prolonged_at(solved, maps, points, elements):
    at_corner = take(solved, maps)
    element = (points >> 9) & (elements - 1)
    total = jnp.zeros(points.shape, F32)
    for q, corner in enumerate(corners(points)):
        total = total + corner * take(at_corner, element + q * elements)
    return total


def total_of(array):
    return jnp.sum(jnp.sum(array, axis=0, keepdims=True), axis=1, keepdims=True)


def packed(values):
    lane = lax.broadcasted_iota(jnp.int32, (1, LANES), 1)
    out = jnp.zeros((1, LANES), F32)
    for k, value in enumerate(values):
        out = jnp.where(lane == k, value, out)
    return out


def unpacked(row, count):
    lane = lax.broadcasted_iota(jnp.int32, row.shape, 1)
    return [
        jnp.sum(jnp.where(lane == k, row, 0.0), axis=1, keepdims=True) for k in range(count)
    ]


def first_kernel(
    right_hbm, jacobi_hbm, inverse_hbm, map_hbm, slot_hbm, face_hbm,
    sent_ref, fields_ref, points_ref, far_hot_ref,
    right_ref, jacobi_ref, inverse_ref, map_ref, slot_ref, face_ref, sems,
):
    copies = []
    for k, (source, target) in enumerate(
        (
            (face_hbm, face_ref),
            (slot_hbm, slot_ref),
            (right_hbm, right_ref),
            (jacobi_hbm, jacobi_ref),
            (map_hbm, map_ref),
            (inverse_hbm, inverse_ref),
        )
    ):
        copy = pltpu.make_async_copy(source, target, sems.at[k])
        copy.start()
        copies.append(copy)
    for copy in copies:
        copy.wait()
    elements = right_ref.shape[0]
    peers = slot_ref.shape[1]
    faces = face_ref[...]
    faces = jnp.concatenate(halves(faces[0:1]) + halves(faces[1:2]), axis=0)
    points = jnp.concatenate([slot_ref[0], faces], axis=0)
    points_ref[...] = points
    resid = rows_of(right_ref[...])
    flat = flat_map(map_ref[...])
    smoothed = rows_of(jacobi_ref[...]) * resid
    fields_ref[0 : 4 * elements, :] = resid
    fields_ref[4 * elements : 8 * elements, :] = smoothed
    fields_ref[8 * elements :, :] = jnp.broadcast_to(flat, (8, LANES))
    part = coarse_part(resid, one_vertex(flat), inverse_ref[0])
    values = gather(smoothed, built(far_places(points, elements), far_hot_ref))
    send_values(sent_ref, FIRST_ROWS, values, peers)
    send_same(sent_ref, FIRST_ROWS, TERMS, part)
    send_same(sent_ref, FIRST_ROWS, TERMS + 1, flat)
    send_rows(sent_ref, FIRST_ROWS, TERMS + 2, points.astype(F32), peers)


def far_maps(received_ref, peers):
    maps = get(received_ref, FIRST_ROWS, TERMS + 1)
    sides = [
        jnp.broadcast_to(get_row(maps, peers, away), (FACE_ROWS, LANES)) for away in (-1, 1)
    ]
    return whole(jnp.concatenate([get_shared(maps, peers)] + sides, axis=0))


def apply(
    rough, smoothed, count, received_ref, flat, maps, far_points, solved, metric_ref, helmholtz_ref,
    first_ref, inner_ref, pair_ref, pairs, points_ref, far, turned_places, dots, back_ref,
    local_ref, sent_ref,
):
    elements = smoothed.shape[0] // 4
    peers = points_ref.shape[0] - 2 * FACE_ROWS
    near = gather(rough, pairs)
    partners = pair_ref[...]
    partners = jnp.concatenate(halves(partners[1:2]) + halves(partners[0:1]), axis=0)
    counts = (peers, FACE_ROWS, FACE_ROWS, partners.shape[0])
    spread = [
        jnp.broadcast_to(part, (n, LANES)) for part, n in zip((*solved, solved[0]), counts)
    ]
    coarse = prolonged_at(
        jnp.concatenate(spread, axis=0),
        jnp.concatenate([maps, jnp.broadcast_to(flat, partners.shape)], axis=0),
        jnp.concatenate([far_points, partners], axis=0),
        elements,
    )
    split_at = points_ref.shape[0]
    incoming = get_rows(received_ref, count, 0, peers) + coarse[:split_at]
    values = [value + more for value, more in zip(swapped(near), joined(coarse[split_at:]))]
    values = values + joined(incoming)
    summed = smoothed + scatter(smoothed.shape[0], turned_places, values)
    back, energy = stiffness(summed, metric_ref, first_ref, inner_ref)
    energy = energy + rows_of(helmholtz_ref[...]) * smoothed * smoothed
    back_ref[...] = back
    values = gather(back, pairs + far)
    near = swapped(values[: len(pairs)])
    for k, value in enumerate(near):
        local_ref[0:1, k * STEP : (k + 1) * STEP] = value
    send_values(sent_ref, ROWS, values[len(pairs) :], peers)
    send_same(sent_ref, ROWS, TERMS, packed(dots + [total_of(energy)]))


def image_of(
    field_ref, back_ref, local_ref, received_ref, helmholtz_ref, pair_ref, points_ref, turned_ref,
):
    elements = field_ref.shape[0] // 4
    peers = points_ref.shape[0] - 2 * FACE_ROWS
    chunks = pair_places(pair_ref, elements) + far_places(points_ref[...], elements)
    chunks = loaded_turned(chunks, turned_ref)
    values = cut(local_ref[...]) + joined(get_rows(received_ref, ROWS, 0, peers))
    summed = back_ref[...] + scatter(field_ref.shape[0], chunks, values)
    return summed + rows_of(helmholtz_ref[...]) * field_ref[...]


def start_kernel(
    received_ref, fields_ref, points_ref, far_hot_ref, pair_ref, metric_ref, helmholtz_ref,
    first_ref, inner_ref,
    smoothed_ref, maps_ref, far_points_ref, back_ref, local_ref, sent_ref, pair_hot_ref, turned_ref,
):
    elements = helmholtz_ref.shape[0]
    peers = points_ref.shape[0] - 2 * FACE_ROWS
    solved = get_solved(received_ref, FIRST_ROWS, peers)
    resid = fields_ref[0 : 4 * elements, :]
    flat = whole(fields_ref[8 * elements : 8 * elements + 1, :])
    rough = fields_ref[4 * elements : 8 * elements, :]
    smoothed = rough + prolonged(solved[0], flat, elements)
    smoothed_ref[...] = smoothed
    maps = far_maps(received_ref, peers)
    maps_ref[...] = maps
    far_points = whole(get_rows(received_ref, FIRST_ROWS, TERMS + 2, peers))
    far_points_ref[...] = far_points
    pairs = built(pair_places(pair_ref, elements), pair_hot_ref)
    far = loaded(far_places(points_ref[...], elements), far_hot_ref)
    apply(
        rough, smoothed, FIRST_ROWS, received_ref, flat, maps, far_points, solved, metric_ref,
        helmholtz_ref, first_ref, inner_ref, pair_ref,
        pairs, points_ref, far, turned(pairs + far, turned_ref),
        [total_of(resid * smoothed)], back_ref, local_ref, sent_ref,
    )


def middle_kernel(
    received_ref, fields_ref, points_ref, far_hot_ref, pair_ref, turned_ref, jacobi_ref, helmholtz_ref,
    inverse_ref, smoothed_ref, back_ref, local_ref,
    image_ref, resid_ref, scalars_ref, sent_ref,
):
    elements = helmholtz_ref.shape[0]
    peers = points_ref.shape[0] - 2 * FACE_ROWS
    dots = jnp.sum(get(received_ref, ROWS, TERMS), axis=0, keepdims=True)
    scalars_ref[...] = dots
    values = unpacked(dots, 2)
    alpha = values[0] / values[1]
    image = image_of(
        smoothed_ref, back_ref, local_ref, received_ref, helmholtz_ref, pair_ref,
        points_ref, turned_ref,
    )
    image_ref[...] = image
    resid = fields_ref[0 : 4 * elements, :] - alpha * image
    resid_ref[...] = resid
    vertices = one_vertex(fields_ref[8 * elements : 8 * elements + 1, :])
    part = coarse_part(resid, vertices, inverse_ref[0])
    values = gather(
        rows_of(jacobi_ref[...]) * resid, loaded(far_places(points_ref[...], elements), far_hot_ref),
    )
    send_values(sent_ref, ROWS, values, peers)
    send_same(sent_ref, ROWS, TERMS, part)


def second_kernel(
    received_ref, fields_ref, points_ref, far_hot_ref, pair_ref, pair_hot_ref, turned_ref, resid_ref, image_ref,
    maps_ref, far_points_ref, jacobi_ref, metric_ref, helmholtz_ref, first_ref, inner_ref,
    smoothed_ref, back_ref, local_ref, sent_ref,
):
    elements = helmholtz_ref.shape[0]
    peers = points_ref.shape[0] - 2 * FACE_ROWS
    solved = get_solved(received_ref, ROWS, peers)
    resid = resid_ref[...]
    flat = whole(fields_ref[8 * elements : 8 * elements + 1, :])
    rough = rows_of(jacobi_ref[...]) * resid
    smoothed = rough + prolonged(solved[0], flat, elements)
    smoothed_ref[...] = smoothed
    pairs = loaded(pair_places(pair_ref, elements), pair_hot_ref)
    far = loaded(far_places(points_ref[...], elements), far_hot_ref)
    apply(
        rough, smoothed, ROWS, received_ref, flat, maps_ref[...], far_points_ref[...], solved, metric_ref,
        helmholtz_ref, first_ref, inner_ref, pair_ref,
        pairs, points_ref, far, loaded_turned(pairs + far, turned_ref),
        [total_of(resid * smoothed), total_of(image_ref[...] * smoothed)],
        back_ref, local_ref, sent_ref,
    )


def final_kernel(
    received_ref, points_ref, pair_ref, turned_ref, old_ref, field_ref, resid_ref, old_image_ref,
    scalars_ref, back_ref, local_ref, helmholtz_ref,
    solution_ref, residual_ref,
):
    before = unpacked(scalars_ref[...], 2)
    now = unpacked(jnp.sum(get(received_ref, ROWS, TERMS), axis=0, keepdims=True), 3)
    alpha = before[0] / before[1]
    beta = now[0] / before[0]
    curved = now[2] + beta * (2.0 * now[1] + beta * before[1])
    step = now[0] / curved
    old = old_ref[...]
    direction = field_ref[...] + beta * old
    solution_ref[...] = wide_of(alpha * old + step * direction)
    image = image_of(
        field_ref, back_ref, local_ref, received_ref, helmholtz_ref, pair_ref,
        points_ref, turned_ref,
    )
    image = image + beta * old_image_ref[...]
    residual_ref[...] = wide_of(resid_ref[...] - step * image)


def call(kernel, outs, *args, copied=False):
    space = pl.ANY if copied else pltpu.VMEM
    scratch = [pltpu.VMEM(arg.shape, arg.dtype) for arg in args] if copied else []
    if copied:
        args = [pltpu.with_memory_space_constraint(arg, pltpu.HBM) for arg in args]
    return pl.pallas_call(
        kernel,
        out_shape=[
            jax.ShapeDtypeStruct(*(out if isinstance(out[0], tuple) else (out, F32))) for out in outs
        ],
        in_specs=[pl.BlockSpec(memory_space=space)] * len(args),
        out_specs=[pl.BlockSpec(memory_space=pltpu.VMEM)] * len(outs),
        scratch_shapes=scratch + ([pltpu.SemaphoreType.DMA((len(args),))] if copied else []),
        compiler_params=pltpu.CompilerParams(vmem_limit_bytes=24 * 1024 * 1024),
    )(*args)


def body(
    right_side,
    metric,
    helmholtz,
    jacobi,
    pair_list,
    shared_slots,
    face_points,
    coarse_map,
    coarse_inverse,
):
    peers = lax.axis_size("sub")
    groups = lax.axis_size("grp")
    t = {name: jnp.asarray(value) for name, value in tables().items()}
    elements = right_side.shape[0]
    field = (4 * elements, LANES)
    local = (1, pair_list.shape[0] * pair_list.shape[1])
    points_shape = (peers + 2 * FACE_ROWS, LANES)
    sent_shape = (groups * peers * ROWS, LANES)

    def exchange(sent):
        rows = sent.reshape(groups * peers, 1, -1)
        return lax.all_to_all(rows, ("grp", "sub"), 0, 0, tiled=True).reshape(sent.shape)

    far_hot_shape = (points_shape[0] * LANES // 2, STEP)
    pair_hot_shape = (local[1] * LANES // STEP, STEP)
    turned_shape = (local[1] + points_shape[0] * LANES, LANES)

    sent, fields, points, far_hot = call(
        first_kernel,
        [
            (groups * peers * FIRST_ROWS, LANES),
            (8 * elements + 8, LANES),
            (points_shape, jnp.int32),
            (far_hot_shape, BF16),
        ],
        right_side, jacobi, coarse_inverse, coarse_map, shared_slots, face_points, copied=True,
    )
    smoothed, maps, far_points, back, near, sent, pair_hot, turned_hot = call(
        start_kernel,
        [field, (points_shape, jnp.int32), (points_shape, jnp.int32), field, local, sent_shape,
         (pair_hot_shape, BF16), (turned_shape, BF16)],
        exchange(sent), fields, points, far_hot, pair_list, metric, helmholtz,
        t["first"], t["inner"],
    )
    image, resid, scalars, sent = call(
        middle_kernel, [field, field, (1, LANES), sent_shape],
        exchange(sent), fields, points, far_hot, pair_list, turned_hot, jacobi, helmholtz, coarse_inverse,
        smoothed, back, near,
    )
    second, back, near, sent = call(
        second_kernel, [field, field, local, sent_shape],
        exchange(sent), fields, points, far_hot, pair_list, pair_hot, turned_hot, resid, image, maps, far_points, jacobi,
        metric, helmholtz, t["first"], t["inner"],
    )
    return tuple(
        call(
            final_kernel, [right_side.shape, right_side.shape],
            exchange(sent), points, pair_list, turned_hot, smoothed, second, resid, image, scalars,
            back, near, helmholtz,
        )
    )


def solution(mesh):
    in_specs = (
        P(("grp", "sub"), None),
        P(("grp", "sub"), None),
        P(("grp", "sub"), None),
        P(("grp", "sub"), None),
        P(None, ("grp", "sub")),
        P(("grp", "sub"), None, None),
        P(None, ("grp", "sub")),
        P(None, ("grp", "sub")),
        P("grp", None, None),
    )
    out_specs = (P(("grp", "sub"), None), P(("grp", "sub"), None))
    return jax.shard_map(body, mesh=mesh, in_specs=in_specs, out_specs=out_specs, check_vma=False)
```

```python
import jax
import jax.numpy as jnp
import ml_dtypes
import numpy as np
from jax import lax
from jax.experimental import pallas as pl
from jax.experimental.pallas import tpu as pltpu
from jax.sharding import PartitionSpec as P

NC = 64
POINTS = 512
LANES = 128
STEP = 256
FACE_ROWS = 4
ROWS = 5
FIRST_ROWS = 10
TERMS = FACE_ROWS
F32 = jnp.float32
BF16 = jnp.bfloat16
NT = (((1,), (1,)), ((), ()))


def split_constant(array):
    high = array.astype(ml_dtypes.bfloat16)
    low = (array - high.astype(np.float64)).astype(ml_dtypes.bfloat16)
    return high, low


def tables():
    order_index = np.arange(8)
    colloc = np.cos(np.pi * order_index / 7.0)
    end_weights = (
        np.where((order_index == 0) | (order_index == 7), 2.0, 1.0) * (-1.0) ** order_index
    )
    spacing = colloc[:, None] - colloc[None, :] + np.eye(8)
    raw_matrix = np.outer(end_weights, 1.0 / end_weights) / spacing
    off_part = raw_matrix * (1.0 - np.eye(8))
    derivative = 0.25 * (off_part - np.eye(8) * off_part.sum(axis=1)[:, None])
    along_inner = np.concatenate(
        [np.kron(np.eye(2), np.kron(derivative, np.eye(8))).T, np.kron(np.eye(16), derivative).T],
        axis=1,
    )
    high, low = split_constant(along_inner)
    inner = np.concatenate([high, low], axis=0)

    half = np.arange(LANES) // 64

    def first_rows(matrix):
        rows = []
        for to in range(4):
            for at in range(4):
                rows.append(matrix[2 * to + half, 2 * at + half])
                rows.append(matrix[2 * to + half, 2 * at + 1 - half])
        return np.stack(rows).astype(np.float32)

    return {
        "inner": inner,
        "first": np.concatenate([first_rows(derivative), first_rows(derivative.T)], axis=0),
    }


def split(value):
    high = value.astype(BF16)
    return high, (value - high.astype(F32)).astype(BF16)


def rows_of(wide):
    return jnp.concatenate([wide[:, LANES * c : LANES * (c + 1)] for c in range(4)], axis=0)


def wide_of(rows):
    elements = rows.shape[0] // 4
    return jnp.concatenate([rows[c * elements : (c + 1) * elements] for c in range(4)], axis=1)


def locate(points, elements):
    element = points >> 9
    chunk = (points >> 7) & 3
    row = jnp.where(points < elements * POINTS, chunk * elements + element, 4 * elements)
    return row, points & (LANES - 1)


def one_hot(index, count):
    steps = lax.broadcasted_iota(jnp.int32, (count, index.shape[1]), 0)
    return steps == index


def lane_hot(lane):
    steps = lax.broadcasted_iota(jnp.int32, (LANES, lane.shape[1]), 0).astype(F32).astype(BF16)
    one = jnp.ones(steps.shape, BF16)
    return jnp.where(steps == lane.astype(F32).astype(BF16), one, jnp.zeros_like(one))


def take(values, lanes):
    return jnp.take_along_axis(values, lanes, axis=1, mode="promise_in_bounds")


def gather(field, chunks):
    count = field.shape[0]
    both = jnp.concatenate(split(field), axis=0)
    out = []
    for row, hot in chunks:
        picked = jnp.dot(both, hot, preferred_element_type=F32)
        mine = jnp.where(one_hot(row, count), picked[:count] + picked[count:], 0.0)
        out.append(jnp.sum(mine, axis=0, keepdims=True))
    return out


def scatter(rows, chunks, values):
    total = jnp.zeros((2 * rows, LANES), F32)
    for (row, hot), value in zip(chunks, values):
        steps = lax.broadcasted_iota(jnp.int32, (rows, row.shape[1]), 0).astype(F32).astype(BF16)
        mine = steps == row.astype(F32).astype(BF16)
        parts = [jnp.where(mine, part, jnp.zeros_like(steps)) for part in split(value)]
        total = total + lax.dot_general(
            jnp.concatenate(parts, axis=0), hot, NT, preferred_element_type=F32
        )
    return total[:rows] + total[rows:]


def chunked(row, lane):
    return [
        (row[:, at : at + STEP], lane[:, at : at + STEP]) for at in range(0, row.shape[1], STEP)
    ]


def cut(row):
    return [row[:, at : at + STEP] for at in range(0, row.shape[1], STEP)]


def pair_places(pair_ref, elements):
    row, lane = locate(pair_ref[...], elements)
    return chunked(row[0:1], lane[0:1]) + chunked(row[1:2], lane[1:2])


def joined(rows):
    return [
        jnp.concatenate([rows[at : at + 1], rows[at + 1 : at + 2]], axis=1)
        for at in range(0, rows.shape[0], 2)
    ]


def far_places(points, elements):
    row, lane = locate(points, elements)
    return list(zip(joined(row), joined(lane)))


def built(places, hot_ref):
    out = []
    for k, (row, lane) in enumerate(places):
        hot = lane_hot(lane)
        hot_ref[k * LANES : (k + 1) * LANES, :] = hot
        out.append((row, hot))
    return out


def loaded(places, hot_ref):
    return [
        (row, hot_ref[k * LANES : (k + 1) * LANES, :]) for k, (row, lane) in enumerate(places)
    ]


def halves(wide):
    return [wide[:, at : at + LANES] for at in range(0, wide.shape[1], LANES)]


def own_group(devices, peers, away=0):
    shape = (devices, LANES)
    return lax.broadcasted_iota(jnp.int32, shape, 0) // peers - lax.axis_index("grp") == away


def send_rows(sent_ref, count, at, rows, peers):
    devices = sent_ref.shape[0] // count
    above = own_group(devices, peers, 1)
    shared = jnp.concatenate([rows[:peers]] * (devices // peers), axis=0)
    for r in range(FACE_ROWS):
        down = rows[peers + r : peers + r + 1]
        up = rows[peers + FACE_ROWS + r : peers + FACE_ROWS + r + 1]
        out = jnp.where(above, up, down)
        if r == 0:
            out = jnp.where(own_group(devices, peers), shared, out)
        sent_ref[pl.ds(at + r, devices, count), :] = out


def send_same(sent_ref, count, at, row):
    devices = sent_ref.shape[0] // count
    sent_ref[pl.ds(at, devices, count), :] = jnp.broadcast_to(row, (devices, LANES))


def send_values(sent_ref, count, values, peers):
    rows = jnp.concatenate([row for pair in values for row in halves(pair)], axis=0)
    send_rows(sent_ref, count, 0, rows, peers)


def get(received_ref, count, at):
    return received_ref[pl.ds(at, received_ref.shape[0] // count, count), :]


def inside(received_ref, count, peers, away):
    groups = received_ref.shape[0] // (count * peers)
    group = lax.axis_index("grp") + away
    kept = jnp.clip(group, 0, groups - 1)
    return kept, jnp.where(group == kept, 1.0, 0.0)


def get_group(received_ref, count, at, peers, away=0):
    group, kept = inside(received_ref, count, peers, away)
    return received_ref[pl.ds(group * (peers * count) + at, peers, count), :] * kept


def get_side(received_ref, count, at, rows, peers, away):
    group, kept = inside(received_ref, count, peers, away)
    place = group * peers + lax.axis_index("sub")
    return received_ref[pl.ds(place * count + at, rows), :] * kept


def get_rows(received_ref, count, at, peers):
    sides = [get_side(received_ref, count, at, FACE_ROWS, peers, away) for away in (-1, 1)]
    return jnp.concatenate([get_group(received_ref, count, at, peers)] + sides, axis=0)


def swapped(values):
    count = len(values) // 2
    return values[count:] + values[:count]


def along_first(field, table_ref, base):
    elements = field.shape[0] // 4
    turned = pltpu.roll(field, 64, axis=1)
    out = []
    for to in range(4):
        total = None
        for at in range(4):
            place = base + 2 * (4 * to + at)
            rows = slice(at * elements, (at + 1) * elements)
            term = (
                table_ref[place : place + 1, :] * field[rows]
                + table_ref[place + 1 : place + 2, :] * turned[rows]
            )
            total = term if total is None else total + term
        out.append(total)
    return jnp.concatenate(out, axis=0)


def stiffness(field, metric_ref, first_ref, inner_ref):
    metric = [rows_of(metric_ref[:, POINTS * d : POINTS * (d + 1)]) for d in range(3)]
    count = field.shape[0]
    grad_first = along_first(field, first_ref, 0)
    high, low = split(field)
    both = jnp.dot(
        jnp.concatenate([high, low], axis=0), inner_ref[:LANES], preferred_element_type=F32
    )
    inner = both[:count] + both[count:]
    inner = inner + jnp.dot(high, inner_ref[LANES:], preferred_element_type=F32)
    flux_first = metric[0] * grad_first
    flux = jnp.concatenate([metric[1], metric[2]], axis=1) * inner
    high, low = split(flux)
    both = lax.dot_general(
        jnp.concatenate([high, low], axis=0), inner_ref[:LANES], NT, preferred_element_type=F32
    )
    back = both[:count] + both[count:]
    back = back + lax.dot_general(high, inner_ref[LANES:], NT, preferred_element_type=F32)
    back = back + along_first(flux_first, first_ref, 32)
    energy = flux * inner
    return back, flux_first * grad_first + energy[:, :LANES] + energy[:, LANES:]


def factors(points):
    nodes = 0.5 * (1.0 + np.cos(np.pi * np.arange(8) / 7.0))
    out = []
    for shift in (6, 3, 0):
        index = (points >> shift) & 7
        near = jnp.full(points.shape, nodes[7], F32)
        far = jnp.full(points.shape, nodes[0], F32)
        for m in range(7):
            near = jnp.where(index == m, float(nodes[m]), near)
            far = jnp.where(index == m, float(nodes[7 - m]), far)
        out.append((near, far))
    return out


def corners(points):
    first, second, third = factors(points)
    return [
        first[q >> 2 & 1] * (second[q >> 1 & 1] * third[q & 1]) for q in range(8)
    ]


def own_corners():
    return corners(lax.broadcasted_iota(jnp.int32, (1, POINTS), 1))


def flat_map(mapped):
    elements = mapped.shape[1]
    shape = (8, 8 * elements)
    lane = lax.broadcasted_iota(jnp.int32, shape, 1)
    padded = jnp.concatenate(
        [mapped.astype(F32), jnp.zeros((8, shape[1] - elements), F32)], axis=1
    )
    wide = take(padded, lane & (elements - 1))
    keep = lax.broadcasted_iota(jnp.int32, shape, 0) == lane // elements
    return jnp.sum(jnp.where(keep, wide, 0.0), axis=0, keepdims=True)


def one_vertex(flat):
    return jnp.where(one_hot(whole(flat), NC), 1.0, 0.0)


def whole(values):
    return (values + 0.5).astype(jnp.int32)


def own_element(elements, width):
    shape = (elements, width)
    return lax.broadcasted_iota(jnp.int32, shape, 0) == (
        lax.broadcasted_iota(jnp.int32, shape, 1) % elements
    )


def own_place(elements, q):
    shape = (elements, 8 * elements)
    lane = lax.broadcasted_iota(jnp.int32, shape, 1)
    return lane == lax.broadcasted_iota(jnp.int32, shape, 0) + q * elements


def coarse_part(field, vertices, inverse):
    elements = field.shape[0] // 4
    flat = jnp.zeros((elements, 8 * elements), F32)
    for q, corner in enumerate(own_corners()):
        inner = None
        for c in range(4):
            term = field[c * elements : (c + 1) * elements] * corner[:, c * LANES : (c + 1) * LANES]
            inner = term if inner is None else inner + term
        flat = jnp.where(own_place(elements, q), jnp.sum(inner, axis=1, keepdims=True), flat)
    flat = jnp.sum(flat, axis=0, keepdims=True)
    part = jnp.sum(vertices * flat, axis=1, keepdims=True)
    part = jnp.sum(inverse * part, axis=0, keepdims=True)
    return jnp.concatenate([part, jnp.zeros((1, LANES - NC), F32)], axis=1)


def get_solved(received_ref, count, peers):
    return [
        jnp.sum(get_group(received_ref, count, TERMS, peers, away), axis=0, keepdims=True)
        for away in (0, -1, 1)
    ]


def prolonged(solved, flat, elements):
    shape = (elements, LANES)
    element = lax.broadcasted_iota(jnp.int32, shape, 0)
    at_corner = take(jnp.broadcast_to(solved, shape), jnp.broadcast_to(flat, shape))
    out = [None] * 4
    for q, corner in enumerate(own_corners()):
        value = take(at_corner, element + q * elements)
        for c in range(4):
            term = value * corner[:, c * LANES : (c + 1) * LANES]
            out[c] = term if out[c] is None else out[c] + term
    return jnp.concatenate(out, axis=0)


def prolonged_at(solved, maps, points, elements):
    at_corner = take(solved, maps)
    element = (points >> 9) & (elements - 1)
    total = jnp.zeros(points.shape, F32)
    for q, corner in enumerate(corners(points)):
        total = total + corner * take(at_corner, element + q * elements)
    return total


def total_of(array):
    return jnp.sum(jnp.sum(array, axis=0, keepdims=True), axis=1, keepdims=True)


def packed(values):
    lane = lax.broadcasted_iota(jnp.int32, (1, LANES), 1)
    out = jnp.zeros((1, LANES), F32)
    for k, value in enumerate(values):
        out = jnp.where(lane == k, value, out)
    return out


def unpacked(row, count):
    lane = lax.broadcasted_iota(jnp.int32, row.shape, 1)
    return [
        jnp.sum(jnp.where(lane == k, row, 0.0), axis=1, keepdims=True) for k in range(count)
    ]


def first_kernel(
    right_hbm, jacobi_hbm, inverse_hbm, map_hbm, slot_hbm, face_hbm,
    sent_ref, fields_ref, points_ref, far_hot_ref,
    right_ref, jacobi_ref, inverse_ref, map_ref, slot_ref, face_ref, sems,
):
    copies = []
    for k, (source, target) in enumerate(
        (
            (face_hbm, face_ref),
            (slot_hbm, slot_ref),
            (right_hbm, right_ref),
            (jacobi_hbm, jacobi_ref),
            (map_hbm, map_ref),
            (inverse_hbm, inverse_ref),
        )
    ):
        copy = pltpu.make_async_copy(source, target, sems.at[k])
        copy.start()
        copies.append(copy)
    elements = right_ref.shape[0]
    peers = slot_ref.shape[1]
    for copy in copies[:2]:
        copy.wait()
    faces = face_ref[...]
    faces = jnp.concatenate(halves(faces[0:1]) + halves(faces[1:2]), axis=0)
    points = jnp.concatenate([slot_ref[0], faces], axis=0)
    points_ref[...] = points
    places = built(far_places(points, elements), far_hot_ref)
    send_rows(sent_ref, FIRST_ROWS, TERMS + 2, points.astype(F32), peers)
    for copy in copies[2:]:
        copy.wait()
    resid = rows_of(right_ref[...])
    flat = flat_map(map_ref[...])
    smoothed = rows_of(jacobi_ref[...]) * resid
    fields_ref[0 : 4 * elements, :] = resid
    fields_ref[4 * elements : 8 * elements, :] = smoothed
    fields_ref[8 * elements :, :] = jnp.broadcast_to(flat, (8, LANES))
    part = coarse_part(resid, one_vertex(flat), inverse_ref[0])
    values = gather(smoothed, places)
    send_values(sent_ref, FIRST_ROWS, values, peers)
    send_same(sent_ref, FIRST_ROWS, TERMS, part)
    send_same(sent_ref, FIRST_ROWS, TERMS + 1, flat)


def far_maps(received_ref, peers):
    own = get_group(received_ref, FIRST_ROWS, TERMS + 1, peers)
    sides = [
        jnp.broadcast_to(
            get_side(received_ref, FIRST_ROWS, TERMS + 1, 1, peers, away), (FACE_ROWS, LANES)
        )
        for away in (-1, 1)
    ]
    return whole(jnp.concatenate([own] + sides, axis=0))


def apply(
    rough, smoothed, count, received_ref, flat, maps, far_points, solved, metric_ref, helmholtz_ref,
    first_ref, inner_ref, pair_ref, pairs, points_ref, far_hot_ref, dots, back_ref, local_ref,
    sent_ref,
):
    elements = smoothed.shape[0] // 4
    peers = points_ref.shape[0] - 2 * FACE_ROWS
    far = loaded(far_places(points_ref[...], elements), far_hot_ref)
    near = gather(rough, pairs)
    partners = pair_ref[...]
    partners = jnp.concatenate(halves(partners[1:2]) + halves(partners[0:1]), axis=0)
    counts = (peers, FACE_ROWS, FACE_ROWS, partners.shape[0])
    spread = [
        jnp.broadcast_to(part, (n, LANES)) for part, n in zip((*solved, solved[0]), counts)
    ]
    coarse = prolonged_at(
        jnp.concatenate(spread, axis=0),
        jnp.concatenate([maps, jnp.broadcast_to(flat, partners.shape)], axis=0),
        jnp.concatenate([far_points, partners], axis=0),
        elements,
    )
    split_at = points_ref.shape[0]
    incoming = get_rows(received_ref, count, 0, peers) + coarse[:split_at]
    values = [value + more for value, more in zip(swapped(near), joined(coarse[split_at:]))]
    values = values + joined(incoming)
    summed = smoothed + scatter(smoothed.shape[0], pairs + far, values)
    back, energy = stiffness(summed, metric_ref, first_ref, inner_ref)
    energy = energy + rows_of(helmholtz_ref[...]) * smoothed * smoothed
    back_ref[...] = back
    values = gather(back, pairs + far)
    near = swapped(values[: len(pairs)])
    for k, value in enumerate(near):
        local_ref[0:1, k * STEP : (k + 1) * STEP] = value
    send_values(sent_ref, ROWS, values[len(pairs) :], peers)
    send_same(sent_ref, ROWS, TERMS, packed(dots + [total_of(energy)]))


def image_of(
    field_ref, back_ref, local_ref, received_ref, helmholtz_ref, pair_ref, pair_hot_ref, points_ref,
    far_hot_ref,
):
    elements = field_ref.shape[0] // 4
    peers = points_ref.shape[0] - 2 * FACE_ROWS
    chunks = loaded(pair_places(pair_ref, elements), pair_hot_ref)
    chunks = chunks + loaded(far_places(points_ref[...], elements), far_hot_ref)
    values = cut(local_ref[...]) + joined(get_rows(received_ref, ROWS, 0, peers))
    summed = back_ref[...] + scatter(field_ref.shape[0], chunks, values)
    return summed + rows_of(helmholtz_ref[...]) * field_ref[...]


def start_kernel(
    received_ref, fields_ref, points_ref, far_hot_ref, pair_ref, metric_ref, helmholtz_ref,
    first_ref, inner_ref,
    smoothed_ref, maps_ref, far_points_ref, back_ref, local_ref, sent_ref, pair_hot_ref,
):
    elements = helmholtz_ref.shape[0]
    peers = points_ref.shape[0] - 2 * FACE_ROWS
    solved = get_solved(received_ref, FIRST_ROWS, peers)
    resid = fields_ref[0 : 4 * elements, :]
    flat = whole(fields_ref[8 * elements : 8 * elements + 1, :])
    rough = fields_ref[4 * elements : 8 * elements, :]
    smoothed = rough + prolonged(solved[0], flat, elements)
    smoothed_ref[...] = smoothed
    maps = far_maps(received_ref, peers)
    maps_ref[...] = maps
    far_points = whole(get_rows(received_ref, FIRST_ROWS, TERMS + 2, peers))
    far_points_ref[...] = far_points
    apply(
        rough, smoothed, FIRST_ROWS, received_ref, flat, maps, far_points, solved, metric_ref,
        helmholtz_ref, first_ref, inner_ref, pair_ref,
        built(pair_places(pair_ref, elements), pair_hot_ref), points_ref, far_hot_ref,
        [total_of(resid * smoothed)], back_ref, local_ref, sent_ref,
    )


def middle_kernel(
    received_ref, fields_ref, points_ref, far_hot_ref, pair_ref, pair_hot_ref, jacobi_ref, helmholtz_ref,
    inverse_ref, smoothed_ref, back_ref, local_ref,
    image_ref, resid_ref, scalars_ref, sent_ref,
):
    elements = helmholtz_ref.shape[0]
    peers = points_ref.shape[0] - 2 * FACE_ROWS
    dots = jnp.sum(get(received_ref, ROWS, TERMS), axis=0, keepdims=True)
    scalars_ref[...] = dots
    values = unpacked(dots, 2)
    alpha = values[0] / values[1]
    image = image_of(
        smoothed_ref, back_ref, local_ref, received_ref, helmholtz_ref, pair_ref,
        pair_hot_ref, points_ref, far_hot_ref,
    )
    image_ref[...] = image
    resid = fields_ref[0 : 4 * elements, :] - alpha * image
    resid_ref[...] = resid
    vertices = one_vertex(fields_ref[8 * elements : 8 * elements + 1, :])
    part = coarse_part(resid, vertices, inverse_ref[0])
    values = gather(
        rows_of(jacobi_ref[...]) * resid, loaded(far_places(points_ref[...], elements), far_hot_ref),
    )
    send_values(sent_ref, ROWS, values, peers)
    send_same(sent_ref, ROWS, TERMS, part)


def second_kernel(
    received_ref, fields_ref, points_ref, far_hot_ref, pair_ref, pair_hot_ref, resid_ref, image_ref,
    maps_ref, far_points_ref, jacobi_ref, metric_ref, helmholtz_ref, first_ref, inner_ref,
    smoothed_ref, back_ref, local_ref, sent_ref,
):
    elements = helmholtz_ref.shape[0]
    peers = points_ref.shape[0] - 2 * FACE_ROWS
    solved = get_solved(received_ref, ROWS, peers)
    resid = resid_ref[...]
    flat = whole(fields_ref[8 * elements : 8 * elements + 1, :])
    rough = rows_of(jacobi_ref[...]) * resid
    smoothed = rough + prolonged(solved[0], flat, elements)
    smoothed_ref[...] = smoothed
    apply(
        rough, smoothed, ROWS, received_ref, flat, maps_ref[...], far_points_ref[...], solved, metric_ref,
        helmholtz_ref, first_ref, inner_ref, pair_ref,
        loaded(pair_places(pair_ref, elements), pair_hot_ref), points_ref, far_hot_ref,
        [total_of(resid * smoothed), total_of(image_ref[...] * smoothed)],
        back_ref, local_ref, sent_ref,
    )


def final_kernel(
    received_ref, points_ref, far_hot_ref, pair_ref, pair_hot_ref, old_ref, field_ref, resid_ref, old_image_ref,
    scalars_ref, back_ref, local_ref, helmholtz_ref,
    solution_ref, residual_ref,
):
    before = unpacked(scalars_ref[...], 2)
    now = unpacked(jnp.sum(get(received_ref, ROWS, TERMS), axis=0, keepdims=True), 3)
    alpha = before[0] / before[1]
    beta = now[0] / before[0]
    curved = now[2] + beta * (2.0 * now[1] + beta * before[1])
    step = now[0] / curved
    old = old_ref[...]
    direction = field_ref[...] + beta * old
    solution_ref[...] = wide_of(alpha * old + step * direction)
    image = image_of(
        field_ref, back_ref, local_ref, received_ref, helmholtz_ref, pair_ref,
        pair_hot_ref, points_ref, far_hot_ref,
    )
    image = image + beta * old_image_ref[...]
    residual_ref[...] = wide_of(resid_ref[...] - step * image)


def call(kernel, outs, *args, copied=False):
    space = pl.ANY if copied else pltpu.VMEM
    scratch = [pltpu.VMEM(arg.shape, arg.dtype) for arg in args] if copied else []
    if copied:
        args = [pltpu.with_memory_space_constraint(arg, pltpu.HBM) for arg in args]
    return pl.pallas_call(
        kernel,
        out_shape=[
            jax.ShapeDtypeStruct(*(out if isinstance(out[0], tuple) else (out, F32))) for out in outs
        ],
        in_specs=[pl.BlockSpec(memory_space=space)] * len(args),
        out_specs=[pl.BlockSpec(memory_space=pltpu.VMEM)] * len(outs),
        scratch_shapes=scratch + ([pltpu.SemaphoreType.DMA((len(args),))] if copied else []),
        compiler_params=pltpu.CompilerParams(vmem_limit_bytes=24 * 1024 * 1024),
    )(*args)


def body(
    right_side,
    metric,
    helmholtz,
    jacobi,
    pair_list,
    shared_slots,
    face_points,
    coarse_map,
    coarse_inverse,
):
    peers = lax.axis_size("sub")
    groups = lax.axis_size("grp")
    t = {name: jnp.asarray(value) for name, value in tables().items()}
    elements = right_side.shape[0]
    field = (4 * elements, LANES)
    local = (1, pair_list.shape[0] * pair_list.shape[1])
    points_shape = (peers + 2 * FACE_ROWS, LANES)
    sent_shape = (groups * peers * ROWS, LANES)

    def exchange(sent):
        rows = sent.reshape(groups * peers, 1, -1)
        return lax.all_to_all(rows, ("grp", "sub"), 0, 0, tiled=True).reshape(sent.shape)

    far_hot_shape = (points_shape[0] * LANES // 2, STEP)
    pair_hot_shape = (local[1] * LANES // STEP, STEP)

    sent, fields, points, far_hot = call(
        first_kernel,
        [
            (groups * peers * FIRST_ROWS, LANES),
            (8 * elements + 8, LANES),
            (points_shape, jnp.int32),
            (far_hot_shape, BF16),
        ],
        right_side, jacobi, coarse_inverse, coarse_map, shared_slots, face_points, copied=True,
    )
    smoothed, maps, far_points, back, near, sent, pair_hot = call(
        start_kernel,
        [field, (points_shape, jnp.int32), (points_shape, jnp.int32), field, local, sent_shape,
         (pair_hot_shape, BF16)],
        exchange(sent), fields, points, far_hot, pair_list, metric, helmholtz,
        t["first"], t["inner"],
    )
    image, resid, scalars, sent = call(
        middle_kernel, [field, field, (1, LANES), sent_shape],
        exchange(sent), fields, points, far_hot, pair_list, pair_hot, jacobi, helmholtz, coarse_inverse,
        smoothed, back, near,
    )
    second, back, near, sent = call(
        second_kernel, [field, field, local, sent_shape],
        exchange(sent), fields, points, far_hot, pair_list, pair_hot, resid, image, maps, far_points, jacobi,
        metric, helmholtz, t["first"], t["inner"],
    )
    return tuple(
        call(
            final_kernel, [right_side.shape, right_side.shape],
            exchange(sent), points, far_hot, pair_list, pair_hot, smoothed, second, resid, image, scalars,
            back, near, helmholtz,
        )
    )


def solution(mesh):
    in_specs = (
        P(("grp", "sub"), None),
        P(("grp", "sub"), None),
        P(("grp", "sub"), None),
        P(("grp", "sub"), None),
        P(None, ("grp", "sub")),
        P(("grp", "sub"), None, None),
        P(None, ("grp", "sub")),
        P(None, ("grp", "sub")),
        P("grp", None, None),
    )
    out_specs = (P(("grp", "sub"), None), P(("grp", "sub"), None))
    return jax.shard_map(body, mesh=mesh, in_specs=in_specs, out_specs=out_specs, check_vma=False)
```

```python
import jax
import jax.numpy as jnp
import ml_dtypes
import numpy as np
from jax import lax
from jax.experimental import pallas as pl
from jax.experimental.pallas import tpu as pltpu
from jax.sharding import PartitionSpec as P

NC = 64
POINTS = 512
LANES = 128
STEP = 256
FACE_ROWS = 4
ROWS = 5
FIRST_ROWS = 10
TERMS = FACE_ROWS
F32 = jnp.float32
BF16 = jnp.bfloat16
NT = (((1,), (1,)), ((), ()))


def split_constant(array):
    high = array.astype(ml_dtypes.bfloat16)
    low = (array - high.astype(np.float64)).astype(ml_dtypes.bfloat16)
    return high, low


def tables():
    order_index = np.arange(8)
    colloc = np.cos(np.pi * order_index / 7.0)
    end_weights = (
        np.where((order_index == 0) | (order_index == 7), 2.0, 1.0) * (-1.0) ** order_index
    )
    spacing = colloc[:, None] - colloc[None, :] + np.eye(8)
    raw_matrix = np.outer(end_weights, 1.0 / end_weights) / spacing
    off_part = raw_matrix * (1.0 - np.eye(8))
    derivative = 0.25 * (off_part - np.eye(8) * off_part.sum(axis=1)[:, None])
    along_inner = np.concatenate(
        [np.kron(np.eye(2), np.kron(derivative, np.eye(8))).T, np.kron(np.eye(16), derivative).T],
        axis=1,
    )
    high, low = split_constant(along_inner)
    inner = np.concatenate([high, low], axis=0)

    half = np.arange(LANES) // 64

    def first_rows(matrix):
        rows = []
        for to in range(4):
            for at in range(4):
                rows.append(matrix[2 * to + half, 2 * at + half])
                rows.append(matrix[2 * to + half, 2 * at + 1 - half])
        return np.stack(rows).astype(np.float32)

    return {
        "inner": inner,
        "first": np.concatenate([first_rows(derivative), first_rows(derivative.T)], axis=0),
    }


def split(value):
    high = value.astype(BF16)
    return high, (value - high.astype(F32)).astype(BF16)


def rows_of(wide):
    return jnp.concatenate([wide[:, LANES * c : LANES * (c + 1)] for c in range(4)], axis=0)


def wide_of(rows):
    elements = rows.shape[0] // 4
    return jnp.concatenate([rows[c * elements : (c + 1) * elements] for c in range(4)], axis=1)


def locate(points, elements):
    element = points >> 9
    chunk = (points >> 7) & 3
    row = jnp.where(points < elements * POINTS, chunk * elements + element, 4 * elements)
    return row, points & (LANES - 1)


def one_hot(index, count):
    steps = lax.broadcasted_iota(jnp.int32, (count, index.shape[1]), 0)
    return steps == index


def lane_hot(lane):
    steps = lax.broadcasted_iota(jnp.int32, (LANES, lane.shape[1]), 0).astype(F32).astype(BF16)
    one = jnp.ones(steps.shape, BF16)
    return jnp.where(steps == lane.astype(F32).astype(BF16), one, jnp.zeros_like(one))


def take(values, lanes):
    return jnp.take_along_axis(values, lanes, axis=1, mode="promise_in_bounds")


def gather(field, chunks):
    count = field.shape[0]
    both = jnp.concatenate(split(field), axis=0)
    out = []
    for row, hot in chunks:
        picked = jnp.dot(both, hot, preferred_element_type=F32)
        mine = jnp.where(one_hot(row, count), picked[:count] + picked[count:], 0.0)
        out.append(jnp.sum(mine, axis=0, keepdims=True))
    return out


def scatter(rows, chunks, values):
    total = jnp.zeros((2 * rows, LANES), F32)
    for (row, hot), value in zip(chunks, values):
        steps = lax.broadcasted_iota(jnp.int32, (rows, row.shape[1]), 0).astype(F32).astype(BF16)
        mine = steps == row.astype(F32).astype(BF16)
        parts = [jnp.where(mine, part, jnp.zeros_like(steps)) for part in split(value)]
        total = total + lax.dot_general(
            jnp.concatenate(parts, axis=0), hot, NT, preferred_element_type=F32
        )
    return total[:rows] + total[rows:]


def chunked(row, lane):
    return [
        (row[:, at : at + STEP], lane[:, at : at + STEP]) for at in range(0, row.shape[1], STEP)
    ]


def cut(row):
    return [row[:, at : at + STEP] for at in range(0, row.shape[1], STEP)]


def pair_places(pair_ref, elements):
    row, lane = locate(pair_ref[...], elements)
    return chunked(row[0:1], lane[0:1]) + chunked(row[1:2], lane[1:2])


def joined(rows):
    return [
        jnp.concatenate([rows[at : at + 1], rows[at + 1 : at + 2]], axis=1)
        for at in range(0, rows.shape[0], 2)
    ]


def far_places(points, elements):
    row, lane = locate(points, elements)
    return list(zip(joined(row), joined(lane)))


def built(places, hot_ref):
    out = []
    for k, (row, lane) in enumerate(places):
        hot = lane_hot(lane)
        hot_ref[k * LANES : (k + 1) * LANES, :] = hot
        out.append((row, hot))
    return out


def loaded(places, hot_ref):
    return [
        (row, hot_ref[k * LANES : (k + 1) * LANES, :]) for k, (row, lane) in enumerate(places)
    ]


def halves(wide):
    return [wide[:, at : at + LANES] for at in range(0, wide.shape[1], LANES)]


def inside(received_ref, count, peers, away):
    groups = received_ref.shape[0] // (count * peers)
    group = lax.axis_index("grp") + away
    kept = jnp.clip(group, 0, groups - 1)
    return kept, jnp.where(group == kept, 1.0, 0.0)


def send_rows(sent_ref, count, at, rows, peers):
    group = lax.axis_index("grp")
    for b in range(peers):
        sent_ref[pl.ds((group * peers + b) * count + at, 1), :] = rows[b : b + 1]
    for side, away in enumerate((-1, 1)):
        kept, _ = inside(sent_ref, count, peers, away)
        place = kept * peers + lax.axis_index("sub")
        for r in range(FACE_ROWS):
            k = peers + side * FACE_ROWS + r
            sent_ref[pl.ds(place * count + at + r, 1), :] = rows[k : k + 1]


def send_same(sent_ref, count, at, row):
    devices = sent_ref.shape[0] // count
    sent_ref[pl.ds(at, devices, count), :] = jnp.broadcast_to(row, (devices, LANES))


def send_values(sent_ref, count, values, peers):
    rows = jnp.concatenate([row for pair in values for row in halves(pair)], axis=0)
    send_rows(sent_ref, count, 0, rows, peers)


def get(received_ref, count, at):
    return received_ref[pl.ds(at, received_ref.shape[0] // count, count), :]


def get_group(received_ref, count, at, peers, away=0):
    group, kept = inside(received_ref, count, peers, away)
    return received_ref[pl.ds(group * (peers * count) + at, peers, count), :] * kept


def get_side(received_ref, count, at, rows, peers, away):
    group, kept = inside(received_ref, count, peers, away)
    place = group * peers + lax.axis_index("sub")
    return received_ref[pl.ds(place * count + at, rows), :] * kept


def get_rows(received_ref, count, at, peers):
    sides = [get_side(received_ref, count, at, FACE_ROWS, peers, away) for away in (-1, 1)]
    return jnp.concatenate([get_group(received_ref, count, at, peers)] + sides, axis=0)


def swapped(values):
    count = len(values) // 2
    return values[count:] + values[:count]


def along_first(field, table_ref, base):
    elements = field.shape[0] // 4
    turned = pltpu.roll(field, 64, axis=1)
    out = []
    for to in range(4):
        total = None
        for at in range(4):
            place = base + 2 * (4 * to + at)
            rows = slice(at * elements, (at + 1) * elements)
            term = (
                table_ref[place : place + 1, :] * field[rows]
                + table_ref[place + 1 : place + 2, :] * turned[rows]
            )
            total = term if total is None else total + term
        out.append(total)
    return jnp.concatenate(out, axis=0)


def stiffness(field, metric_ref, first_ref, inner_ref):
    metric = [rows_of(metric_ref[:, POINTS * d : POINTS * (d + 1)]) for d in range(3)]
    count = field.shape[0]
    grad_first = along_first(field, first_ref, 0)
    high, low = split(field)
    both = jnp.dot(
        jnp.concatenate([high, low], axis=0), inner_ref[:LANES], preferred_element_type=F32
    )
    inner = both[:count] + both[count:]
    inner = inner + jnp.dot(high, inner_ref[LANES:], preferred_element_type=F32)
    flux_first = metric[0] * grad_first
    flux = jnp.concatenate([metric[1], metric[2]], axis=1) * inner
    high, low = split(flux)
    both = lax.dot_general(
        jnp.concatenate([high, low], axis=0), inner_ref[:LANES], NT, preferred_element_type=F32
    )
    back = both[:count] + both[count:]
    back = back + lax.dot_general(high, inner_ref[LANES:], NT, preferred_element_type=F32)
    back = back + along_first(flux_first, first_ref, 32)
    energy = flux * inner
    return back, flux_first * grad_first + energy[:, :LANES] + energy[:, LANES:]


def factors(points):
    nodes = 0.5 * (1.0 + np.cos(np.pi * np.arange(8) / 7.0))
    out = []
    for shift in (6, 3, 0):
        index = (points >> shift) & 7
        near = jnp.full(points.shape, nodes[7], F32)
        far = jnp.full(points.shape, nodes[0], F32)
        for m in range(7):
            near = jnp.where(index == m, float(nodes[m]), near)
            far = jnp.where(index == m, float(nodes[7 - m]), far)
        out.append((near, far))
    return out


def corners(points):
    first, second, third = factors(points)
    return [
        first[q >> 2 & 1] * (second[q >> 1 & 1] * third[q & 1]) for q in range(8)
    ]


def own_corners():
    return corners(lax.broadcasted_iota(jnp.int32, (1, POINTS), 1))


def flat_map(mapped):
    elements = mapped.shape[1]
    shape = (8, 8 * elements)
    lane = lax.broadcasted_iota(jnp.int32, shape, 1)
    padded = jnp.concatenate(
        [mapped.astype(F32), jnp.zeros((8, shape[1] - elements), F32)], axis=1
    )
    wide = take(padded, lane & (elements - 1))
    keep = lax.broadcasted_iota(jnp.int32, shape, 0) == lane // elements
    return jnp.sum(jnp.where(keep, wide, 0.0), axis=0, keepdims=True)


def one_vertex(flat):
    return jnp.where(one_hot(whole(flat), NC), 1.0, 0.0)


def whole(values):
    return (values + 0.5).astype(jnp.int32)


def own_element(elements, width):
    shape = (elements, width)
    return lax.broadcasted_iota(jnp.int32, shape, 0) == (
        lax.broadcasted_iota(jnp.int32, shape, 1) % elements
    )


def own_place(elements, q):
    shape = (elements, 8 * elements)
    lane = lax.broadcasted_iota(jnp.int32, shape, 1)
    return lane == lax.broadcasted_iota(jnp.int32, shape, 0) + q * elements


def coarse_part(field, vertices, inverse):
    elements = field.shape[0] // 4
    flat = jnp.zeros((elements, 8 * elements), F32)
    for q, corner in enumerate(own_corners()):
        inner = None
        for c in range(4):
            term = field[c * elements : (c + 1) * elements] * corner[:, c * LANES : (c + 1) * LANES]
            inner = term if inner is None else inner + term
        flat = jnp.where(own_place(elements, q), jnp.sum(inner, axis=1, keepdims=True), flat)
    flat = jnp.sum(flat, axis=0, keepdims=True)
    part = jnp.sum(vertices * flat, axis=1, keepdims=True)
    part = jnp.sum(inverse * part, axis=0, keepdims=True)
    return jnp.concatenate([part, jnp.zeros((1, LANES - NC), F32)], axis=1)


def get_solved(received_ref, count, peers):
    return [
        jnp.sum(get_group(received_ref, count, TERMS, peers, away), axis=0, keepdims=True)
        for away in (0, -1, 1)
    ]


def prolonged(solved, flat, elements):
    shape = (elements, LANES)
    element = lax.broadcasted_iota(jnp.int32, shape, 0)
    at_corner = take(jnp.broadcast_to(solved, shape), jnp.broadcast_to(flat, shape))
    out = [None] * 4
    for q, corner in enumerate(own_corners()):
        value = take(at_corner, element + q * elements)
        for c in range(4):
            term = value * corner[:, c * LANES : (c + 1) * LANES]
            out[c] = term if out[c] is None else out[c] + term
    return jnp.concatenate(out, axis=0)


def prolonged_at(solved, maps, points, elements):
    at_corner = take(solved, maps)
    element = (points >> 9) & (elements - 1)
    total = jnp.zeros(points.shape, F32)
    for q, corner in enumerate(corners(points)):
        total = total + corner * take(at_corner, element + q * elements)
    return total


def total_of(array):
    return jnp.sum(jnp.sum(array, axis=0, keepdims=True), axis=1, keepdims=True)


def packed(values):
    lane = lax.broadcasted_iota(jnp.int32, (1, LANES), 1)
    out = jnp.zeros((1, LANES), F32)
    for k, value in enumerate(values):
        out = jnp.where(lane == k, value, out)
    return out


def unpacked(row, count):
    lane = lax.broadcasted_iota(jnp.int32, row.shape, 1)
    return [
        jnp.sum(jnp.where(lane == k, row, 0.0), axis=1, keepdims=True) for k in range(count)
    ]


def first_kernel(
    right_hbm, jacobi_hbm, inverse_hbm, map_hbm, slot_hbm, face_hbm,
    sent_ref, fields_ref, points_ref, far_hot_ref,
    right_ref, jacobi_ref, inverse_ref, map_ref, slot_ref, face_ref, sems,
):
    copies = []
    for k, (source, target) in enumerate(
        (
            (face_hbm, face_ref),
            (slot_hbm, slot_ref),
            (right_hbm, right_ref),
            (jacobi_hbm, jacobi_ref),
            (map_hbm, map_ref),
            (inverse_hbm, inverse_ref),
        )
    ):
        copy = pltpu.make_async_copy(source, target, sems.at[k])
        copy.start()
        copies.append(copy)
    elements = right_ref.shape[0]
    peers = slot_ref.shape[1]
    for copy in copies[:2]:
        copy.wait()
    faces = face_ref[...]
    faces = jnp.concatenate(halves(faces[0:1]) + halves(faces[1:2]), axis=0)
    points = jnp.concatenate([slot_ref[0], faces], axis=0)
    points_ref[...] = points
    places = built(far_places(points, elements), far_hot_ref)
    send_rows(sent_ref, FIRST_ROWS, TERMS + 2, points.astype(F32), peers)
    for copy in copies[2:]:
        copy.wait()
    resid = rows_of(right_ref[...])
    flat = flat_map(map_ref[...])
    smoothed = rows_of(jacobi_ref[...]) * resid
    fields_ref[0 : 4 * elements, :] = resid
    fields_ref[4 * elements : 8 * elements, :] = smoothed
    fields_ref[8 * elements :, :] = jnp.broadcast_to(flat, (8, LANES))
    part = coarse_part(resid, one_vertex(flat), inverse_ref[0])
    values = gather(smoothed, places)
    send_values(sent_ref, FIRST_ROWS, values, peers)
    send_same(sent_ref, FIRST_ROWS, TERMS, part)
    send_same(sent_ref, FIRST_ROWS, TERMS + 1, flat)


def far_maps(received_ref, peers):
    own = get_group(received_ref, FIRST_ROWS, TERMS + 1, peers)
    sides = [
        jnp.broadcast_to(
            get_side(received_ref, FIRST_ROWS, TERMS + 1, 1, peers, away), (FACE_ROWS, LANES)
        )
        for away in (-1, 1)
    ]
    return whole(jnp.concatenate([own] + sides, axis=0))


def apply(
    rough, smoothed, count, received_ref, flat, maps, far_points, solved, metric_ref, helmholtz_ref,
    first_ref, inner_ref, pair_ref, pairs, points_ref, far_hot_ref, dots, back_ref, local_ref,
    sent_ref,
):
    elements = smoothed.shape[0] // 4
    peers = points_ref.shape[0] - 2 * FACE_ROWS
    far = loaded(far_places(points_ref[...], elements), far_hot_ref)
    near = gather(rough, pairs)
    partners = pair_ref[...]
    partners = jnp.concatenate(halves(partners[1:2]) + halves(partners[0:1]), axis=0)
    counts = (peers, FACE_ROWS, FACE_ROWS, partners.shape[0])
    spread = [
        jnp.broadcast_to(part, (n, LANES)) for part, n in zip((*solved, solved[0]), counts)
    ]
    coarse = prolonged_at(
        jnp.concatenate(spread, axis=0),
        jnp.concatenate([maps, jnp.broadcast_to(flat, partners.shape)], axis=0),
        jnp.concatenate([far_points, partners], axis=0),
        elements,
    )
    split_at = points_ref.shape[0]
    incoming = get_rows(received_ref, count, 0, peers) + coarse[:split_at]
    values = [value + more for value, more in zip(swapped(near), joined(coarse[split_at:]))]
    values = values + joined(incoming)
    summed = smoothed + scatter(smoothed.shape[0], pairs + far, values)
    back, energy = stiffness(summed, metric_ref, first_ref, inner_ref)
    energy = energy + rows_of(helmholtz_ref[...]) * smoothed * smoothed
    back_ref[...] = back
    values = gather(back, pairs + far)
    near = swapped(values[: len(pairs)])
    for k, value in enumerate(near):
        local_ref[0:1, k * STEP : (k + 1) * STEP] = value
    send_values(sent_ref, ROWS, values[len(pairs) :], peers)
    send_same(sent_ref, ROWS, TERMS, packed(dots + [total_of(energy)]))


def image_of(
    field_ref, back_ref, local_ref, received_ref, helmholtz_ref, pair_ref, pair_hot_ref, points_ref,
    far_hot_ref,
):
    elements = field_ref.shape[0] // 4
    peers = points_ref.shape[0] - 2 * FACE_ROWS
    chunks = loaded(pair_places(pair_ref, elements), pair_hot_ref)
    chunks = chunks + loaded(far_places(points_ref[...], elements), far_hot_ref)
    values = cut(local_ref[...]) + joined(get_rows(received_ref, ROWS, 0, peers))
    summed = back_ref[...] + scatter(field_ref.shape[0], chunks, values)
    return summed + rows_of(helmholtz_ref[...]) * field_ref[...]


def start_kernel(
    received_ref, fields_ref, points_ref, far_hot_ref, pair_ref, metric_ref, helmholtz_ref,
    first_ref, inner_ref,
    smoothed_ref, maps_ref, far_points_ref, back_ref, local_ref, sent_ref, pair_hot_ref,
):
    elements = helmholtz_ref.shape[0]
    peers = points_ref.shape[0] - 2 * FACE_ROWS
    solved = get_solved(received_ref, FIRST_ROWS, peers)
    resid = fields_ref[0 : 4 * elements, :]
    flat = whole(fields_ref[8 * elements : 8 * elements + 1, :])
    rough = fields_ref[4 * elements : 8 * elements, :]
    smoothed = rough + prolonged(solved[0], flat, elements)
    smoothed_ref[...] = smoothed
    maps = far_maps(received_ref, peers)
    maps_ref[...] = maps
    far_points = whole(get_rows(received_ref, FIRST_ROWS, TERMS + 2, peers))
    far_points_ref[...] = far_points
    apply(
        rough, smoothed, FIRST_ROWS, received_ref, flat, maps, far_points, solved, metric_ref,
        helmholtz_ref, first_ref, inner_ref, pair_ref,
        built(pair_places(pair_ref, elements), pair_hot_ref), points_ref, far_hot_ref,
        [total_of(resid * smoothed)], back_ref, local_ref, sent_ref,
    )


def middle_kernel(
    received_ref, fields_ref, points_ref, far_hot_ref, pair_ref, pair_hot_ref, jacobi_ref, helmholtz_ref,
    inverse_ref, smoothed_ref, back_ref, local_ref,
    image_ref, resid_ref, scalars_ref, sent_ref,
):
    elements = helmholtz_ref.shape[0]
    peers = points_ref.shape[0] - 2 * FACE_ROWS
    dots = jnp.sum(get(received_ref, ROWS, TERMS), axis=0, keepdims=True)
    scalars_ref[...] = dots
    values = unpacked(dots, 2)
    alpha = values[0] / values[1]
    image = image_of(
        smoothed_ref, back_ref, local_ref, received_ref, helmholtz_ref, pair_ref,
        pair_hot_ref, points_ref, far_hot_ref,
    )
    image_ref[...] = image
    resid = fields_ref[0 : 4 * elements, :] - alpha * image
    resid_ref[...] = resid
    vertices = one_vertex(fields_ref[8 * elements : 8 * elements + 1, :])
    part = coarse_part(resid, vertices, inverse_ref[0])
    values = gather(
        rows_of(jacobi_ref[...]) * resid, loaded(far_places(points_ref[...], elements), far_hot_ref),
    )
    send_values(sent_ref, ROWS, values, peers)
    send_same(sent_ref, ROWS, TERMS, part)


def second_kernel(
    received_ref, fields_ref, points_ref, far_hot_ref, pair_ref, pair_hot_ref, resid_ref, image_ref,
    maps_ref, far_points_ref, jacobi_ref, metric_ref, helmholtz_ref, first_ref, inner_ref,
    smoothed_ref, back_ref, local_ref, sent_ref,
):
    elements = helmholtz_ref.shape[0]
    peers = points_ref.shape[0] - 2 * FACE_ROWS
    solved = get_solved(received_ref, ROWS, peers)
    resid = resid_ref[...]
    flat = whole(fields_ref[8 * elements : 8 * elements + 1, :])
    rough = rows_of(jacobi_ref[...]) * resid
    smoothed = rough + prolonged(solved[0], flat, elements)
    smoothed_ref[...] = smoothed
    apply(
        rough, smoothed, ROWS, received_ref, flat, maps_ref[...], far_points_ref[...], solved, metric_ref,
        helmholtz_ref, first_ref, inner_ref, pair_ref,
        loaded(pair_places(pair_ref, elements), pair_hot_ref), points_ref, far_hot_ref,
        [total_of(resid * smoothed), total_of(image_ref[...] * smoothed)],
        back_ref, local_ref, sent_ref,
    )


def final_kernel(
    received_ref, points_ref, far_hot_ref, pair_ref, pair_hot_ref, old_ref, field_ref, resid_ref, old_image_ref,
    scalars_ref, back_ref, local_ref, helmholtz_ref,
    solution_ref, residual_ref,
):
    before = unpacked(scalars_ref[...], 2)
    now = unpacked(jnp.sum(get(received_ref, ROWS, TERMS), axis=0, keepdims=True), 3)
    alpha = before[0] / before[1]
    beta = now[0] / before[0]
    curved = now[2] + beta * (2.0 * now[1] + beta * before[1])
    step = now[0] / curved
    old = old_ref[...]
    direction = field_ref[...] + beta * old
    solution_ref[...] = wide_of(alpha * old + step * direction)
    image = image_of(
        field_ref, back_ref, local_ref, received_ref, helmholtz_ref, pair_ref,
        pair_hot_ref, points_ref, far_hot_ref,
    )
    image = image + beta * old_image_ref[...]
    residual_ref[...] = wide_of(resid_ref[...] - step * image)


def call(kernel, outs, *args, copied=False):
    space = pl.ANY if copied else pltpu.VMEM
    scratch = [pltpu.VMEM(arg.shape, arg.dtype) for arg in args] if copied else []
    if copied:
        args = [pltpu.with_memory_space_constraint(arg, pltpu.HBM) for arg in args]
    return pl.pallas_call(
        kernel,
        out_shape=[
            jax.ShapeDtypeStruct(*(out if isinstance(out[0], tuple) else (out, F32))) for out in outs
        ],
        in_specs=[pl.BlockSpec(memory_space=space)] * len(args),
        out_specs=[pl.BlockSpec(memory_space=pltpu.VMEM)] * len(outs),
        scratch_shapes=scratch + ([pltpu.SemaphoreType.DMA((len(args),))] if copied else []),
        compiler_params=pltpu.CompilerParams(vmem_limit_bytes=24 * 1024 * 1024),
    )(*args)


def body(
    right_side,
    metric,
    helmholtz,
    jacobi,
    pair_list,
    shared_slots,
    face_points,
    coarse_map,
    coarse_inverse,
):
    peers = lax.axis_size("sub")
    groups = lax.axis_size("grp")
    t = {name: jnp.asarray(value) for name, value in tables().items()}
    elements = right_side.shape[0]
    field = (4 * elements, LANES)
    local = (1, pair_list.shape[0] * pair_list.shape[1])
    points_shape = (peers + 2 * FACE_ROWS, LANES)
    sent_shape = (groups * peers * ROWS, LANES)

    def exchange(sent):
        rows = sent.reshape(groups * peers, 1, -1)
        return lax.all_to_all(rows, ("grp", "sub"), 0, 0, tiled=True).reshape(sent.shape)

    far_hot_shape = (points_shape[0] * LANES // 2, STEP)
    pair_hot_shape = (local[1] * LANES // STEP, STEP)

    sent, fields, points, far_hot = call(
        first_kernel,
        [
            (groups * peers * FIRST_ROWS, LANES),
            (8 * elements + 8, LANES),
            (points_shape, jnp.int32),
            (far_hot_shape, BF16),
        ],
        right_side, jacobi, coarse_inverse, coarse_map, shared_slots, face_points, copied=True,
    )
    smoothed, maps, far_points, back, near, sent, pair_hot = call(
        start_kernel,
        [field, (points_shape, jnp.int32), (points_shape, jnp.int32), field, local, sent_shape,
         (pair_hot_shape, BF16)],
        exchange(sent), fields, points, far_hot, pair_list, metric, helmholtz,
        t["first"], t["inner"],
    )
    image, resid, scalars, sent = call(
        middle_kernel, [field, field, (1, LANES), sent_shape],
        exchange(sent), fields, points, far_hot, pair_list, pair_hot, jacobi, helmholtz, coarse_inverse,
        smoothed, back, near,
    )
    second, back, near, sent = call(
        second_kernel, [field, field, local, sent_shape],
        exchange(sent), fields, points, far_hot, pair_list, pair_hot, resid, image, maps, far_points, jacobi,
        metric, helmholtz, t["first"], t["inner"],
    )
    return tuple(
        call(
            final_kernel, [right_side.shape, right_side.shape],
            exchange(sent), points, far_hot, pair_list, pair_hot, smoothed, second, resid, image, scalars,
            back, near, helmholtz,
        )
    )


def solution(mesh):
    in_specs = (
        P(("grp", "sub"), None),
        P(("grp", "sub"), None),
        P(("grp", "sub"), None),
        P(("grp", "sub"), None),
        P(None, ("grp", "sub")),
        P(("grp", "sub"), None, None),
        P(None, ("grp", "sub")),
        P(None, ("grp", "sub")),
        P("grp", None, None),
    )
    out_specs = (P(("grp", "sub"), None), P(("grp", "sub"), None))
    return jax.shard_map(body, mesh=mesh, in_specs=in_specs, out_specs=out_specs, check_vma=False)
```

```python
import jax
import jax.numpy as jnp
import ml_dtypes
import numpy as np
from jax import lax
from jax.experimental import pallas as pl
from jax.experimental.pallas import tpu as pltpu
from jax.sharding import PartitionSpec as P

NC = 64
POINTS = 512
LANES = 128
STEP = 256
FACE_ROWS = 4
ROWS = 5
FIRST_ROWS = 10
TERMS = FACE_ROWS
F32 = jnp.float32
BF16 = jnp.bfloat16
NT = (((1,), (1,)), ((), ()))


def split_constant(array):
    high = array.astype(ml_dtypes.bfloat16)
    low = (array - high.astype(np.float64)).astype(ml_dtypes.bfloat16)
    return high, low


def tables():
    order_index = np.arange(8)
    colloc = np.cos(np.pi * order_index / 7.0)
    end_weights = (
        np.where((order_index == 0) | (order_index == 7), 2.0, 1.0) * (-1.0) ** order_index
    )
    spacing = colloc[:, None] - colloc[None, :] + np.eye(8)
    raw_matrix = np.outer(end_weights, 1.0 / end_weights) / spacing
    off_part = raw_matrix * (1.0 - np.eye(8))
    derivative = 0.25 * (off_part - np.eye(8) * off_part.sum(axis=1)[:, None])
    along_inner = np.concatenate(
        [np.kron(np.eye(2), np.kron(derivative, np.eye(8))).T, np.kron(np.eye(16), derivative).T],
        axis=1,
    )
    high, low = split_constant(along_inner)
    inner = np.concatenate([high, low], axis=0)

    half = np.arange(LANES) // 64

    def first_rows(matrix):
        rows = []
        for to in range(4):
            for at in range(4):
                rows.append(matrix[2 * to + half, 2 * at + half])
                rows.append(matrix[2 * to + half, 2 * at + 1 - half])
        return np.stack(rows).astype(np.float32)

    return {
        "inner": inner,
        "first": np.concatenate([first_rows(derivative), first_rows(derivative.T)], axis=0),
    }


def split(value):
    high = value.astype(BF16)
    return high, (value - high.astype(F32)).astype(BF16)


def rows_of(wide):
    return jnp.concatenate([wide[:, LANES * c : LANES * (c + 1)] for c in range(4)], axis=0)


def wide_of(rows):
    elements = rows.shape[0] // 4
    return jnp.concatenate([rows[c * elements : (c + 1) * elements] for c in range(4)], axis=1)


def locate(points, elements):
    element = points >> 9
    chunk = (points >> 7) & 3
    row = jnp.where(points < elements * POINTS, chunk * elements + element, 4 * elements)
    return row, points & (LANES - 1)


def one_hot(index, count):
    steps = lax.broadcasted_iota(jnp.int32, (count, index.shape[1]), 0)
    return steps == index


def lane_hot(lane):
    steps = lax.broadcasted_iota(jnp.int32, (LANES, lane.shape[1]), 0).astype(F32).astype(BF16)
    one = jnp.ones(steps.shape, BF16)
    return jnp.where(steps == lane.astype(F32).astype(BF16), one, jnp.zeros_like(one))


def take(values, lanes):
    return jnp.take_along_axis(values, lanes, axis=1, mode="promise_in_bounds")


def gather(field, chunks):
    count = field.shape[0]
    both = jnp.concatenate(split(field), axis=0)
    out = []
    for row, hot in chunks:
        picked = jnp.dot(both, hot, preferred_element_type=F32)
        mine = jnp.where(one_hot(row, count), picked[:count] + picked[count:], 0.0)
        out.append(jnp.sum(mine, axis=0, keepdims=True))
    return out


def scatter(rows, chunks, values):
    total = jnp.zeros((2 * rows, LANES), F32)
    for (row, hot), value in zip(chunks, values):
        steps = lax.broadcasted_iota(jnp.int32, (rows, row.shape[1]), 0).astype(F32).astype(BF16)
        mine = steps == row.astype(F32).astype(BF16)
        parts = [jnp.where(mine, part, jnp.zeros_like(steps)) for part in split(value)]
        total = total + lax.dot_general(
            jnp.concatenate(parts, axis=0), hot, NT, preferred_element_type=F32
        )
    return total[:rows] + total[rows:]


def chunked(row, lane):
    return [
        (row[:, at : at + STEP], lane[:, at : at + STEP]) for at in range(0, row.shape[1], STEP)
    ]


def cut(row):
    return [row[:, at : at + STEP] for at in range(0, row.shape[1], STEP)]


def pair_places(pair_ref, elements):
    row, lane = locate(pair_ref[...], elements)
    return chunked(row[0:1], lane[0:1]) + chunked(row[1:2], lane[1:2])


def joined(rows):
    return [
        jnp.concatenate([rows[at : at + 1], rows[at + 1 : at + 2]], axis=1)
        for at in range(0, rows.shape[0], 2)
    ]


def far_places(points, elements):
    row, lane = locate(points, elements)
    return list(zip(joined(row), joined(lane)))


def built(places, hot_ref):
    out = []
    for k, (row, lane) in enumerate(places):
        hot = lane_hot(lane)
        hot_ref[k * LANES : (k + 1) * LANES, :] = hot
        out.append((row, hot))
    return out


def loaded(places, hot_ref):
    return [
        (row, hot_ref[k * LANES : (k + 1) * LANES, :]) for k, (row, lane) in enumerate(places)
    ]


def halves(wide):
    return [wide[:, at : at + LANES] for at in range(0, wide.shape[1], LANES)]


def own_group(devices, peers, away=0):
    shape = (devices, LANES)
    return lax.broadcasted_iota(jnp.int32, shape, 0) // peers - lax.axis_index("grp") == away


def send_rows(sent_ref, count, at, rows, peers):
    devices = sent_ref.shape[0] // count
    above = own_group(devices, peers, 1)
    shared = jnp.concatenate([rows[:peers]] * (devices // peers), axis=0)
    for r in range(FACE_ROWS):
        down = rows[peers + r : peers + r + 1]
        up = rows[peers + FACE_ROWS + r : peers + FACE_ROWS + r + 1]
        out = jnp.where(above, up, down)
        if r == 0:
            out = jnp.where(own_group(devices, peers), shared, out)
        sent_ref[pl.ds(at + r, devices, count), :] = out


def send_same(sent_ref, count, at, row):
    devices = sent_ref.shape[0] // count
    sent_ref[pl.ds(at, devices, count), :] = jnp.broadcast_to(row, (devices, LANES))


def send_values(sent_ref, count, values, peers):
    rows = jnp.concatenate([row for pair in values for row in halves(pair)], axis=0)
    send_rows(sent_ref, count, 0, rows, peers)


def get(received_ref, count, at):
    return received_ref[pl.ds(at, received_ref.shape[0] // count, count), :]


def inside(received_ref, count, peers, away):
    groups = received_ref.shape[0] // (count * peers)
    group = lax.axis_index("grp") + away
    kept = jnp.clip(group, 0, groups - 1)
    return kept, jnp.where(group == kept, 1.0, 0.0)


def get_group(received_ref, count, at, peers, away=0):
    group, kept = inside(received_ref, count, peers, away)
    return received_ref[pl.ds(group * (peers * count) + at, peers, count), :] * kept


def get_side(received_ref, count, at, rows, peers, away):
    group, kept = inside(received_ref, count, peers, away)
    place = group * peers + lax.axis_index("sub")
    return received_ref[pl.ds(place * count + at, rows), :] * kept


def get_rows(received_ref, count, at, peers):
    sides = [get_side(received_ref, count, at, FACE_ROWS, peers, away) for away in (-1, 1)]
    return jnp.concatenate([get_group(received_ref, count, at, peers)] + sides, axis=0)


def swapped(values):
    count = len(values) // 2
    return values[count:] + values[:count]


def along_first(field, table_ref, base):
    elements = field.shape[0] // 4
    turned = pltpu.roll(field, 64, axis=1)
    out = []
    for to in range(4):
        total = None
        for at in range(4):
            place = base + 2 * (4 * to + at)
            rows = slice(at * elements, (at + 1) * elements)
            term = (
                table_ref[place : place + 1, :] * field[rows]
                + table_ref[place + 1 : place + 2, :] * turned[rows]
            )
            total = term if total is None else total + term
        out.append(total)
    return jnp.concatenate(out, axis=0)


def stiffness(field, metric_ref, first_ref, inner_ref):
    metric = [rows_of(metric_ref[:, POINTS * d : POINTS * (d + 1)]) for d in range(3)]
    count = field.shape[0]
    grad_first = along_first(field, first_ref, 0)
    high, low = split(field)
    both = jnp.dot(
        jnp.concatenate([high, low], axis=0), inner_ref[:LANES], preferred_element_type=F32
    )
    inner = both[:count] + both[count:]
    inner = inner + jnp.dot(high, inner_ref[LANES:], preferred_element_type=F32)
    flux_first = metric[0] * grad_first
    flux = jnp.concatenate([metric[1], metric[2]], axis=1) * inner
    high, low = split(flux)
    both = lax.dot_general(
        jnp.concatenate([high, low], axis=0), inner_ref[:LANES], NT, preferred_element_type=F32
    )
    back = both[:count] + both[count:]
    back = back + lax.dot_general(high, inner_ref[LANES:], NT, preferred_element_type=F32)
    back = back + along_first(flux_first, first_ref, 32)
    energy = flux * inner
    return back, flux_first * grad_first + energy[:, :LANES] + energy[:, LANES:]


def factors(points):
    nodes = 0.5 * (1.0 + np.cos(np.pi * np.arange(8) / 7.0))
    out = []
    for shift in (6, 3, 0):
        index = (points >> shift) & 7
        near = jnp.full(points.shape, nodes[7], F32)
        far = jnp.full(points.shape, nodes[0], F32)
        for m in range(7):
            near = jnp.where(index == m, float(nodes[m]), near)
            far = jnp.where(index == m, float(nodes[7 - m]), far)
        out.append((near, far))
    return out


def corners(points):
    first, second, third = factors(points)
    return [
        first[q >> 2 & 1] * (second[q >> 1 & 1] * third[q & 1]) for q in range(8)
    ]


def own_corners():
    return corners(lax.broadcasted_iota(jnp.int32, (1, POINTS), 1))


def flat_map(mapped):
    elements = mapped.shape[1]
    shape = (8, 8 * elements)
    lane = lax.broadcasted_iota(jnp.int32, shape, 1)
    padded = jnp.concatenate(
        [mapped.astype(F32), jnp.zeros((8, shape[1] - elements), F32)], axis=1
    )
    wide = take(padded, lane & (elements - 1))
    keep = lax.broadcasted_iota(jnp.int32, shape, 0) == lane // elements
    return jnp.sum(jnp.where(keep, wide, 0.0), axis=0, keepdims=True)


def one_vertex(flat):
    return jnp.where(one_hot(whole(flat), NC), 1.0, 0.0)


def whole(values):
    return (values + 0.5).astype(jnp.int32)


def own_element(elements, width):
    shape = (elements, width)
    return lax.broadcasted_iota(jnp.int32, shape, 0) == (
        lax.broadcasted_iota(jnp.int32, shape, 1) % elements
    )


def own_place(elements, q):
    shape = (elements, 8 * elements)
    lane = lax.broadcasted_iota(jnp.int32, shape, 1)
    return lane == lax.broadcasted_iota(jnp.int32, shape, 0) + q * elements


def coarse_part(field, vertices, inverse):
    elements = field.shape[0] // 4
    flat = jnp.zeros((elements, 8 * elements), F32)
    for q, corner in enumerate(own_corners()):
        inner = None
        for c in range(4):
            term = field[c * elements : (c + 1) * elements] * corner[:, c * LANES : (c + 1) * LANES]
            inner = term if inner is None else inner + term
        flat = jnp.where(own_place(elements, q), jnp.sum(inner, axis=1, keepdims=True), flat)
    flat = jnp.sum(flat, axis=0, keepdims=True)
    part = jnp.sum(vertices * flat, axis=1, keepdims=True)
    part = jnp.sum(inverse * part, axis=0, keepdims=True)
    return jnp.concatenate([part, jnp.zeros((1, LANES - NC), F32)], axis=1)


def get_solved(received_ref, count, peers):
    return [
        jnp.sum(get_group(received_ref, count, TERMS, peers, away), axis=0, keepdims=True)
        for away in (0, -1, 1)
    ]


def prolonged(solved, flat, elements):
    shape = (elements, LANES)
    element = lax.broadcasted_iota(jnp.int32, shape, 0)
    at_corner = take(jnp.broadcast_to(solved, shape), jnp.broadcast_to(flat, shape))
    out = [None] * 4
    for q, corner in enumerate(own_corners()):
        value = take(at_corner, element + q * elements)
        for c in range(4):
            term = value * corner[:, c * LANES : (c + 1) * LANES]
            out[c] = term if out[c] is None else out[c] + term
    return jnp.concatenate(out, axis=0)


def prolonged_at(solved, maps, points, elements):
    at_corner = take(solved, maps)
    element = (points >> 9) & (elements - 1)
    total = jnp.zeros(points.shape, F32)
    for q, corner in enumerate(corners(points)):
        total = total + corner * take(at_corner, element + q * elements)
    return total


def total_of(array):
    return jnp.sum(jnp.sum(array, axis=0, keepdims=True), axis=1, keepdims=True)


def packed(values):
    lane = lax.broadcasted_iota(jnp.int32, (1, LANES), 1)
    out = jnp.zeros((1, LANES), F32)
    for k, value in enumerate(values):
        out = jnp.where(lane == k, value, out)
    return out


def unpacked(row, count):
    lane = lax.broadcasted_iota(jnp.int32, row.shape, 1)
    return [
        jnp.sum(jnp.where(lane == k, row, 0.0), axis=1, keepdims=True) for k in range(count)
    ]


def first_kernel(
    right_hbm, jacobi_hbm, inverse_hbm, map_hbm, slot_hbm, face_hbm,
    sent_ref, fields_ref, points_ref, far_hot_ref, smoother_ref, solver_ref,
    right_ref, jacobi_ref, inverse_ref, map_ref, slot_ref, face_ref, sems,
):
    copies = []
    for k, (source, target) in enumerate(
        (
            (face_hbm, face_ref),
            (slot_hbm, slot_ref),
            (right_hbm, right_ref),
            (jacobi_hbm, jacobi_ref),
            (map_hbm, map_ref),
            (inverse_hbm, inverse_ref),
        )
    ):
        copy = pltpu.make_async_copy(source, target, sems.at[k])
        copy.start()
        copies.append(copy)
    elements = right_ref.shape[0]
    peers = slot_ref.shape[1]
    for copy in copies[:2]:
        copy.wait()
    faces = face_ref[...]
    faces = jnp.concatenate(halves(faces[0:1]) + halves(faces[1:2]), axis=0)
    points = jnp.concatenate([slot_ref[0], faces], axis=0)
    points_ref[...] = points
    places = built(far_places(points, elements), far_hot_ref)
    send_rows(sent_ref, FIRST_ROWS, TERMS + 2, points.astype(F32), peers)
    for copy in copies[2:]:
        copy.wait()
    resid = rows_of(right_ref[...])
    flat = flat_map(map_ref[...])
    smoother = rows_of(jacobi_ref[...])
    smoother_ref[...] = smoother
    solver_ref[...] = inverse_ref[0]
    smoothed = smoother * resid
    fields_ref[0 : 4 * elements, :] = resid
    fields_ref[4 * elements : 8 * elements, :] = smoothed
    fields_ref[8 * elements :, :] = jnp.broadcast_to(flat, (8, LANES))
    part = coarse_part(resid, one_vertex(flat), inverse_ref[0])
    values = gather(smoothed, places)
    send_values(sent_ref, FIRST_ROWS, values, peers)
    send_same(sent_ref, FIRST_ROWS, TERMS, part)
    send_same(sent_ref, FIRST_ROWS, TERMS + 1, flat)


def far_maps(received_ref, peers):
    own = get_group(received_ref, FIRST_ROWS, TERMS + 1, peers)
    sides = [
        jnp.broadcast_to(
            get_side(received_ref, FIRST_ROWS, TERMS + 1, 1, peers, away), (FACE_ROWS, LANES)
        )
        for away in (-1, 1)
    ]
    return whole(jnp.concatenate([own] + sides, axis=0))


def apply(
    rough, smoothed, count, received_ref, flat, maps, far_points, solved, metric_ref, helmholtz_ref,
    first_ref, inner_ref, pair_ref, pairs, points_ref, far_hot_ref, dots, back_ref, local_ref,
    sent_ref,
):
    elements = smoothed.shape[0] // 4
    peers = points_ref.shape[0] - 2 * FACE_ROWS
    far = loaded(far_places(points_ref[...], elements), far_hot_ref)
    near = gather(rough, pairs)
    partners = pair_ref[...]
    partners = jnp.concatenate(halves(partners[1:2]) + halves(partners[0:1]), axis=0)
    counts = (peers, FACE_ROWS, FACE_ROWS, partners.shape[0])
    spread = [
        jnp.broadcast_to(part, (n, LANES)) for part, n in zip((*solved, solved[0]), counts)
    ]
    coarse = prolonged_at(
        jnp.concatenate(spread, axis=0),
        jnp.concatenate([maps, jnp.broadcast_to(flat, partners.shape)], axis=0),
        jnp.concatenate([far_points, partners], axis=0),
        elements,
    )
    split_at = points_ref.shape[0]
    incoming = get_rows(received_ref, count, 0, peers) + coarse[:split_at]
    values = [value + more for value, more in zip(swapped(near), joined(coarse[split_at:]))]
    values = values + joined(incoming)
    summed = smoothed + scatter(smoothed.shape[0], pairs + far, values)
    back, energy = stiffness(summed, metric_ref, first_ref, inner_ref)
    energy = energy + rows_of(helmholtz_ref[...]) * smoothed * smoothed
    back_ref[...] = back
    values = gather(back, pairs + far)
    near = swapped(values[: len(pairs)])
    for k, value in enumerate(near):
        local_ref[0:1, k * STEP : (k + 1) * STEP] = value
    send_values(sent_ref, ROWS, values[len(pairs) :], peers)
    send_same(sent_ref, ROWS, TERMS, packed(dots + [total_of(energy)]))


def image_of(
    field_ref, back_ref, local_ref, received_ref, helmholtz_ref, pair_ref, pair_hot_ref, points_ref,
    far_hot_ref,
):
    elements = field_ref.shape[0] // 4
    peers = points_ref.shape[0] - 2 * FACE_ROWS
    chunks = loaded(pair_places(pair_ref, elements), pair_hot_ref)
    chunks = chunks + loaded(far_places(points_ref[...], elements), far_hot_ref)
    values = cut(local_ref[...]) + joined(get_rows(received_ref, ROWS, 0, peers))
    summed = back_ref[...] + scatter(field_ref.shape[0], chunks, values)
    return summed + rows_of(helmholtz_ref[...]) * field_ref[...]


def start_kernel(
    received_ref, fields_ref, points_ref, far_hot_ref, pair_ref, metric_ref, helmholtz_ref,
    first_ref, inner_ref,
    smoothed_ref, maps_ref, far_points_ref, back_ref, local_ref, sent_ref, pair_hot_ref,
):
    elements = helmholtz_ref.shape[0]
    peers = points_ref.shape[0] - 2 * FACE_ROWS
    solved = get_solved(received_ref, FIRST_ROWS, peers)
    resid = fields_ref[0 : 4 * elements, :]
    flat = whole(fields_ref[8 * elements : 8 * elements + 1, :])
    rough = fields_ref[4 * elements : 8 * elements, :]
    smoothed = rough + prolonged(solved[0], flat, elements)
    smoothed_ref[...] = smoothed
    maps = far_maps(received_ref, peers)
    maps_ref[...] = maps
    far_points = whole(get_rows(received_ref, FIRST_ROWS, TERMS + 2, peers))
    far_points_ref[...] = far_points
    apply(
        rough, smoothed, FIRST_ROWS, received_ref, flat, maps, far_points, solved, metric_ref,
        helmholtz_ref, first_ref, inner_ref, pair_ref,
        built(pair_places(pair_ref, elements), pair_hot_ref), points_ref, far_hot_ref,
        [total_of(resid * smoothed)], back_ref, local_ref, sent_ref,
    )


def middle_kernel(
    received_ref, fields_ref, points_ref, far_hot_ref, pair_ref, pair_hot_ref, smoother_ref, helmholtz_ref,
    solver_ref, smoothed_ref, back_ref, local_ref,
    image_ref, resid_ref, scalars_ref, sent_ref,
):
    elements = helmholtz_ref.shape[0]
    peers = points_ref.shape[0] - 2 * FACE_ROWS
    dots = jnp.sum(get(received_ref, ROWS, TERMS), axis=0, keepdims=True)
    scalars_ref[...] = dots
    values = unpacked(dots, 2)
    alpha = values[0] / values[1]
    image = image_of(
        smoothed_ref, back_ref, local_ref, received_ref, helmholtz_ref, pair_ref,
        pair_hot_ref, points_ref, far_hot_ref,
    )
    image_ref[...] = image
    resid = fields_ref[0 : 4 * elements, :] - alpha * image
    resid_ref[...] = resid
    vertices = one_vertex(fields_ref[8 * elements : 8 * elements + 1, :])
    part = coarse_part(resid, vertices, solver_ref[...])
    values = gather(
        smoother_ref[...] * resid, loaded(far_places(points_ref[...], elements), far_hot_ref),
    )
    send_values(sent_ref, ROWS, values, peers)
    send_same(sent_ref, ROWS, TERMS, part)


def second_kernel(
    received_ref, fields_ref, points_ref, far_hot_ref, pair_ref, pair_hot_ref, resid_ref, image_ref,
    maps_ref, far_points_ref, smoother_ref, metric_ref, helmholtz_ref, first_ref, inner_ref,
    smoothed_ref, back_ref, local_ref, sent_ref,
):
    elements = helmholtz_ref.shape[0]
    peers = points_ref.shape[0] - 2 * FACE_ROWS
    solved = get_solved(received_ref, ROWS, peers)
    resid = resid_ref[...]
    flat = whole(fields_ref[8 * elements : 8 * elements + 1, :])
    rough = smoother_ref[...] * resid
    smoothed = rough + prolonged(solved[0], flat, elements)
    smoothed_ref[...] = smoothed
    apply(
        rough, smoothed, ROWS, received_ref, flat, maps_ref[...], far_points_ref[...], solved, metric_ref,
        helmholtz_ref, first_ref, inner_ref, pair_ref,
        loaded(pair_places(pair_ref, elements), pair_hot_ref), points_ref, far_hot_ref,
        [total_of(resid * smoothed), total_of(image_ref[...] * smoothed)],
        back_ref, local_ref, sent_ref,
    )


def final_kernel(
    received_ref, points_ref, far_hot_ref, pair_ref, pair_hot_ref, old_ref, field_ref, resid_ref, old_image_ref,
    scalars_ref, back_ref, local_ref, helmholtz_ref,
    solution_ref, residual_ref,
):
    before = unpacked(scalars_ref[...], 2)
    now = unpacked(jnp.sum(get(received_ref, ROWS, TERMS), axis=0, keepdims=True), 3)
    alpha = before[0] / before[1]
    beta = now[0] / before[0]
    curved = now[2] + beta * (2.0 * now[1] + beta * before[1])
    step = now[0] / curved
    old = old_ref[...]
    direction = field_ref[...] + beta * old
    solution_ref[...] = wide_of(alpha * old + step * direction)
    image = image_of(
        field_ref, back_ref, local_ref, received_ref, helmholtz_ref, pair_ref,
        pair_hot_ref, points_ref, far_hot_ref,
    )
    image = image + beta * old_image_ref[...]
    residual_ref[...] = wide_of(resid_ref[...] - step * image)


def call(kernel, outs, *args, copied=False):
    space = pl.ANY if copied else pltpu.VMEM
    scratch = [pltpu.VMEM(arg.shape, arg.dtype) for arg in args] if copied else []
    if copied:
        args = [pltpu.with_memory_space_constraint(arg, pltpu.HBM) for arg in args]
    return pl.pallas_call(
        kernel,
        out_shape=[
            jax.ShapeDtypeStruct(*(out if isinstance(out[0], tuple) else (out, F32))) for out in outs
        ],
        in_specs=[pl.BlockSpec(memory_space=space)] * len(args),
        out_specs=[pl.BlockSpec(memory_space=pltpu.VMEM)] * len(outs),
        scratch_shapes=scratch + ([pltpu.SemaphoreType.DMA((len(args),))] if copied else []),
        compiler_params=pltpu.CompilerParams(vmem_limit_bytes=24 * 1024 * 1024),
    )(*args)


def body(
    right_side,
    metric,
    helmholtz,
    jacobi,
    pair_list,
    shared_slots,
    face_points,
    coarse_map,
    coarse_inverse,
):
    peers = lax.axis_size("sub")
    groups = lax.axis_size("grp")
    t = {name: jnp.asarray(value) for name, value in tables().items()}
    elements = right_side.shape[0]
    field = (4 * elements, LANES)
    local = (1, pair_list.shape[0] * pair_list.shape[1])
    points_shape = (peers + 2 * FACE_ROWS, LANES)
    sent_shape = (groups * peers * ROWS, LANES)

    def exchange(sent):
        rows = sent.reshape(groups * peers, 1, -1)
        return lax.all_to_all(rows, ("grp", "sub"), 0, 0, tiled=True).reshape(sent.shape)

    far_hot_shape = (points_shape[0] * LANES // 2, STEP)
    pair_hot_shape = (local[1] * LANES // STEP, STEP)

    sent, fields, points, far_hot, smoother, solver = call(
        first_kernel,
        [
            (groups * peers * FIRST_ROWS, LANES),
            (8 * elements + 8, LANES),
            (points_shape, jnp.int32),
            (far_hot_shape, BF16),
            field,
            (NC, NC),
        ],
        right_side, jacobi, coarse_inverse, coarse_map, shared_slots, face_points, copied=True,
    )
    smoothed, maps, far_points, back, near, sent, pair_hot = call(
        start_kernel,
        [field, (points_shape, jnp.int32), (points_shape, jnp.int32), field, local, sent_shape,
         (pair_hot_shape, BF16)],
        exchange(sent), fields, points, far_hot, pair_list, metric, helmholtz,
        t["first"], t["inner"],
    )
    image, resid, scalars, sent = call(
        middle_kernel, [field, field, (1, LANES), sent_shape],
        exchange(sent), fields, points, far_hot, pair_list, pair_hot, smoother, helmholtz, solver,
        smoothed, back, near,
    )
    second, back, near, sent = call(
        second_kernel, [field, field, local, sent_shape],
        exchange(sent), fields, points, far_hot, pair_list, pair_hot, resid, image, maps, far_points, smoother,
        metric, helmholtz, t["first"], t["inner"],
    )
    return tuple(
        call(
            final_kernel, [right_side.shape, right_side.shape],
            exchange(sent), points, far_hot, pair_list, pair_hot, smoothed, second, resid, image, scalars,
            back, near, helmholtz,
        )
    )


def solution(mesh):
    in_specs = (
        P(("grp", "sub"), None),
        P(("grp", "sub"), None),
        P(("grp", "sub"), None),
        P(("grp", "sub"), None),
        P(None, ("grp", "sub")),
        P(("grp", "sub"), None, None),
        P(None, ("grp", "sub")),
        P(None, ("grp", "sub")),
        P("grp", None, None),
    )
    out_specs = (P(("grp", "sub"), None), P(("grp", "sub"), None))
    return jax.shard_map(body, mesh=mesh, in_specs=in_specs, out_specs=out_specs, check_vma=False)
```

```python
import jax
import jax.numpy as jnp
import ml_dtypes
import numpy as np
from jax import lax
from jax.experimental import pallas as pl
from jax.experimental.pallas import tpu as pltpu
from jax.sharding import PartitionSpec as P

NC = 64
POINTS = 512
LANES = 128
STEP = 256
FACE_ROWS = 4
ROWS = 5
FIRST_ROWS = 10
TERMS = FACE_ROWS
F32 = jnp.float32
BF16 = jnp.bfloat16
NT = (((1,), (1,)), ((), ()))


def split_constant(array):
    high = array.astype(ml_dtypes.bfloat16)
    low = (array - high.astype(np.float64)).astype(ml_dtypes.bfloat16)
    return high, low


def tables():
    order_index = np.arange(8)
    colloc = np.cos(np.pi * order_index / 7.0)
    end_weights = (
        np.where((order_index == 0) | (order_index == 7), 2.0, 1.0) * (-1.0) ** order_index
    )
    spacing = colloc[:, None] - colloc[None, :] + np.eye(8)
    raw_matrix = np.outer(end_weights, 1.0 / end_weights) / spacing
    off_part = raw_matrix * (1.0 - np.eye(8))
    derivative = 0.25 * (off_part - np.eye(8) * off_part.sum(axis=1)[:, None])
    along_inner = np.concatenate(
        [np.kron(np.eye(2), np.kron(derivative, np.eye(8))).T, np.kron(np.eye(16), derivative).T],
        axis=1,
    )
    high, low = split_constant(along_inner)
    inner = np.concatenate([high, low], axis=0)

    half = np.arange(LANES) // 64

    def first_rows(matrix):
        rows = []
        for to in range(4):
            for at in range(4):
                rows.append(matrix[2 * to + half, 2 * at + half])
                rows.append(matrix[2 * to + half, 2 * at + 1 - half])
        return np.stack(rows).astype(np.float32)

    return {
        "inner": inner,
        "first": np.concatenate([first_rows(derivative), first_rows(derivative.T)], axis=0),
    }


def split(value):
    high = value.astype(BF16)
    return high, (value - high.astype(F32)).astype(BF16)


def rows_of(wide):
    return jnp.concatenate([wide[:, LANES * c : LANES * (c + 1)] for c in range(4)], axis=0)


def wide_of(rows):
    elements = rows.shape[0] // 4
    return jnp.concatenate([rows[c * elements : (c + 1) * elements] for c in range(4)], axis=1)


def locate(points, elements):
    element = points >> 9
    chunk = (points >> 7) & 3
    row = jnp.where(points < elements * POINTS, chunk * elements + element, 4 * elements)
    return row, points & (LANES - 1)


def one_hot(index, count):
    steps = lax.broadcasted_iota(jnp.int32, (count, index.shape[1]), 0)
    return steps == index


def lane_hot(lane):
    steps = lax.broadcasted_iota(jnp.int32, (LANES, lane.shape[1]), 0).astype(F32).astype(BF16)
    one = jnp.ones(steps.shape, BF16)
    return jnp.where(steps == lane.astype(F32).astype(BF16), one, jnp.zeros_like(one))


def take(values, lanes):
    return jnp.take_along_axis(values, lanes, axis=1, mode="promise_in_bounds")


def gather(field, chunks):
    count = field.shape[0]
    both = jnp.concatenate(split(field), axis=0)
    out = []
    for row, hot in chunks:
        picked = jnp.dot(both, hot, preferred_element_type=F32)
        mine = jnp.where(one_hot(row, count), picked[:count] + picked[count:], 0.0)
        out.append(jnp.sum(mine, axis=0, keepdims=True))
    return out


def scatter(rows, chunks, values):
    total = jnp.zeros((2 * rows, LANES), F32)
    for (row, hot), value in zip(chunks, values):
        steps = lax.broadcasted_iota(jnp.int32, (rows, row.shape[1]), 0).astype(F32).astype(BF16)
        mine = steps == row.astype(F32).astype(BF16)
        parts = [jnp.where(mine, part, jnp.zeros_like(steps)) for part in split(value)]
        total = total + lax.dot_general(
            jnp.concatenate(parts, axis=0), hot, NT, preferred_element_type=F32
        )
    return total[:rows] + total[rows:]


def chunked(row, lane):
    return [
        (row[:, at : at + STEP], lane[:, at : at + STEP]) for at in range(0, row.shape[1], STEP)
    ]


def cut(row):
    return [row[:, at : at + STEP] for at in range(0, row.shape[1], STEP)]


def pair_places(pair_ref, elements):
    row, lane = locate(pair_ref[...], elements)
    return chunked(row[0:1], lane[0:1]) + chunked(row[1:2], lane[1:2])


def joined(rows):
    return [
        jnp.concatenate([rows[at : at + 1], rows[at + 1 : at + 2]], axis=1)
        for at in range(0, rows.shape[0], 2)
    ]


def far_places(points, elements):
    row, lane = locate(points, elements)
    return list(zip(joined(row), joined(lane)))


def built(places, hot_ref):
    out = []
    for k, (row, lane) in enumerate(places):
        hot = lane_hot(lane)
        hot_ref[k * LANES : (k + 1) * LANES, :] = hot
        out.append((row, hot))
    return out


def loaded(places, hot_ref):
    return [
        (row, hot_ref[k * LANES : (k + 1) * LANES, :]) for k, (row, lane) in enumerate(places)
    ]


def halves(wide):
    return [wide[:, at : at + LANES] for at in range(0, wide.shape[1], LANES)]


def own_group(devices, peers, away=0):
    shape = (devices, LANES)
    return lax.broadcasted_iota(jnp.int32, shape, 0) // peers - lax.axis_index("grp") == away


def send_rows(sent_ref, count, at, rows, peers):
    devices = sent_ref.shape[0] // count
    above = own_group(devices, peers, 1)
    shared = jnp.concatenate([rows[:peers]] * (devices // peers), axis=0)
    for r in range(FACE_ROWS):
        down = rows[peers + r : peers + r + 1]
        up = rows[peers + FACE_ROWS + r : peers + FACE_ROWS + r + 1]
        out = jnp.where(above, up, down)
        if r == 0:
            out = jnp.where(own_group(devices, peers), shared, out)
        sent_ref[pl.ds(at + r, devices, count), :] = out


def send_same(sent_ref, count, at, row):
    devices = sent_ref.shape[0] // count
    sent_ref[pl.ds(at, devices, count), :] = jnp.broadcast_to(row, (devices, LANES))


def send_values(sent_ref, count, values, peers):
    rows = jnp.concatenate([row for pair in values for row in halves(pair)], axis=0)
    send_rows(sent_ref, count, 0, rows, peers)


def get(received_ref, count, at):
    return received_ref[pl.ds(at, received_ref.shape[0] // count, count), :]


def inside(received_ref, count, peers, away):
    groups = received_ref.shape[0] // (count * peers)
    group = lax.axis_index("grp") + away
    kept = jnp.clip(group, 0, groups - 1)
    return kept, jnp.where(group == kept, 1.0, 0.0)


def get_group(received_ref, count, at, peers, away=0):
    group, kept = inside(received_ref, count, peers, away)
    return received_ref[pl.ds(group * (peers * count) + at, peers, count), :] * kept


def get_side(received_ref, count, at, rows, peers, away):
    group, kept = inside(received_ref, count, peers, away)
    place = group * peers + lax.axis_index("sub")
    return received_ref[pl.ds(place * count + at, rows), :] * kept


def get_rows(received_ref, count, at, peers):
    sides = [get_side(received_ref, count, at, FACE_ROWS, peers, away) for away in (-1, 1)]
    return jnp.concatenate([get_group(received_ref, count, at, peers)] + sides, axis=0)


def swapped(values):
    count = len(values) // 2
    return values[count:] + values[:count]


def along_first(field, table_ref, base):
    elements = field.shape[0] // 4
    turned = pltpu.roll(field, 64, axis=1)
    out = []
    for to in range(4):
        total = None
        for at in range(4):
            place = base + 2 * (4 * to + at)
            rows = slice(at * elements, (at + 1) * elements)
            term = (
                table_ref[place : place + 1, :] * field[rows]
                + table_ref[place + 1 : place + 2, :] * turned[rows]
            )
            total = term if total is None else total + term
        out.append(total)
    return jnp.concatenate(out, axis=0)


def stiffness(field, metric_ref, first_ref, inner_ref):
    metric = [rows_of(metric_ref[:, POINTS * d : POINTS * (d + 1)]) for d in range(3)]
    count = field.shape[0]
    grad_first = along_first(field, first_ref, 0)
    high, low = split(field)
    both = jnp.dot(
        jnp.concatenate([high, low], axis=0), inner_ref[:LANES], preferred_element_type=F32
    )
    inner = both[:count] + both[count:]
    inner = inner + jnp.dot(high, inner_ref[LANES:], preferred_element_type=F32)
    flux_first = metric[0] * grad_first
    flux = jnp.concatenate([metric[1], metric[2]], axis=1) * inner
    high, low = split(flux)
    both = lax.dot_general(
        jnp.concatenate([high, low], axis=0), inner_ref[:LANES], NT, preferred_element_type=F32
    )
    back = both[:count] + both[count:]
    back = back + lax.dot_general(high, inner_ref[LANES:], NT, preferred_element_type=F32)
    back = back + along_first(flux_first, first_ref, 32)
    energy = flux * inner
    return back, flux_first * grad_first + energy[:, :LANES] + energy[:, LANES:]


def factors(points):
    nodes = 0.5 * (1.0 + np.cos(np.pi * np.arange(8) / 7.0))
    lane = lax.broadcasted_iota(jnp.int32, (1, LANES), 1)
    table = jnp.full(lane.shape, nodes[7], F32)
    for m in range(7):
        table = jnp.where(lane == m, float(nodes[m]), table)
    table = jnp.broadcast_to(table, points.shape)
    out = []
    for shift in (6, 3, 0):
        near = take(table, (points >> shift) & 7)
        out.append((near, 1.0 - near))
    return out


def corners(points):
    first, second, third = factors(points)
    return [
        first[q >> 2 & 1] * (second[q >> 1 & 1] * third[q & 1]) for q in range(8)
    ]


def own_corners():
    shape = (8, LANES)
    chunk = lax.broadcasted_iota(jnp.int32, shape, 0) & 3
    return corners(chunk * LANES + lax.broadcasted_iota(jnp.int32, shape, 1))


def flat_map(mapped):
    elements = mapped.shape[1]
    shape = (8, 8 * elements)
    lane = lax.broadcasted_iota(jnp.int32, shape, 1)
    padded = jnp.concatenate(
        [mapped.astype(F32), jnp.zeros((8, shape[1] - elements), F32)], axis=1
    )
    wide = take(padded, lane & (elements - 1))
    keep = lax.broadcasted_iota(jnp.int32, shape, 0) == lane // elements
    return jnp.sum(jnp.where(keep, wide, 0.0), axis=0, keepdims=True)


def one_vertex(flat):
    return jnp.where(one_hot(whole(flat), NC), 1.0, 0.0)


def whole(values):
    return (values + 0.5).astype(jnp.int32)


def own_element(elements, width):
    shape = (elements, width)
    return lax.broadcasted_iota(jnp.int32, shape, 0) == (
        lax.broadcasted_iota(jnp.int32, shape, 1) % elements
    )


def own_place(elements, q):
    shape = (elements, 8 * elements)
    lane = lax.broadcasted_iota(jnp.int32, shape, 1)
    return lane == lax.broadcasted_iota(jnp.int32, shape, 0) + q * elements


def coarse_part(field, vertices, inverse):
    elements = field.shape[0] // 4
    flat = jnp.zeros((elements, 8 * elements), F32)
    for q, corner in enumerate(own_corners()):
        inner = None
        for c in range(4):
            term = field[c * elements : (c + 1) * elements] * corner[c : c + 1]
            inner = term if inner is None else inner + term
        flat = jnp.where(own_place(elements, q), jnp.sum(inner, axis=1, keepdims=True), flat)
    flat = jnp.sum(flat, axis=0, keepdims=True)
    part = jnp.sum(vertices * flat, axis=1, keepdims=True)
    part = jnp.sum(inverse * part, axis=0, keepdims=True)
    return jnp.concatenate([part, jnp.zeros((1, LANES - NC), F32)], axis=1)


def get_solved(received_ref, count, peers):
    return [
        jnp.sum(get_group(received_ref, count, TERMS, peers, away), axis=0, keepdims=True)
        for away in (0, -1, 1)
    ]


def prolonged(solved, flat, elements):
    shape = (elements, LANES)
    element = lax.broadcasted_iota(jnp.int32, shape, 0)
    at_corner = take(jnp.broadcast_to(solved, shape), jnp.broadcast_to(flat, shape))
    out = [None] * 4
    for q, corner in enumerate(own_corners()):
        value = take(at_corner, element + q * elements)
        for c in range(4):
            term = value * corner[c : c + 1]
            out[c] = term if out[c] is None else out[c] + term
    return jnp.concatenate(out, axis=0)


def prolonged_at(solved, maps, points, elements):
    at_corner = take(solved, maps)
    element = (points >> 9) & (elements - 1)
    total = jnp.zeros(points.shape, F32)
    for q, corner in enumerate(corners(points)):
        total = total + corner * take(at_corner, element + q * elements)
    return total


def total_of(array):
    return jnp.sum(jnp.sum(array, axis=0, keepdims=True), axis=1, keepdims=True)


def packed(values):
    lane = lax.broadcasted_iota(jnp.int32, (1, LANES), 1)
    out = jnp.zeros((1, LANES), F32)
    for k, value in enumerate(values):
        out = jnp.where(lane == k, value, out)
    return out


def unpacked(row, count):
    lane = lax.broadcasted_iota(jnp.int32, row.shape, 1)
    return [
        jnp.sum(jnp.where(lane == k, row, 0.0), axis=1, keepdims=True) for k in range(count)
    ]


def first_kernel(
    right_hbm, jacobi_hbm, inverse_hbm, map_hbm, slot_hbm, face_hbm,
    sent_ref, fields_ref, points_ref, far_hot_ref,
    right_ref, jacobi_ref, inverse_ref, map_ref, slot_ref, face_ref, sems,
):
    copies = []
    for k, (source, target) in enumerate(
        (
            (face_hbm, face_ref),
            (slot_hbm, slot_ref),
            (right_hbm, right_ref),
            (jacobi_hbm, jacobi_ref),
            (map_hbm, map_ref),
            (inverse_hbm, inverse_ref),
        )
    ):
        copy = pltpu.make_async_copy(source, target, sems.at[k])
        copy.start()
        copies.append(copy)
    elements = right_ref.shape[0]
    peers = slot_ref.shape[1]
    for copy in copies[:2]:
        copy.wait()
    faces = face_ref[...]
    faces = jnp.concatenate(halves(faces[0:1]) + halves(faces[1:2]), axis=0)
    points = jnp.concatenate([slot_ref[0], faces], axis=0)
    points_ref[...] = points
    places = built(far_places(points, elements), far_hot_ref)
    send_rows(sent_ref, FIRST_ROWS, TERMS + 2, points.astype(F32), peers)
    for copy in copies[2:]:
        copy.wait()
    resid = rows_of(right_ref[...])
    flat = flat_map(map_ref[...])
    smoothed = rows_of(jacobi_ref[...]) * resid
    fields_ref[0 : 4 * elements, :] = resid
    fields_ref[4 * elements : 8 * elements, :] = smoothed
    fields_ref[8 * elements :, :] = jnp.broadcast_to(flat, (8, LANES))
    part = coarse_part(resid, one_vertex(flat), inverse_ref[0])
    values = gather(smoothed, places)
    send_values(sent_ref, FIRST_ROWS, values, peers)
    send_same(sent_ref, FIRST_ROWS, TERMS, part)
    send_same(sent_ref, FIRST_ROWS, TERMS + 1, flat)


def far_maps(received_ref, peers):
    own = get_group(received_ref, FIRST_ROWS, TERMS + 1, peers)
    sides = [
        jnp.broadcast_to(
            get_side(received_ref, FIRST_ROWS, TERMS + 1, 1, peers, away), (FACE_ROWS, LANES)
        )
        for away in (-1, 1)
    ]
    return whole(jnp.concatenate([own] + sides, axis=0))


def apply(
    rough, smoothed, count, received_ref, flat, maps, far_points, solved, metric_ref, helmholtz_ref,
    first_ref, inner_ref, pair_ref, pairs, points_ref, far_hot_ref, dots, back_ref, local_ref,
    sent_ref,
):
    elements = smoothed.shape[0] // 4
    peers = points_ref.shape[0] - 2 * FACE_ROWS
    far = loaded(far_places(points_ref[...], elements), far_hot_ref)
    near = gather(rough, pairs)
    partners = pair_ref[...]
    partners = jnp.concatenate(halves(partners[1:2]) + halves(partners[0:1]), axis=0)
    counts = (peers, FACE_ROWS, FACE_ROWS, partners.shape[0])
    spread = [
        jnp.broadcast_to(part, (n, LANES)) for part, n in zip((*solved, solved[0]), counts)
    ]
    coarse = prolonged_at(
        jnp.concatenate(spread, axis=0),
        jnp.concatenate([maps, jnp.broadcast_to(flat, partners.shape)], axis=0),
        jnp.concatenate([far_points, partners], axis=0),
        elements,
    )
    split_at = points_ref.shape[0]
    incoming = get_rows(received_ref, count, 0, peers) + coarse[:split_at]
    values = [value + more for value, more in zip(swapped(near), joined(coarse[split_at:]))]
    values = values + joined(incoming)
    summed = smoothed + scatter(smoothed.shape[0], pairs + far, values)
    back, energy = stiffness(summed, metric_ref, first_ref, inner_ref)
    energy = energy + rows_of(helmholtz_ref[...]) * smoothed * smoothed
    back_ref[...] = back
    values = gather(back, pairs + far)
    near = swapped(values[: len(pairs)])
    for k, value in enumerate(near):
        local_ref[0:1, k * STEP : (k + 1) * STEP] = value
    send_values(sent_ref, ROWS, values[len(pairs) :], peers)
    send_same(sent_ref, ROWS, TERMS, packed(dots + [total_of(energy)]))


def image_of(
    field_ref, back_ref, local_ref, received_ref, helmholtz_ref, pair_ref, pair_hot_ref, points_ref,
    far_hot_ref,
):
    elements = field_ref.shape[0] // 4
    peers = points_ref.shape[0] - 2 * FACE_ROWS
    chunks = loaded(pair_places(pair_ref, elements), pair_hot_ref)
    chunks = chunks + loaded(far_places(points_ref[...], elements), far_hot_ref)
    values = cut(local_ref[...]) + joined(get_rows(received_ref, ROWS, 0, peers))
    summed = back_ref[...] + scatter(field_ref.shape[0], chunks, values)
    return summed + rows_of(helmholtz_ref[...]) * field_ref[...]


def start_kernel(
    received_ref, fields_ref, points_ref, far_hot_ref, pair_ref, metric_ref, helmholtz_ref,
    first_ref, inner_ref,
    smoothed_ref, maps_ref, far_points_ref, back_ref, local_ref, sent_ref, pair_hot_ref,
):
    elements = helmholtz_ref.shape[0]
    peers = points_ref.shape[0] - 2 * FACE_ROWS
    solved = get_solved(received_ref, FIRST_ROWS, peers)
    resid = fields_ref[0 : 4 * elements, :]
    flat = whole(fields_ref[8 * elements : 8 * elements + 1, :])
    rough = fields_ref[4 * elements : 8 * elements, :]
    smoothed = rough + prolonged(solved[0], flat, elements)
    smoothed_ref[...] = smoothed
    maps = far_maps(received_ref, peers)
    maps_ref[...] = maps
    far_points = whole(get_rows(received_ref, FIRST_ROWS, TERMS + 2, peers))
    far_points_ref[...] = far_points
    apply(
        rough, smoothed, FIRST_ROWS, received_ref, flat, maps, far_points, solved, metric_ref,
        helmholtz_ref, first_ref, inner_ref, pair_ref,
        built(pair_places(pair_ref, elements), pair_hot_ref), points_ref, far_hot_ref,
        [total_of(resid * smoothed)], back_ref, local_ref, sent_ref,
    )


def middle_kernel(
    received_ref, fields_ref, points_ref, far_hot_ref, pair_ref, pair_hot_ref, jacobi_ref, helmholtz_ref,
    inverse_ref, smoothed_ref, back_ref, local_ref,
    image_ref, resid_ref, scalars_ref, sent_ref,
):
    elements = helmholtz_ref.shape[0]
    peers = points_ref.shape[0] - 2 * FACE_ROWS
    dots = jnp.sum(get(received_ref, ROWS, TERMS), axis=0, keepdims=True)
    scalars_ref[...] = dots
    values = unpacked(dots, 2)
    alpha = values[0] / values[1]
    image = image_of(
        smoothed_ref, back_ref, local_ref, received_ref, helmholtz_ref, pair_ref,
        pair_hot_ref, points_ref, far_hot_ref,
    )
    image_ref[...] = image
    resid = fields_ref[0 : 4 * elements, :] - alpha * image
    resid_ref[...] = resid
    vertices = one_vertex(fields_ref[8 * elements : 8 * elements + 1, :])
    part = coarse_part(resid, vertices, inverse_ref[0])
    values = gather(
        rows_of(jacobi_ref[...]) * resid, loaded(far_places(points_ref[...], elements), far_hot_ref),
    )
    send_values(sent_ref, ROWS, values, peers)
    send_same(sent_ref, ROWS, TERMS, part)


def second_kernel(
    received_ref, fields_ref, points_ref, far_hot_ref, pair_ref, pair_hot_ref, resid_ref, image_ref,
    maps_ref, far_points_ref, jacobi_ref, metric_ref, helmholtz_ref, first_ref, inner_ref,
    smoothed_ref, back_ref, local_ref, sent_ref,
):
    elements = helmholtz_ref.shape[0]
    peers = points_ref.shape[0] - 2 * FACE_ROWS
    solved = get_solved(received_ref, ROWS, peers)
    resid = resid_ref[...]
    flat = whole(fields_ref[8 * elements : 8 * elements + 1, :])
    rough = rows_of(jacobi_ref[...]) * resid
    smoothed = rough + prolonged(solved[0], flat, elements)
    smoothed_ref[...] = smoothed
    apply(
        rough, smoothed, ROWS, received_ref, flat, maps_ref[...], far_points_ref[...], solved, metric_ref,
        helmholtz_ref, first_ref, inner_ref, pair_ref,
        loaded(pair_places(pair_ref, elements), pair_hot_ref), points_ref, far_hot_ref,
        [total_of(resid * smoothed), total_of(image_ref[...] * smoothed)],
        back_ref, local_ref, sent_ref,
    )


def final_kernel(
    received_ref, points_ref, far_hot_ref, pair_ref, pair_hot_ref, old_ref, field_ref, resid_ref, old_image_ref,
    scalars_ref, back_ref, local_ref, helmholtz_ref,
    solution_ref, residual_ref,
):
    before = unpacked(scalars_ref[...], 2)
    now = unpacked(jnp.sum(get(received_ref, ROWS, TERMS), axis=0, keepdims=True), 3)
    alpha = before[0] / before[1]
    beta = now[0] / before[0]
    curved = now[2] + beta * (2.0 * now[1] + beta * before[1])
    step = now[0] / curved
    old = old_ref[...]
    direction = field_ref[...] + beta * old
    solution_ref[...] = wide_of(alpha * old + step * direction)
    image = image_of(
        field_ref, back_ref, local_ref, received_ref, helmholtz_ref, pair_ref,
        pair_hot_ref, points_ref, far_hot_ref,
    )
    image = image + beta * old_image_ref[...]
    residual_ref[...] = wide_of(resid_ref[...] - step * image)


def call(kernel, outs, *args, copied=False):
    space = pl.ANY if copied else pltpu.VMEM
    scratch = [pltpu.VMEM(arg.shape, arg.dtype) for arg in args] if copied else []
    if copied:
        args = [pltpu.with_memory_space_constraint(arg, pltpu.HBM) for arg in args]
    return pl.pallas_call(
        kernel,
        out_shape=[
            jax.ShapeDtypeStruct(*(out if isinstance(out[0], tuple) else (out, F32))) for out in outs
        ],
        in_specs=[pl.BlockSpec(memory_space=space)] * len(args),
        out_specs=[pl.BlockSpec(memory_space=pltpu.VMEM)] * len(outs),
        scratch_shapes=scratch + ([pltpu.SemaphoreType.DMA((len(args),))] if copied else []),
        compiler_params=pltpu.CompilerParams(vmem_limit_bytes=24 * 1024 * 1024),
    )(*args)


def body(
    right_side,
    metric,
    helmholtz,
    jacobi,
    pair_list,
    shared_slots,
    face_points,
    coarse_map,
    coarse_inverse,
):
    peers = lax.axis_size("sub")
    groups = lax.axis_size("grp")
    t = {name: jnp.asarray(value) for name, value in tables().items()}
    elements = right_side.shape[0]
    field = (4 * elements, LANES)
    local = (1, pair_list.shape[0] * pair_list.shape[1])
    points_shape = (peers + 2 * FACE_ROWS, LANES)
    sent_shape = (groups * peers * ROWS, LANES)

    def exchange(sent):
        rows = sent.reshape(groups * peers, 1, -1)
        return lax.all_to_all(rows, ("grp", "sub"), 0, 0, tiled=True).reshape(sent.shape)

    far_hot_shape = (points_shape[0] * LANES // 2, STEP)
    pair_hot_shape = (local[1] * LANES // STEP, STEP)

    sent, fields, points, far_hot = call(
        first_kernel,
        [
            (groups * peers * FIRST_ROWS, LANES),
            (8 * elements + 8, LANES),
            (points_shape, jnp.int32),
            (far_hot_shape, BF16),
        ],
        right_side, jacobi, coarse_inverse, coarse_map, shared_slots, face_points, copied=True,
    )
    smoothed, maps, far_points, back, near, sent, pair_hot = call(
        start_kernel,
        [field, (points_shape, jnp.int32), (points_shape, jnp.int32), field, local, sent_shape,
         (pair_hot_shape, BF16)],
        exchange(sent), fields, points, far_hot, pair_list, metric, helmholtz,
        t["first"], t["inner"],
    )
    image, resid, scalars, sent = call(
        middle_kernel, [field, field, (1, LANES), sent_shape],
        exchange(sent), fields, points, far_hot, pair_list, pair_hot, jacobi, helmholtz, coarse_inverse,
        smoothed, back, near,
    )
    second, back, near, sent = call(
        second_kernel, [field, field, local, sent_shape],
        exchange(sent), fields, points, far_hot, pair_list, pair_hot, resid, image, maps, far_points, jacobi,
        metric, helmholtz, t["first"], t["inner"],
    )
    return tuple(
        call(
            final_kernel, [right_side.shape, right_side.shape],
            exchange(sent), points, far_hot, pair_list, pair_hot, smoothed, second, resid, image, scalars,
            back, near, helmholtz,
        )
    )


def solution(mesh):
    in_specs = (
        P(("grp", "sub"), None),
        P(("grp", "sub"), None),
        P(("grp", "sub"), None),
        P(("grp", "sub"), None),
        P(None, ("grp", "sub")),
        P(("grp", "sub"), None, None),
        P(None, ("grp", "sub")),
        P(None, ("grp", "sub")),
        P("grp", None, None),
    )
    out_specs = (P(("grp", "sub"), None), P(("grp", "sub"), None))
    return jax.shard_map(body, mesh=mesh, in_specs=in_specs, out_specs=out_specs, check_vma=False)
```

```python
import jax
import jax.numpy as jnp
import ml_dtypes
import numpy as np
from jax import lax
from jax.experimental import pallas as pl
from jax.experimental.pallas import tpu as pltpu
from jax.sharding import PartitionSpec as P

NC = 64
POINTS = 512
LANES = 128
STEP = 256
FACE_ROWS = 4
ROWS = 5
FIRST_ROWS = 10
TERMS = FACE_ROWS
F32 = jnp.float32
BF16 = jnp.bfloat16
NT = (((1,), (1,)), ((), ()))


def split_constant(array):
    high = array.astype(ml_dtypes.bfloat16)
    low = (array - high.astype(np.float64)).astype(ml_dtypes.bfloat16)
    return high, low


def tables():
    order_index = np.arange(8)
    colloc = np.cos(np.pi * order_index / 7.0)
    end_weights = (
        np.where((order_index == 0) | (order_index == 7), 2.0, 1.0) * (-1.0) ** order_index
    )
    spacing = colloc[:, None] - colloc[None, :] + np.eye(8)
    raw_matrix = np.outer(end_weights, 1.0 / end_weights) / spacing
    off_part = raw_matrix * (1.0 - np.eye(8))
    derivative = 0.25 * (off_part - np.eye(8) * off_part.sum(axis=1)[:, None])
    along_inner = np.concatenate(
        [np.kron(np.eye(2), np.kron(derivative, np.eye(8))).T, np.kron(np.eye(16), derivative).T],
        axis=1,
    )
    high, low = split_constant(along_inner)
    inner = np.concatenate([high, low], axis=0)

    half = np.arange(LANES) // 64

    def first_rows(matrix):
        rows = []
        for to in range(4):
            for at in range(4):
                rows.append(matrix[2 * to + half, 2 * at + half])
                rows.append(matrix[2 * to + half, 2 * at + 1 - half])
        return np.stack(rows).astype(np.float32)

    return {
        "inner": inner,
        "first": np.concatenate([first_rows(derivative), first_rows(derivative.T)], axis=0),
    }


def split(value):
    high = value.astype(BF16)
    return high, (value - high.astype(F32)).astype(BF16)


def rows_of(wide):
    return jnp.concatenate([wide[:, LANES * c : LANES * (c + 1)] for c in range(4)], axis=0)


def wide_of(rows):
    elements = rows.shape[0] // 4
    return jnp.concatenate([rows[c * elements : (c + 1) * elements] for c in range(4)], axis=1)


def locate(points, elements):
    element = points >> 9
    chunk = (points >> 7) & 3
    row = jnp.where(points < elements * POINTS, chunk * elements + element, 4 * elements)
    return row, points & (LANES - 1)


def one_hot(index, count):
    steps = lax.broadcasted_iota(jnp.int32, (count, index.shape[1]), 0)
    return steps == index


def lane_hot(lane):
    steps = lax.broadcasted_iota(jnp.int32, (LANES, lane.shape[1]), 0).astype(F32).astype(BF16)
    one = jnp.ones(steps.shape, BF16)
    return jnp.where(steps == lane.astype(F32).astype(BF16), one, jnp.zeros_like(one))


def take(values, lanes):
    return jnp.take_along_axis(values, lanes, axis=1, mode="promise_in_bounds")


def gather(field, chunks):
    count = field.shape[0]
    both = jnp.concatenate(split(field), axis=0)
    out = []
    for row, hot in chunks:
        picked = jnp.dot(both, hot, preferred_element_type=F32)
        mine = jnp.where(one_hot(row, count), picked[:count] + picked[count:], 0.0)
        out.append(jnp.sum(mine, axis=0, keepdims=True))
    return out


def scatter(rows, chunks, values):
    total = jnp.zeros((2 * rows, LANES), F32)
    for at in range(0, len(chunks), 2):
        left, right = [], []
        for (row, hot), value in zip(chunks[at : at + 2], values[at : at + 2]):
            steps = lax.broadcasted_iota(jnp.int32, (rows, STEP), 0).astype(F32).astype(BF16)
            mine = steps == row.astype(F32).astype(BF16)
            parts = [jnp.where(mine, part, jnp.zeros_like(steps)) for part in split(value)]
            left.append(jnp.concatenate(parts, axis=0))
            right.append(hot)
        total = total + lax.dot_general(
            jnp.concatenate(left, axis=1),
            jnp.concatenate(right, axis=1),
            NT,
            preferred_element_type=F32,
        )
    return total[:rows] + total[rows:]


def chunked(row, lane):
    return [
        (row[:, at : at + STEP], lane[:, at : at + STEP]) for at in range(0, row.shape[1], STEP)
    ]


def cut(row):
    return [row[:, at : at + STEP] for at in range(0, row.shape[1], STEP)]


def pair_places(pair_ref, elements):
    row, lane = locate(pair_ref[...], elements)
    return chunked(row[0:1], lane[0:1]) + chunked(row[1:2], lane[1:2])


def joined(rows):
    return [
        jnp.concatenate([rows[at : at + 1], rows[at + 1 : at + 2]], axis=1)
        for at in range(0, rows.shape[0], 2)
    ]


def far_places(points, elements):
    row, lane = locate(points, elements)
    return list(zip(joined(row), joined(lane)))


def built(places, hot_ref):
    out = []
    for k, (row, lane) in enumerate(places):
        hot = lane_hot(lane)
        hot_ref[k * LANES : (k + 1) * LANES, :] = hot
        out.append((row, hot))
    return out


def loaded(places, hot_ref):
    return [
        (row, hot_ref[k * LANES : (k + 1) * LANES, :]) for k, (row, lane) in enumerate(places)
    ]


def halves(wide):
    return [wide[:, at : at + LANES] for at in range(0, wide.shape[1], LANES)]


def own_group(devices, peers, away=0):
    shape = (devices, LANES)
    return lax.broadcasted_iota(jnp.int32, shape, 0) // peers - lax.axis_index("grp") == away


def send_rows(sent_ref, count, at, rows, peers):
    devices = sent_ref.shape[0] // count
    above = own_group(devices, peers, 1)
    shared = jnp.concatenate([rows[:peers]] * (devices // peers), axis=0)
    for r in range(FACE_ROWS):
        down = rows[peers + r : peers + r + 1]
        up = rows[peers + FACE_ROWS + r : peers + FACE_ROWS + r + 1]
        out = jnp.where(above, up, down)
        if r == 0:
            out = jnp.where(own_group(devices, peers), shared, out)
        sent_ref[pl.ds(at + r, devices, count), :] = out


def send_same(sent_ref, count, at, row):
    devices = sent_ref.shape[0] // count
    sent_ref[pl.ds(at, devices, count), :] = jnp.broadcast_to(row, (devices, LANES))


def send_values(sent_ref, count, values, peers):
    rows = jnp.concatenate([row for pair in values for row in halves(pair)], axis=0)
    send_rows(sent_ref, count, 0, rows, peers)


def get(received_ref, count, at):
    return received_ref[pl.ds(at, received_ref.shape[0] // count, count), :]


def inside(received_ref, count, peers, away):
    groups = received_ref.shape[0] // (count * peers)
    group = lax.axis_index("grp") + away
    kept = jnp.clip(group, 0, groups - 1)
    return kept, jnp.where(group == kept, 1.0, 0.0)


def get_group(received_ref, count, at, peers, away=0):
    group, kept = inside(received_ref, count, peers, away)
    return received_ref[pl.ds(group * (peers * count) + at, peers, count), :] * kept


def get_side(received_ref, count, at, rows, peers, away):
    group, kept = inside(received_ref, count, peers, away)
    place = group * peers + lax.axis_index("sub")
    return received_ref[pl.ds(place * count + at, rows), :] * kept


def get_rows(received_ref, count, at, peers):
    sides = [get_side(received_ref, count, at, FACE_ROWS, peers, away) for away in (-1, 1)]
    return jnp.concatenate([get_group(received_ref, count, at, peers)] + sides, axis=0)


def swapped(values):
    count = len(values) // 2
    return values[count:] + values[:count]


def along_first(field, table_ref, base):
    elements = field.shape[0] // 4
    turned = pltpu.roll(field, 64, axis=1)
    out = []
    for to in range(4):
        total = None
        for at in range(4):
            place = base + 2 * (4 * to + at)
            rows = slice(at * elements, (at + 1) * elements)
            term = (
                table_ref[place : place + 1, :] * field[rows]
                + table_ref[place + 1 : place + 2, :] * turned[rows]
            )
            total = term if total is None else total + term
        out.append(total)
    return jnp.concatenate(out, axis=0)


def stiffness(field, metric_ref, first_ref, inner_ref):
    metric = [rows_of(metric_ref[:, POINTS * d : POINTS * (d + 1)]) for d in range(3)]
    count = field.shape[0]
    grad_first = along_first(field, first_ref, 0)
    high, low = split(field)
    both = jnp.dot(
        jnp.concatenate([high, low], axis=0), inner_ref[:LANES], preferred_element_type=F32
    )
    inner = both[:count] + both[count:]
    inner = inner + jnp.dot(high, inner_ref[LANES:], preferred_element_type=F32)
    flux_first = metric[0] * grad_first
    flux = jnp.concatenate([metric[1], metric[2]], axis=1) * inner
    high, low = split(flux)
    both = lax.dot_general(
        jnp.concatenate([high, low], axis=0), inner_ref[:LANES], NT, preferred_element_type=F32
    )
    back = both[:count] + both[count:]
    back = back + lax.dot_general(high, inner_ref[LANES:], NT, preferred_element_type=F32)
    back = back + along_first(flux_first, first_ref, 32)
    energy = flux * inner
    return back, flux_first * grad_first + energy[:, :LANES] + energy[:, LANES:]


def factors(points):
    nodes = 0.5 * (1.0 + np.cos(np.pi * np.arange(8) / 7.0))
    lane = lax.broadcasted_iota(jnp.int32, (1, LANES), 1)
    table = jnp.full(lane.shape, nodes[7], F32)
    for m in range(7):
        table = jnp.where(lane == m, float(nodes[m]), table)
    table = jnp.broadcast_to(table, points.shape)
    out = []
    for shift in (6, 3, 0):
        near = take(table, (points >> shift) & 7)
        out.append((near, 1.0 - near))
    return out


def corners(points):
    first, second, third = factors(points)
    return [
        first[q >> 2 & 1] * (second[q >> 1 & 1] * third[q & 1]) for q in range(8)
    ]


def own_corners():
    shape = (8, LANES)
    chunk = lax.broadcasted_iota(jnp.int32, shape, 0) & 3
    return corners(chunk * LANES + lax.broadcasted_iota(jnp.int32, shape, 1))


def flat_map(mapped):
    elements = mapped.shape[1]
    shape = (8, 8 * elements)
    lane = lax.broadcasted_iota(jnp.int32, shape, 1)
    padded = jnp.concatenate(
        [mapped.astype(F32), jnp.zeros((8, shape[1] - elements), F32)], axis=1
    )
    wide = take(padded, lane & (elements - 1))
    keep = lax.broadcasted_iota(jnp.int32, shape, 0) == lane // elements
    return jnp.sum(jnp.where(keep, wide, 0.0), axis=0, keepdims=True)


def one_vertex(flat):
    return jnp.where(one_hot(whole(flat), NC), 1.0, 0.0)


def whole(values):
    return (values + 0.5).astype(jnp.int32)


def own_element(elements, width):
    shape = (elements, width)
    return lax.broadcasted_iota(jnp.int32, shape, 0) == (
        lax.broadcasted_iota(jnp.int32, shape, 1) % elements
    )


def own_place(elements, q):
    shape = (elements, 8 * elements)
    lane = lax.broadcasted_iota(jnp.int32, shape, 1)
    return lane == lax.broadcasted_iota(jnp.int32, shape, 0) + q * elements


def coarse_part(field, vertices, inverse):
    elements = field.shape[0] // 4
    flat = jnp.zeros((elements, 8 * elements), F32)
    for q, corner in enumerate(own_corners()):
        inner = None
        for c in range(4):
            term = field[c * elements : (c + 1) * elements] * corner[c : c + 1]
            inner = term if inner is None else inner + term
        flat = jnp.where(own_place(elements, q), jnp.sum(inner, axis=1, keepdims=True), flat)
    flat = jnp.sum(flat, axis=0, keepdims=True)
    part = jnp.sum(vertices * flat, axis=1, keepdims=True)
    part = jnp.sum(inverse * part, axis=0, keepdims=True)
    return jnp.concatenate([part, jnp.zeros((1, LANES - NC), F32)], axis=1)


def get_solved(received_ref, count, peers):
    return [
        jnp.sum(get_group(received_ref, count, TERMS, peers, away), axis=0, keepdims=True)
        for away in (0, -1, 1)
    ]


def prolonged(solved, flat, elements):
    shape = (elements, LANES)
    element = lax.broadcasted_iota(jnp.int32, shape, 0)
    at_corner = take(jnp.broadcast_to(solved, shape), jnp.broadcast_to(flat, shape))
    out = [None] * 4
    for q, corner in enumerate(own_corners()):
        value = take(at_corner, element + q * elements)
        for c in range(4):
            term = value * corner[c : c + 1]
            out[c] = term if out[c] is None else out[c] + term
    return jnp.concatenate(out, axis=0)


def prolonged_at(solved, maps, points, elements):
    at_corner = take(solved, maps)
    element = (points >> 9) & (elements - 1)
    total = jnp.zeros(points.shape, F32)
    for q, corner in enumerate(corners(points)):
        total = total + corner * take(at_corner, element + q * elements)
    return total


def total_of(array):
    return jnp.sum(jnp.sum(array, axis=0, keepdims=True), axis=1, keepdims=True)


def packed(values):
    lane = lax.broadcasted_iota(jnp.int32, (1, LANES), 1)
    out = jnp.zeros((1, LANES), F32)
    for k, value in enumerate(values):
        out = jnp.where(lane == k, value, out)
    return out


def unpacked(row, count):
    lane = lax.broadcasted_iota(jnp.int32, row.shape, 1)
    return [
        jnp.sum(jnp.where(lane == k, row, 0.0), axis=1, keepdims=True) for k in range(count)
    ]


def first_kernel(
    right_hbm, jacobi_hbm, inverse_hbm, map_hbm, slot_hbm, face_hbm,
    sent_ref, fields_ref, points_ref, far_hot_ref,
    right_ref, jacobi_ref, inverse_ref, map_ref, slot_ref, face_ref, sems,
):
    copies = []
    for k, (source, target) in enumerate(
        (
            (face_hbm, face_ref),
            (slot_hbm, slot_ref),
            (right_hbm, right_ref),
            (jacobi_hbm, jacobi_ref),
            (map_hbm, map_ref),
            (inverse_hbm, inverse_ref),
        )
    ):
        copy = pltpu.make_async_copy(source, target, sems.at[k])
        copy.start()
        copies.append(copy)
    elements = right_ref.shape[0]
    peers = slot_ref.shape[1]
    for copy in copies[:2]:
        copy.wait()
    faces = face_ref[...]
    faces = jnp.concatenate(halves(faces[0:1]) + halves(faces[1:2]), axis=0)
    points = jnp.concatenate([slot_ref[0], faces], axis=0)
    points_ref[...] = points
    places = built(far_places(points, elements), far_hot_ref)
    send_rows(sent_ref, FIRST_ROWS, TERMS + 2, points.astype(F32), peers)
    for copy in copies[2:]:
        copy.wait()
    resid = rows_of(right_ref[...])
    flat = flat_map(map_ref[...])
    smoothed = rows_of(jacobi_ref[...]) * resid
    fields_ref[0 : 4 * elements, :] = resid
    fields_ref[4 * elements : 8 * elements, :] = smoothed
    fields_ref[8 * elements :, :] = jnp.broadcast_to(flat, (8, LANES))
    part = coarse_part(resid, one_vertex(flat), inverse_ref[0])
    values = gather(smoothed, places)
    send_values(sent_ref, FIRST_ROWS, values, peers)
    send_same(sent_ref, FIRST_ROWS, TERMS, part)
    send_same(sent_ref, FIRST_ROWS, TERMS + 1, flat)


def far_maps(received_ref, peers):
    own = get_group(received_ref, FIRST_ROWS, TERMS + 1, peers)
    sides = [
        jnp.broadcast_to(
            get_side(received_ref, FIRST_ROWS, TERMS + 1, 1, peers, away), (FACE_ROWS, LANES)
        )
        for away in (-1, 1)
    ]
    return whole(jnp.concatenate([own] + sides, axis=0))


def apply(
    rough, smoothed, count, received_ref, flat, maps, far_points, solved, metric_ref, helmholtz_ref,
    first_ref, inner_ref, pair_ref, pairs, points_ref, far_hot_ref, dots, back_ref, local_ref,
    sent_ref,
):
    elements = smoothed.shape[0] // 4
    peers = points_ref.shape[0] - 2 * FACE_ROWS
    far = loaded(far_places(points_ref[...], elements), far_hot_ref)
    near = gather(rough, pairs)
    partners = pair_ref[...]
    partners = jnp.concatenate(halves(partners[1:2]) + halves(partners[0:1]), axis=0)
    counts = (peers, FACE_ROWS, FACE_ROWS, partners.shape[0])
    spread = [
        jnp.broadcast_to(part, (n, LANES)) for part, n in zip((*solved, solved[0]), counts)
    ]
    coarse = prolonged_at(
        jnp.concatenate(spread, axis=0),
        jnp.concatenate([maps, jnp.broadcast_to(flat, partners.shape)], axis=0),
        jnp.concatenate([far_points, partners], axis=0),
        elements,
    )
    split_at = points_ref.shape[0]
    incoming = get_rows(received_ref, count, 0, peers) + coarse[:split_at]
    values = [value + more for value, more in zip(swapped(near), joined(coarse[split_at:]))]
    values = values + joined(incoming)
    summed = smoothed + scatter(smoothed.shape[0], pairs + far, values)
    back, energy = stiffness(summed, metric_ref, first_ref, inner_ref)
    energy = energy + rows_of(helmholtz_ref[...]) * smoothed * smoothed
    back_ref[...] = back
    values = gather(back, pairs + far)
    near = swapped(values[: len(pairs)])
    for k, value in enumerate(near):
        local_ref[0:1, k * STEP : (k + 1) * STEP] = value
    send_values(sent_ref, ROWS, values[len(pairs) :], peers)
    send_same(sent_ref, ROWS, TERMS, packed(dots + [total_of(energy)]))


def image_of(
    field_ref, back_ref, local_ref, received_ref, helmholtz_ref, pair_ref, pair_hot_ref, points_ref,
    far_hot_ref,
):
    elements = field_ref.shape[0] // 4
    peers = points_ref.shape[0] - 2 * FACE_ROWS
    chunks = loaded(pair_places(pair_ref, elements), pair_hot_ref)
    chunks = chunks + loaded(far_places(points_ref[...], elements), far_hot_ref)
    values = cut(local_ref[...]) + joined(get_rows(received_ref, ROWS, 0, peers))
    summed = back_ref[...] + scatter(field_ref.shape[0], chunks, values)
    return summed + rows_of(helmholtz_ref[...]) * field_ref[...]


def start_kernel(
    received_ref, fields_ref, points_ref, far_hot_ref, pair_ref, metric_ref, helmholtz_ref,
    first_ref, inner_ref,
    smoothed_ref, maps_ref, far_points_ref, back_ref, local_ref, sent_ref, pair_hot_ref,
):
    elements = helmholtz_ref.shape[0]
    peers = points_ref.shape[0] - 2 * FACE_ROWS
    solved = get_solved(received_ref, FIRST_ROWS, peers)
    resid = fields_ref[0 : 4 * elements, :]
    flat = whole(fields_ref[8 * elements : 8 * elements + 1, :])
    rough = fields_ref[4 * elements : 8 * elements, :]
    smoothed = rough + prolonged(solved[0], flat, elements)
    smoothed_ref[...] = smoothed
    maps = far_maps(received_ref, peers)
    maps_ref[...] = maps
    far_points = whole(get_rows(received_ref, FIRST_ROWS, TERMS + 2, peers))
    far_points_ref[...] = far_points
    apply(
        rough, smoothed, FIRST_ROWS, received_ref, flat, maps, far_points, solved, metric_ref,
        helmholtz_ref, first_ref, inner_ref, pair_ref,
        built(pair_places(pair_ref, elements), pair_hot_ref), points_ref, far_hot_ref,
        [total_of(resid * smoothed)], back_ref, local_ref, sent_ref,
    )


def middle_kernel(
    received_ref, fields_ref, points_ref, far_hot_ref, pair_ref, pair_hot_ref, jacobi_ref, helmholtz_ref,
    inverse_ref, smoothed_ref, back_ref, local_ref,
    image_ref, resid_ref, scalars_ref, sent_ref,
):
    elements = helmholtz_ref.shape[0]
    peers = points_ref.shape[0] - 2 * FACE_ROWS
    dots = jnp.sum(get(received_ref, ROWS, TERMS), axis=0, keepdims=True)
    scalars_ref[...] = dots
    values = unpacked(dots, 2)
    alpha = values[0] / values[1]
    image = image_of(
        smoothed_ref, back_ref, local_ref, received_ref, helmholtz_ref, pair_ref,
        pair_hot_ref, points_ref, far_hot_ref,
    )
    image_ref[...] = image
    resid = fields_ref[0 : 4 * elements, :] - alpha * image
    resid_ref[...] = resid
    vertices = one_vertex(fields_ref[8 * elements : 8 * elements + 1, :])
    part = coarse_part(resid, vertices, inverse_ref[0])
    values = gather(
        rows_of(jacobi_ref[...]) * resid, loaded(far_places(points_ref[...], elements), far_hot_ref),
    )
    send_values(sent_ref, ROWS, values, peers)
    send_same(sent_ref, ROWS, TERMS, part)


def second_kernel(
    received_ref, fields_ref, points_ref, far_hot_ref, pair_ref, pair_hot_ref, resid_ref, image_ref,
    maps_ref, far_points_ref, jacobi_ref, metric_ref, helmholtz_ref, first_ref, inner_ref,
    smoothed_ref, back_ref, local_ref, sent_ref,
):
    elements = helmholtz_ref.shape[0]
    peers = points_ref.shape[0] - 2 * FACE_ROWS
    solved = get_solved(received_ref, ROWS, peers)
    resid = resid_ref[...]
    flat = whole(fields_ref[8 * elements : 8 * elements + 1, :])
    rough = rows_of(jacobi_ref[...]) * resid
    smoothed = rough + prolonged(solved[0], flat, elements)
    smoothed_ref[...] = smoothed
    apply(
        rough, smoothed, ROWS, received_ref, flat, maps_ref[...], far_points_ref[...], solved, metric_ref,
        helmholtz_ref, first_ref, inner_ref, pair_ref,
        loaded(pair_places(pair_ref, elements), pair_hot_ref), points_ref, far_hot_ref,
        [total_of(resid * smoothed), total_of(image_ref[...] * smoothed)],
        back_ref, local_ref, sent_ref,
    )


def final_kernel(
    received_ref, points_ref, far_hot_ref, pair_ref, pair_hot_ref, old_ref, field_ref, resid_ref, old_image_ref,
    scalars_ref, back_ref, local_ref, helmholtz_ref,
    solution_ref, residual_ref,
):
    before = unpacked(scalars_ref[...], 2)
    now = unpacked(jnp.sum(get(received_ref, ROWS, TERMS), axis=0, keepdims=True), 3)
    alpha = before[0] / before[1]
    beta = now[0] / before[0]
    curved = now[2] + beta * (2.0 * now[1] + beta * before[1])
    step = now[0] / curved
    old = old_ref[...]
    direction = field_ref[...] + beta * old
    solution_ref[...] = wide_of(alpha * old + step * direction)
    image = image_of(
        field_ref, back_ref, local_ref, received_ref, helmholtz_ref, pair_ref,
        pair_hot_ref, points_ref, far_hot_ref,
    )
    image = image + beta * old_image_ref[...]
    residual_ref[...] = wide_of(resid_ref[...] - step * image)


def call(kernel, outs, *args, copied=False):
    space = pl.ANY if copied else pltpu.VMEM
    scratch = [pltpu.VMEM(arg.shape, arg.dtype) for arg in args] if copied else []
    if copied:
        args = [pltpu.with_memory_space_constraint(arg, pltpu.HBM) for arg in args]
    return pl.pallas_call(
        kernel,
        out_shape=[
            jax.ShapeDtypeStruct(*(out if isinstance(out[0], tuple) else (out, F32))) for out in outs
        ],
        in_specs=[pl.BlockSpec(memory_space=space)] * len(args),
        out_specs=[pl.BlockSpec(memory_space=pltpu.VMEM)] * len(outs),
        scratch_shapes=scratch + ([pltpu.SemaphoreType.DMA((len(args),))] if copied else []),
        compiler_params=pltpu.CompilerParams(vmem_limit_bytes=24 * 1024 * 1024),
    )(*args)


def body(
    right_side,
    metric,
    helmholtz,
    jacobi,
    pair_list,
    shared_slots,
    face_points,
    coarse_map,
    coarse_inverse,
):
    peers = lax.axis_size("sub")
    groups = lax.axis_size("grp")
    t = {name: jnp.asarray(value) for name, value in tables().items()}
    elements = right_side.shape[0]
    field = (4 * elements, LANES)
    local = (1, pair_list.shape[0] * pair_list.shape[1])
    points_shape = (peers + 2 * FACE_ROWS, LANES)
    sent_shape = (groups * peers * ROWS, LANES)

    def exchange(sent):
        rows = sent.reshape(groups * peers, 1, -1)
        return lax.all_to_all(rows, ("grp", "sub"), 0, 0, tiled=True).reshape(sent.shape)

    far_hot_shape = (points_shape[0] * LANES // 2, STEP)
    pair_hot_shape = (local[1] * LANES // STEP, STEP)

    sent, fields, points, far_hot = call(
        first_kernel,
        [
            (groups * peers * FIRST_ROWS, LANES),
            (8 * elements + 8, LANES),
            (points_shape, jnp.int32),
            (far_hot_shape, BF16),
        ],
        right_side, jacobi, coarse_inverse, coarse_map, shared_slots, face_points, copied=True,
    )
    smoothed, maps, far_points, back, near, sent, pair_hot = call(
        start_kernel,
        [field, (points_shape, jnp.int32), (points_shape, jnp.int32), field, local, sent_shape,
         (pair_hot_shape, BF16)],
        exchange(sent), fields, points, far_hot, pair_list, metric, helmholtz,
        t["first"], t["inner"],
    )
    image, resid, scalars, sent = call(
        middle_kernel, [field, field, (1, LANES), sent_shape],
        exchange(sent), fields, points, far_hot, pair_list, pair_hot, jacobi, helmholtz, coarse_inverse,
        smoothed, back, near,
    )
    second, back, near, sent = call(
        second_kernel, [field, field, local, sent_shape],
        exchange(sent), fields, points, far_hot, pair_list, pair_hot, resid, image, maps, far_points, jacobi,
        metric, helmholtz, t["first"], t["inner"],
    )
    return tuple(
        call(
            final_kernel, [right_side.shape, right_side.shape],
            exchange(sent), points, far_hot, pair_list, pair_hot, smoothed, second, resid, image, scalars,
            back, near, helmholtz,
        )
    )


def solution(mesh):
    in_specs = (
        P(("grp", "sub"), None),
        P(("grp", "sub"), None),
        P(("grp", "sub"), None),
        P(("grp", "sub"), None),
        P(None, ("grp", "sub")),
        P(("grp", "sub"), None, None),
        P(None, ("grp", "sub")),
        P(None, ("grp", "sub")),
        P("grp", None, None),
    )
    out_specs = (P(("grp", "sub"), None), P(("grp", "sub"), None))
    return jax.shard_map(body, mesh=mesh, in_specs=in_specs, out_specs=out_specs, check_vma=False)
```

```python
import jax
import jax.numpy as jnp
import ml_dtypes
import numpy as np
from jax import lax
from jax.experimental import pallas as pl
from jax.experimental.pallas import tpu as pltpu
from jax.sharding import PartitionSpec as P

NC = 64
POINTS = 512
LANES = 128
STEP = 256
FACE_ROWS = 4
ROWS = 5
FIRST_ROWS = 10
TERMS = FACE_ROWS
F32 = jnp.float32
BF16 = jnp.bfloat16
NT = (((1,), (1,)), ((), ()))


def split_constant(array):
    high = array.astype(ml_dtypes.bfloat16)
    low = (array - high.astype(np.float64)).astype(ml_dtypes.bfloat16)
    return high, low


def tables():
    order_index = np.arange(8)
    colloc = np.cos(np.pi * order_index / 7.0)
    end_weights = (
        np.where((order_index == 0) | (order_index == 7), 2.0, 1.0) * (-1.0) ** order_index
    )
    spacing = colloc[:, None] - colloc[None, :] + np.eye(8)
    raw_matrix = np.outer(end_weights, 1.0 / end_weights) / spacing
    off_part = raw_matrix * (1.0 - np.eye(8))
    derivative = 0.25 * (off_part - np.eye(8) * off_part.sum(axis=1)[:, None])
    along_inner = np.concatenate(
        [np.kron(np.eye(2), np.kron(derivative, np.eye(8))).T, np.kron(np.eye(16), derivative).T],
        axis=1,
    )
    high, low = split_constant(along_inner)
    inner = np.concatenate([high, low], axis=0)

    half = np.arange(LANES) // 64

    def first_rows(matrix):
        rows = []
        for to in range(4):
            for at in range(4):
                rows.append(matrix[2 * to + half, 2 * at + half])
                rows.append(matrix[2 * to + half, 2 * at + 1 - half])
        return np.stack(rows).astype(np.float32)

    return {
        "inner": inner,
        "first": np.concatenate([first_rows(derivative), first_rows(derivative.T)], axis=0),
    }


def split(value):
    high = value.astype(BF16)
    return high, (value - high.astype(F32)).astype(BF16)


def rows_of(wide):
    return jnp.concatenate([wide[:, LANES * c : LANES * (c + 1)] for c in range(4)], axis=0)


def wide_of(rows):
    elements = rows.shape[0] // 4
    return jnp.concatenate([rows[c * elements : (c + 1) * elements] for c in range(4)], axis=1)


def locate(points, elements):
    element = points >> 9
    chunk = (points >> 7) & 3
    row = jnp.where(points < elements * POINTS, chunk * elements + element, 4 * elements)
    return row, points & (LANES - 1)


def one_hot(index, count):
    steps = lax.broadcasted_iota(jnp.int32, (count, index.shape[1]), 0)
    return steps == index


def lane_hot(lane):
    steps = lax.broadcasted_iota(jnp.int32, (LANES, lane.shape[1]), 0).astype(F32).astype(BF16)
    one = jnp.ones(steps.shape, BF16)
    return jnp.where(steps == lane.astype(F32).astype(BF16), one, jnp.zeros_like(one))


def take(values, lanes):
    return jnp.take_along_axis(values, lanes, axis=1, mode="promise_in_bounds")


def gather(field, chunks):
    count = field.shape[0]
    both = jnp.concatenate(split(field), axis=0)
    out = []
    for row, hot in chunks:
        picked = jnp.dot(both, hot, preferred_element_type=F32)
        mine = jnp.where(one_hot(row, count), picked[:count] + picked[count:], 0.0)
        out.append(jnp.sum(mine, axis=0, keepdims=True))
    return out


def scatter(rows, chunks, values):
    total = jnp.zeros((2 * rows, LANES), F32)
    for at in range(0, len(chunks), 2):
        left, right = [], []
        for (row, hot), value in zip(chunks[at : at + 2], values[at : at + 2]):
            steps = lax.broadcasted_iota(jnp.int32, (rows, STEP), 0).astype(F32).astype(BF16)
            mine = steps == row.astype(F32).astype(BF16)
            parts = [jnp.where(mine, part, jnp.zeros_like(steps)) for part in split(value)]
            left.append(jnp.concatenate(parts, axis=0))
            right.append(hot)
        total = total + lax.dot_general(
            jnp.concatenate(left, axis=1),
            jnp.concatenate(right, axis=1),
            NT,
            preferred_element_type=F32,
        )
    return total[:rows] + total[rows:]


def chunked(row, lane):
    return [
        (row[:, at : at + STEP], lane[:, at : at + STEP]) for at in range(0, row.shape[1], STEP)
    ]


def cut(row):
    return [row[:, at : at + STEP] for at in range(0, row.shape[1], STEP)]


def pair_places(pair_ref, elements):
    row, lane = locate(pair_ref[...], elements)
    return chunked(row[0:1], lane[0:1]) + chunked(row[1:2], lane[1:2])


def joined(rows):
    return [
        jnp.concatenate([rows[at : at + 1], rows[at + 1 : at + 2]], axis=1)
        for at in range(0, rows.shape[0], 2)
    ]


def far_places(points, elements):
    row, lane = locate(points, elements)
    return list(zip(joined(row), joined(lane)))


def built(places, hot_ref):
    out = []
    for k, (row, lane) in enumerate(places):
        hot = lane_hot(lane)
        hot_ref[k * LANES : (k + 1) * LANES, :] = hot
        out.append((row, hot))
    return out


def loaded(places, hot_ref):
    return [
        (row, hot_ref[k * LANES : (k + 1) * LANES, :]) for k, (row, lane) in enumerate(places)
    ]


def halves(wide):
    return [wide[:, at : at + LANES] for at in range(0, wide.shape[1], LANES)]


def own_group(devices, peers, away=0):
    shape = (devices, LANES)
    return lax.broadcasted_iota(jnp.int32, shape, 0) // peers - lax.axis_index("grp") == away


def send_rows(sent_ref, count, at, rows, peers):
    devices = sent_ref.shape[0] // count
    above = own_group(devices, peers, 1)
    shared = jnp.concatenate([rows[:peers]] * (devices // peers), axis=0)
    for r in range(FACE_ROWS):
        down = rows[peers + r : peers + r + 1]
        up = rows[peers + FACE_ROWS + r : peers + FACE_ROWS + r + 1]
        out = jnp.where(above, up, down)
        if r == 0:
            out = jnp.where(own_group(devices, peers), shared, out)
        sent_ref[pl.ds(at + r, devices, count), :] = out


def send_same(sent_ref, count, at, row):
    devices = sent_ref.shape[0] // count
    sent_ref[pl.ds(at, devices, count), :] = jnp.broadcast_to(row, (devices, LANES))


def send_values(sent_ref, count, values, peers):
    rows = jnp.concatenate([row for pair in values for row in halves(pair)], axis=0)
    send_rows(sent_ref, count, 0, rows, peers)


def get(received_ref, count, at):
    return received_ref[pl.ds(at, received_ref.shape[0] // count, count), :]


def inside(received_ref, count, peers, away):
    groups = received_ref.shape[0] // (count * peers)
    group = lax.axis_index("grp") + away
    kept = jnp.clip(group, 0, groups - 1)
    return kept, jnp.where(group == kept, 1.0, 0.0)


def get_group(received_ref, count, at, peers, away=0):
    group, kept = inside(received_ref, count, peers, away)
    return received_ref[pl.ds(group * (peers * count) + at, peers, count), :] * kept


def get_side(received_ref, count, at, rows, peers, away):
    group, kept = inside(received_ref, count, peers, away)
    place = group * peers + lax.axis_index("sub")
    return received_ref[pl.ds(place * count + at, rows), :] * kept


def get_rows(received_ref, count, at, peers):
    sides = [get_side(received_ref, count, at, FACE_ROWS, peers, away) for away in (-1, 1)]
    return jnp.concatenate([get_group(received_ref, count, at, peers)] + sides, axis=0)


def swapped(values):
    count = len(values) // 2
    return values[count:] + values[:count]


def along_first(field, table_ref, base):
    elements = field.shape[0] // 4
    turned = pltpu.roll(field, 64, axis=1)
    out = []
    for to in range(4):
        total = None
        for at in range(4):
            place = base + 2 * (4 * to + at)
            rows = slice(at * elements, (at + 1) * elements)
            term = (
                table_ref[place : place + 1, :] * field[rows]
                + table_ref[place + 1 : place + 2, :] * turned[rows]
            )
            total = term if total is None else total + term
        out.append(total)
    return jnp.concatenate(out, axis=0)


def stiffness(field, metric_ref, first_ref, inner_ref):
    metric = [rows_of(metric_ref[:, POINTS * d : POINTS * (d + 1)]) for d in range(3)]
    count = field.shape[0]
    grad_first = along_first(field, first_ref, 0)
    high, low = split(field)
    both = jnp.dot(
        jnp.concatenate([high, low], axis=0), inner_ref[:LANES], preferred_element_type=F32
    )
    inner = both[:count] + both[count:]
    inner = inner + jnp.dot(high, inner_ref[LANES:], preferred_element_type=F32)
    flux_first = metric[0] * grad_first
    flux = jnp.concatenate([metric[1], metric[2]], axis=1) * inner
    high, low = split(flux)
    both = lax.dot_general(
        jnp.concatenate([high, low], axis=0), inner_ref[:LANES], NT, preferred_element_type=F32
    )
    back = both[:count] + both[count:]
    back = back + lax.dot_general(high, inner_ref[LANES:], NT, preferred_element_type=F32)
    back = back + along_first(flux_first, first_ref, 32)
    energy = flux * inner
    return back, flux_first * grad_first + energy[:, :LANES] + energy[:, LANES:]


def factors(points):
    nodes = 0.5 * (1.0 + np.cos(np.pi * np.arange(8) / 7.0))
    lane = lax.broadcasted_iota(jnp.int32, (1, LANES), 1)
    table = jnp.full(lane.shape, nodes[7], F32)
    for m in range(7):
        table = jnp.where(lane == m, float(nodes[m]), table)
    table = jnp.broadcast_to(table, points.shape)
    out = []
    for shift in (6, 3, 0):
        near = take(table, (points >> shift) & 7)
        out.append((near, 1.0 - near))
    return out


def corners(points):
    first, second, third = factors(points)
    return [
        first[q >> 2 & 1] * (second[q >> 1 & 1] * third[q & 1]) for q in range(8)
    ]


def own_corners():
    shape = (8, LANES)
    chunk = lax.broadcasted_iota(jnp.int32, shape, 0) & 3
    return corners(chunk * LANES + lax.broadcasted_iota(jnp.int32, shape, 1))


def flat_map(mapped):
    elements = mapped.shape[1]
    shape = (8, 8 * elements)
    lane = lax.broadcasted_iota(jnp.int32, shape, 1)
    padded = jnp.concatenate(
        [mapped.astype(F32), jnp.zeros((8, shape[1] - elements), F32)], axis=1
    )
    wide = take(padded, lane & (elements - 1))
    keep = lax.broadcasted_iota(jnp.int32, shape, 0) == lane // elements
    return jnp.sum(jnp.where(keep, wide, 0.0), axis=0, keepdims=True)


def one_vertex(flat):
    return jnp.where(one_hot(whole(flat), NC), 1.0, 0.0)


def whole(values):
    return (values + 0.5).astype(jnp.int32)


def own_element(elements, width):
    shape = (elements, width)
    return lax.broadcasted_iota(jnp.int32, shape, 0) == (
        lax.broadcasted_iota(jnp.int32, shape, 1) % elements
    )


def own_place(elements, q):
    shape = (elements, 8 * elements)
    lane = lax.broadcasted_iota(jnp.int32, shape, 1)
    return lane == lax.broadcasted_iota(jnp.int32, shape, 0) + q * elements


def coarse_part(field, vertices, inverse):
    elements = field.shape[0] // 4
    flat = jnp.zeros((elements, 8 * elements), F32)
    for q, corner in enumerate(own_corners()):
        inner = None
        for c in range(4):
            term = field[c * elements : (c + 1) * elements] * corner[c : c + 1]
            inner = term if inner is None else inner + term
        flat = jnp.where(own_place(elements, q), jnp.sum(inner, axis=1, keepdims=True), flat)
    flat = jnp.sum(flat, axis=0, keepdims=True)
    part = jnp.sum(vertices * flat, axis=1, keepdims=True)
    part = jnp.sum(inverse * part, axis=0, keepdims=True)
    return jnp.concatenate([part, jnp.zeros((1, LANES - NC), F32)], axis=1)


def get_solved(received_ref, count, peers):
    return [
        jnp.sum(get_group(received_ref, count, TERMS, peers, away), axis=0, keepdims=True)
        for away in (0, -1, 1)
    ]


def prolonged(solved, flat, elements):
    shape = (elements, LANES)
    element = lax.broadcasted_iota(jnp.int32, shape, 0)
    at_corner = take(jnp.broadcast_to(solved, shape), jnp.broadcast_to(flat, shape))
    out = [None] * 4
    for q, corner in enumerate(own_corners()):
        value = take(at_corner, element + q * elements)
        for c in range(4):
            term = value * corner[c : c + 1]
            out[c] = term if out[c] is None else out[c] + term
    return jnp.concatenate(out, axis=0)


def prolonged_at(solved, maps, points, elements):
    at_corner = take(solved, maps)
    element = (points >> 9) & (elements - 1)
    total = jnp.zeros(points.shape, F32)
    for q, corner in enumerate(corners(points)):
        total = total + corner * take(at_corner, element + q * elements)
    return total


def total_of(array):
    return jnp.sum(jnp.sum(array, axis=0, keepdims=True), axis=1, keepdims=True)


def packed(values):
    lane = lax.broadcasted_iota(jnp.int32, (1, LANES), 1)
    out = jnp.zeros((1, LANES), F32)
    for k, value in enumerate(values):
        out = jnp.where(lane == k, value, out)
    return out


def unpacked(row, count):
    lane = lax.broadcasted_iota(jnp.int32, row.shape, 1)
    return [
        jnp.sum(jnp.where(lane == k, row, 0.0), axis=1, keepdims=True) for k in range(count)
    ]


def first_kernel(
    right_hbm, jacobi_hbm, inverse_hbm, map_hbm, slot_hbm, face_hbm,
    sent_ref, fields_ref, points_ref, far_hot_ref, smoother_ref, solver_ref,
    right_ref, jacobi_ref, inverse_ref, map_ref, slot_ref, face_ref, sems,
):
    copies = []
    for k, (source, target) in enumerate(
        (
            (face_hbm, face_ref),
            (slot_hbm, slot_ref),
            (right_hbm, right_ref),
            (jacobi_hbm, jacobi_ref),
            (map_hbm, map_ref),
            (inverse_hbm, inverse_ref),
        )
    ):
        copy = pltpu.make_async_copy(source, target, sems.at[k])
        copy.start()
        copies.append(copy)
    elements = right_ref.shape[0]
    peers = slot_ref.shape[1]
    for copy in copies[:2]:
        copy.wait()
    faces = face_ref[...]
    faces = jnp.concatenate(halves(faces[0:1]) + halves(faces[1:2]), axis=0)
    points = jnp.concatenate([slot_ref[0], faces], axis=0)
    points_ref[...] = points
    places = built(far_places(points, elements), far_hot_ref)
    send_rows(sent_ref, FIRST_ROWS, TERMS + 2, points.astype(F32), peers)
    for copy in copies[2:]:
        copy.wait()
    resid = rows_of(right_ref[...])
    flat = flat_map(map_ref[...])
    smoother = rows_of(jacobi_ref[...])
    smoother_ref[...] = smoother
    solver_ref[...] = inverse_ref[0]
    smoothed = smoother * resid
    fields_ref[0 : 4 * elements, :] = resid
    fields_ref[4 * elements : 8 * elements, :] = smoothed
    fields_ref[8 * elements :, :] = jnp.broadcast_to(flat, (8, LANES))
    part = coarse_part(resid, one_vertex(flat), inverse_ref[0])
    values = gather(smoothed, places)
    send_values(sent_ref, FIRST_ROWS, values, peers)
    send_same(sent_ref, FIRST_ROWS, TERMS, part)
    send_same(sent_ref, FIRST_ROWS, TERMS + 1, flat)


def far_maps(received_ref, peers):
    own = get_group(received_ref, FIRST_ROWS, TERMS + 1, peers)
    sides = [
        jnp.broadcast_to(
            get_side(received_ref, FIRST_ROWS, TERMS + 1, 1, peers, away), (FACE_ROWS, LANES)
        )
        for away in (-1, 1)
    ]
    return whole(jnp.concatenate([own] + sides, axis=0))


def apply(
    rough, smoothed, count, received_ref, flat, maps, far_points, solved, metric_ref, helmholtz_ref,
    first_ref, inner_ref, pair_ref, pairs, points_ref, far_hot_ref, dots, back_ref, local_ref,
    sent_ref,
):
    elements = smoothed.shape[0] // 4
    peers = points_ref.shape[0] - 2 * FACE_ROWS
    far = loaded(far_places(points_ref[...], elements), far_hot_ref)
    near = gather(rough, pairs)
    partners = pair_ref[...]
    partners = jnp.concatenate(halves(partners[1:2]) + halves(partners[0:1]), axis=0)
    counts = (peers, FACE_ROWS, FACE_ROWS, partners.shape[0])
    spread = [
        jnp.broadcast_to(part, (n, LANES)) for part, n in zip((*solved, solved[0]), counts)
    ]
    coarse = prolonged_at(
        jnp.concatenate(spread, axis=0),
        jnp.concatenate([maps, jnp.broadcast_to(flat, partners.shape)], axis=0),
        jnp.concatenate([far_points, partners], axis=0),
        elements,
    )
    split_at = points_ref.shape[0]
    incoming = get_rows(received_ref, count, 0, peers) + coarse[:split_at]
    values = [value + more for value, more in zip(swapped(near), joined(coarse[split_at:]))]
    values = values + joined(incoming)
    summed = smoothed + scatter(smoothed.shape[0], pairs + far, values)
    back, energy = stiffness(summed, metric_ref, first_ref, inner_ref)
    energy = energy + rows_of(helmholtz_ref[...]) * smoothed * smoothed
    back_ref[...] = back
    values = gather(back, pairs + far)
    near = swapped(values[: len(pairs)])
    for k, value in enumerate(near):
        local_ref[0:1, k * STEP : (k + 1) * STEP] = value
    send_values(sent_ref, ROWS, values[len(pairs) :], peers)
    send_same(sent_ref, ROWS, TERMS, packed(dots + [total_of(energy)]))


def image_of(
    field_ref, back_ref, local_ref, received_ref, helmholtz_ref, pair_ref, pair_hot_ref, points_ref,
    far_hot_ref,
):
    elements = field_ref.shape[0] // 4
    peers = points_ref.shape[0] - 2 * FACE_ROWS
    chunks = loaded(pair_places(pair_ref, elements), pair_hot_ref)
    chunks = chunks + loaded(far_places(points_ref[...], elements), far_hot_ref)
    values = cut(local_ref[...]) + joined(get_rows(received_ref, ROWS, 0, peers))
    summed = back_ref[...] + scatter(field_ref.shape[0], chunks, values)
    return summed + rows_of(helmholtz_ref[...]) * field_ref[...]


def start_kernel(
    received_ref, fields_ref, points_ref, far_hot_ref, pair_ref, metric_ref, helmholtz_ref,
    first_ref, inner_ref,
    smoothed_ref, maps_ref, far_points_ref, back_ref, local_ref, sent_ref, pair_hot_ref,
):
    elements = helmholtz_ref.shape[0]
    peers = points_ref.shape[0] - 2 * FACE_ROWS
    solved = get_solved(received_ref, FIRST_ROWS, peers)
    resid = fields_ref[0 : 4 * elements, :]
    flat = whole(fields_ref[8 * elements : 8 * elements + 1, :])
    rough = fields_ref[4 * elements : 8 * elements, :]
    smoothed = rough + prolonged(solved[0], flat, elements)
    smoothed_ref[...] = smoothed
    maps = far_maps(received_ref, peers)
    maps_ref[...] = maps
    far_points = whole(get_rows(received_ref, FIRST_ROWS, TERMS + 2, peers))
    far_points_ref[...] = far_points
    apply(
        rough, smoothed, FIRST_ROWS, received_ref, flat, maps, far_points, solved, metric_ref,
        helmholtz_ref, first_ref, inner_ref, pair_ref,
        built(pair_places(pair_ref, elements), pair_hot_ref), points_ref, far_hot_ref,
        [total_of(resid * smoothed)], back_ref, local_ref, sent_ref,
    )


def middle_kernel(
    received_ref, fields_ref, points_ref, far_hot_ref, pair_ref, pair_hot_ref, smoother_ref, helmholtz_ref,
    solver_ref, smoothed_ref, back_ref, local_ref,
    image_ref, resid_ref, scalars_ref, sent_ref,
):
    elements = helmholtz_ref.shape[0]
    peers = points_ref.shape[0] - 2 * FACE_ROWS
    dots = jnp.sum(get(received_ref, ROWS, TERMS), axis=0, keepdims=True)
    scalars_ref[...] = dots
    values = unpacked(dots, 2)
    alpha = values[0] / values[1]
    image = image_of(
        smoothed_ref, back_ref, local_ref, received_ref, helmholtz_ref, pair_ref,
        pair_hot_ref, points_ref, far_hot_ref,
    )
    image_ref[...] = image
    resid = fields_ref[0 : 4 * elements, :] - alpha * image
    resid_ref[...] = resid
    vertices = one_vertex(fields_ref[8 * elements : 8 * elements + 1, :])
    part = coarse_part(resid, vertices, solver_ref[...])
    values = gather(
        smoother_ref[...] * resid, loaded(far_places(points_ref[...], elements), far_hot_ref),
    )
    send_values(sent_ref, ROWS, values, peers)
    send_same(sent_ref, ROWS, TERMS, part)


def second_kernel(
    received_ref, fields_ref, points_ref, far_hot_ref, pair_ref, pair_hot_ref, resid_ref, image_ref,
    maps_ref, far_points_ref, smoother_ref, metric_ref, helmholtz_ref, first_ref, inner_ref,
    smoothed_ref, back_ref, local_ref, sent_ref,
):
    elements = helmholtz_ref.shape[0]
    peers = points_ref.shape[0] - 2 * FACE_ROWS
    solved = get_solved(received_ref, ROWS, peers)
    resid = resid_ref[...]
    flat = whole(fields_ref[8 * elements : 8 * elements + 1, :])
    rough = smoother_ref[...] * resid
    smoothed = rough + prolonged(solved[0], flat, elements)
    smoothed_ref[...] = smoothed
    apply(
        rough, smoothed, ROWS, received_ref, flat, maps_ref[...], far_points_ref[...], solved, metric_ref,
        helmholtz_ref, first_ref, inner_ref, pair_ref,
        loaded(pair_places(pair_ref, elements), pair_hot_ref), points_ref, far_hot_ref,
        [total_of(resid * smoothed), total_of(image_ref[...] * smoothed)],
        back_ref, local_ref, sent_ref,
    )


def final_kernel(
    received_ref, points_ref, far_hot_ref, pair_ref, pair_hot_ref, old_ref, field_ref, resid_ref, old_image_ref,
    scalars_ref, back_ref, local_ref, helmholtz_ref,
    solution_ref, residual_ref,
):
    before = unpacked(scalars_ref[...], 2)
    now = unpacked(jnp.sum(get(received_ref, ROWS, TERMS), axis=0, keepdims=True), 3)
    alpha = before[0] / before[1]
    beta = now[0] / before[0]
    curved = now[2] + beta * (2.0 * now[1] + beta * before[1])
    step = now[0] / curved
    old = old_ref[...]
    direction = field_ref[...] + beta * old
    solution_ref[...] = wide_of(alpha * old + step * direction)
    image = image_of(
        field_ref, back_ref, local_ref, received_ref, helmholtz_ref, pair_ref,
        pair_hot_ref, points_ref, far_hot_ref,
    )
    image = image + beta * old_image_ref[...]
    residual_ref[...] = wide_of(resid_ref[...] - step * image)


def call(kernel, outs, *args, copied=False):
    space = pl.ANY if copied else pltpu.VMEM
    scratch = [pltpu.VMEM(arg.shape, arg.dtype) for arg in args] if copied else []
    if copied:
        args = [pltpu.with_memory_space_constraint(arg, pltpu.HBM) for arg in args]
    return pl.pallas_call(
        kernel,
        out_shape=[
            jax.ShapeDtypeStruct(*(out if isinstance(out[0], tuple) else (out, F32))) for out in outs
        ],
        in_specs=[pl.BlockSpec(memory_space=space)] * len(args),
        out_specs=[pl.BlockSpec(memory_space=pltpu.VMEM)] * len(outs),
        scratch_shapes=scratch + ([pltpu.SemaphoreType.DMA((len(args),))] if copied else []),
        compiler_params=pltpu.CompilerParams(vmem_limit_bytes=24 * 1024 * 1024),
    )(*args)


def body(
    right_side,
    metric,
    helmholtz,
    jacobi,
    pair_list,
    shared_slots,
    face_points,
    coarse_map,
    coarse_inverse,
):
    peers = lax.axis_size("sub")
    groups = lax.axis_size("grp")
    t = {name: jnp.asarray(value) for name, value in tables().items()}
    elements = right_side.shape[0]
    field = (4 * elements, LANES)
    local = (1, pair_list.shape[0] * pair_list.shape[1])
    points_shape = (peers + 2 * FACE_ROWS, LANES)
    sent_shape = (groups * peers * ROWS, LANES)

    def exchange(sent):
        rows = sent.reshape(groups * peers, 1, -1)
        return lax.all_to_all(rows, ("grp", "sub"), 0, 0, tiled=True).reshape(sent.shape)

    far_hot_shape = (points_shape[0] * LANES // 2, STEP)
    pair_hot_shape = (local[1] * LANES // STEP, STEP)

    sent, fields, points, far_hot, smoother, solver = call(
        first_kernel,
        [
            (groups * peers * FIRST_ROWS, LANES),
            (8 * elements + 8, LANES),
            (points_shape, jnp.int32),
            (far_hot_shape, BF16),
            field,
            (NC, NC),
        ],
        right_side, jacobi, coarse_inverse, coarse_map, shared_slots, face_points, copied=True,
    )
    smoothed, maps, far_points, back, near, sent, pair_hot = call(
        start_kernel,
        [field, (points_shape, jnp.int32), (points_shape, jnp.int32), field, local, sent_shape,
         (pair_hot_shape, BF16)],
        exchange(sent), fields, points, far_hot, pair_list, metric, helmholtz,
        t["first"], t["inner"],
    )
    image, resid, scalars, sent = call(
        middle_kernel, [field, field, (1, LANES), sent_shape],
        exchange(sent), fields, points, far_hot, pair_list, pair_hot, smoother, helmholtz, solver,
        smoothed, back, near,
    )
    second, back, near, sent = call(
        second_kernel, [field, field, local, sent_shape],
        exchange(sent), fields, points, far_hot, pair_list, pair_hot, resid, image, maps, far_points, smoother,
        metric, helmholtz, t["first"], t["inner"],
    )
    return tuple(
        call(
            final_kernel, [right_side.shape, right_side.shape],
            exchange(sent), points, far_hot, pair_list, pair_hot, smoothed, second, resid, image, scalars,
            back, near, helmholtz,
        )
    )


def solution(mesh):
    in_specs = (
        P(("grp", "sub"), None),
        P(("grp", "sub"), None),
        P(("grp", "sub"), None),
        P(("grp", "sub"), None),
        P(None, ("grp", "sub")),
        P(("grp", "sub"), None, None),
        P(None, ("grp", "sub")),
        P(None, ("grp", "sub")),
        P("grp", None, None),
    )
    out_specs = (P(("grp", "sub"), None), P(("grp", "sub"), None))
    return jax.shard_map(body, mesh=mesh, in_specs=in_specs, out_specs=out_specs, check_vma=False)
```
